32 devices in a mesh: blk: 2 (over x), dp: 16 (over z, y, core).
Axes of the slice: x: 2, y: 2, z: 4, core: 2. Of those that a mesh axis runs over, the one named last changes fastest.
Arguments:
- hidden: bfloat16 [16, 4096, 768], P('dp', 'blk'), may hold values from -6 to 6
- separators: int32 [16], P('dp'), may hold values from 1 to 4095, as said below
- out_grad: bfloat16 [16, 4096, 768], P('dp', 'blk'), may hold values from -6 to 6
- w_query: float32 [768, 384], P('dp'), may hold values from -0.21875 to 0.21875
- b_query: float32 [384], P('dp'), may hold values from -2 to 2
- w_key: float32 [768, 384], P('dp'), may hold values from -0.21875 to 0.21875
- w_value: float32 [768, 384], P('dp'), may hold values from -0.21875 to 0.21875
- b_value: float32 [384], P('dp'), may hold values from -2 to 2
- depth_kernel: float32 [768, 9], P('dp'), may hold values from -2 to 2
- w_point: float32 [768, 384], P('dp'), may hold values from -0.21875 to 0.21875
- b_keyconv: float32 [384], P('dp'), may hold values from -2 to 2
- w_kernel: float32 [384, 54], P('dp'), may hold values from -0.3125 to 0.3125
- kernel_bias: float32 [54], replicated, may hold values from -3 to 3
- w_convout: float32 [768, 384], P('dp'), may hold values from -0.21875 to 0.21875
- b_convout: float32 [384], P('dp'), may hold values from -2 to 2
- w_dense: float32 [768, 768], P('dp'), may hold values from -0.3125 to 0.3125
- b_dense: float32 [768], P('dp'), may hold values from -2 to 2
- gain_attn: float32 [768], P('dp'), may hold values from 0.5 to 1.5
- shift_attn: float32 [768], P('dp'), may hold values from -2 to 2
- w_up: float32 [2, 384, 1536], P(None, 'dp'), may hold values from -0.3125 to 0.3125
- b_up: float32 [3072], P('dp'), may hold values from -2 to 2
- w_down: float32 [2, 1536, 384], P(None, 'dp'), may hold values from -0.15625 to 0.15625
- b_down: float32 [768], P('dp'), may hold values from -2 to 2
- gain_out: float32 [768], P('dp'), may hold values from 0.5 to 1.5
- shift_out: float32 [768], P('dp'), may hold values from -2 to 2
Outputs:
- output: bfloat16 [16, 4096, 768], P('dp', 'blk')
- grad_hidden: bfloat16 [16, 4096, 768], P('dp', 'blk')
- grad_w_query: float32 [768, 384], P('dp')
- grad_b_query: float32 [384], P('dp')
- grad_w_key: float32 [768, 384], P('dp')
- grad_w_value: float32 [768, 384], P('dp')
- grad_b_value: float32 [384], P('dp')
- grad_depth_kernel: float32 [768, 9], P('dp')
- grad_w_point: float32 [768, 384], P('dp')
- grad_b_keyconv: float32 [384], P('dp')
- grad_w_kernel: float32 [384, 54], P('dp')
- grad_kernel_bias: float32 [54], replicated
- grad_w_convout: float32 [768, 384], P('dp')
- grad_b_convout: float32 [384], P('dp')
- grad_w_dense: float32 [768, 768], P('dp')
- grad_b_dense: float32 [768], P('dp')
- grad_gain_attn: float32 [768], P('dp')
- grad_shift_attn: float32 [768], P('dp')
- grad_w_up: float32 [2, 384, 1536], P(None, 'dp')
- grad_b_up: float32 [3072], P('dp')
- grad_w_down: float32 [2, 1536, 384], P(None, 'dp')
- grad_b_down: float32 [768], P('dp')
- grad_gain_out: float32 [768], P('dp')
- grad_shift_out: float32 [768], P('dp')
The draws below stay inside these ranges and needn't reach their ends.
Inputs may be any that keep to these rules, and one draw needn't show every extreme that they name: Each row's second segment starts at its separator, so both segments are nonempty. Either all even rows or all odd rows, which ones drawn from the seed, have their separator below 2048 or above 2048; the other rows' separators may lie anywhere.
All inputs are finite; a program needn't handle non-finite values.
Results may differ from the reference program's by a relative error of at most 0.034.
Values may be sent and summed in bfloat16 or wider, within the bound.
A program may use at most 256 MiB of HBM per device.

```python
import jax
import jax.numpy as jnp
from jax import lax

D = 768
FF = 3072
HEADS = 6
HD = 64
KSIZE = 9
GROUPS = 2
ATT = 384
GIN = 384
GFF = 1536
SEQ_DEV = 2048
SEQ = 4096
ROWS = 16


def draw_separators(key, part):
    key = jax.random.fold_in(key, 11)
    pick_key, side_key, edge_key, free_key = jax.random.split(key, 4)
    parity = jax.random.randint(pick_key, (), 0, 2)
    early = jax.random.randint(edge_key, (ROWS,), 1, SEQ_DEV)
    late = SEQ - early
    at_end = jax.random.randint(side_key, (ROWS,), 0, 2) == 1
    edge = jnp.where(at_end, late, early)
    anywhere = jax.random.randint(free_key, (ROWS,), 1, SEQ)
    spanning = jnp.arange(ROWS, dtype=jnp.int32) % 2 == parity
    return jnp.where(spanning, edge, anywhere).astype(jnp.int32)


def block_levels(stream_key, shape, shards, low, largest):
    level, own = 1.0, jax.random.fold_in(stream_key, 6)
    for axis_at, blocks in shards:
        heights = jnp.exp(jax.random.uniform(jax.random.fold_in(own, axis_at), (blocks,), jnp.float32, low / len(shards), largest / len(shards)))
        level = level * jnp.repeat(heights, shape[axis_at] // blocks).reshape([-1 if axis == axis_at else 1 for axis in range(len(shape))])
    return level


def scatter_about(rng, dims, scale, most, cuts=(), held_as=jnp.bfloat16):
    factor_of = block_levels(rng, dims, cuts, -0.22, 0.18) if cuts else 1.0
    values = jax.random.normal(rng, dims, jnp.float32) * scale * factor_of
    return jnp.minimum(jnp.maximum(values, -most), most).astype(held_as)


def setup_inputs(seed: int = 0) -> dict:
    splits = jax.random.split(jax.random.key(seed), 26)
    hidden = scatter_about(splits[0], (ROWS, SEQ, D), 1.0, 6.0, ((0, 16), (1, 2)))
    separators = draw_separators(jax.random.fold_in(splits[25], 71), 0)
    out_grad = scatter_about(splits[2], (ROWS, SEQ, D), 1.0, 6.0, ((0, 16), (1, 2)))
    w_query = scatter_about(splits[3], (D, ATT), D ** -0.5, 0.21875, ((0, 16),), jnp.float32)
    b_query = scatter_about(splits[4], (ATT,), 0.3, 2.0, ((0, 16),), jnp.float32)
    w_key = scatter_about(splits[5], (D, ATT), D ** -0.5, 0.21875, ((0, 16),), jnp.float32)
    w_value = scatter_about(splits[6], (D, ATT), D ** -0.5, 0.21875, ((0, 16),), jnp.float32)
    b_value = scatter_about(splits[7], (ATT,), 0.3, 2.0, ((0, 16),), jnp.float32)
    depth_kernel = scatter_about(splits[8], (D, KSIZE), KSIZE ** -0.5, 2.0, ((0, 16),), jnp.float32)
    w_point = scatter_about(splits[9], (D, ATT), D ** -0.5, 0.21875, ((0, 16),), jnp.float32)
    b_keyconv = scatter_about(splits[10], (ATT,), 0.3, 2.0, ((0, 16),), jnp.float32)
    w_kernel = scatter_about(splits[11], (ATT, HEADS * KSIZE), ATT ** -0.5, 0.3125, ((0, 16),), jnp.float32)
    kernel_bias = scatter_about(splits[12], (HEADS * KSIZE,), 0.5, 3.0, (), jnp.float32)
    w_convout = scatter_about(splits[13], (D, ATT), D ** -0.5, 0.21875, ((0, 16),), jnp.float32)
    b_convout = scatter_about(splits[14], (ATT,), 0.3, 2.0, ((0, 16),), jnp.float32)
    w_dense = scatter_about(splits[15], (D, D), ATT ** -0.5, 0.3125, ((0, 16),), jnp.float32)
    b_dense = scatter_about(splits[16], (D,), 0.3, 2.0, ((0, 16),), jnp.float32)
    gain_attn = jnp.clip(1.0 + 0.1 * jax.random.normal(splits[17], (D,), jnp.float32), 0.5, 1.5)
    shift_attn = scatter_about(splits[18], (D,), 0.3, 2.0, ((0, 16),), jnp.float32)
    w_up = scatter_about(splits[19], (GROUPS, GIN, GFF), GIN ** -0.5, 0.3125, ((1, 16),), jnp.float32)
    b_up = scatter_about(splits[20], (FF,), 0.3, 2.0, ((0, 16),), jnp.float32)
    w_down = scatter_about(splits[21], (GROUPS, GFF, GIN), GFF ** -0.5, 0.15625, ((1, 16),), jnp.float32)
    b_down = scatter_about(splits[22], (D,), 0.3, 2.0, ((0, 16),), jnp.float32)
    gain_out = jnp.clip(1.0 + 0.1 * jax.random.normal(splits[23], (D,), jnp.float32), 0.5, 1.5)
    shift_out = scatter_about(splits[24], (D,), 0.3, 2.0, ((0, 16),), jnp.float32)
    return {"hidden": hidden, "separators": separators, "out_grad": out_grad, "w_query": w_query, "b_query": b_query, "w_key": w_key, "w_value": w_value, "b_value": b_value, "depth_kernel": depth_kernel, "w_point": w_point, "b_keyconv": b_keyconv, "w_kernel": w_kernel, "kernel_bias": kernel_bias, "w_convout": w_convout, "b_convout": b_convout, "w_dense": w_dense, "b_dense": b_dense, "gain_attn": gain_attn, "shift_attn": shift_attn, "w_up": w_up, "b_up": b_up, "w_down": w_down, "b_down": b_down, "gain_out": gain_out, "shift_out": shift_out}


EPS = 1e-12
NEGATIVE = -1e+30
HIGH = lax.Precision.HIGHEST

@jax.custom_vjp
def low(v):
    return lax.optimization_barrier(v.astype(jnp.bfloat16)).astype(jnp.float32)

@jax.custom_vjp
def low_back(v):
    return v

def low_keep(v):
    return (low(v), None)

def low_pass(kept, grad):
    return (grad,)

def back_keep(v):
    return (v, None)

def back_low(kept, grad):
    return (low(grad),)
low.defvjp(low_keep, low_pass)
low_back.defvjp(back_keep, back_low)

def matmul(left, right):
    return jnp.dot(left, right, precision=HIGH, preferred_element_type=jnp.float32)

def grouped(inputs, weight):
    groups, inner, outer = weight.shape
    parts = inputs.reshape(inputs.shape[0], groups, inner)
    mixed = jnp.einsum('ngi,gio->ngo', parts, weight, precision=HIGH)
    return mixed.reshape(inputs.shape[0], groups * outer)

def layer_norm(values, gain, shift):
    centre = values - lax.optimization_barrier(jnp.mean(values, axis=-1, keepdims=True))
    spread = lax.optimization_barrier(jnp.mean(centre * centre, axis=-1, keepdims=True))
    return centre * lax.rsqrt(spread + EPS) * gain + shift

def gelu_exact(values):
    return jax.nn.gelu(values, approximate=False)

def attend_block(queries, query_seg, keys, values, key_seg):
    scale = float(HD) ** (-0.5)
    raw = jnp.einsum('qhd,khd->hqk', queries, keys, precision=HIGH) * scale
    same = query_seg[:, None] == key_seg[None, :]
    scores = low_back(jnp.where(same[None], raw, NEGATIVE))
    probs = low(jax.nn.softmax(scores, axis=-1))
    return jnp.einsum('hqk,khd->qhd', probs, values, precision=HIGH)

def forward_row(params, tokens, separator):
    lowered = tuple((item if index == 9 else low(item) for index, item in enumerate(params)))
    w_query, b_query, w_key, w_value, b_value, depth_kernel, w_point, b_keyconv, w_kernel, kernel_bias, w_convout, b_convout, w_dense, b_dense, gain_attn, shift_attn, w_up, b_up, w_down, b_down, gain_out, shift_out = lowered
    length = tokens.shape[0]
    reach = KSIZE // 2
    query = low_back(low(matmul(tokens, w_query) + b_query))
    key = low_back(low(matmul(tokens, w_key)))
    value = low_back(low(matmul(tokens, w_value) + b_value))
    convout = low_back(low(matmul(tokens, w_convout) + b_convout))
    padded = jnp.pad(tokens, ((reach, reach), (0, 0)))
    depth = sum((padded[tap:tap + length] * depth_kernel[:, tap] for tap in range(KSIZE)))
    depth = low_back(low(depth))
    keyconv = low_back(matmul(depth, w_point) + b_keyconv)
    attn_key = low_back(low(keyconv * query))
    logits = low_back(matmul(attn_key, w_kernel) + kernel_bias).reshape(length, HEADS, KSIZE)
    kernel = jax.nn.softmax(logits, axis=-1)
    conv_pad = jnp.pad(convout, ((reach, reach), (0, 0))).reshape(length + 2 * reach, HEADS, HD)
    conv = sum((kernel[:, :, tap, None] * conv_pad[tap:tap + length] for tap in range(KSIZE)))
    conv = conv.reshape(length, HEADS * HD)
    positions = jnp.arange(length, dtype=jnp.int32)
    segment = (positions >= separator).astype(jnp.int32)
    block = min(512, length)
    count = length // block
    query_blocks = query.reshape(count, block, HEADS, HD)
    key_heads = key.reshape(length, HEADS, HD)
    value_heads = value.reshape(length, HEADS, HD)

    def one_block(item):
        return attend_block(item[0], item[1], key_heads, value_heads, segment)
    attended = lax.map(jax.checkpoint(one_block), (query_blocks, segment.reshape(count, block)))
    attended = attended.reshape(length, HEADS * HD)
    context = low_back(low(jnp.concatenate([attended, conv], axis=-1)))
    dense = low_back(matmul(context, w_dense) + b_dense)
    normed = layer_norm(dense + tokens, gain_attn, shift_attn)
    upward = low_back(grouped(low(normed), w_up) + b_up)
    activated = low(gelu_exact(upward))
    downward = low_back(grouped(activated, w_down) + b_down)
    return layer_norm(downward + normed, gain_out, shift_out)

def reference(hidden, separators, out_grad, w_query, b_query, w_key, w_value, b_value, depth_kernel, w_point, b_keyconv, w_kernel, kernel_bias, w_convout, b_convout, w_dense, b_dense, gain_attn, shift_attn, w_up, b_up, w_down, b_down, gain_out, shift_out):
    params = (w_query, b_query, w_key, w_value, b_value, depth_kernel, w_point, b_keyconv, w_kernel, kernel_bias, w_convout, b_convout, w_dense, b_dense, gain_attn, shift_attn, w_up, b_up, w_down, b_down, gain_out, shift_out)

    def row_step(summed, item):
        tokens, separator, cotangent = item

        def apply(weights, inputs):
            return forward_row(weights, inputs, separator)
        result, pullback = jax.vjp(apply, params, tokens.astype(jnp.float32))
        grad_params, grad_tokens = pullback(cotangent.astype(jnp.float32))
        summed = jax.tree.map(lambda a, b: a + b, summed, grad_params)
        return (summed, (result.astype(jnp.bfloat16), grad_tokens.astype(jnp.bfloat16)))
    zeros = jax.tree.map(jnp.zeros_like, params)
    summed, outputs = lax.scan(row_step, zeros, (hidden, separators, out_grad))
    grad_w_query, grad_b_query, grad_w_key, grad_w_value, grad_b_value, grad_depth_kernel, grad_w_point, grad_b_keyconv, grad_w_kernel, grad_kernel_bias, grad_w_convout, grad_b_convout, grad_w_dense, grad_b_dense, grad_gain_attn, grad_shift_attn, grad_w_up, grad_b_up, grad_w_down, grad_b_down, grad_gain_out, grad_shift_out = summed
    return (outputs[0], outputs[1], grad_w_query, grad_b_query, grad_w_key, grad_w_value, grad_b_value, grad_depth_kernel, grad_w_point, grad_b_keyconv, grad_w_kernel, grad_kernel_bias, grad_w_convout, grad_b_convout, grad_w_dense, grad_b_dense, grad_gain_attn, grad_shift_attn, grad_w_up, grad_b_up, grad_w_down, grad_b_down, grad_gain_out, grad_shift_out)
```

```python
import functools, math
import jax, jax.numpy as jnp
from jax import lax
from jax.experimental import pallas as pl
from jax.experimental.pallas import tpu as pltpu
from jax.sharding import PartitionSpec as P

HEADS = 6
HD = 64
KSIZE = 9
REACH = 4
ATT = 384
EPS = 1e-12
BF = jnp.bfloat16
F32 = jnp.float32
MIB = 2**20
EXCLUDED = 2.0**100
SAFE_SCORE = 50.0


def mm(left, right):
    return jnp.dot(left, right, preferred_element_type=F32)


def mm_nt(left, right):
    return lax.dot_general(left, right, (((1,), (1,)), ((), ())), preferred_element_type=F32)


def mm_tn(left, right):
    return lax.dot_general(left, right, (((0,), (0,)), ((), ())), preferred_element_type=F32)


def in_lanes(rows, columns):
    lane = lax.broadcasted_iota(jnp.int32, (rows, 128), 1)
    out = jnp.zeros((rows, 128), F32)
    for at, column in enumerate(columns):
        out = jnp.where(lane == at, column, out)
    return out.astype(BF)


def in_rows(columns, rows):
    row = lax.broadcasted_iota(jnp.int32, (16, columns), 0)
    out = jnp.zeros((16, columns), F32)
    for at, values in enumerate(rows):
        out = jnp.where(row == at, values, out)
    return out.astype(BF)


def three_parts(values):
    high = values.astype(BF).astype(F32)
    rest = values - high
    middle = rest.astype(BF).astype(F32)
    return high, middle, (rest - middle).astype(BF).astype(F32)


def put_head(ref, head, values):
    odd = lax.rem(head, 2) == 1
    none = jnp.zeros_like(values)
    ref[0:HD, :] = jnp.where(odd, none, values)
    ref[HD : 2 * HD, :] = jnp.where(odd, values, none)


def attend_kernel(keys, queries, chunk, at_ref, q_ref, k_ref, v_ref, norm_ref, o_ref, p_ref, key_side, query_side):
    head, tile = pl.program_id(0), pl.program_id(1)
    separator, first_query, first_key = at_ref[0], at_ref[1], at_ref[2]

    @pl.when((head == 0) & (tile == 0))
    def start():
        position = first_key + lax.broadcasted_iota(jnp.int32, (keys, 128), 0)
        late = (position >= separator).astype(F32)
        key_side[...] = in_lanes(keys, [1.0 - late, late, 1.0, 1.0, 1.0])
        query_side[2 * HD + 16 :, :] = jnp.zeros((2 * HD - 16, queries), BF)

    put_head(query_side, head, q_ref[...])
    position = first_query + tile * queries + lax.broadcasted_iota(jnp.int32, (16, queries), 1)
    late = (position >= separator).astype(F32)
    excluded = [-EXCLUDED * late, -EXCLUDED * (1.0 - late)]
    query_side[2 * HD : 2 * HD + 16, :] = in_rows(queries, excluded)
    o_ref[0, HD + 8 : HD + 16, :] = jnp.zeros((8, queries), F32)
    wide = q_ref[...].astype(F32)
    largest = jnp.max(jnp.sum(wide * wide, axis=0, keepdims=True)) * jnp.max(norm_ref[...])

    def scores(at):
        part = slice(at * chunk, (at + 1) * chunk)
        return mm(
            jnp.concatenate([k_ref[part, :], key_side[part, :]], axis=1), query_side[...]
        )

    @pl.when(jnp.logical_not(largest <= SAFE_SCORE * SAFE_SCORE))
    def shifted():
        best = jnp.full((1, queries), -4.0 * EXCLUDED, F32)
        for at in range(keys // chunk):
            best = jnp.maximum(best, jnp.max(scores(at), axis=0, keepdims=True))
        parts = three_parts(jnp.where(best < -0.5 * EXCLUDED, 0.0, best))
        query_side[2 * HD : 2 * HD + 16, :] = in_rows(queries, excluded + [-part for part in parts])
        o_ref[0, HD + 8 : HD + 16, :] = jnp.broadcast_to(
            jnp.where(best < -0.5 * EXCLUDED, best, parts[0] + parts[1] + parts[2]), (8, queries)
        )

    ones = in_rows(chunk, [1.0])
    total = jnp.zeros((HD + 16, queries), F32)
    for at in range(keys // chunk):
        part = slice(at * chunk, (at + 1) * chunk)
        probs = jnp.exp(scores(at)).astype(BF)
        p_ref[0, part, :] = probs
        total = total + mm(jnp.concatenate([v_ref[:, part], ones], axis=0), probs)
    o_ref[0, 0 : HD + 8, :] = total[0 : HD + 8, :]


def attend(at, query_t, key, value_t, norms):
    tokens, keys = query_t.shape[1], key.shape[0]
    queries, chunk = math.gcd(tokens, 1024), math.gcd(keys, 512)
    return pl.pallas_call(
        functools.partial(attend_kernel, keys, queries, chunk),
        grid=(HEADS, tokens // queries),
        in_specs=[
            pl.BlockSpec(memory_space=pltpu.SMEM),
            pl.BlockSpec((HD, queries), lambda h, i: (h, i)),
            pl.BlockSpec((keys, 2 * HD), lambda h, i: (0, h // 2)),
            pl.BlockSpec((HD, keys), lambda h, i: (h, 0)),
            pl.BlockSpec(norms.shape, lambda h, i: (0, 0)),
        ],
        out_specs=[
            pl.BlockSpec((1, HD + 16, queries), lambda h, i: (h, 0, i)),
            pl.BlockSpec((1, keys, queries), lambda h, i: (h, 0, i)),
        ],
        out_shape=[
            jax.ShapeDtypeStruct((HEADS, HD + 16, tokens), F32),
            jax.ShapeDtypeStruct((HEADS, keys, tokens), BF),
        ],
        scratch_shapes=[pltpu.VMEM((keys, 128), BF), pltpu.VMEM((4 * HD, queries), BF)],
        compiler_params=pltpu.CompilerParams(vmem_limit_bytes=56 * MIB),
        cost_estimate=pl.CostEstimate(
            flops=16 * ATT * tokens * keys,
            bytes_accessed=2 * HEADS * tokens * keys,
            transcendentals=HEADS * tokens * keys,
        ),
        name="attend",
    )(at, query_t, key, value_t, norms)


def attend_back_kernel(keys, queries, chunk, p_ref, v_ref, kt_ref, g_ref, side_ref, q_ref, dq_ref, dk_ref, dv_ref, value_side, grad_side, dk_sum, dv_sum):
    head, tile = pl.program_id(0), pl.program_id(1)

    @pl.when((head == 0) & (tile == 0))
    def start():
        value_side[...] = in_lanes(chunk, [1.0, 1.0, 1.0])
        grad_side[2 * HD + 16 :, :] = jnp.zeros((2 * HD - 16, queries), BF)

    @pl.when(tile == 0)
    def fresh():
        dk_sum[...] = jnp.zeros_like(dk_sum)
        dv_sum[...] = jnp.zeros_like(dv_sum)

    put_head(grad_side, head, g_ref[...])
    grad_side[2 * HD : 2 * HD + 16, :] = side_ref[0]
    total = jnp.zeros((HD, queries), F32)
    for at in range(keys // chunk):
        part = slice(at * chunk, (at + 1) * chunk)
        probs = p_ref[0, part, :]
        spread = mm(jnp.concatenate([v_ref[part, :], value_side[...]], axis=1), grad_side[...])
        grad_scores = (probs.astype(F32) * spread).astype(BF)
        dv_sum[:, part] += mm_nt(g_ref[...], probs)
        dk_sum[:, part] += mm_nt(q_ref[...], grad_scores)
        total = total + mm(kt_ref[:, part], grad_scores)
    dq_ref[...] = total * (HD**-0.5)

    @pl.when(tile == pl.num_programs(1) - 1)
    def finish():
        dk_ref[...] = dk_sum[...].astype(dk_ref.dtype)
        dv_ref[...] = dv_sum[...].astype(dv_ref.dtype)


def attend_back(probs, value, key_t, grad_t, side, query_t, out_type):
    tokens, keys = query_t.shape[1], value.shape[0]
    queries, chunk = math.gcd(tokens, 512), math.gcd(keys, 512)
    by_token = pl.BlockSpec((HD, queries), lambda h, i: (h, i))
    by_key = pl.BlockSpec((HD, keys), lambda h, i: (h, 0))
    return pl.pallas_call(
        functools.partial(attend_back_kernel, keys, queries, chunk),
        grid=(HEADS, tokens // queries),
        in_specs=[
            pl.BlockSpec((1, keys, queries), lambda h, i: (h, 0, i)),
            pl.BlockSpec((keys, 2 * HD), lambda h, i: (0, h // 2)),
            by_key,
            by_token,
            pl.BlockSpec((1, 16, queries), lambda h, i: (h, 0, i)),
            by_token,
        ],
        out_specs=[by_token, by_key, by_key],
        out_shape=[
            jax.ShapeDtypeStruct((ATT, tokens), F32),
            jax.ShapeDtypeStruct((ATT, keys), out_type),
            jax.ShapeDtypeStruct((ATT, keys), out_type),
        ],
        scratch_shapes=[
            pltpu.VMEM((chunk, 128), BF),
            pltpu.VMEM((4 * HD, queries), BF),
            pltpu.VMEM((HD, keys), F32),
            pltpu.VMEM((HD, keys), F32),
        ],
        compiler_params=pltpu.CompilerParams(vmem_limit_bytes=56 * MIB),
        cost_estimate=pl.CostEstimate(
            flops=32 * ATT * tokens * keys,
            bytes_accessed=2 * HEADS * tokens * keys,
            transcendentals=0,
        ),
        name="attend_back",
    )(probs, value, key_t, grad_t, side, query_t)


def all_of(shape):
    return pl.BlockSpec(shape, lambda *at: (0,) * len(shape))


def rows_of(rows, width):
    return pl.BlockSpec((rows, width), lambda i: (i, 0))


def columns_of(height, columns):
    return pl.BlockSpec((height, columns), lambda i: (0, i))


def run_tiles(kernel, name, steps, inputs, outputs, scratch, flops):
    args, in_specs = zip(*inputs)
    shapes, out_specs = zip(*outputs)
    size = sum(math.prod(v.shape) * v.dtype.itemsize for v in args + shapes)
    return pl.pallas_call(
        kernel,
        grid=(steps,),
        in_specs=list(in_specs),
        out_specs=list(out_specs),
        out_shape=list(shapes),
        scratch_shapes=scratch,
        compiler_params=pltpu.CompilerParams(vmem_limit_bytes=60 * MIB),
        cost_estimate=pl.CostEstimate(flops=flops, bytes_accessed=size, transcendentals=0),
        name=name,
    )(*args)


def shaped(shape, dtype):
    return jax.ShapeDtypeStruct(shape, dtype)


def project_kernel(parts, x_ref, w_ref, bias_ref, bias_t_ref, *refs):
    norm_ref, flipped = refs[2 * parts], refs[2 * parts + 1]

    @pl.when(pl.program_id(0) == 0)
    def start():
        norm_ref[...] = jnp.zeros_like(norm_ref)
        flipped[...] = w_ref[...].T

    x = x_ref[...]
    plain = mm(x, w_ref[...]) + bias_ref[...]
    turned = mm_nt(flipped[...], x) + bias_t_ref[...]
    for part in range(parts):
        own = slice(part * ATT, (part + 1) * ATT)
        refs[2 * part][...] = plain[:, own].astype(BF)
        across = turned[own].astype(BF)
        if part == parts - 2:
            wide = across.astype(F32)
            for head in range(HEADS):
                cells = wide[head * HD : (head + 1) * HD]
                size = jnp.sum(cells * cells, axis=0, keepdims=True)
                norm_ref[...] = jnp.maximum(norm_ref[...], size)
        if part < parts - 2:
            across = (turned[own].astype(BF).astype(F32) * (HD**-0.5)).astype(BF)
        refs[2 * part + 1][...] = across


def project(x, weight, bias):
    tokens, width = x.shape
    parts = weight.shape[1] // ATT
    tile = math.gcd(tokens, 512)
    outputs = []
    for part in range(parts):
        outputs.append((shaped((tokens, ATT), BF), rows_of(tile, ATT)))
        outputs.append((shaped((ATT, tokens), BF), columns_of(ATT, tile)))
    outputs.append((shaped((8, tile), F32), all_of((8, tile))))
    return run_tiles(
        functools.partial(project_kernel, parts),
        "project",
        tokens // tile,
        [
            (x, rows_of(tile, width)),
            (weight, all_of(weight.shape)),
            (bias, all_of(bias.shape)),
            (bias.reshape(-1, 1), all_of((bias.shape[1], 1))),
        ],
        outputs,
        [pltpu.VMEM((weight.shape[1], width), BF)],
        4 * tokens * width * weight.shape[1],
    )


def fill_window(window, x_ref, halo_ref, tile, rows):
    first = tile * rows
    tokens = x_ref.shape[0]
    before = x_ref[pl.ds(pl.multiple_of(jnp.maximum(first - 16, 0), 16), 16), :]
    after = x_ref[pl.ds(pl.multiple_of(jnp.minimum(first + rows, tokens - 16), 16), 16), :]
    window[0:16, :] = jnp.where(tile == 0, halo_ref[0:16, :], before).astype(window.dtype)
    window[16 : 16 + rows, :] = x_ref[pl.ds(pl.multiple_of(first, rows), rows), :].astype(window.dtype)
    window[16 + rows :, :] = jnp.where(
        tile == pl.num_programs(0) - 1, halo_ref[16:32, :], after
    ).astype(window.dtype)


def fill_spread(spread):
    row = lax.broadcasted_iota(jnp.int32, (128, ATT), 0)
    head = lax.broadcasted_iota(jnp.int32, (128, ATT), 1) // HD
    for tap in range(KSIZE):
        spread[:, tap * ATT : (tap + 1) * ATT] = (row == tap * 8 + head).astype(F32).astype(BF)


def mix_kernel(rows, at_ref, x_ref, halo_ref, q_ref, taps_ref, wc_ref, bc_ref, wp_ref, bp_ref, wk_ref, bk_ref, depth_ref, keyconv_ref, attn_ref, kernt_ref, kern_ref, conv_ref, out_ref, rim_ref, window, conv_window, spread):
    tile = pl.program_id(0)
    last = pl.num_programs(0) - 1

    @pl.when(tile == 0)
    def start():
        fill_spread(spread)

    fill_window(window, x_ref, halo_ref, tile, rows)
    width = window.shape[1]
    for at in range(0, width, 128):
        some = slice(at, at + 128)
        total = jnp.zeros((rows, 128), F32)
        for tap in range(KSIZE):
            total = total + window[12 + tap : 12 + tap + rows, some] * taps_ref[tap : tap + 1, some]
        depth_ref[:, some] = total.astype(BF)
    position = (
        at_ref[1] + tile * rows - 16 + lax.broadcasted_iota(jnp.int32, (rows + 32, ATT), 0)
    )
    inside = (position >= 0) & (position < at_ref[3])
    values = mm(window[...].astype(BF), wc_ref[...]) + bc_ref[...]
    values = jnp.where(inside, values, 0.0).astype(BF)
    out_ref[...] = values[16 : 16 + rows]

    @pl.when(tile == 0)
    def first_rim():
        rim_ref[0:16, :] = values[0:16]

    @pl.when(tile == last)
    def last_rim():
        rim_ref[16:32, :] = values[16 + rows :]

    conv_window[...] = values.astype(F32)
    keyconv = mm(depth_ref[...], wp_ref[...]) + bp_ref[...]
    keyconv_ref[...] = keyconv
    attn_key = (keyconv * q_ref[...].astype(F32)).astype(BF)
    attn_ref[...] = attn_key
    logits = mm_nt(wk_ref[...], attn_key) + bk_ref[...]
    slabs = [logits[8 * tap : 8 * tap + 8] for tap in range(KSIZE)]
    best = functools.reduce(jnp.maximum, slabs)
    slabs = [jnp.exp(slab - best) for slab in slabs]
    share = 1.0 / functools.reduce(jnp.add, slabs)
    slabs = [slab * share for slab in slabs]
    kernt = jnp.concatenate(slabs + [jnp.zeros((128 - 8 * KSIZE, rows), F32)], axis=0)
    kernt_ref[...] = kernt[0 : 8 * KSIZE]
    kern = kernt.astype(BF).T
    kern_ref[...] = kern
    total = jnp.zeros((rows, ATT), F32)
    for tap in range(KSIZE):
        total = total + mm(kern, spread[:, tap * ATT : (tap + 1) * ATT]) * conv_window[12 + tap : 12 + tap + rows, :]
    conv_ref[...] = total.astype(BF)


def mix(at, x, halo, query, taps, w_convout, b_convout, w_point, b_keyconv, w_kernel, kernel_bias):
    tokens, width = x.shape
    rows = math.gcd(tokens, 256)
    whole = [(v, all_of(v.shape)) for v in (taps, w_convout, b_convout, w_point, b_keyconv, w_kernel, kernel_bias)]
    return run_tiles(
        functools.partial(mix_kernel, rows),
        "mix",
        tokens // rows,
        [
            (at, pl.BlockSpec(memory_space=pltpu.SMEM)),
            (x, all_of(x.shape)),
            (halo, all_of(halo.shape)),
            (query, rows_of(rows, ATT)),
        ]
        + whole,
        [
            (shaped((tokens, width), BF), rows_of(rows, width)),
            (shaped((tokens, ATT), F32), rows_of(rows, ATT)),
            (shaped((tokens, ATT), BF), rows_of(rows, ATT)),
            (shaped((8 * KSIZE, tokens), F32), columns_of(8 * KSIZE, rows)),
            (shaped((tokens, 128), BF), rows_of(rows, 128)),
            (shaped((tokens, ATT), BF), rows_of(rows, ATT)),
            (shaped((tokens, ATT), BF), rows_of(rows, ATT)),
            (shaped((32, ATT), BF), all_of((32, ATT))),
        ],
        [
            pltpu.VMEM((rows + 32, width), F32),
            pltpu.VMEM((rows + 32, ATT), F32),
            pltpu.VMEM((128, KSIZE * ATT), BF),
        ],
        4 * tokens * width * ATT * 4,
    )


def normal(values):
    centre = values - jnp.mean(values, axis=-1, keepdims=True)
    scale = lax.rsqrt(jnp.mean(centre * centre, axis=-1, keepdims=True) + EPS)
    return centre * scale, scale


def normal_back(grad, unit, scale):
    return scale * (
        grad
        - jnp.mean(grad, axis=-1, keepdims=True)
        - unit * jnp.mean(grad * unit, axis=-1, keepdims=True)
    )


def gelu_parts(values):
    size = jnp.abs(values)
    t = 1.0 / (1.0 + (0.3275911 * math.sqrt(0.5)) * size)
    tail = t * (
        0.5 * 0.254829592
        + t * (0.5 * -0.284496736 + t * (0.5 * 1.421413741 + t * (0.5 * -1.453152027 + t * (0.5 * 1.061405429))))
    )
    bell = jnp.exp(-0.5 * values * values)
    tail = tail * bell
    share = jnp.where(values < 0.0, tail, 1.0 - tail)
    return values * share, share + values * (bell * (1.0 / math.sqrt(2.0 * math.pi)))


def middle_kernel(blocks, rows, units, *refs):
    o_refs, refs = refs[:blocks], refs[blocks:]
    (conv_ref, x_ref, og_ref, wd_ref, wu_ref, wn_ref, vec_ref, bu_ref), refs = refs[:8], refs[8:]
    (out_ref, sum_ref, gconv_ref), refs = refs[:3], refs[3:]
    g_refs, refs = refs[:blocks], refs[blocks:]
    side_refs, refs = refs[:blocks], refs[blocks:]
    (gwd_ref, gwu_ref, gwn_ref, gvec_ref, gbu_ref, wd_sum, wu_sum, wn_sum, acts, slopes) = refs
    tile = pl.program_id(0)
    hidden_units = wu_ref.shape[1]
    groups = 2
    inner = ATT
    outer = hidden_units // groups

    @pl.when(tile == 0)
    def start():
        for ref in (wd_sum, wu_sum, wn_sum, gvec_ref, gbu_ref):
            ref[...] = jnp.zeros_like(ref)

    shifts = [ref[:, HD + 8 : HD + 9, :] for ref in o_refs]
    top = functools.reduce(jnp.maximum, shifts)
    weights = [jnp.exp(shift - top) for shift in shifts]
    mass = functools.reduce(jnp.add, [w * ref[:, HD : HD + 1, :] for w, ref in zip(weights, o_refs)])
    weights = [w / mass for w in weights]
    heads = functools.reduce(jnp.add, [w * ref[:, 0:HD, :] for w, ref in zip(weights, o_refs)])
    att_t = heads.reshape(ATT, rows).astype(BF)
    conv = conv_ref[...]
    vec = [vec_ref[at : at + 1, :] for at in range(6)]
    dense = mm(att_t.T, wd_ref[0:ATT, :]) + mm(conv, wd_ref[ATT:, :]) + vec[0]
    unit_one, scale_one = normal(dense + x_ref[...].astype(F32))
    normed = unit_one * vec[1] + vec[2]
    low = normed.astype(BF)
    downs = []
    for group in range(groups):
        mine = low[:, group * inner : (group + 1) * inner]
        down = jnp.zeros((rows, inner), F32)
        for at in range(0, outer, units):
            here = slice(group * outer + at, group * outer + at + units)
            upward = mm(mine, wu_ref[:, here]) + bu_ref[:, here]
            act, slope = gelu_parts(upward)
            act = act.astype(BF)
            acts[:, here] = act
            slopes[:, here] = slope.astype(BF)
            down = down + mm(act, wn_ref[at : at + units, group * inner : (group + 1) * inner])
        downs.append(down)
    unit_two, scale_two = normal(jnp.concatenate(downs, axis=1) + vec[3] + normed)
    out_ref[...] = (unit_two * vec[4] + vec[5]).astype(BF)
    og = og_ref[...].astype(F32)
    gvec_ref[4:5, :] += jnp.sum(og * unit_two, axis=0, keepdims=True)
    gvec_ref[5:6, :] += jnp.sum(og, axis=0, keepdims=True)
    grad_two = normal_back(og * vec[4], unit_two, scale_two)
    grad_down = grad_two.astype(BF)
    gvec_ref[3:4, :] += jnp.sum(grad_down.astype(F32), axis=0, keepdims=True)
    backs = []
    for group in range(groups):
        lanes = slice(group * inner, (group + 1) * inner)
        mine, grads = low[:, lanes], grad_down[:, lanes]
        mine_t = mine.T
        back = jnp.zeros((rows, inner), F32)
        for at in range(0, outer, units):
            here = slice(group * outer + at, group * outer + at + units)
            grad_act = mm_nt(grads, wn_ref[at : at + units, lanes])
            grad_up = (grad_act * slopes[:, here].astype(F32)).astype(BF)
            gbu_ref[0:1, here] += jnp.sum(grad_up.astype(F32), axis=0, keepdims=True)
            wn_sum[at : at + units, lanes] += mm_tn(acts[:, here], grads)
            wu_sum[:, here] += mm(mine_t, grad_up)
            back = back + mm_nt(grad_up, wu_ref[:, here])
        backs.append(back)
    grad_normed = grad_two + jnp.concatenate(backs, axis=1)
    gvec_ref[1:2, :] += jnp.sum(grad_normed * unit_one, axis=0, keepdims=True)
    gvec_ref[2:3, :] += jnp.sum(grad_normed, axis=0, keepdims=True)
    grad_one = normal_back(grad_normed * vec[1], unit_one, scale_one)
    sum_ref[...] = grad_one
    grad_dense = grad_one.astype(BF)
    gvec_ref[0:1, :] += jnp.sum(grad_dense.astype(F32), axis=0, keepdims=True)
    wd_sum[0:ATT, :] += mm(att_t, grad_dense)
    wd_sum[ATT:, :] += mm_tn(conv, grad_dense)
    gconv_ref[...] = mm_nt(grad_dense, wd_ref[ATT:, :]).astype(BF)
    grad_att = mm_nt(wd_ref[0:ATT, :], grad_dense).astype(BF).astype(F32).reshape(HEADS, HD, rows)
    for weight, g_ref, side_ref in zip(weights, g_refs, side_refs):
        share = (grad_att * weight).astype(BF)
        g_ref[...] = share.reshape(ATT, rows)
        delta = -jnp.sum(share.astype(F32) * heads, axis=1, keepdims=True)
        row = lax.broadcasted_iota(jnp.int32, (HEADS, 16, rows), 1)
        side = jnp.zeros((HEADS, 16, rows), F32)
        for at, part in enumerate(three_parts(delta)):
            side = jnp.where(row == at, part, side)
        side_ref[...] = side.astype(BF)

    @pl.when(tile == pl.num_programs(0) - 1)
    def finish():
        gwd_ref[...] = wd_sum[...].astype(BF)
        gwu_ref[...] = wu_sum[...].astype(BF)
        gwn_ref[...] = wn_sum[...].astype(BF)


def middle(outs, conv, x, out_grad, w_dense, w_up, w_down, vectors, b_up):
    tokens, width = x.shape
    rows = math.gcd(tokens, 256)
    blocks = len(outs)
    heads = pl.BlockSpec((HEADS, HD + 16, rows), lambda i: (0, 0, i))
    side = pl.BlockSpec((HEADS, 16, rows), lambda i: (0, 0, i))
    once = [(v, all_of(v.shape)) for v in (w_dense, w_up, w_down, vectors, b_up)]
    results = run_tiles(
        functools.partial(middle_kernel, blocks, rows, 512),
        "middle",
        tokens // rows,
        [(o, heads) for o in outs]
        + [
            (conv, rows_of(rows, ATT)),
            (x, rows_of(rows, width)),
            (out_grad, rows_of(rows, width)),
        ]
        + once,
        [
            (shaped((tokens, width), BF), rows_of(rows, width)),
            (shaped((tokens, width), F32), rows_of(rows, width)),
            (shaped((tokens, ATT), BF), rows_of(rows, ATT)),
        ]
        + [(shaped((ATT, tokens), BF), columns_of(ATT, rows))] * blocks
        + [(shaped((HEADS, 16, tokens), BF), side)] * blocks
        + [
            (shaped(w_dense.shape, BF), all_of(w_dense.shape)),
            (shaped(w_up.shape, BF), all_of(w_up.shape)),
            (shaped(w_down.shape, BF), all_of(w_down.shape)),
            (shaped((8, width), F32), all_of((8, width))),
            (shaped((8, w_up.shape[1]), F32), all_of((8, w_up.shape[1]))),
        ],
        [
            pltpu.VMEM(w_dense.shape, F32),
            pltpu.VMEM(w_up.shape, F32),
            pltpu.VMEM(w_down.shape, F32),
            pltpu.VMEM((rows, w_up.shape[1]), BF),
            pltpu.VMEM((rows, w_up.shape[1]), BF),
        ],
        6 * tokens * (w_dense.size + w_up.size + w_down.size),
    )
    output, grad_sum, grad_conv = results[:3]
    return output, grad_sum, grad_conv, results[3 : 3 + blocks], results[3 + blocks : 3 + 2 * blocks], results[3 + 2 * blocks :]


def mix_back_kernel(rows, x_ref, halo_ref, values_ref, rim_ref, gconv_ref, kernt_ref, kern_ref, q_ref, keyconv_ref, attn_ref, depth_ref, wp_ref, wk_ref, gq_ref, gdepth_ref, gvalues_ref, gwp_ref, gwk_ref, gbias_ref, gtaps_ref, window, conv_window, summed, products, spread, wp_sum):
    tile = pl.program_id(0)

    @pl.when(tile == 0)
    def start():
        fill_spread(spread)
        for ref in (gvalues_ref, wp_sum, gwk_ref, gbias_ref, gtaps_ref):
            ref[...] = jnp.zeros_like(ref)

    fill_window(window, x_ref, halo_ref, tile, rows)
    fill_window(conv_window, values_ref, rim_ref, tile, rows)
    summed[...] = jnp.zeros_like(summed)
    grad_conv = gconv_ref[...].astype(F32)
    for tap in range(KSIZE):
        here = slice(tap * ATT, (tap + 1) * ATT)
        there = slice(12 + tap, 12 + tap + rows)
        products[:, here] = (grad_conv * conv_window[there, :]).astype(BF)
        summed[there, :] += mm(kern_ref[...], spread[:, here]) * grad_conv
    first = pl.multiple_of(tile * rows, rows)
    gvalues_ref[pl.ds(first, rows + 32), :] += summed[...]
    grad_kernel = mm_nt(spread[...], products[...])
    slabs = [slice(8 * tap, 8 * tap + 8) for tap in range(KSIZE)]
    kernels = [kernt_ref[slab, :] for slab in slabs]
    mean = functools.reduce(jnp.add, [k * grad_kernel[slab] for k, slab in zip(kernels, slabs)])
    grad_logits = jnp.concatenate(
        [k * (grad_kernel[slab] - mean) for k, slab in zip(kernels, slabs)], axis=0
    ).astype(BF)
    wide_logits = grad_logits.astype(F32)
    gbias_ref[...] += jnp.concatenate(
        [
            jnp.broadcast_to(jnp.sum(wide_logits, axis=1, keepdims=True), (8 * KSIZE, 128)),
            jnp.zeros((8, 128), F32),
        ],
        axis=0,
    )
    gwk_ref[0 : 8 * KSIZE, :] += mm(grad_logits, attn_ref[...])
    grad_attn = mm_tn(grad_logits, wk_ref[...]).astype(BF).astype(F32)
    grad_keyconv = (grad_attn * q_ref[...].astype(F32)).astype(BF)
    gq_ref[...] = grad_attn * keyconv_ref[...]
    gwk_ref[8 * KSIZE : 8 * KSIZE + 1, :] += jnp.sum(grad_keyconv.astype(F32), axis=0, keepdims=True)
    wp_sum[...] += mm_tn(depth_ref[...], grad_keyconv)
    grad_depth = mm_nt(grad_keyconv, wp_ref[...]).astype(BF)
    gdepth_ref[...] = grad_depth
    wide = grad_depth.astype(F32)
    for at in range(0, window.shape[1], 128):
        some = slice(at, at + 128)
        for tap in range(KSIZE):
            gtaps_ref[tap : tap + 1, some] += jnp.sum(
                wide[:, some] * window[12 + tap : 12 + tap + rows, some], axis=0, keepdims=True
            )

    @pl.when(tile == pl.num_programs(0) - 1)
    def finish():
        gwp_ref[...] = wp_sum[...].astype(BF)


def mix_back(x, halo, values, rim, grad_conv, kernt, kern, query, keyconv, attn_key, depth, w_point, w_kernel):
    tokens, width = x.shape
    rows = math.gcd(tokens, 256)
    by_rows = [(v, rows_of(rows, v.shape[1])) for v in (kern, query, keyconv, attn_key, depth)]
    return run_tiles(
        functools.partial(mix_back_kernel, rows),
        "mix_back",
        tokens // rows,
        [(v, all_of(v.shape)) for v in (x, halo, values, rim)]
        + [(grad_conv, rows_of(rows, ATT)), (kernt, columns_of(8 * KSIZE, rows))]
        + by_rows
        + [(v, all_of(v.shape)) for v in (w_point, w_kernel)],
        [
            (shaped((tokens, ATT), F32), rows_of(rows, ATT)),
            (shaped((tokens, width), BF), rows_of(rows, width)),
            (shaped((tokens + 32, ATT), F32), all_of((tokens + 32, ATT))),
            (shaped(w_point.shape, BF), all_of(w_point.shape)),
            (shaped((8 * KSIZE + 8, ATT), F32), all_of((8 * KSIZE + 8, ATT))),
            (shaped((8 * KSIZE + 8, 128), F32), all_of((8 * KSIZE + 8, 128))),
            (shaped((16, width), F32), all_of((16, width))),
        ],
        [
            pltpu.VMEM((rows + 32, width), F32),
            pltpu.VMEM((rows + 32, ATT), F32),
            pltpu.VMEM((rows + 32, ATT), F32),
            pltpu.VMEM((rows, KSIZE * ATT), BF),
            pltpu.VMEM((128, KSIZE * ATT), BF),
            pltpu.VMEM(w_point.shape, F32),
        ],
        4 * tokens * width * ATT * 4,
    )


def finish_kernel(blocks, rows, *refs):
    dq_refs, refs = refs[:blocks], refs[blocks:]
    dk_refs, refs = refs[:blocks], refs[blocks:]
    dv_refs, refs = refs[:blocks], refs[blocks:]
    (x_ref, gq_ref, gvalues_ref, rim_ref, gdepth_ref, halo_ref, sum_ref, w_ref, taps_ref), refs = refs[:9], refs[9:]
    gh_ref, gw_ref, gb_ref, window, w_sum, grads = refs
    tile = pl.program_id(0)
    last = pl.num_programs(0) - 1

    @pl.when(tile == 0)
    def start():
        w_sum[...] = jnp.zeros_like(w_sum)
        gb_ref[...] = jnp.zeros_like(gb_ref)

    def total(some):
        return functools.reduce(jnp.add, [ref[...].astype(F32) for ref in some])

    grads[:, 0:ATT] = (total(dq_refs).T + gq_ref[...]).astype(BF)
    grads[:, ATT : 2 * ATT] = total(dk_refs).astype(BF).T
    grads[:, 2 * ATT : 3 * ATT] = total(dv_refs).astype(BF).T
    first = pl.multiple_of(tile * rows, rows)
    own = gvalues_ref[pl.ds(first + 16, rows), :]
    zero = jnp.zeros((16, ATT), F32)
    before = jnp.where(tile == 0, rim_ref[0:16, :].astype(F32), zero)
    after = jnp.where(tile == last, rim_ref[16:32, :].astype(F32), zero)
    own = jnp.concatenate([own[0:16] + before, own[16 : rows - 16], own[rows - 16 :] + after], axis=0)
    grads[:, 3 * ATT :] = own.astype(BF)
    every = grads[...]
    gb_ref[0:1, :] += jnp.sum(every.astype(F32), axis=0, keepdims=True)
    w_sum[...] += mm(x_ref[...].T, every)
    back = mm_nt(every, w_ref[...])
    fill_window(window, gdepth_ref, halo_ref, tile, rows)
    for at in range(0, window.shape[1], 128):
        some = slice(at, at + 128)
        depth = back[:, some] + sum_ref[:, some]
        for tap in range(KSIZE):
            depth = depth + window[20 - tap : 20 - tap + rows, some] * taps_ref[tap : tap + 1, some]
        gh_ref[:, some] = depth.astype(BF)

    @pl.when(tile == last)
    def finish():
        gw_ref[...] = w_sum[...].astype(BF)


def finish(dqs, dks, dvs, x, grad_query, grad_values, rim, grad_depth, halo, grad_sum, weight, taps):
    tokens, width = x.shape
    rows = math.gcd(tokens, 256)
    blocks = len(dqs)
    return run_tiles(
        functools.partial(finish_kernel, blocks, rows),
        "finish",
        tokens // rows,
        [(v, columns_of(ATT, rows)) for v in list(dqs) + list(dks) + list(dvs)]
        + [
            (x, rows_of(rows, width)),
            (grad_query, rows_of(rows, ATT)),
            (grad_values, all_of(grad_values.shape)),
            (rim, all_of(rim.shape)),
            (grad_depth, all_of(grad_depth.shape)),
            (halo, all_of(halo.shape)),
            (grad_sum, rows_of(rows, width)),
            (weight, all_of(weight.shape)),
            (taps, all_of(taps.shape)),
        ],
        [
            (shaped((tokens, width), BF), rows_of(rows, width)),
            (shaped(weight.shape, BF), all_of(weight.shape)),
            (shaped((8, weight.shape[1]), F32), all_of((8, weight.shape[1]))),
        ],
        [
            pltpu.VMEM((rows + 32, width), F32),
            pltpu.VMEM(weight.shape, F32),
            pltpu.VMEM((rows, weight.shape[1]), BF),
        ],
        4 * tokens * weight.size,
    )


def shifted_from(value, axis, step):
    count = lax.axis_size(axis)
    return lax.ppermute(value, axis, [((i + step) % count, i) for i in range(count)])


def local(
    hidden,
    separators,
    out_grad,
    w_query,
    b_query,
    w_key,
    w_value,
    b_value,
    depth_kernel,
    w_point,
    b_keyconv,
    w_kernel,
    kernel_bias,
    w_convout,
    b_convout,
    w_dense,
    b_dense,
    gain_attn,
    shift_attn,
    w_up,
    b_up,
    w_down,
    b_down,
    gain_out,
    shift_out,
):
    count = lax.axis_size("blk")
    sharers = lax.axis_size("dp")
    me = lax.axis_index("blk")
    x, cotangent = hidden[0], out_grad[0]
    tokens, width = x.shape
    first = me * tokens
    last = count - 1

    others = [shifted_from(x, "blk", step) for step in range(1, count)]
    groups, units = w_up.shape[0], w_up.shape[2]
    columns = jnp.concatenate([w_query, w_key, w_value, w_convout, w_point], axis=1).astype(BF)
    small = jnp.concatenate(
        [v for v in (b_dense, gain_attn, shift_attn, b_down, gain_out, shift_out)]
        + [depth_kernel.T.reshape(-1), b_query, b_value, b_keyconv, b_convout, b_up, w_kernel.reshape(-1)]
    ).astype(BF)
    shard = w_query.shape[0]
    wide = columns.shape[1]
    small_rows = -(-small.size // wide)
    small = jnp.pad(small, (0, small_rows * wide - small.size)).reshape(small_rows, wide)
    early = lax.all_gather(jnp.concatenate([columns, small], axis=0), "dp", axis=0, tiled=False)
    wt_columns = early[:, :shard].reshape(sharers * shard, wide)
    small = early[:, shard:].reshape(sharers, small_rows * wide)
    wt_dense = lax.all_gather(w_dense.astype(BF), "dp", axis=0, tiled=True)
    wt_up = lax.all_gather(
        jnp.concatenate([w_up[g] for g in range(groups)], axis=1).astype(BF), "dp", axis=0, tiled=True
    )
    wt_down = lax.all_gather(
        jnp.concatenate([w_down[g] for g in range(groups)], axis=1).astype(BF), "dp", axis=0, tiled=True
    )
    at = 0
    wide_vectors = small[:, : 15 * shard].reshape(sharers, 15, shard).transpose(1, 0, 2).reshape(15, width).astype(F32)
    at += 15 * shard
    part = b_query.shape[0]
    thin_vectors = small[:, at : at + 4 * part].reshape(sharers, 4, part).transpose(1, 0, 2).reshape(4, ATT).astype(F32)
    at += 4 * part
    bias_up = small[:, at : at + b_up.size].reshape(1, -1).astype(F32)
    at += b_up.size
    wt_kernel = small[:, at : at + w_kernel.size].reshape(ATT, HEADS, KSIZE)
    vectors = jnp.pad(wide_vectors[:6], ((0, 2), (0, 0)))
    taps = jnp.pad(wide_vectors[6:], ((0, 16 - KSIZE), (0, 0)))
    wt_kernel = jnp.pad(wt_kernel.transpose(2, 1, 0), ((0, 0), (0, 8 - HEADS), (0, 0))).reshape(8 * KSIZE, ATT)
    bias_kernel = jnp.pad(kernel_bias.reshape(HEADS, KSIZE).T, ((0, 0), (0, 8 - HEADS))).reshape(8 * KSIZE, 1)
    wt_qkv = wt_columns[:, : 3 * ATT]
    wt_kv = wt_columns[:, ATT : 3 * ATT]
    wt_all = wt_columns[:, : 4 * ATT]
    wt_convout = wt_columns[:, 3 * ATT : 4 * ATT]
    wt_point = wt_columns[:, 4 * ATT :]
    none = jnp.zeros((ATT,), F32)
    bias_kv = jnp.concatenate([none, thin_vectors[1]])[None]
    bias_qkv = jnp.concatenate([thin_vectors[0], none, thin_vectors[1]])[None]

    query, query_t, key, key_t, value, value_t, norms = project(x, wt_qkv, bias_qkv)
    keys = [(key, key_t, value, value_t, norms)]
    outs, probs = [], []
    for step in range(count):
        if step > 0:
            keys.append(project(others[step - 1], wt_kv, bias_kv))
        places = jnp.stack(
            [separators[0], first, lax.rem(me + step, count) * tokens, count * tokens]
        ).astype(jnp.int32)
        out, prob = attend(places, query_t, keys[step][0], keys[step][3], keys[step][4])
        outs.append(out)
        probs.append(prob)
    nothing = jnp.zeros((16, width), BF)
    if count > 1:
        before = jnp.where(me > 0, others[count - 2][tokens - 16 :], nothing)
        after = jnp.where(me < last, others[0][:16], nothing)
    else:
        before = after = nothing
    halo = jnp.concatenate([before, after], axis=0)
    depth, keyconv, attn_key, kernt, kern, conv, values, rim = mix(
        places, x, halo, query, taps, wt_convout, thin_vectors[3][None], wt_point, thin_vectors[2][None], wt_kernel, bias_kernel
    )
    output, grad_sum, grad_conv, grads_t, sides, (gw_dense, gw_up, gw_down, g_vectors, gb_up) = middle(
        outs, conv, x, cotangent, wt_dense, wt_up, wt_down, vectors, bias_up
    )
    packed = jnp.concatenate(
        [
            gw_dense.reshape(sharers, -1, width),
            gw_up.reshape(sharers, -1, width),
            gw_down.reshape(sharers, -1, width),
        ],
        axis=1,
    )
    packed = lax.psum_scatter(packed, "dp", scatter_dimension=0, tiled=False)
    packed = lax.psum(packed, "blk").astype(F32)
    grad_w_dense, grad_w_up, grad_w_down = (
        packed[:shard],
        packed[shard : shard + groups * units * w_up.shape[1] // width],
        packed[-w_down.shape[1] :],
    )
    grad_w_up = grad_w_up.reshape(w_up.shape[1], groups, units).transpose(1, 0, 2)
    grad_w_down = grad_w_down.reshape(w_down.shape[1], groups, -1).transpose(1, 0, 2)

    grad_query_conv, grad_depth, grad_values, gw_point, gw_kernel, g_bias, g_taps = mix_back(
        x, halo, values, rim, grad_conv, kernt, kern, query, keyconv, attn_key, depth, wt_point, wt_kernel
    )
    low_rows = jnp.concatenate([grad_values[:16].astype(BF), grad_depth[:16]], axis=1)
    high_rows = jnp.concatenate([grad_values[tokens + 16 :].astype(BF), grad_depth[tokens - 16 :]], axis=1)
    from_before = lax.ppermute(high_rows, "blk", [(i, i + 1) for i in range(last)])
    from_after = lax.ppermute(low_rows, "blk", [(i + 1, i) for i in range(last)])
    rims = jnp.concatenate([from_before, from_after], axis=0)

    dqs, dks, dvs = [], [], []
    for step in list(range(1, count)) + [0]:
        key, key_t, value, value_t, norms = keys[step]
        dq, dk, dv = attend_back(probs[step], value, key_t, grads_t[step], sides[step], query_t, BF if step else F32)
        if step:
            dk, dv = shifted_from(dk, "blk", count - step), shifted_from(dv, "blk", count - step)
        dqs.append(dq)
        dks.append(dk)
        dvs.append(dv)
    grad_hidden, gw_all, gb_all = finish(
        dqs, dks, dvs, x, grad_query_conv, grad_values, rims[:, :ATT], grad_depth, rims[:, ATT:], grad_sum, wt_all, taps
    )
    gw_kernel, gb_keyconv = (
        gw_kernel[: 8 * KSIZE].reshape(KSIZE, 8, ATT)[:, :HEADS].transpose(2, 1, 0),
        gw_kernel[8 * KSIZE],
    )
    g_bias = g_bias[: 8 * KSIZE, 0].reshape(KSIZE, 8)[:, :HEADS].T.reshape(-1)
    by_device = [
        g_vectors[:6].reshape(6, sharers, shard).transpose(1, 0, 2).reshape(sharers, -1),
        g_taps[:KSIZE].reshape(KSIZE, sharers, shard).transpose(1, 0, 2).reshape(sharers, -1),
        gb_all[0, :ATT].reshape(sharers, -1),
        gb_all[0, 2 * ATT : 3 * ATT].reshape(sharers, -1),
        gb_keyconv.reshape(sharers, -1),
        gb_all[0, 3 * ATT :].reshape(sharers, -1),
        gb_up[0].reshape(sharers, -1),
        gw_kernel.reshape(sharers, -1),
        jnp.broadcast_to(g_bias[None], (sharers, HEADS * KSIZE)),
    ]
    sizes = [v.shape[1] for v in by_device]
    gathered = jnp.concatenate(by_device, axis=1)
    extra_rows = -(-gathered.shape[1] // wide)
    gathered = jnp.pad(gathered, ((0, 0), (0, extra_rows * wide - gathered.shape[1])))
    tail = jnp.concatenate(
        [
            jnp.concatenate([gw_all, gw_point], axis=1).reshape(sharers, shard, wide),
            gathered.astype(BF).reshape(sharers, extra_rows, wide),
        ],
        axis=1,
    )
    tail = lax.psum(lax.psum_scatter(tail, "dp", scatter_dimension=0, tiled=False), "blk").astype(F32)
    gw = [tail[:shard, at * ATT : (at + 1) * ATT] for at in range(5)]
    flat = tail[shard:].reshape(-1)
    ends = [sum(sizes[: at + 1]) for at in range(len(sizes))]
    fields = [flat[end - size : end] for end, size in zip(ends, sizes)]
    grad_vec = fields[0].reshape(6, shard)
    return (
        output[None],
        grad_hidden[None],
        gw[0],
        fields[2],
        gw[1],
        gw[2],
        fields[3],
        fields[1].reshape(KSIZE, shard).T,
        gw[4],
        fields[4],
        fields[7].reshape(w_kernel.shape),
        fields[8],
        gw[3],
        fields[5],
        grad_w_dense,
        grad_vec[0],
        grad_vec[1],
        grad_vec[2],
        grad_w_up,
        fields[6],
        grad_w_down,
        grad_vec[3],
        grad_vec[4],
        grad_vec[5],
    )


def solution(mesh):
    placed = (
        P("dp", "blk", None),
        P("dp"),
        P("dp", "blk", None),
        P("dp", None),
        P("dp"),
        P("dp", None),
        P("dp", None),
        P("dp"),
        P("dp", None),
        P("dp", None),
        P("dp"),
        P("dp", None),
        P(),
        P("dp", None),
        P("dp"),
        P("dp", None),
        P("dp"),
        P("dp"),
        P("dp"),
        P(None, "dp", None),
        P("dp"),
        P(None, "dp", None),
        P("dp"),
        P("dp"),
        P("dp"),
    )
    return jax.shard_map(
        local,
        mesh=mesh,
        in_specs=placed,
        out_specs=(
            P("dp", "blk", None),
            P("dp", "blk", None),
            P("dp", None),
            P("dp"),
            P("dp", None),
            P("dp", None),
            P("dp"),
            P("dp", None),
            P("dp", None),
            P("dp"),
            P("dp", None),
            P(),
            P("dp", None),
            P("dp"),
            P("dp", None),
            P("dp"),
            P("dp"),
            P("dp"),
            P(None, "dp", None),
            P("dp"),
            P(None, "dp", None),
            P("dp"),
            P("dp"),
            P("dp"),
        ),
        check_vma=False,
    )
```

```python
import functools, math
import jax, jax.numpy as jnp
from jax import lax
from jax.experimental import pallas as pl
from jax.experimental.pallas import tpu as pltpu
from jax.sharding import PartitionSpec as P

HEADS = 6
HD = 64
KSIZE = 9
REACH = 4
ATT = 384
EPS = 1e-12
BF = jnp.bfloat16
F32 = jnp.float32
MIB = 2**20
EXCLUDED = 2.0**100
SAFE_SCORE = 50.0


def mm(left, right):
    return jnp.dot(left, right, preferred_element_type=F32)


def mm_nt(left, right):
    return lax.dot_general(left, right, (((1,), (1,)), ((), ())), preferred_element_type=F32)


def mm_tn(left, right):
    return lax.dot_general(left, right, (((0,), (0,)), ((), ())), preferred_element_type=F32)


def in_lanes(rows, columns):
    lane = lax.broadcasted_iota(jnp.int32, (rows, 128), 1)
    out = jnp.zeros((rows, 128), F32)
    for at, column in enumerate(columns):
        out = jnp.where(lane == at, column, out)
    return out.astype(BF)


def in_rows(columns, rows):
    row = lax.broadcasted_iota(jnp.int32, (16, columns), 0)
    out = jnp.zeros((16, columns), F32)
    for at, values in enumerate(rows):
        out = jnp.where(row == at, values, out)
    return out.astype(BF)


def three_parts(values):
    high = values.astype(BF).astype(F32)
    rest = values - high
    middle = rest.astype(BF).astype(F32)
    return high, middle, (rest - middle).astype(BF).astype(F32)


def put_head(ref, head, values):
    odd = lax.rem(head, 2) == 1
    none = jnp.zeros_like(values)
    ref[0:HD, :] = jnp.where(odd, none, values)
    ref[HD : 2 * HD, :] = jnp.where(odd, values, none)


def attend_kernel(keys, queries, chunk, at_ref, q_ref, k_ref, v_ref, norm_ref, o_ref, p_ref, key_side, query_side):
    head, tile = pl.program_id(0), pl.program_id(1)
    separator, first_query, first_key = at_ref[0], at_ref[1], at_ref[2]

    @pl.when((head == 0) & (tile == 0))
    def start():
        position = first_key + lax.broadcasted_iota(jnp.int32, (keys, 128), 0)
        late = (position >= separator).astype(F32)
        key_side[...] = in_lanes(keys, [1.0 - late, late, 1.0, 1.0, 1.0])
        query_side[2 * HD + 16 :, :] = jnp.zeros((2 * HD - 16, queries), BF)

    put_head(query_side, head, q_ref[...])
    position = first_query + tile * queries + lax.broadcasted_iota(jnp.int32, (16, queries), 1)
    late = (position >= separator).astype(F32)
    excluded = [-EXCLUDED * late, -EXCLUDED * (1.0 - late)]
    query_side[2 * HD : 2 * HD + 16, :] = in_rows(queries, excluded)
    o_ref[0, HD + 8 : HD + 16, :] = jnp.zeros((8, queries), F32)
    wide = q_ref[...].astype(F32)
    largest = jnp.max(jnp.sum(wide * wide, axis=0, keepdims=True)) * jnp.max(norm_ref[...])

    def scores(at):
        part = slice(at * chunk, (at + 1) * chunk)
        return mm(
            jnp.concatenate([k_ref[part, :], key_side[part, :]], axis=1), query_side[...]
        )

    @pl.when(jnp.logical_not(largest <= SAFE_SCORE * SAFE_SCORE))
    def shifted():
        best = jnp.full((1, queries), -4.0 * EXCLUDED, F32)
        for at in range(keys // chunk):
            best = jnp.maximum(best, jnp.max(scores(at), axis=0, keepdims=True))
        parts = three_parts(jnp.where(best < -0.5 * EXCLUDED, 0.0, best))
        query_side[2 * HD : 2 * HD + 16, :] = in_rows(queries, excluded + [-part for part in parts])
        o_ref[0, HD + 8 : HD + 16, :] = jnp.broadcast_to(
            jnp.where(best < -0.5 * EXCLUDED, best, parts[0] + parts[1] + parts[2]), (8, queries)
        )

    ones = in_rows(chunk, [1.0])
    total = jnp.zeros((HD + 16, queries), F32)
    for at in range(keys // chunk):
        part = slice(at * chunk, (at + 1) * chunk)
        probs = jnp.exp(scores(at)).astype(BF)
        p_ref[0, part, :] = probs
        total = total + mm(jnp.concatenate([v_ref[:, part], ones], axis=0), probs)
    o_ref[0, 0 : HD + 8, :] = total[0 : HD + 8, :]


def attend(at, query_t, key, value_t, norms):
    tokens, keys = query_t.shape[1], key.shape[0]
    queries, chunk = math.gcd(tokens, 1024), math.gcd(keys, 512)
    return pl.pallas_call(
        functools.partial(attend_kernel, keys, queries, chunk),
        grid=(HEADS, tokens // queries),
        in_specs=[
            pl.BlockSpec(memory_space=pltpu.SMEM),
            pl.BlockSpec((HD, queries), lambda h, i: (h, i)),
            pl.BlockSpec((keys, 2 * HD), lambda h, i: (0, h // 2)),
            pl.BlockSpec((HD, keys), lambda h, i: (h, 0)),
            pl.BlockSpec(norms.shape, lambda h, i: (0, 0)),
        ],
        out_specs=[
            pl.BlockSpec((1, HD + 16, queries), lambda h, i: (h, 0, i)),
            pl.BlockSpec((1, keys, queries), lambda h, i: (h, 0, i)),
        ],
        out_shape=[
            jax.ShapeDtypeStruct((HEADS, HD + 16, tokens), F32),
            jax.ShapeDtypeStruct((HEADS, keys, tokens), BF),
        ],
        scratch_shapes=[pltpu.VMEM((keys, 128), BF), pltpu.VMEM((4 * HD, queries), BF)],
        compiler_params=pltpu.CompilerParams(vmem_limit_bytes=56 * MIB),
        cost_estimate=pl.CostEstimate(
            flops=16 * ATT * tokens * keys,
            bytes_accessed=2 * HEADS * tokens * keys,
            transcendentals=HEADS * tokens * keys,
        ),
        name="attend",
    )(at, query_t, key, value_t, norms)


def attend_back_kernel(keys, queries, chunk, p_ref, v_ref, kt_ref, g_ref, side_ref, q_ref, dq_ref, dk_ref, dv_ref, value_side, grad_side, dk_sum, dv_sum):
    head, tile = pl.program_id(0), pl.program_id(1)

    @pl.when((head == 0) & (tile == 0))
    def start():
        value_side[...] = in_lanes(chunk, [1.0, 1.0, 1.0])
        grad_side[2 * HD + 16 :, :] = jnp.zeros((2 * HD - 16, queries), BF)

    @pl.when(tile == 0)
    def fresh():
        dk_sum[...] = jnp.zeros_like(dk_sum)
        dv_sum[...] = jnp.zeros_like(dv_sum)

    put_head(grad_side, head, g_ref[...])
    grad_side[2 * HD : 2 * HD + 16, :] = side_ref[0]
    total = jnp.zeros((HD, queries), F32)
    for at in range(keys // chunk):
        part = slice(at * chunk, (at + 1) * chunk)
        probs = p_ref[0, part, :]
        spread = mm(jnp.concatenate([v_ref[part, :], value_side[...]], axis=1), grad_side[...])
        grad_scores = (probs.astype(F32) * spread).astype(BF)
        dv_sum[:, part] += mm_nt(g_ref[...], probs)
        dk_sum[:, part] += mm_nt(q_ref[...], grad_scores)
        total = total + mm(kt_ref[:, part], grad_scores)
    dq_ref[...] = total * (HD**-0.5)

    @pl.when(tile == pl.num_programs(1) - 1)
    def finish():
        dk_ref[...] = dk_sum[...].astype(dk_ref.dtype)
        dv_ref[...] = dv_sum[...].astype(dv_ref.dtype)


def attend_back(probs, value, key_t, grad_t, side, query_t, out_type):
    tokens, keys = query_t.shape[1], value.shape[0]
    queries, chunk = math.gcd(tokens, 512), math.gcd(keys, 512)
    by_token = pl.BlockSpec((HD, queries), lambda h, i: (h, i))
    by_key = pl.BlockSpec((HD, keys), lambda h, i: (h, 0))
    return pl.pallas_call(
        functools.partial(attend_back_kernel, keys, queries, chunk),
        grid=(HEADS, tokens // queries),
        in_specs=[
            pl.BlockSpec((1, keys, queries), lambda h, i: (h, 0, i)),
            pl.BlockSpec((keys, 2 * HD), lambda h, i: (0, h // 2)),
            by_key,
            by_token,
            pl.BlockSpec((1, 16, queries), lambda h, i: (h, 0, i)),
            by_token,
        ],
        out_specs=[by_token, by_key, by_key],
        out_shape=[
            jax.ShapeDtypeStruct((ATT, tokens), F32),
            jax.ShapeDtypeStruct((ATT, keys), out_type),
            jax.ShapeDtypeStruct((ATT, keys), out_type),
        ],
        scratch_shapes=[
            pltpu.VMEM((chunk, 128), BF),
            pltpu.VMEM((4 * HD, queries), BF),
            pltpu.VMEM((HD, keys), F32),
            pltpu.VMEM((HD, keys), F32),
        ],
        compiler_params=pltpu.CompilerParams(vmem_limit_bytes=56 * MIB),
        cost_estimate=pl.CostEstimate(
            flops=32 * ATT * tokens * keys,
            bytes_accessed=2 * HEADS * tokens * keys,
            transcendentals=0,
        ),
        name="attend_back",
    )(probs, value, key_t, grad_t, side, query_t)


def all_of(shape):
    return pl.BlockSpec(shape, lambda *at: (0,) * len(shape))


def rows_of(rows, width):
    return pl.BlockSpec((rows, width), lambda i: (i, 0))


def columns_of(height, columns):
    return pl.BlockSpec((height, columns), lambda i: (0, i))


def run_tiles(kernel, name, steps, inputs, outputs, scratch, flops):
    args, in_specs = zip(*inputs)
    shapes, out_specs = zip(*outputs)
    size = sum(math.prod(v.shape) * v.dtype.itemsize for v in args + shapes)
    return pl.pallas_call(
        kernel,
        grid=(steps,),
        in_specs=list(in_specs),
        out_specs=list(out_specs),
        out_shape=list(shapes),
        scratch_shapes=scratch,
        compiler_params=pltpu.CompilerParams(vmem_limit_bytes=60 * MIB),
        cost_estimate=pl.CostEstimate(flops=flops, bytes_accessed=size, transcendentals=0),
        name=name,
    )(*args)


def shaped(shape, dtype):
    return jax.ShapeDtypeStruct(shape, dtype)


def project_kernel(parts, x_ref, w_ref, bias_ref, bias_t_ref, *refs):
    norm_ref, flipped = refs[2 * parts], refs[2 * parts + 1]

    skip = (3 - parts) * ATT

    @pl.when(pl.program_id(0) == 0)
    def start():
        norm_ref[...] = jnp.zeros_like(norm_ref)
        flipped[...] = w_ref[:, skip:].T

    x = x_ref[...]
    plain = mm(x, w_ref[:, skip:]) + bias_ref[:, skip:]
    turned = mm_nt(flipped[...], x) + bias_t_ref[skip:, :]
    for part in range(parts):
        own = slice(part * ATT, (part + 1) * ATT)
        refs[2 * part][...] = plain[:, own].astype(BF)
        across = turned[own].astype(BF)
        if part == parts - 2:
            wide = across.astype(F32)
            for head in range(HEADS):
                cells = wide[head * HD : (head + 1) * HD]
                size = jnp.sum(cells * cells, axis=0, keepdims=True)
                norm_ref[...] = jnp.maximum(norm_ref[...], size)
        if part < parts - 2:
            across = (turned[own].astype(BF).astype(F32) * (HD**-0.5)).astype(BF)
        refs[2 * part + 1][...] = across


def project(x, weight, bias, bias_t, parts):
    tokens, width = x.shape
    wide = 3 * ATT
    tile = math.gcd(tokens, 512)
    outputs = []
    for part in range(parts):
        outputs.append((shaped((tokens, ATT), BF), rows_of(tile, ATT)))
        outputs.append((shaped((ATT, tokens), BF), columns_of(ATT, tile)))
    outputs.append((shaped((8, tile), F32), all_of((8, tile))))
    return run_tiles(
        functools.partial(project_kernel, parts),
        "project",
        tokens // tile,
        [
            (x, rows_of(tile, width)),
            (weight, all_of((width, wide))),
            (bias, all_of(bias.shape)),
            (bias_t, all_of(bias_t.shape)),
        ],
        outputs,
        [pltpu.VMEM((parts * ATT, width), BF)],
        4 * tokens * width * parts * ATT,
    )


def fill_rows(window, x_ref, halo_ref, tile, tiles, rows):
    first = tile * rows
    tokens = x_ref.shape[0]
    before = x_ref[pl.ds(pl.multiple_of(jnp.maximum(first - 16, 0), 16), 16), :]
    after = x_ref[pl.ds(pl.multiple_of(jnp.minimum(first + rows, tokens - 16), 16), 16), :]
    window[0:16, :] = jnp.where(tile == 0, halo_ref[0:16, :], before).astype(window.dtype)
    window[16 : 16 + rows, :] = x_ref[pl.ds(pl.multiple_of(first, rows), rows), :].astype(window.dtype)
    window[16 + rows :, :] = jnp.where(
        tile == tiles - 1, halo_ref[16:32, :], after
    ).astype(window.dtype)


def fill_window(window, x_ref, halo_ref, tile, rows):
    fill_rows(window, x_ref, halo_ref, tile, pl.num_programs(0), rows)


def fill_spread(spread):
    row = lax.broadcasted_iota(jnp.int32, (128, ATT), 0)
    head = lax.broadcasted_iota(jnp.int32, (128, ATT), 1) // HD
    for tap in range(KSIZE):
        spread[:, tap * ATT : (tap + 1) * ATT] = (row == tap * 8 + head).astype(F32).astype(BF)


def mix_kernel(rows, at_ref, x_ref, halo_ref, q_ref, taps_ref, wc_ref, bc_ref, wp_ref, bp_ref, wk_ref, bk_ref, depth_ref, keyconv_ref, attn_ref, kernt_ref, kern_ref, conv_ref, out_ref, rim_ref, window, conv_window, spread):
    tile = pl.program_id(0)
    last = pl.num_programs(0) - 1

    @pl.when(tile == 0)
    def start():
        fill_spread(spread)

    fill_window(window, x_ref, halo_ref, tile, rows)
    width = window.shape[1]
    for at in range(0, width, 128):
        some = slice(at, at + 128)
        total = jnp.zeros((rows, 128), F32)
        for tap in range(KSIZE):
            total = total + window[12 + tap : 12 + tap + rows, some] * taps_ref[tap : tap + 1, some]
        depth_ref[:, some] = total.astype(BF)
    position = (
        at_ref[1] + tile * rows - 16 + lax.broadcasted_iota(jnp.int32, (rows + 32, ATT), 0)
    )
    inside = (position >= 0) & (position < at_ref[3])
    values = mm(window[...].astype(BF), wc_ref[...]) + bc_ref[...]
    values = jnp.where(inside, values, 0.0).astype(BF)
    out_ref[...] = values[16 : 16 + rows]

    @pl.when(tile == 0)
    def first_rim():
        rim_ref[0:16, :] = values[0:16]

    @pl.when(tile == last)
    def last_rim():
        rim_ref[16:32, :] = values[16 + rows :]

    conv_window[...] = values.astype(F32)
    keyconv = mm(depth_ref[...], wp_ref[...]) + bp_ref[...]
    keyconv_ref[...] = keyconv
    attn_key = (keyconv * q_ref[...].astype(F32)).astype(BF)
    attn_ref[...] = attn_key
    logits = mm_nt(wk_ref[...], attn_key) + bk_ref[...]
    slabs = [logits[8 * tap : 8 * tap + 8] for tap in range(KSIZE)]
    best = functools.reduce(jnp.maximum, slabs)
    slabs = [jnp.exp(slab - best) for slab in slabs]
    share = 1.0 / functools.reduce(jnp.add, slabs)
    slabs = [slab * share for slab in slabs]
    kernt = jnp.concatenate(slabs + [jnp.zeros((128 - 8 * KSIZE, rows), F32)], axis=0)
    kernt_ref[...] = kernt[0 : 8 * KSIZE]
    kern = kernt.astype(BF).T
    kern_ref[...] = kern
    total = jnp.zeros((rows, ATT), F32)
    for tap in range(KSIZE):
        total = total + mm(kern, spread[:, tap * ATT : (tap + 1) * ATT]) * conv_window[12 + tap : 12 + tap + rows, :]
    conv_ref[...] = total.astype(BF)


def column_block(weight, place):
    return pl.BlockSpec((weight.shape[0], ATT), lambda i: (0, place))


def mix(at, x, halo, query, taps, weight, b_convout, b_keyconv, w_kernel, kernel_bias):
    tokens, width = x.shape
    rows = math.gcd(tokens, 256)
    taps, b_convout, b_keyconv, w_kernel, kernel_bias = [
        (v, all_of(v.shape)) for v in (taps, b_convout, b_keyconv, w_kernel, kernel_bias)
    ]
    whole = [
        taps,
        (weight, column_block(weight, 3)),
        b_convout,
        (weight, column_block(weight, 4)),
        b_keyconv,
        w_kernel,
        kernel_bias,
    ]
    return run_tiles(
        functools.partial(mix_kernel, rows),
        "mix",
        tokens // rows,
        [
            (at, pl.BlockSpec(memory_space=pltpu.SMEM)),
            (x, all_of(x.shape)),
            (halo, all_of(halo.shape)),
            (query, rows_of(rows, ATT)),
        ]
        + whole,
        [
            (shaped((tokens, width), BF), rows_of(rows, width)),
            (shaped((tokens, ATT), F32), rows_of(rows, ATT)),
            (shaped((tokens, ATT), BF), rows_of(rows, ATT)),
            (shaped((8 * KSIZE, tokens), F32), columns_of(8 * KSIZE, rows)),
            (shaped((tokens, 128), BF), rows_of(rows, 128)),
            (shaped((tokens, ATT), BF), rows_of(rows, ATT)),
            (shaped((tokens, ATT), BF), rows_of(rows, ATT)),
            (shaped((32, ATT), BF), all_of((32, ATT))),
        ],
        [
            pltpu.VMEM((rows + 32, width), F32),
            pltpu.VMEM((rows + 32, ATT), F32),
            pltpu.VMEM((128, KSIZE * ATT), BF),
        ],
        4 * tokens * width * ATT * 4,
    )


def normal(values):
    centre = values - jnp.mean(values, axis=-1, keepdims=True)
    scale = lax.rsqrt(jnp.mean(centre * centre, axis=-1, keepdims=True) + EPS)
    return centre * scale, scale


def normal_back(grad, unit, scale):
    return scale * (
        grad
        - jnp.mean(grad, axis=-1, keepdims=True)
        - unit * jnp.mean(grad * unit, axis=-1, keepdims=True)
    )


def gelu_parts(values):
    size = jnp.abs(values)
    t = 1.0 / (1.0 + (0.3275911 * math.sqrt(0.5)) * size)
    tail = t * (
        0.5 * 0.254829592
        + t * (0.5 * -0.284496736 + t * (0.5 * 1.421413741 + t * (0.5 * -1.453152027 + t * (0.5 * 1.061405429))))
    )
    bell = jnp.exp(-0.5 * values * values)
    tail = tail * bell
    share = jnp.where(values < 0.0, tail, 1.0 - tail)
    return values * share, share + values * (bell * (1.0 / math.sqrt(2.0 * math.pi)))


def middle_kernel(blocks, rows, units, *refs):
    o_refs, refs = refs[:blocks], refs[blocks:]
    (conv_ref, x_ref, og_ref, wd_ref, wu_ref, wn_ref, vec_ref, bu_ref), refs = refs[:8], refs[8:]
    (out_ref, sum_ref, gconv_ref), refs = refs[:3], refs[3:]
    g_refs, refs = refs[:blocks], refs[blocks:]
    side_refs, refs = refs[:blocks], refs[blocks:]
    (gwd_ref, gwu_ref, gwn_ref, gvec_ref, gbu_ref, wd_sum, wu_sum, wn_sum, acts, slopes) = refs
    tile = pl.program_id(0)
    hidden_units = wu_ref.shape[1]
    groups = 2
    inner = ATT
    outer = hidden_units // groups

    @pl.when(tile == 0)
    def start():
        for ref in (wd_sum, wu_sum, wn_sum, gvec_ref, gbu_ref):
            ref[...] = jnp.zeros_like(ref)

    shifts = [ref[:, HD + 8 : HD + 9, :] for ref in o_refs]
    top = functools.reduce(jnp.maximum, shifts)
    weights = [jnp.exp(shift - top) for shift in shifts]
    mass = functools.reduce(jnp.add, [w * ref[:, HD : HD + 1, :] for w, ref in zip(weights, o_refs)])
    weights = [w / mass for w in weights]
    heads = functools.reduce(jnp.add, [w * ref[:, 0:HD, :] for w, ref in zip(weights, o_refs)])
    att_t = heads.reshape(ATT, rows).astype(BF)
    conv = conv_ref[...]
    vec = [vec_ref[at : at + 1, :] for at in range(6)]
    dense = mm(att_t.T, wd_ref[0:ATT, :]) + mm(conv, wd_ref[ATT:, :]) + vec[0]
    unit_one, scale_one = normal(dense + x_ref[...].astype(F32))
    normed = unit_one * vec[1] + vec[2]
    low = normed.astype(BF)
    downs = []
    for group in range(groups):
        mine = low[:, group * inner : (group + 1) * inner]
        down = jnp.zeros((rows, inner), F32)
        for at in range(0, outer, units):
            here = slice(group * outer + at, group * outer + at + units)
            upward = mm(mine, wu_ref[:, here]) + bu_ref[:, here]
            act, slope = gelu_parts(upward)
            act = act.astype(BF)
            acts[:, here] = act
            slopes[:, here] = slope.astype(BF)
            down = down + mm(act, wn_ref[at : at + units, group * inner : (group + 1) * inner])
        downs.append(down)
    unit_two, scale_two = normal(jnp.concatenate(downs, axis=1) + vec[3] + normed)
    out_ref[...] = (unit_two * vec[4] + vec[5]).astype(BF)
    og = og_ref[...].astype(F32)
    gvec_ref[4:5, :] += jnp.sum(og * unit_two, axis=0, keepdims=True)
    gvec_ref[5:6, :] += jnp.sum(og, axis=0, keepdims=True)
    grad_two = normal_back(og * vec[4], unit_two, scale_two)
    grad_down = grad_two.astype(BF)
    gvec_ref[3:4, :] += jnp.sum(grad_down.astype(F32), axis=0, keepdims=True)
    backs = []
    for group in range(groups):
        lanes = slice(group * inner, (group + 1) * inner)
        mine, grads = low[:, lanes], grad_down[:, lanes]
        mine_t = mine.T
        back = jnp.zeros((rows, inner), F32)
        for at in range(0, outer, units):
            here = slice(group * outer + at, group * outer + at + units)
            grad_act = mm_nt(grads, wn_ref[at : at + units, lanes])
            grad_up = (grad_act * slopes[:, here].astype(F32)).astype(BF)
            gbu_ref[0:1, here] += jnp.sum(grad_up.astype(F32), axis=0, keepdims=True)
            wn_sum[at : at + units, lanes] += mm_tn(acts[:, here], grads)
            wu_sum[:, here] += mm(mine_t, grad_up)
            back = back + mm_nt(grad_up, wu_ref[:, here])
        backs.append(back)
    grad_normed = grad_two + jnp.concatenate(backs, axis=1)
    gvec_ref[1:2, :] += jnp.sum(grad_normed * unit_one, axis=0, keepdims=True)
    gvec_ref[2:3, :] += jnp.sum(grad_normed, axis=0, keepdims=True)
    grad_one = normal_back(grad_normed * vec[1], unit_one, scale_one)
    sum_ref[...] = grad_one
    grad_dense = grad_one.astype(BF)
    gvec_ref[0:1, :] += jnp.sum(grad_dense.astype(F32), axis=0, keepdims=True)
    wd_sum[0:ATT, :] += mm(att_t, grad_dense)
    wd_sum[ATT:, :] += mm_tn(conv, grad_dense)
    gconv_ref[...] = mm_nt(grad_dense, wd_ref[ATT:, :]).astype(BF)
    grad_att = mm_nt(wd_ref[0:ATT, :], grad_dense).astype(BF).astype(F32).reshape(HEADS, HD, rows)
    for weight, g_ref, side_ref in zip(weights, g_refs, side_refs):
        share = (grad_att * weight).astype(BF)
        g_ref[...] = share.reshape(ATT, rows)
        delta = -jnp.sum(share.astype(F32) * heads, axis=1, keepdims=True)
        row = lax.broadcasted_iota(jnp.int32, (HEADS, 16, rows), 1)
        side = jnp.zeros((HEADS, 16, rows), F32)
        for at, part in enumerate(three_parts(delta)):
            side = jnp.where(row == at, part, side)
        side_ref[...] = side.astype(BF)

    @pl.when(tile == pl.num_programs(0) - 1)
    def finish():
        gwd_ref[...] = wd_sum[...].astype(BF)
        gwu_ref[...] = wu_sum[...].astype(BF)
        gwn_ref[...] = wn_sum[...].astype(BF)


def middle(outs, conv, x, out_grad, w_dense, w_up, w_down, vectors, b_up):
    tokens, width = x.shape
    rows = math.gcd(tokens, 256)
    blocks = len(outs)
    heads = pl.BlockSpec((HEADS, HD + 16, rows), lambda i: (0, 0, i))
    side = pl.BlockSpec((HEADS, 16, rows), lambda i: (0, 0, i))
    once = [(v, all_of(v.shape)) for v in (w_dense, w_up, w_down, vectors, b_up)]
    results = run_tiles(
        functools.partial(middle_kernel, blocks, rows, 512),
        "middle",
        tokens // rows,
        [(o, heads) for o in outs]
        + [
            (conv, rows_of(rows, ATT)),
            (x, rows_of(rows, width)),
            (out_grad, rows_of(rows, width)),
        ]
        + once,
        [
            (shaped((tokens, width), BF), rows_of(rows, width)),
            (shaped((tokens, width), F32), rows_of(rows, width)),
            (shaped((tokens, ATT), BF), rows_of(rows, ATT)),
        ]
        + [(shaped((ATT, tokens), BF), columns_of(ATT, rows))] * blocks
        + [(shaped((HEADS, 16, tokens), BF), side)] * blocks
        + [
            (shaped(w_dense.shape, BF), all_of(w_dense.shape)),
            (shaped(w_up.shape, BF), all_of(w_up.shape)),
            (shaped(w_down.shape, BF), all_of(w_down.shape)),
            (shaped((8, width), F32), all_of((8, width))),
            (shaped((8, w_up.shape[1]), F32), all_of((8, w_up.shape[1]))),
        ],
        [
            pltpu.VMEM(w_dense.shape, F32),
            pltpu.VMEM(w_up.shape, F32),
            pltpu.VMEM(w_down.shape, F32),
            pltpu.VMEM((rows, w_up.shape[1]), BF),
            pltpu.VMEM((rows, w_up.shape[1]), BF),
        ],
        6 * tokens * (w_dense.size + w_up.size + w_down.size),
    )
    output, grad_sum, grad_conv = results[:3]
    return output, grad_sum, grad_conv, results[3 : 3 + blocks], results[3 + blocks : 3 + 2 * blocks], results[3 + 2 * blocks :]


def mix_back_kernel(rows, x_ref, halo_ref, values_ref, rim_ref, gconv_ref, kernt_ref, kern_ref, q_ref, keyconv_ref, attn_ref, depth_ref, wp_ref, wk_ref, gq_ref, gdepth_ref, gvalues_ref, gwp_ref, gwk_ref, gbias_ref, gtaps_ref, window, conv_window, summed, products, spread, wp_sum):
    tile = pl.program_id(0)

    @pl.when(tile == 0)
    def start():
        fill_spread(spread)
        for ref in (gvalues_ref, wp_sum, gwk_ref, gbias_ref, gtaps_ref):
            ref[...] = jnp.zeros_like(ref)

    fill_window(window, x_ref, halo_ref, tile, rows)
    fill_window(conv_window, values_ref, rim_ref, tile, rows)
    summed[...] = jnp.zeros_like(summed)
    grad_conv = gconv_ref[...].astype(F32)
    for tap in range(KSIZE):
        here = slice(tap * ATT, (tap + 1) * ATT)
        there = slice(12 + tap, 12 + tap + rows)
        products[:, here] = (grad_conv * conv_window[there, :]).astype(BF)
        summed[there, :] += mm(kern_ref[...], spread[:, here]) * grad_conv
    first = pl.multiple_of(tile * rows, rows)
    gvalues_ref[pl.ds(first, rows + 32), :] += summed[...]
    grad_kernel = mm_nt(spread[...], products[...])
    slabs = [slice(8 * tap, 8 * tap + 8) for tap in range(KSIZE)]
    kernels = [kernt_ref[slab, :] for slab in slabs]
    mean = functools.reduce(jnp.add, [k * grad_kernel[slab] for k, slab in zip(kernels, slabs)])
    grad_logits = jnp.concatenate(
        [k * (grad_kernel[slab] - mean) for k, slab in zip(kernels, slabs)], axis=0
    ).astype(BF)
    wide_logits = grad_logits.astype(F32)
    gbias_ref[...] += jnp.concatenate(
        [
            jnp.broadcast_to(jnp.sum(wide_logits, axis=1, keepdims=True), (8 * KSIZE, 128)),
            jnp.zeros((8, 128), F32),
        ],
        axis=0,
    )
    gwk_ref[0 : 8 * KSIZE, :] += mm(grad_logits, attn_ref[...])
    grad_attn = mm_tn(grad_logits, wk_ref[...]).astype(BF).astype(F32)
    grad_keyconv = (grad_attn * q_ref[...].astype(F32)).astype(BF)
    gq_ref[...] = grad_attn * keyconv_ref[...]
    gwk_ref[8 * KSIZE : 8 * KSIZE + 1, :] += jnp.sum(grad_keyconv.astype(F32), axis=0, keepdims=True)
    wp_sum[...] += mm_tn(depth_ref[...], grad_keyconv)
    grad_depth = mm_nt(grad_keyconv, wp_ref[...]).astype(BF)
    gdepth_ref[...] = grad_depth
    wide = grad_depth.astype(F32)
    for at in range(0, window.shape[1], 128):
        some = slice(at, at + 128)
        for tap in range(KSIZE):
            gtaps_ref[tap : tap + 1, some] += jnp.sum(
                wide[:, some] * window[12 + tap : 12 + tap + rows, some], axis=0, keepdims=True
            )

    @pl.when(tile == pl.num_programs(0) - 1)
    def finish():
        gwp_ref[...] = wp_sum[...].astype(BF)


def mix_back(x, halo, values, rim, grad_conv, kernt, kern, query, keyconv, attn_key, depth, weight, w_kernel):
    tokens, width = x.shape
    rows = math.gcd(tokens, 256)
    by_rows = [(v, rows_of(rows, v.shape[1])) for v in (kern, query, keyconv, attn_key, depth)]
    return run_tiles(
        functools.partial(mix_back_kernel, rows),
        "mix_back",
        tokens // rows,
        [(v, all_of(v.shape)) for v in (x, halo, values, rim)]
        + [(grad_conv, rows_of(rows, ATT)), (kernt, columns_of(8 * KSIZE, rows))]
        + by_rows
        + [(weight, column_block(weight, 4)), (w_kernel, all_of(w_kernel.shape))],
        [
            (shaped((tokens, ATT), F32), rows_of(rows, ATT)),
            (shaped((tokens, width), BF), rows_of(rows, width)),
            (shaped((tokens + 32, ATT), F32), all_of((tokens + 32, ATT))),
            (shaped((width, ATT), BF), all_of((width, ATT))),
            (shaped((8 * KSIZE + 8, ATT), F32), all_of((8 * KSIZE + 8, ATT))),
            (shaped((8 * KSIZE + 8, 128), F32), all_of((8 * KSIZE + 8, 128))),
            (shaped((16, width), F32), all_of((16, width))),
        ],
        [
            pltpu.VMEM((rows + 32, width), F32),
            pltpu.VMEM((rows + 32, ATT), F32),
            pltpu.VMEM((rows + 32, ATT), F32),
            pltpu.VMEM((rows, KSIZE * ATT), BF),
            pltpu.VMEM((128, KSIZE * ATT), BF),
            pltpu.VMEM((width, ATT), F32),
        ],
        4 * tokens * width * ATT * 4,
    )


MESH = pl.DeviceIdType.MESH
LINE = 4
LANES = 128


def my_place(sharers):
    columns = sharers // (2 * LINE)
    me = lax.axis_index("dp")
    return me, me // (2 * columns), lax.rem(me // 2, columns), lax.rem(me, 2), columns


def greet(partners):
    barrier = pltpu.get_barrier_semaphore()
    for partner in partners:
        pl.semaphore_signal(barrier, inc=1, device_id=partner, device_id_type=MESH)
    return barrier


def send(source, target, send_sem, recv_sem, device):
    copy = pltpu.make_async_remote_copy(
        src_ref=source,
        dst_ref=target,
        send_sem=send_sem,
        recv_sem=recv_sem,
        device_id=device,
        device_id_type=MESH,
    )
    copy.start()
    return copy


def gather_kernel(sharers, *refs):
    w_refs, small_ref, out_ref, send_sem, recv_sem = refs[:5], refs[5], refs[6], refs[7], refs[8]
    me, line, column, core, columns = my_place(sharers)

    def at(line, column, core):
        return (line * columns + column) * 2 + core

    lines = [lax.rem(line + step, LINE) for step in range(1, LINE)]
    sides = [lax.rem(column + step, columns) for step in range(1, columns)]
    partners = [{"dp": at(other, column, core)} for other in lines]
    across = [{"dp": at(line, other, core)} for other in sides]
    mate = {"dp": at(line, column, 1 - core)}
    barrier = greet(partners + across + [mate])
    for place, ref in enumerate(w_refs):
        out_ref[me, :, place * ATT : (place + 1) * ATT] = ref[...].astype(BF)
    out_ref[me, :, len(w_refs) * ATT :] = small_ref[...].astype(BF)
    pl.semaphore_wait(barrier, len(partners) + len(across) + 1)
    copies = []

    def pass_on(block, devices):
        for device in devices:
            copies.append(
                send(out_ref.at[block], out_ref.at[block], send_sem.at[len(copies)], recv_sem.at[block], device)
            )

    def arrived(block):
        pltpu.make_async_copy(out_ref.at[block], out_ref.at[block], recv_sem.at[block]).wait()

    pass_on(me, across + partners + [mate])
    for other in lines:
        block = at(other, column, core)
        arrived(block)
        pass_on(block, across + [mate])
    for side in sides:
        for other in [line] + lines:
            block = at(other, side, core)
            arrived(block)
            pass_on(block, [mate])
    for side in [column] + sides:
        for other in [line] + lines:
            arrived(at(other, side, 1 - core))
    for copy in copies:
        copy.wait_send()


def gather_columns(weights, small, sharers):
    rows = weights[0].shape[0]
    wide = len(weights) * ATT + LANES
    columns = sharers // (2 * LINE)
    copies = LINE - 1 + columns - 1 + 1 + (LINE - 1) * columns + LINE * (columns - 1)
    vmem = pl.BlockSpec(memory_space=pltpu.VMEM)
    out = pl.pallas_call(
        functools.partial(gather_kernel, sharers),
        in_specs=[vmem] * (len(weights) + 1),
        out_specs=vmem,
        out_shape=shaped((sharers, rows, wide), BF),
        scratch_shapes=[pltpu.SemaphoreType.DMA((copies,)), pltpu.SemaphoreType.DMA((sharers,))],
        compiler_params=pltpu.CompilerParams(
            collective_id=0, has_side_effects=True, vmem_limit_bytes=32 * MIB
        ),
        name="gather_columns",
    )(*weights, small)
    return out.reshape(sharers * rows, wide)


class Shares:
    def __init__(self, sharers, rows, wide, count):
        self.sharers, self.rows, self.wide, self.count = sharers, rows, wide, count
        self.columns = sharers // (2 * LINE)
        self.chips = sharers // 2
        cut = wide // (2 * LANES) * LANES
        self.lanes = [slice(0, cut), slice(cut, wide)]
        self.widths = [cut, wide - cut]
        self.copies = 1 + self.columns - 1 + LINE - 1 + count - 1

    def scratch(self):
        shapes = []
        for chain, width in enumerate(self.widths):
            side = (self.columns - 1, LINE if chain == 0 else 1, self.rows, width)
            line = (LINE - 1, 1 if chain == 0 else self.columns, self.rows, width)
            shapes += [pltpu.VMEM((self.chips, self.rows, width), BF)] * 2
            shapes += [pltpu.VMEM(side, BF)] * 2 + [pltpu.VMEM(line, BF)] * 2
            shapes += [pltpu.VMEM((self.rows, width), BF), pltpu.VMEM((self.count, self.rows, width), BF)]
        return shapes + [
            pltpu.VMEM((self.sharers, self.rows, self.wide), F32),
            pltpu.SemaphoreType.DMA((2 * self.copies,)),
            pltpu.SemaphoreType.DMA((2 * self.copies,)),
        ]

    def bind(self, refs):
        self.buffers = [refs[:8], refs[8:16]]
        self.total, self.send_sem, self.recv_sem = refs[16:19]
        self.me, self.line, self.column, self.core, unused = my_place(self.sharers)
        self.block = lax.axis_index("blk")
        self.others_line = [lax.rem(self.line + step, LINE) for step in range(1, LINE)]
        self.others_side = [lax.rem(self.column + step, self.columns) for step in range(1, self.columns)]
        self.others_block = [lax.rem(self.block + step, self.count) for step in range(1, self.count)]

    def at(self, line, column, core):
        return (line * self.columns + column) * 2 + core

    def greet(self):
        devices = [{"dp": self.at(self.line, self.column, 1 - self.core)}]
        devices += [{"dp": self.at(self.line, other, self.core)} for other in self.others_side]
        devices += [{"dp": self.at(other, self.column, self.core)} for other in self.others_line]
        devices += [{"blk": other} for other in self.others_block]
        greet(devices)

    def met(self):
        pl.semaphore_wait(pltpu.get_barrier_semaphore(), 1 + self.columns - 1 + LINE - 1 + self.count - 1)

    def copy(self, chain, number, source, target, device):
        sem = chain * self.copies + number
        return pltpu.make_async_remote_copy(
            src_ref=source,
            dst_ref=target,
            send_sem=self.send_sem.at[sem],
            recv_sem=self.recv_sem.at[sem],
            device_id=device,
            device_id_type=MESH,
        )

    def mate_copy(self, chain):
        mate = {"dp": self.at(self.line, self.column, 1 - self.core)}
        return self.copy(chain, 0, self.buffers[chain][0], self.buffers[chain][1], mate)

    def mate_start(self, chain):
        for chip in range(self.chips):
            self.buffers[chain][0][chip] = self.total[2 * chip + 1 - self.core, :, self.lanes[chain]].astype(BF)
        self.mate_copy(chain).start()

    def mate_end(self, chain):
        self.mate_copy(chain).wait()
        for chip in range(self.chips):
            self.total[2 * chip + self.core, :, self.lanes[chain]] += self.buffers[chain][1][chip].astype(F32)

    def side_copies(self, chain):
        source, target = self.buffers[chain][2:4]
        return [
            self.copy(chain, 1 + step, source.at[step], target.at[step], {"dp": self.at(self.line, other, self.core)})
            for step, other in enumerate(self.others_side)
        ]

    def side_lines(self, chain):
        return range(LINE) if chain == 0 else [self.line]

    def side_start(self, chain):
        for step, other in enumerate(self.others_side):
            for place, line in enumerate(self.side_lines(chain)):
                self.buffers[chain][2][step, place] = self.total[self.at(line, other, self.core), :, self.lanes[chain]].astype(BF)
        for copy in self.side_copies(chain):
            copy.start()

    def side_end(self, chain):
        for step, copy in enumerate(self.side_copies(chain)):
            copy.wait()
            for place, line in enumerate(self.side_lines(chain)):
                self.total[self.at(line, self.column, self.core), :, self.lanes[chain]] += self.buffers[chain][3][step, place].astype(F32)

    def line_copies(self, chain):
        source, target = self.buffers[chain][4:6]
        return [
            self.copy(chain, self.columns + step, source.at[step], target.at[step], {"dp": self.at(other, self.column, self.core)})
            for step, other in enumerate(self.others_line)
        ]

    def line_columns(self, chain):
        return [self.column] if chain == 0 else range(self.columns)

    def line_start(self, chain):
        for step, other in enumerate(self.others_line):
            for place, column in enumerate(self.line_columns(chain)):
                self.buffers[chain][4][step, place] = self.total[self.at(other, column, self.core), :, self.lanes[chain]].astype(BF)
        for copy in self.line_copies(chain):
            copy.start()

    def line_end(self, chain):
        for step, copy in enumerate(self.line_copies(chain)):
            copy.wait()
            for place, column in enumerate(self.line_columns(chain)):
                self.total[self.at(self.line, column, self.core), :, self.lanes[chain]] += self.buffers[chain][5][step, place].astype(F32)

    def block_copies(self, chain):
        source, target = self.buffers[chain][6:8]
        return [
            self.copy(chain, self.columns + LINE - 1 + step, source, target.at[self.block], {"blk": other})
            for step, other in enumerate(self.others_block)
        ]

    def block_start(self, chain):
        own = self.total[self.me, :, self.lanes[chain]].astype(BF)
        self.buffers[chain][6][...] = own
        self.buffers[chain][7][self.block] = own
        for copy in self.block_copies(chain):
            copy.start()

    def block_end(self, chain, out_ref):
        for copy in self.block_copies(chain):
            copy.wait()
        parts = [self.buffers[chain][7][at].astype(F32) for at in range(self.count)]
        out_ref[:, self.lanes[chain]] = functools.reduce(jnp.add, parts)


def finish_kernel(blocks, rows, tiles, shares, *refs):
    dq_refs, refs = refs[:blocks], refs[blocks:]
    dk_refs, refs = refs[:blocks], refs[blocks:]
    dv_refs, refs = refs[:blocks], refs[blocks:]
    (x_ref, gq_ref, gvalues_ref, rim_ref, gdepth_ref, halo_ref, sum_ref, w_ref, taps_ref), refs = refs[:9], refs[9:]
    gh_ref, share_ref, window, grads, bias_sum = refs[:5]
    shares.bind(refs[5:])
    step = pl.program_id(0)
    wide = w_ref.shape[1]
    shard = shares.rows

    @pl.when(step == 0)
    def start():
        shares.greet()
        shares.total[...] = jnp.zeros_like(shares.total)
        bias_sum[...] = jnp.zeros_like(bias_sum)

    def total(some):
        return functools.reduce(jnp.add, [ref[...].astype(F32) for ref in some])

    @pl.when(step < tiles)
    def weights():
        first = pl.multiple_of(step * rows, rows)
        here = pl.ds(first, rows)
        own = gvalues_ref[pl.ds(first + 16, rows), :]
        zero = jnp.zeros((16, ATT), F32)
        before = jnp.where(step == 0, rim_ref[0:16, :].astype(F32), zero)
        after = jnp.where(step == tiles - 1, rim_ref[16:32, :].astype(F32), zero)
        own = jnp.concatenate([own[0:16] + before, own[16 : rows - 16], own[rows - 16 :] + after], axis=0)
        every = jnp.concatenate(
            [
                (total(dq_refs).T + gq_ref[...]).astype(BF),
                total(dk_refs).astype(BF).T,
                total(dv_refs).astype(BF).T,
                own.astype(BF),
            ],
            axis=1,
        )
        grads[here, :] = every
        bias_sum[0:1, :] += jnp.sum(every.astype(F32), axis=0, keepdims=True)
        turned = x_ref[...].T
        for at in range(shares.sharers):
            shares.total[at, :, :wide] += mm(turned[at * shard : (at + 1) * shard], every)

    @pl.when(step >= tiles)
    def tokens():
        tile = step - tiles
        first = pl.multiple_of(tile * rows, rows)
        fill_rows(window, gdepth_ref, halo_ref, tile, tiles, rows)
        back = mm_nt(grads[pl.ds(first, rows), :], w_ref[...])
        for at in range(0, window.shape[1], 128):
            some = slice(at, at + 128)
            depth = back[:, some] + sum_ref[:, some]
            for tap in range(KSIZE):
                depth = depth + window[20 - tap : 20 - tap + rows, some] * taps_ref[tap : tap + 1, some]
            gh_ref[:, some] = depth.astype(BF)

    @pl.when(step == tiles - 1)
    def launch():
        for at in range(wide // LANES):
            values = bias_sum[0:1, at * LANES : (at + 1) * LANES]
            for block in range(shares.sharers):
                shares.total[block, at : at + 1, wide:] = values
        shares.met()
        shares.mate_start(0)
        shares.mate_start(1)

    plan = [
        (tiles, [(shares.mate_end, 0), (shares.side_start, 0), (shares.mate_end, 1), (shares.line_start, 1)]),
        (tiles + tiles // 2 - 1, [(shares.side_end, 0), (shares.line_start, 0)]),
        (2 * tiles - 2, [(shares.line_end, 1), (shares.side_start, 1), (shares.line_end, 0), (shares.block_start, 0)]),
        (2 * tiles - 1, [(shares.side_end, 1), (shares.block_start, 1)]),
    ]
    for when in range(tiles, 2 * tiles):
        actions = [action for place, some in plan if place == when for action in some]
        if actions:

            @pl.when(step == when)
            def act():
                for action, chain in actions:
                    action(chain)

    @pl.when(step == 2 * tiles - 1)
    def end():
        shares.block_end(0, share_ref)
        shares.block_end(1, share_ref)


def finish(dqs, dks, dvs, x, grad_query, grad_values, rim, grad_depth, halo, grad_sum, weight, taps, sharers, count):
    tokens, width = x.shape
    rows = math.gcd(tokens, 256)
    tiles = tokens // rows
    blocks = len(dqs)
    wide = 4 * ATT
    shares = Shares(sharers, width // sharers, wide + LANES, count)
    early_columns = pl.BlockSpec((ATT, rows), lambda i: (0, jnp.minimum(i, tiles - 1)))

    def early_rows(columns):
        return pl.BlockSpec((rows, columns), lambda i: (jnp.minimum(i, tiles - 1), 0))

    late_rows = pl.BlockSpec((rows, width), lambda i: (jnp.maximum(i - tiles, 0), 0))
    args = list(dqs) + list(dks) + list(dvs)
    args += [x, grad_query, grad_values, rim, grad_depth, halo, grad_sum, weight, taps]
    return pl.pallas_call(
        functools.partial(finish_kernel, blocks, rows, tiles, shares),
        grid=(2 * tiles,),
        in_specs=[early_columns] * (3 * blocks)
        + [
            early_rows(width),
            early_rows(ATT),
            all_of(grad_values.shape),
            all_of(rim.shape),
            all_of(grad_depth.shape),
            all_of(halo.shape),
            late_rows,
            all_of((width, wide)),
            all_of(taps.shape),
        ],
        out_specs=[late_rows, all_of((shares.rows, wide + LANES))],
        out_shape=[shaped((tokens, width), BF), shaped((shares.rows, wide + LANES), F32)],
        scratch_shapes=[
            pltpu.VMEM((rows + 32, width), F32),
            pltpu.VMEM((tokens, wide), BF),
            pltpu.VMEM((8, wide), F32),
        ]
        + shares.scratch(),
        compiler_params=pltpu.CompilerParams(
            collective_id=1, has_side_effects=True, vmem_limit_bytes=60 * MIB
        ),
        cost_estimate=pl.CostEstimate(
            flops=4 * tokens * width * wide, bytes_accessed=40 * tokens * width, transcendentals=0
        ),
        name="finish",
    )(*args)


def shifted_from(value, axis, step):
    count = lax.axis_size(axis)
    return lax.ppermute(value, axis, [((i + step) % count, i) for i in range(count)])


def local(
    hidden,
    separators,
    out_grad,
    w_query,
    b_query,
    w_key,
    w_value,
    b_value,
    depth_kernel,
    w_point,
    b_keyconv,
    w_kernel,
    kernel_bias,
    w_convout,
    b_convout,
    w_dense,
    b_dense,
    gain_attn,
    shift_attn,
    w_up,
    b_up,
    w_down,
    b_down,
    gain_out,
    shift_out,
):
    count = lax.axis_size("blk")
    sharers = lax.axis_size("dp")
    me = lax.axis_index("blk")
    x, cotangent = hidden[0], out_grad[0]
    tokens, width = x.shape
    first = me * tokens
    last = count - 1

    others = [shifted_from(x, "blk", step) for step in range(1, count)]
    groups, units = w_up.shape[0], w_up.shape[2]
    shard, part = w_query.shape[0], b_query.shape[0]
    thin = jnp.pad(jnp.stack([b_query, b_value, b_keyconv, b_convout], axis=1), ((0, shard - part), (0, 0)))
    small = jnp.concatenate(
        [
            jnp.stack([b_dense, gain_attn, shift_attn, b_down, gain_out, shift_out], axis=1),
            depth_kernel,
            thin,
            b_up.reshape(-1, shard).T,
            jnp.pad(w_kernel, ((0, shard - part), (0, 0))),
        ],
        axis=1,
    )
    fields = small.shape[1]
    small = jnp.pad(small, ((0, 0), (0, LANES - fields)))
    weight = gather_columns([w_query, w_key, w_value, w_convout, w_point], small, sharers)
    late = [
        w_dense.astype(BF),
        jnp.concatenate([w_up[g] for g in range(groups)], axis=1).astype(BF),
        jnp.concatenate([w_down[g] for g in range(groups)], axis=1).astype(BF),
    ]
    weight, late = lax.optimization_barrier((weight, late))
    wt_dense, wt_up, wt_down = [lax.all_gather(v, "dp", axis=0, tiled=True) for v in late]
    small = weight[:, 5 * ATT :]
    wide_vectors = small[:, :15].astype(F32).T
    vectors = jnp.pad(wide_vectors[:6], ((0, 2), (0, 0)))
    taps = jnp.pad(wide_vectors[6:], ((0, 16 - KSIZE), (0, 0)))
    small = small.reshape(sharers, shard, LANES)
    thin = small[:, :part, 15:19].reshape(ATT, 4).astype(F32).T
    ups = b_up.shape[0] // shard
    bias_up = small[:, :, 19 : 19 + ups].transpose(0, 2, 1).reshape(1, -1).astype(F32)
    wt_kernel = small[:, :part, 19 + ups : fields].reshape(ATT, HEADS, KSIZE)
    wt_kernel = jnp.pad(wt_kernel.transpose(2, 1, 0), ((0, 0), (0, 8 - HEADS), (0, 0))).reshape(8 * KSIZE, ATT)
    bias_kernel = jnp.pad(kernel_bias.reshape(HEADS, KSIZE).T, ((0, 0), (0, 8 - HEADS))).reshape(8 * KSIZE, 1)
    bias_qkv = jnp.concatenate([thin[0], jnp.zeros((ATT,), F32), thin[1]])
    bias, bias_t = bias_qkv.reshape(1, -1), bias_qkv.reshape(-1, 1)

    query, query_t, key, key_t, value, value_t, norms = project(x, weight, bias, bias_t, 3)
    keys = [(key, key_t, value, value_t, norms)]
    outs, probs = [], []
    for step in range(count):
        if step > 0:
            keys.append(project(others[step - 1], weight, bias, bias_t, 2))
        places = jnp.stack(
            [separators[0], first, lax.rem(me + step, count) * tokens, count * tokens]
        ).astype(jnp.int32)
        out, prob = attend(places, query_t, keys[step][0], keys[step][3], keys[step][4])
        outs.append(out)
        probs.append(prob)
    nothing = jnp.zeros((16, width), BF)
    if count > 1:
        before = jnp.where(me > 0, others[count - 2][tokens - 16 :], nothing)
        after = jnp.where(me < last, others[0][:16], nothing)
    else:
        before = after = nothing
    halo = jnp.concatenate([before, after], axis=0)
    depth, keyconv, attn_key, kernt, kern, conv, values, rim = mix(
        places, x, halo, query, taps, weight, thin[3:4], thin[2:3], wt_kernel, bias_kernel
    )
    output, grad_sum, grad_conv, grads_t, sides, (gw_dense, gw_up, gw_down, g_vectors, gb_up) = middle(
        outs, conv, x, cotangent, wt_dense, wt_up, wt_down, vectors, bias_up
    )
    grad_query_conv, grad_depth, grad_values, gw_point, gw_kernel, g_bias, g_taps = mix_back(
        x, halo, values, rim, grad_conv, kernt, kern, query, keyconv, attn_key, depth, weight, wt_kernel
    )
    low_rows = jnp.concatenate([grad_values[:16].astype(BF), grad_depth[:16]], axis=1)
    high_rows = jnp.concatenate([grad_values[tokens + 16 :].astype(BF), grad_depth[tokens - 16 :]], axis=1)
    from_before = lax.ppermute(high_rows, "blk", [(i, i + 1) for i in range(last)])
    from_after = lax.ppermute(low_rows, "blk", [(i + 1, i) for i in range(last)])
    rims = jnp.concatenate([from_before, from_after], axis=0)

    gw_kernel, gb_keyconv = (
        gw_kernel[: 8 * KSIZE].reshape(KSIZE, 8, ATT)[:, :HEADS].transpose(2, 1, 0),
        gw_kernel[8 * KSIZE],
    )
    g_bias = g_bias[: 8 * KSIZE, 0].reshape(KSIZE, 8)[:, :HEADS].T.reshape(-1)
    by_device = [
        jnp.concatenate([g_vectors[:6], g_taps[:KSIZE]], axis=0)
        .reshape(15, sharers, shard)
        .transpose(1, 0, 2)
        .reshape(sharers, -1),
        gb_keyconv.reshape(sharers, -1),
        gb_up[0].reshape(sharers, -1),
        gw_kernel.reshape(sharers, -1),
        jnp.broadcast_to(g_bias[None], (sharers, HEADS * KSIZE)),
    ]
    sizes = [v.shape[1] for v in by_device]
    gathered = jnp.concatenate(by_device, axis=1)
    extra = -(-gathered.shape[1] // width)
    gathered = jnp.pad(gathered, ((0, 0), (0, extra * width - gathered.shape[1])))
    pieces = [gw_dense, gw_up, gw_down, gw_point]
    pieces = [v.reshape(sharers, -1, width) for v in pieces] + [gathered.astype(BF).reshape(sharers, extra, width)]
    heights = [v.shape[1] for v in pieces]
    packed = jnp.concatenate(pieces, axis=1)
    packed, sides = lax.optimization_barrier((packed, sides))
    packed = lax.psum_scatter(packed, "dp", scatter_dimension=0, tiled=False)
    packed = lax.psum(packed, "blk").astype(F32)

    dqs, dks, dvs = [], [], []
    for step in list(range(1, count)) + [0]:
        key, key_t, value, value_t, norms = keys[step]
        dq, dk, dv = attend_back(probs[step], value, key_t, grads_t[step], sides[step], query_t, BF if step else F32)
        if step:
            dk, dv = shifted_from(dk, "blk", count - step), shifted_from(dv, "blk", count - step)
        dqs.append(dq)
        dks.append(dk)
        dvs.append(dv)
    grad_hidden, share = finish(
        dqs, dks, dvs, x, grad_query_conv, grad_values, rims[:, :ATT], grad_depth, rims[:, ATT:], grad_sum, weight, taps, sharers, count
    )
    gw = [share[:, at * ATT : (at + 1) * ATT] for at in range(4)]
    biases = share[: 4 * ATT // LANES, 4 * ATT :].reshape(4, sharers, part)
    biases = lax.dynamic_index_in_dim(biases, lax.axis_index("dp"), 1, keepdims=False)

    def ends_of(sizes):
        return [sum(sizes[: at + 1]) for at in range(len(sizes))]

    rows = [packed[end - size : end] for end, size in zip(ends_of(heights), heights)]
    grad_w_up = rows[1].reshape(w_up.shape[1], groups, units).transpose(1, 0, 2)
    grad_w_down = rows[2].reshape(w_down.shape[1], groups, -1).transpose(1, 0, 2)
    flat = rows[4].reshape(-1)
    fields = [flat[end - size : end] for end, size in zip(ends_of(sizes), sizes)]
    grad_vec = fields[0].reshape(15, shard)
    return (
        output[None],
        grad_hidden[None],
        gw[0],
        biases[0],
        gw[1],
        gw[2],
        biases[2],
        grad_vec[6:].T,
        rows[3].reshape(shard, ATT),
        fields[1],
        fields[3].reshape(w_kernel.shape),
        fields[4],
        gw[3],
        biases[3],
        rows[0],
        grad_vec[0],
        grad_vec[1],
        grad_vec[2],
        grad_w_up,
        fields[2],
        grad_w_down,
        grad_vec[3],
        grad_vec[4],
        grad_vec[5],
    )


def solution(mesh):
    placed = (
        P("dp", "blk", None),
        P("dp"),
        P("dp", "blk", None),
        P("dp", None),
        P("dp"),
        P("dp", None),
        P("dp", None),
        P("dp"),
        P("dp", None),
        P("dp", None),
        P("dp"),
        P("dp", None),
        P(),
        P("dp", None),
        P("dp"),
        P("dp", None),
        P("dp"),
        P("dp"),
        P("dp"),
        P(None, "dp", None),
        P("dp"),
        P(None, "dp", None),
        P("dp"),
        P("dp"),
        P("dp"),
    )
    return jax.shard_map(
        local,
        mesh=mesh,
        in_specs=placed,
        out_specs=(
            P("dp", "blk", None),
            P("dp", "blk", None),
            P("dp", None),
            P("dp"),
            P("dp", None),
            P("dp", None),
            P("dp"),
            P("dp", None),
            P("dp", None),
            P("dp"),
            P("dp", None),
            P(),
            P("dp", None),
            P("dp"),
            P("dp", None),
            P("dp"),
            P("dp"),
            P("dp"),
            P(None, "dp", None),
            P("dp"),
            P(None, "dp", None),
            P("dp"),
            P("dp"),
            P("dp"),
        ),
        check_vma=False,
    )
```

```python
import functools, math
import jax, jax.numpy as jnp
from jax import lax
from jax.experimental import pallas as pl
from jax.experimental.pallas import tpu as pltpu
from jax.sharding import PartitionSpec as P

HEADS = 6
HD = 64
KSIZE = 9
REACH = 4
ATT = 384
EPS = 1e-12
BF = jnp.bfloat16
F32 = jnp.float32
MIB = 2**20
EXCLUDED = 2.0**100
SAFE_SCORE = 50.0


def mm(left, right):
    return jnp.dot(left, right, preferred_element_type=F32)


def mm_nt(left, right):
    return lax.dot_general(left, right, (((1,), (1,)), ((), ())), preferred_element_type=F32)


def mm_tn(left, right):
    return lax.dot_general(left, right, (((0,), (0,)), ((), ())), preferred_element_type=F32)


def in_lanes(rows, columns):
    lane = lax.broadcasted_iota(jnp.int32, (rows, 128), 1)
    out = jnp.zeros((rows, 128), F32)
    for at, column in enumerate(columns):
        out = jnp.where(lane == at, column, out)
    return out.astype(BF)


def in_rows(columns, rows):
    row = lax.broadcasted_iota(jnp.int32, (16, columns), 0)
    out = jnp.zeros((16, columns), F32)
    for at, values in enumerate(rows):
        out = jnp.where(row == at, values, out)
    return out.astype(BF)


def three_parts(values):
    high = values.astype(BF).astype(F32)
    rest = values - high
    middle = rest.astype(BF).astype(F32)
    return high, middle, (rest - middle).astype(BF).astype(F32)


def put_head(ref, head, values):
    odd = lax.rem(head, 2) == 1
    none = jnp.zeros_like(values)
    ref[0:HD, :] = jnp.where(odd, none, values)
    ref[HD : 2 * HD, :] = jnp.where(odd, values, none)


def attend_kernel(keys, queries, chunk, at_ref, q_ref, k_ref, v_ref, norm_ref, o_ref, p_ref, key_side, query_side):
    head, tile = pl.program_id(0), pl.program_id(1)
    separator, first_query, first_key = at_ref[0], at_ref[1], at_ref[2]

    @pl.when((head == 0) & (tile == 0))
    def start():
        position = first_key + lax.broadcasted_iota(jnp.int32, (keys, 128), 0)
        late = (position >= separator).astype(F32)
        key_side[...] = in_lanes(keys, [1.0 - late, late, 1.0, 1.0, 1.0])
        query_side[2 * HD + 16 :, :] = jnp.zeros((2 * HD - 16, queries), BF)

    put_head(query_side, head, q_ref[...])
    position = first_query + tile * queries + lax.broadcasted_iota(jnp.int32, (16, queries), 1)
    late = (position >= separator).astype(F32)
    excluded = [-EXCLUDED * late, -EXCLUDED * (1.0 - late)]
    query_side[2 * HD : 2 * HD + 16, :] = in_rows(queries, excluded)
    o_ref[0, HD + 8 : HD + 16, :] = jnp.zeros((8, queries), F32)
    wide = q_ref[...].astype(F32)
    largest = jnp.max(jnp.sum(wide * wide, axis=0, keepdims=True)) * jnp.max(norm_ref[...])

    def scores(at):
        part = slice(at * chunk, (at + 1) * chunk)
        return mm(
            jnp.concatenate([k_ref[part, :], key_side[part, :]], axis=1), query_side[...]
        )

    @pl.when(jnp.logical_not(largest <= SAFE_SCORE * SAFE_SCORE))
    def shifted():
        best = jnp.full((1, queries), -4.0 * EXCLUDED, F32)
        for at in range(keys // chunk):
            best = jnp.maximum(best, jnp.max(scores(at), axis=0, keepdims=True))
        parts = three_parts(jnp.where(best < -0.5 * EXCLUDED, 0.0, best))
        query_side[2 * HD : 2 * HD + 16, :] = in_rows(queries, excluded + [-part for part in parts])
        o_ref[0, HD + 8 : HD + 16, :] = jnp.broadcast_to(
            jnp.where(best < -0.5 * EXCLUDED, best, parts[0] + parts[1] + parts[2]), (8, queries)
        )

    ones = in_rows(chunk, [1.0])
    total = jnp.zeros((HD + 16, queries), F32)
    for at in range(keys // chunk):
        part = slice(at * chunk, (at + 1) * chunk)
        probs = jnp.exp(scores(at)).astype(BF)
        p_ref[0, part, :] = probs
        total = total + mm(jnp.concatenate([v_ref[:, part], ones], axis=0), probs)
    o_ref[0, 0 : HD + 8, :] = total[0 : HD + 8, :]


def attend(at, query_t, key, value_t, norms):
    tokens, keys = query_t.shape[1], key.shape[0]
    queries, chunk = math.gcd(tokens, 1024), math.gcd(keys, 512)
    return pl.pallas_call(
        functools.partial(attend_kernel, keys, queries, chunk),
        grid=(HEADS, tokens // queries),
        in_specs=[
            pl.BlockSpec(memory_space=pltpu.SMEM),
            pl.BlockSpec((HD, queries), lambda h, i: (h, i)),
            pl.BlockSpec((keys, 2 * HD), lambda h, i: (0, h // 2)),
            pl.BlockSpec((HD, keys), lambda h, i: (h, 0)),
            pl.BlockSpec(norms.shape, lambda h, i: (0, 0)),
        ],
        out_specs=[
            pl.BlockSpec((1, HD + 16, queries), lambda h, i: (h, 0, i)),
            pl.BlockSpec((1, keys, queries), lambda h, i: (h, 0, i)),
        ],
        out_shape=[
            jax.ShapeDtypeStruct((HEADS, HD + 16, tokens), F32),
            jax.ShapeDtypeStruct((HEADS, keys, tokens), BF),
        ],
        scratch_shapes=[pltpu.VMEM((keys, 128), BF), pltpu.VMEM((4 * HD, queries), BF)],
        compiler_params=pltpu.CompilerParams(vmem_limit_bytes=56 * MIB),
        cost_estimate=pl.CostEstimate(
            flops=16 * ATT * tokens * keys,
            bytes_accessed=2 * HEADS * tokens * keys,
            transcendentals=HEADS * tokens * keys,
        ),
        name="attend",
    )(at, query_t, key, value_t, norms)


def attend_back_kernel(first, keys, queries, chunk, p_ref, v_ref, kt_ref, g_ref, side_ref, q_ref, dq_ref, dk_ref, dv_ref, value_side, grad_side, dk_sum, dv_sum):
    head, tile = pl.program_id(0), pl.program_id(1)

    @pl.when((head == 0) & (tile == 0))
    def start():
        value_side[...] = in_lanes(chunk, [1.0, 1.0, 1.0])
        grad_side[2 * HD + 16 :, :] = jnp.zeros((2 * HD - 16, queries), BF)

    @pl.when(tile == 0)
    def fresh():
        dk_sum[...] = jnp.zeros_like(dk_sum)
        dv_sum[...] = jnp.zeros_like(dv_sum)

    put_head(grad_side, first + head, g_ref[...])
    grad_side[2 * HD : 2 * HD + 16, :] = side_ref[0]
    total = jnp.zeros((HD, queries), F32)
    for at in range(keys // chunk):
        part = slice(at * chunk, (at + 1) * chunk)
        probs = p_ref[0, part, :]
        spread = mm(jnp.concatenate([v_ref[part, :], value_side[...]], axis=1), grad_side[...])
        grad_scores = (probs.astype(F32) * spread).astype(BF)
        dv_sum[:, part] += mm_nt(g_ref[...], probs)
        dk_sum[:, part] += mm_nt(q_ref[...], grad_scores)
        total = total + mm(kt_ref[:, part], grad_scores)
    dq_ref[...] = (total * (HD**-0.5)).astype(BF)

    @pl.when(tile == pl.num_programs(1) - 1)
    def finish():
        dk_ref[...] = dk_sum[...].astype(BF)
        dv_ref[...] = dv_sum[...].astype(BF)


def attend_back(probs, value, key_t, grad_t, side, query_t, first, heads):
    tokens, keys = query_t.shape[1], value.shape[0]
    queries, chunk = math.gcd(tokens, 512), math.gcd(keys, 512)
    by_token = pl.BlockSpec((HD, queries), lambda h, i: (first + h, i))
    by_key = pl.BlockSpec((HD, keys), lambda h, i: (first + h, 0))
    return pl.pallas_call(
        functools.partial(attend_back_kernel, first, keys, queries, chunk),
        grid=(heads, tokens // queries),
        in_specs=[
            pl.BlockSpec((1, keys, queries), lambda h, i: (first + h, 0, i)),
            pl.BlockSpec((keys, 2 * HD), lambda h, i: (0, (first + h) // 2)),
            by_key,
            by_token,
            pl.BlockSpec((1, 16, queries), lambda h, i: (first + h, 0, i)),
            by_token,
        ],
        out_specs=[
            pl.BlockSpec((HD, queries), lambda h, i: (h, i)),
            pl.BlockSpec((HD, keys), lambda h, i: (h, 0)),
            pl.BlockSpec((HD, keys), lambda h, i: (h, 0)),
        ],
        out_shape=[
            jax.ShapeDtypeStruct((heads * HD, tokens), BF),
            jax.ShapeDtypeStruct((heads * HD, keys), BF),
            jax.ShapeDtypeStruct((heads * HD, keys), BF),
        ],
        scratch_shapes=[
            pltpu.VMEM((chunk, 128), BF),
            pltpu.VMEM((4 * HD, queries), BF),
            pltpu.VMEM((HD, keys), F32),
            pltpu.VMEM((HD, keys), F32),
        ],
        compiler_params=pltpu.CompilerParams(vmem_limit_bytes=56 * MIB),
        cost_estimate=pl.CostEstimate(
            flops=32 * heads * HD * tokens * keys,
            bytes_accessed=2 * heads * tokens * keys,
            transcendentals=0,
        ),
        name="attend_back",
    )(probs, value, key_t, grad_t, side, query_t)


def all_of(shape):
    return pl.BlockSpec(shape, lambda *at: (0,) * len(shape))


def rows_of(rows, width):
    return pl.BlockSpec((rows, width), lambda i: (i, 0))


def columns_of(height, columns):
    return pl.BlockSpec((height, columns), lambda i: (0, i))


def run_tiles(kernel, name, steps, inputs, outputs, scratch, flops, aliases=None):
    args, in_specs = zip(*inputs)
    shapes, out_specs = zip(*outputs)
    size = sum(math.prod(v.shape) * v.dtype.itemsize for v in args + shapes)
    return pl.pallas_call(
        kernel,
        grid=(steps,),
        in_specs=list(in_specs),
        out_specs=list(out_specs),
        out_shape=list(shapes),
        scratch_shapes=scratch,
        input_output_aliases=aliases or {},
        compiler_params=pltpu.CompilerParams(vmem_limit_bytes=60 * MIB),
        cost_estimate=pl.CostEstimate(flops=flops, bytes_accessed=size, transcendentals=0),
        name=name,
    )(*args)


def shaped(shape, dtype):
    return jax.ShapeDtypeStruct(shape, dtype)


def project_kernel(parts, x_ref, w_ref, thin_ref, thin_columns_ref, *refs):
    norm_ref, flipped = refs[2 * parts], refs[2 * parts + 1]
    skip = (3 - parts) * ATT

    @pl.when(pl.program_id(0) == 0)
    def start():
        norm_ref[...] = jnp.zeros_like(norm_ref)
        flipped[...] = w_ref[:, skip:].T

    x = x_ref[...]
    plain = mm(x, w_ref[:, skip:])
    turned = mm_nt(flipped[...], x)
    for part in range(parts):
        own = slice(part * ATT, (part + 1) * ATT)
        bias, bias_t = 0.0, 0.0
        if part != parts - 2:
            at = 1 if part == parts - 1 else 0
            bias, bias_t = thin_ref[at : at + 1, :], thin_columns_ref[:, THIN_AT + at : THIN_AT + at + 1]
        refs[2 * part][...] = (plain[:, own] + bias).astype(BF)
        across = (turned[own] + bias_t).astype(BF)
        if part == parts - 2:
            wide = across.astype(F32)
            for head in range(HEADS):
                cells = wide[head * HD : (head + 1) * HD]
                size = jnp.sum(cells * cells, axis=0, keepdims=True)
                norm_ref[...] = jnp.maximum(norm_ref[...], size)
        if part < parts - 2:
            across = (across.astype(F32) * (HD**-0.5)).astype(BF)
        refs[2 * part + 1][...] = across


def project(x, weight, thin, thin_columns, parts):
    tokens, width = x.shape
    wide = 3 * ATT
    tile = math.gcd(tokens, 512)
    outputs = []
    for part in range(parts):
        outputs.append((shaped((tokens, ATT), BF), rows_of(tile, ATT)))
        outputs.append((shaped((ATT, tokens), BF), columns_of(ATT, tile)))
    outputs.append((shaped((8, tile), F32), all_of((8, tile))))
    return run_tiles(
        functools.partial(project_kernel, parts),
        "project",
        tokens // tile,
        [
            (x, rows_of(tile, width)),
            (weight, all_of((width, wide))),
            (thin, all_of(thin.shape)),
            (thin_columns, all_of(thin_columns.shape)),
        ],
        outputs,
        [pltpu.VMEM((parts * ATT, width), BF)],
        4 * tokens * width * parts * ATT,
    )


def fill_rows(window, x_ref, halo_ref, tile, tiles, rows):
    first = tile * rows
    tokens = x_ref.shape[0]
    before = x_ref[pl.ds(pl.multiple_of(jnp.maximum(first - 16, 0), 16), 16), :]
    after = x_ref[pl.ds(pl.multiple_of(jnp.minimum(first + rows, tokens - 16), 16), 16), :]
    window[0:16, :] = jnp.where(tile == 0, halo_ref[0:16, :], before).astype(window.dtype)
    window[16 : 16 + rows, :] = x_ref[pl.ds(pl.multiple_of(first, rows), rows), :].astype(window.dtype)
    window[16 + rows :, :] = jnp.where(
        tile == tiles - 1, halo_ref[16:32, :], after
    ).astype(window.dtype)


def fill_window(window, x_ref, halo_ref, tile, rows):
    fill_rows(window, x_ref, halo_ref, tile, pl.num_programs(0), rows)


def fill_spread(spread):
    row = lax.broadcasted_iota(jnp.int32, (128, ATT), 0)
    head = lax.broadcasted_iota(jnp.int32, (128, ATT), 1) // HD
    for tap in range(KSIZE):
        spread[:, tap * ATT : (tap + 1) * ATT] = (row == tap * 8 + head).astype(F32).astype(BF)


def mix_kernel(rows, at_ref, x_ref, halo_ref, q_ref, wc_ref, wp_ref, wide_ref, thin_ref, wk_ref, bk_ref, depth_ref, keyconv_ref, attn_ref, kernt_ref, kern_ref, conv_ref, out_ref, rim_ref, window, conv_window, spread):
    tile = pl.program_id(0)
    last = pl.num_programs(0) - 1

    @pl.when(tile == 0)
    def start():
        fill_spread(spread)

    fill_window(window, x_ref, halo_ref, tile, rows)
    width = window.shape[1]
    for at in range(0, width, 128):
        some = slice(at, at + 128)
        total = jnp.zeros((rows, 128), F32)
        for tap in range(KSIZE):
            total = total + window[12 + tap : 12 + tap + rows, some] * wide_ref[TAPS_AT + tap : TAPS_AT + tap + 1, some]
        depth_ref[:, some] = total.astype(BF)
    position = (
        at_ref[1] + tile * rows - 16 + lax.broadcasted_iota(jnp.int32, (rows + 32, ATT), 0)
    )
    inside = (position >= 0) & (position < at_ref[3])
    values = mm(window[...].astype(BF), wc_ref[...]) + thin_ref[3:4, :]
    values = jnp.where(inside, values, 0.0).astype(BF)
    out_ref[...] = values[16 : 16 + rows]

    @pl.when(tile == 0)
    def first_rim():
        rim_ref[0:16, :] = values[0:16]

    @pl.when(tile == last)
    def last_rim():
        rim_ref[16:32, :] = values[16 + rows :]

    conv_window[...] = values.astype(F32)
    keyconv = mm(depth_ref[...], wp_ref[...]) + thin_ref[2:3, :]
    keyconv_ref[...] = keyconv
    attn_key = (keyconv * q_ref[...].astype(F32)).astype(BF)
    attn_ref[...] = attn_key
    logits = mm_nt(wk_ref[...], attn_key) + bk_ref[:, BIAS_AT : BIAS_AT + 1]
    slabs = [logits[8 * tap : 8 * tap + 8] for tap in range(KSIZE)]
    best = functools.reduce(jnp.maximum, slabs)
    slabs = [jnp.exp(slab - best) for slab in slabs]
    share = 1.0 / functools.reduce(jnp.add, slabs)
    slabs = [slab * share for slab in slabs]
    kernt = jnp.concatenate(slabs + [jnp.zeros((128 - 8 * KSIZE, rows), F32)], axis=0)
    kernt_ref[...] = kernt[0 : 8 * KSIZE]
    kern = kernt.astype(BF).T
    kern_ref[...] = kern
    total = jnp.zeros((rows, ATT), F32)
    for tap in range(KSIZE):
        total = total + mm(kern, spread[:, tap * ATT : (tap + 1) * ATT]) * conv_window[12 + tap : 12 + tap + rows, :]
    conv_ref[...] = total.astype(BF)


def column_block(weight, place):
    return pl.BlockSpec((weight.shape[0], ATT), lambda i: (0, place))


def mix(at, x, halo, query, weight, wide_vectors, thin, w_kernel, kernel_bias):
    tokens, width = x.shape
    rows = math.gcd(tokens, 256)
    whole = [(weight, column_block(weight, 3)), (weight, column_block(weight, 4))]
    whole += [(v, all_of(v.shape)) for v in (wide_vectors, thin, w_kernel, kernel_bias)]
    return run_tiles(
        functools.partial(mix_kernel, rows),
        "mix",
        tokens // rows,
        [
            (at, pl.BlockSpec(memory_space=pltpu.SMEM)),
            (x, all_of(x.shape)),
            (halo, all_of(halo.shape)),
            (query, rows_of(rows, ATT)),
        ]
        + whole,
        [
            (shaped((tokens, width), BF), rows_of(rows, width)),
            (shaped((tokens, ATT), F32), rows_of(rows, ATT)),
            (shaped((tokens, ATT), BF), rows_of(rows, ATT)),
            (shaped((8 * KSIZE, tokens), F32), columns_of(8 * KSIZE, rows)),
            (shaped((tokens, 128), BF), rows_of(rows, 128)),
            (shaped((tokens, ATT), BF), rows_of(rows, ATT)),
            (shaped((tokens, ATT), BF), rows_of(rows, ATT)),
            (shaped((32, ATT), BF), all_of((32, ATT))),
        ],
        [
            pltpu.VMEM((rows + 32, width), F32),
            pltpu.VMEM((rows + 32, ATT), F32),
            pltpu.VMEM((128, KSIZE * ATT), BF),
        ],
        4 * tokens * width * ATT * 4,
    )


def normal(values):
    centre = values - jnp.mean(values, axis=-1, keepdims=True)
    scale = lax.rsqrt(jnp.mean(centre * centre, axis=-1, keepdims=True) + EPS)
    return centre * scale, scale


def normal_back(grad, unit, scale):
    return scale * (
        grad
        - jnp.mean(grad, axis=-1, keepdims=True)
        - unit * jnp.mean(grad * unit, axis=-1, keepdims=True)
    )


def gelu_parts(values):
    size = jnp.abs(values)
    t = 1.0 / (1.0 + (0.3275911 * math.sqrt(0.5)) * size)
    tail = t * (
        0.5 * 0.254829592
        + t * (0.5 * -0.284496736 + t * (0.5 * 1.421413741 + t * (0.5 * -1.453152027 + t * (0.5 * 1.061405429))))
    )
    bell = jnp.exp(-0.5 * values * values)
    tail = tail * bell
    share = jnp.where(values < 0.0, tail, 1.0 - tail)
    return values * share, share + values * (bell * (1.0 / math.sqrt(2.0 * math.pi)))


def middle_kernel(blocks, rows, units, *refs):
    o_refs, refs = refs[:blocks], refs[blocks:]
    (conv_ref, x_ref, og_ref, wd_ref, wu_ref, wn_ref, vec_ref, bu_ref), refs = refs[:8], refs[8:]
    (out_ref, sum_ref, gconv_ref), refs = refs[:3], refs[3:]
    g_refs, refs = refs[:blocks], refs[blocks:]
    side_refs, refs = refs[:blocks], refs[blocks:]
    (packed_ref, gvec_ref, gbu_ref, wd_sum, wu_sum, wn_sum, acts, slopes, staged, sems) = refs
    tile = pl.program_id(0)
    hidden_units = wu_ref.shape[1]
    groups = 2
    inner = ATT
    outer = hidden_units // groups

    @pl.when(tile == 0)
    def start():
        for ref in (wd_sum, wu_sum, wn_sum, gvec_ref, gbu_ref):
            ref[...] = jnp.zeros_like(ref)

    shifts = [ref[:, HD + 8 : HD + 9, :] for ref in o_refs]
    top = functools.reduce(jnp.maximum, shifts)
    weights = [jnp.exp(shift - top) for shift in shifts]
    mass = functools.reduce(jnp.add, [w * ref[:, HD : HD + 1, :] for w, ref in zip(weights, o_refs)])
    weights = [w / mass for w in weights]
    heads = functools.reduce(jnp.add, [w * ref[:, 0:HD, :] for w, ref in zip(weights, o_refs)])
    att_t = heads.reshape(ATT, rows).astype(BF)
    conv = conv_ref[...]
    vec = [vec_ref[at : at + 1, :] for at in range(6)]
    dense = mm(att_t.T, wd_ref[0:ATT, :]) + mm(conv, wd_ref[ATT:, :]) + vec[0]
    unit_one, scale_one = normal(dense + x_ref[...].astype(F32))
    normed = unit_one * vec[1] + vec[2]
    low = normed.astype(BF)
    downs = []
    for group in range(groups):
        mine = low[:, group * inner : (group + 1) * inner]
        down = jnp.zeros((rows, inner), F32)
        for at in range(0, outer, units):
            here = slice(group * outer + at, group * outer + at + units)
            upward = mm(mine, wu_ref[:, here]) + bu_ref[:, here]
            act, slope = gelu_parts(upward)
            act = act.astype(BF)
            acts[:, here] = act
            slopes[:, here] = slope.astype(BF)
            down = down + mm(act, wn_ref[at : at + units, group * inner : (group + 1) * inner])
        downs.append(down)
    unit_two, scale_two = normal(jnp.concatenate(downs, axis=1) + vec[3] + normed)
    out_ref[...] = (unit_two * vec[4] + vec[5]).astype(BF)
    og = og_ref[...].astype(F32)
    gvec_ref[4:5, :] += jnp.sum(og * unit_two, axis=0, keepdims=True)
    gvec_ref[5:6, :] += jnp.sum(og, axis=0, keepdims=True)
    grad_two = normal_back(og * vec[4], unit_two, scale_two)
    grad_down = grad_two.astype(BF)
    gvec_ref[3:4, :] += jnp.sum(grad_down.astype(F32), axis=0, keepdims=True)
    backs = []
    for group in range(groups):
        lanes = slice(group * inner, (group + 1) * inner)
        mine, grads = low[:, lanes], grad_down[:, lanes]
        mine_t = mine.T
        back = jnp.zeros((rows, inner), F32)
        for at in range(0, outer, units):
            here = slice(group * outer + at, group * outer + at + units)
            grad_act = mm_nt(grads, wn_ref[at : at + units, lanes])
            grad_up = (grad_act * slopes[:, here].astype(F32)).astype(BF)
            gbu_ref[0:1, here] += jnp.sum(grad_up.astype(F32), axis=0, keepdims=True)
            wn_sum[at : at + units, lanes] += mm_tn(acts[:, here], grads)
            wu_sum[:, here] += mm(mine_t, grad_up)
            back = back + mm_nt(grad_up, wu_ref[:, here])
        backs.append(back)
    grad_normed = grad_two + jnp.concatenate(backs, axis=1)
    gvec_ref[1:2, :] += jnp.sum(grad_normed * unit_one, axis=0, keepdims=True)
    gvec_ref[2:3, :] += jnp.sum(grad_normed, axis=0, keepdims=True)
    grad_one = normal_back(grad_normed * vec[1], unit_one, scale_one)
    sum_ref[...] = grad_one
    grad_dense = grad_one.astype(BF)
    gvec_ref[0:1, :] += jnp.sum(grad_dense.astype(F32), axis=0, keepdims=True)
    wd_sum[0:ATT, :] += mm(att_t, grad_dense)
    wd_sum[ATT:, :] += mm_tn(conv, grad_dense)
    gconv_ref[...] = mm_nt(grad_dense, wd_ref[ATT:, :]).astype(BF)
    grad_att = mm_nt(wd_ref[0:ATT, :], grad_dense).astype(BF).astype(F32).reshape(HEADS, HD, rows)
    for weight, g_ref, side_ref in zip(weights, g_refs, side_refs):
        share = (grad_att * weight).astype(BF)
        g_ref[...] = share.reshape(ATT, rows)
        delta = -jnp.sum(share.astype(F32) * heads, axis=1, keepdims=True)
        row = lax.broadcasted_iota(jnp.int32, (HEADS, 16, rows), 1)
        side = jnp.zeros((HEADS, 16, rows), F32)
        for at, part in enumerate(three_parts(delta)):
            side = jnp.where(row == at, part, side)
        side_ref[...] = side.astype(BF)

    @pl.when(tile == pl.num_programs(0) - 1)
    def finish():
        sharers = staged.shape[0]
        shard = wd_sum.shape[0] // sharers
        quarter = shard // 2
        width = wd_sum.shape[1]
        copies = []
        for owner in range(sharers):
            staged[owner, 0:shard] = wd_sum[owner * shard : (owner + 1) * shard].astype(BF)
            some = wu_sum[owner * quarter : (owner + 1) * quarter]
            for group in range(groups):
                pair = [some[:, at : at + width] for at in (2 * group * width, (2 * group + 1) * width)]
                staged[owner, (1 + group) * shard : (2 + group) * shard] = jnp.concatenate(pair, axis=0).astype(BF)
            some = wn_sum[owner * 2 * shard : (owner + 1) * 2 * shard]
            staged[owner, 3 * shard : 5 * shard] = some.astype(BF)
            copy = pltpu.make_async_copy(
                staged.at[owner], packed_ref.at[owner, 0 : 5 * shard], sems.at[owner]
            )
            copy.start()
            copies.append(copy)
        for copy in copies:
            copy.wait()


def middle(outs, conv, x, out_grad, w_dense, w_up, w_down, vectors, b_up, sharers):
    tokens, width = x.shape
    shard = width // sharers
    rows = math.gcd(tokens, 256)
    blocks = len(outs)
    heads = pl.BlockSpec((HEADS, HD + 16, rows), lambda i: (0, 0, i))
    side = pl.BlockSpec((HEADS, 16, rows), lambda i: (0, 0, i))
    once = [(v, all_of(v.shape)) for v in (w_dense, w_up, w_down, vectors, b_up)]
    results = run_tiles(
        functools.partial(middle_kernel, blocks, rows, 512),
        "middle",
        tokens // rows,
        [(o, heads) for o in outs]
        + [
            (conv, rows_of(rows, ATT)),
            (x, rows_of(rows, width)),
            (out_grad, rows_of(rows, width)),
        ]
        + once,
        [
            (shaped((tokens, width), BF), rows_of(rows, width)),
            (shaped((tokens, width), F32), rows_of(rows, width)),
            (shaped((tokens, ATT), BF), rows_of(rows, ATT)),
        ]
        + [(shaped((ATT, tokens), BF), columns_of(ATT, rows))] * blocks
        + [(shaped((HEADS, 16, tokens), BF), side)] * blocks
        + [
            (shaped((sharers, 6 * shard, width), BF), pl.BlockSpec(memory_space=pl.ANY)),
            (shaped((8, width), F32), all_of((8, width))),
            (shaped((8, w_up.shape[1]), F32), all_of((8, w_up.shape[1]))),
        ],
        [
            pltpu.VMEM(w_dense.shape, F32),
            pltpu.VMEM(w_up.shape, F32),
            pltpu.VMEM(w_down.shape, F32),
            pltpu.VMEM((rows, w_up.shape[1]), BF),
            pltpu.VMEM((rows, w_up.shape[1]), BF),
            pltpu.VMEM((sharers, 5 * shard, width), BF),
            pltpu.SemaphoreType.DMA((sharers,)),
        ],
        6 * tokens * (w_dense.size + w_up.size + w_down.size),
    )
    output, grad_sum, grad_conv = results[:3]
    return output, grad_sum, grad_conv, results[3 : 3 + blocks], results[3 + blocks : 3 + 2 * blocks], results[3 + 2 * blocks :]


def mix_back_kernel(rows, x_ref, halo_ref, values_ref, rim_ref, gconv_ref, kernt_ref, kern_ref, q_ref, keyconv_ref, attn_ref, depth_ref, wp_ref, wk_ref, gvec_ref, gbu_ref, unused, gq_ref, gdepth_ref, gvalues_ref, packed_ref, window, conv_window, summed, products, spread, wp_sum, values_sum, gwk_ref, gbias_ref, gtaps_ref, turn_wide, turn_thin, side, staged, sem):
    tile = pl.program_id(0)

    @pl.when(tile == 0)
    def start():
        fill_spread(spread)
        for ref in (values_sum, wp_sum, gwk_ref, gbias_ref, gtaps_ref, turn_wide, turn_thin):
            ref[...] = jnp.zeros_like(ref)

    fill_window(window, x_ref, halo_ref, tile, rows)
    fill_window(conv_window, values_ref, rim_ref, tile, rows)
    summed[...] = jnp.zeros_like(summed)
    grad_conv = gconv_ref[...].astype(F32)
    for tap in range(KSIZE):
        here = slice(tap * ATT, (tap + 1) * ATT)
        there = slice(12 + tap, 12 + tap + rows)
        products[:, here] = (grad_conv * conv_window[there, :]).astype(BF)
        summed[there, :] += mm(kern_ref[...], spread[:, here]) * grad_conv
    first = pl.multiple_of(tile * rows, rows)
    values_sum[pl.ds(first, rows + 32), :] += summed[...]
    grad_kernel = mm_nt(spread[...], products[...])
    slabs = [slice(8 * tap, 8 * tap + 8) for tap in range(KSIZE)]
    kernels = [kernt_ref[slab, :] for slab in slabs]
    mean = functools.reduce(jnp.add, [k * grad_kernel[slab] for k, slab in zip(kernels, slabs)])
    grad_logits = jnp.concatenate(
        [k * (grad_kernel[slab] - mean) for k, slab in zip(kernels, slabs)], axis=0
    ).astype(BF)
    wide_logits = grad_logits.astype(F32)
    gbias_ref[...] += jnp.concatenate(
        [
            jnp.broadcast_to(jnp.sum(wide_logits, axis=1, keepdims=True), (8 * KSIZE, 128)),
            jnp.zeros((8, 128), F32),
        ],
        axis=0,
    )
    gwk_ref[0 : 8 * KSIZE, :] += mm(grad_logits, attn_ref[...])
    grad_attn = mm_tn(grad_logits, wk_ref[...]).astype(BF).astype(F32)
    grad_keyconv = (grad_attn * q_ref[...].astype(F32)).astype(BF)
    gq_ref[...] = (grad_attn * keyconv_ref[...]).astype(BF)
    gwk_ref[8 * KSIZE : 8 * KSIZE + 1, :] += jnp.sum(grad_keyconv.astype(F32), axis=0, keepdims=True)
    wp_sum[...] += mm_tn(depth_ref[...], grad_keyconv)
    grad_depth = mm_nt(grad_keyconv, wp_ref[...]).astype(BF)
    gdepth_ref[...] = grad_depth
    wide = grad_depth.astype(F32)
    for at in range(0, window.shape[1], 128):
        some = slice(at, at + 128)
        for tap in range(KSIZE):
            gtaps_ref[tap : tap + 1, some] += jnp.sum(
                wide[:, some] * window[12 + tap : 12 + tap + rows, some], axis=0, keepdims=True
            )

    @pl.when(tile == pl.num_programs(0) - 1)
    def finish():
        gvalues_ref[...] = values_sum[...].astype(BF)
        sharers, shard, width = staged.shape
        part = ATT // sharers
        half = gbu_ref.shape[1] // sharers // 2
        turn_wide[0:6, :] = gvec_ref[0:6, :]
        turn_wide[TAPS_AT : TAPS_AT + KSIZE, :] = gtaps_ref[0:KSIZE, :]
        vectors = turn_wide[...].T
        for h in range(HEADS):
            for j in range(KSIZE):
                turn_wide[h * KSIZE + j : h * KSIZE + j + 1, 0:LANES] = gbias_ref[j * 8 + h : j * 8 + h + 1, :]
                turn_thin[h * KSIZE + j : h * KSIZE + j + 1, :] = gwk_ref[j * 8 + h : j * 8 + h + 1, :]
        bias = turn_wide[:, 0:LANES].T[0:1]
        turn_thin[THIN_AT : THIN_AT + 1, :] = gwk_ref[8 * KSIZE : 8 * KSIZE + 1, :]
        kernels = turn_thin[...].T
        side[...] = jnp.zeros_like(side)
        for owner in range(sharers):
            staged[owner, :, 0:ATT] = wp_sum[owner * shard : (owner + 1) * shard].astype(BF)
            staged[owner, :, ATT : ATT + LANES] = vectors[owner * shard : (owner + 1) * shard].astype(BF)
            side[0:part, :] = kernels[owner * part : (owner + 1) * part]
            for place in range(2):
                first = (2 * owner + place) * half
                side[part + place : part + place + 1, 0:half] = gbu_ref[0:1, first : first + half]
            side[part + 2 : part + 3, :] = bias
            staged[owner, :, ATT + LANES : ATT + 2 * LANES] = side[...].astype(BF)
            staged[owner, :, ATT + 2 * LANES :] = jnp.zeros((shard, width - ATT - 2 * LANES), BF)
        copy = pltpu.make_async_copy(staged, packed_ref.at[:, 5 * shard : 6 * shard], sem)
        copy.start()
        copy.wait()


def mix_back(x, halo, values, rim, grad_conv, kernt, kern, query, keyconv, attn_key, depth, weight, w_kernel, g_vectors, gb_up, packed):
    tokens, width = x.shape
    sharers, shard = packed.shape[0], packed.shape[1] // 6
    away = pl.BlockSpec(memory_space=pl.ANY)
    rows = math.gcd(tokens, 256)
    by_rows = [(v, rows_of(rows, v.shape[1])) for v in (kern, query, keyconv, attn_key, depth)]
    return run_tiles(
        functools.partial(mix_back_kernel, rows),
        "mix_back",
        tokens // rows,
        [(v, all_of(v.shape)) for v in (x, halo, values, rim)]
        + [(grad_conv, rows_of(rows, ATT)), (kernt, columns_of(8 * KSIZE, rows))]
        + by_rows
        + [(weight, column_block(weight, 4))]
        + [(v, all_of(v.shape)) for v in (w_kernel, g_vectors, gb_up)]
        + [(packed, away)],
        [
            (shaped((tokens, ATT), BF), rows_of(rows, ATT)),
            (shaped((tokens, width), BF), rows_of(rows, width)),
            (shaped((tokens + 32, ATT), BF), all_of((tokens + 32, ATT))),
            (shaped(packed.shape, BF), away),
        ],
        [
            pltpu.VMEM((rows + 32, width), F32),
            pltpu.VMEM((rows + 32, ATT), F32),
            pltpu.VMEM((rows + 32, ATT), F32),
            pltpu.VMEM((rows, KSIZE * ATT), BF),
            pltpu.VMEM((128, KSIZE * ATT), BF),
            pltpu.VMEM((width, ATT), F32),
            pltpu.VMEM((tokens + 32, ATT), F32),
            pltpu.VMEM((8 * KSIZE + 8, ATT), F32),
            pltpu.VMEM((8 * KSIZE + 8, LANES), F32),
            pltpu.VMEM((16, width), F32),
            pltpu.VMEM((LANES, width), F32),
            pltpu.VMEM((LANES, ATT), F32),
            pltpu.VMEM((shard, LANES), F32),
            pltpu.VMEM((sharers, shard, width), BF),
            pltpu.SemaphoreType.DMA(()),
        ],
        4 * tokens * width * ATT * 4,
        {15: 3},
    )


MESH = pl.DeviceIdType.MESH
LINE = 4
LANES = 128
TAPS_AT = 16
THIN_AT = 64
BIAS_AT = 100


def my_place(sharers):
    columns = sharers // (2 * LINE)
    me = lax.axis_index("dp")
    return me, me // (2 * columns), lax.rem(me // 2, columns), lax.rem(me, 2), columns


def greet(partners):
    barrier = pltpu.get_barrier_semaphore()
    for partner in partners:
        pl.semaphore_signal(barrier, inc=1, device_id=partner, device_id_type=MESH)
    return barrier


def remote(source, target, send_sem, recv_sem, device):
    return pltpu.make_async_remote_copy(
        src_ref=source,
        dst_ref=target,
        send_sem=send_sem,
        recv_sem=recv_sem,
        device_id=device,
        device_id_type=MESH,
    )


def gather_kernel(sharers, count, part, *refs):
    w_refs, refs = refs[:5], refs[5:]
    vector_refs, refs = refs[:6], refs[6:]
    thin_refs, refs = refs[:4], refs[4:]
    (taps_ref, up_ref, kernel_ref, bias_ref, head_ref, tail_ref), refs = refs[:6], refs[6:]
    (out_ref, wide_ref, thin_ref, thin_columns_ref, bias_up_ref, wk_ref, bk_ref, halo_ref), refs = refs[:8], refs[8:]
    rows, side, flat, thin_flat, edges, send_sem, recv_sem, edge_send, edge_recv = refs
    me, line, column, core, columns = my_place(sharers)
    block = lax.axis_index("blk")
    shard = out_ref.shape[1]
    base = len(w_refs) * ATT
    half = up_ref.shape[0] // 2

    def at(line, column, core):
        return (line * columns + column) * 2 + core

    lines = [lax.rem(line + step, LINE) for step in range(1, LINE)]
    sides = [lax.rem(column + step, columns) for step in range(1, columns)]
    partners = [{"dp": at(other, column, core)} for other in lines]
    across = [{"dp": at(line, other, core)} for other in sides]
    mate = {"dp": at(line, column, 1 - core)}
    ends = []
    if count > 1:
        ends = [{"blk": lax.rem(block + 1, count)}, {"blk": lax.rem(block + count - 1, count)}]
    barrier = greet(partners + across + [mate] + ends)
    for place, ref in enumerate(w_refs):
        out_ref[me, :, place * ATT : (place + 1) * ATT] = ref[...].astype(BF)
    rows[...] = jnp.zeros_like(rows)
    for place, ref in enumerate(vector_refs):
        rows[place : place + 1, 0:shard] = ref[...].reshape(1, shard)
    for place, ref in enumerate(thin_refs):
        rows[THIN_AT + place : THIN_AT + place + 1, 0:part] = ref[...].reshape(1, part)
    rows[BIAS_AT : BIAS_AT + 1, 0 : HEADS * KSIZE] = bias_ref[...].reshape(1, HEADS * KSIZE)
    rows[...] = rows[...].T
    side[...] = rows[0:shard]
    side[:, TAPS_AT : TAPS_AT + KSIZE] = taps_ref[...]
    out_ref[me, :, base : base + LANES] = side[...].astype(BF)
    side[...] = jnp.zeros_like(side)
    side[0:part, 0 : HEADS * KSIZE] = kernel_ref[...]
    side[part : part + 1, 0:half] = up_ref[0:half].reshape(1, half)
    side[part + 1 : part + 2, 0:half] = up_ref[half:].reshape(1, half)
    out_ref[me, :, base + LANES :] = side[...].astype(BF)
    pl.semaphore_wait(barrier, len(partners) + len(across) + 1 + len(ends))
    copies = []

    def pass_on(owner, devices):
        for device in devices:
            copy = remote(out_ref.at[owner], out_ref.at[owner], send_sem.at[len(copies)], recv_sem.at[owner], device)
            copy.start()
            copies.append(copy)

    def arrived(owner):
        pltpu.make_async_copy(out_ref.at[owner], out_ref.at[owner], recv_sem.at[owner]).wait()

    pass_on(me, across + partners + [mate])
    edge_copies = []
    for place, (ref, device) in enumerate(zip((tail_ref, head_ref), ends)):
        copy = remote(ref, edges.at[place], edge_send.at[place], edge_recv.at[place], device)
        copy.start()
        edge_copies.append(copy)
    for other in lines:
        owner = at(other, column, core)
        arrived(owner)
        pass_on(owner, across + [mate])
    for some in sides:
        for other in [line] + lines:
            owner = at(other, some, core)
            arrived(owner)
            pass_on(owner, [mate])
    nothing = jnp.zeros((16, halo_ref.shape[1]), BF)
    halo_ref[0:16, :] = nothing
    halo_ref[16:32, :] = nothing
    if count > 1:
        for copy in edge_copies:
            copy.wait()
        halo_ref[0:16, :] = jnp.where(block > 0, edges[0], nothing)
        halo_ref[16:32, :] = jnp.where(block < count - 1, edges[1], nothing)
    for j in range(KSIZE):
        for h in range(8):
            source = h * KSIZE + j if h < HEADS else 120
            bk_ref[j * 8 + h : j * 8 + h + 1, :] = rows[source : source + 1, :]
    for some in [column] + sides:
        for other in [line] + lines:
            arrived(at(other, some, 1 - core))
    for copy in copies:
        copy.wait_send()
    for owner in range(sharers):
        cells = out_ref[owner, :, base : base + LANES].astype(F32)
        flat[owner * shard : (owner + 1) * shard, :] = cells
        thin_flat[owner * part : (owner + 1) * part, :] = cells[0:part]
    turned = flat[...].T
    wide_ref[...] = turned[0 : wide_ref.shape[0]]
    thin_columns_ref[...] = thin_flat[...]
    thin_ref[...] = thin_flat[...].T[THIN_AT : THIN_AT + 8]
    for owner in range(sharers):
        cells = out_ref[owner, :, base + LANES :].astype(F32)
        thin_flat[owner * part : (owner + 1) * part, :] = cells[0:part]
        for place in range(2):
            first = (2 * owner + place) * half
            bias_up_ref[0:1, first : first + half] = cells[part + place : part + place + 1, 0:half]
    turned = thin_flat[...].T
    slabs = []
    for j in range(KSIZE):
        slabs += [turned[h * KSIZE + j : h * KSIZE + j + 1] for h in range(HEADS)]
        slabs.append(jnp.zeros((8 - HEADS, ATT), F32))
    wk_ref[...] = jnp.concatenate(slabs, axis=0).astype(BF)


def gather_columns(weights, vectors, thin, taps, b_up, w_kernel, kernel_bias, x, sharers, count):
    shard, part = weights[0].shape[0], thin[0].shape[0]
    tokens, width = x.shape
    wide = len(weights) * ATT + 2 * LANES
    columns = sharers // (2 * LINE)
    copies = LINE - 1 + columns - 1 + 1 + (LINE - 1) * columns + LINE * (columns - 1)
    args = list(weights) + list(vectors) + list(thin) + [taps, b_up, w_kernel, kernel_bias]
    shapes = [
        shaped((sharers, shard, wide), BF),
        shaped((32, width), F32),
        shaped((8, ATT), F32),
        shaped((ATT, LANES), F32),
        shaped((1, sharers * b_up.shape[0]), F32),
        shaped((8 * KSIZE, ATT), BF),
        shaped((8 * KSIZE, LANES), F32),
        shaped((32, width), BF),
    ]
    out, *rest = pl.pallas_call(
        functools.partial(gather_kernel, sharers, count, part),
        grid=(1,),
        in_specs=[all_of(v.shape) for v in args]
        + [
            pl.BlockSpec((16, width), lambda i: (0, 0)),
            pl.BlockSpec((16, width), lambda i: (tokens // 16 - 1, 0)),
        ],
        out_specs=[all_of(v.shape) for v in shapes],
        out_shape=shapes,
        scratch_shapes=[
            pltpu.VMEM((LANES, LANES), F32),
            pltpu.VMEM((shard, LANES), F32),
            pltpu.VMEM((width, LANES), F32),
            pltpu.VMEM((ATT, LANES), F32),
            pltpu.VMEM((2, 16, width), BF),
            pltpu.SemaphoreType.DMA((copies,)),
            pltpu.SemaphoreType.DMA((sharers,)),
            pltpu.SemaphoreType.DMA((2,)),
            pltpu.SemaphoreType.DMA((2,)),
        ],
        compiler_params=pltpu.CompilerParams(
            collective_id=0, has_side_effects=True, vmem_limit_bytes=60 * MIB
        ),
        name="gather_columns",
    )(*args, x, x)
    return (out.reshape(sharers * shard, wide), *rest)


class Shares:
    def __init__(self, sharers, rows, widths, line_first, count):
        self.sharers, self.rows, self.widths, self.line_first, self.count = sharers, rows, widths, line_first, count
        self.columns = sharers // (2 * LINE)
        self.chips = sharers // 2
        ends = [sum(widths[: at + 1]) for at in range(len(widths))]
        self.lanes = [slice(end - width, end) for end, width in zip(ends, widths)]
        self.wide = ends[-1]
        self.copies = 1 + self.columns - 1 + LINE - 1 + count - 1

    def scratch(self):
        shapes = []
        for width, line_first in zip(self.widths, self.line_first):
            side = (self.columns - 1, 1 if line_first else LINE, self.rows, width)
            line = (LINE - 1, self.columns if line_first else 1, self.rows, width)
            shapes += [pltpu.VMEM((self.chips, self.rows, width), BF)] * 2
            shapes += [pltpu.VMEM(side, BF)] * 2 + [pltpu.VMEM(line, BF)] * 2
            shapes += [pltpu.VMEM((self.rows, width), BF), pltpu.VMEM((self.count, self.rows, width), BF)]
        sems = len(self.widths) * self.copies
        return shapes + [
            pltpu.VMEM((self.sharers, self.rows, self.wide), F32),
            pltpu.SemaphoreType.DMA((sems,)),
            pltpu.SemaphoreType.DMA((sems,)),
        ]

    def bind(self, refs):
        chains = len(self.widths)
        self.buffers = [refs[8 * chain : 8 * chain + 8] for chain in range(chains)]
        self.total, self.send_sem, self.recv_sem = refs[8 * chains : 8 * chains + 3]
        self.me, self.line, self.column, self.core, unused = my_place(self.sharers)
        self.block = lax.axis_index("blk")
        self.others_line = [lax.rem(self.line + step, LINE) for step in range(1, LINE)]
        self.others_side = [lax.rem(self.column + step, self.columns) for step in range(1, self.columns)]
        self.others_block = [lax.rem(self.block + step, self.count) for step in range(1, self.count)]

    def at(self, line, column, core):
        return (line * self.columns + column) * 2 + core

    def greet(self):
        devices = [{"dp": self.at(self.line, self.column, 1 - self.core)}]
        devices += [{"dp": self.at(self.line, other, self.core)} for other in self.others_side]
        devices += [{"dp": self.at(other, self.column, self.core)} for other in self.others_line]
        devices += [{"blk": other} for other in self.others_block]
        greet(devices)

    def met(self):
        pl.semaphore_wait(pltpu.get_barrier_semaphore(), 1 + self.columns - 1 + LINE - 1 + self.count - 1)

    def copy(self, chain, number, source, target, device):
        sem = chain * self.copies + number
        return remote(source, target, self.send_sem.at[sem], self.recv_sem.at[sem], device)

    def part(self, owner, chain):
        return self.total[owner, :, self.lanes[chain]]

    def add(self, owner, chain, values):
        self.total[owner, :, self.lanes[chain]] += values.astype(F32)

    def mate_copy(self, chain):
        mate = {"dp": self.at(self.line, self.column, 1 - self.core)}
        return self.copy(chain, 0, self.buffers[chain][0], self.buffers[chain][1], mate)

    def mate_start(self, chain):
        for chip in range(self.chips):
            self.buffers[chain][0][chip] = self.part(2 * chip + 1 - self.core, chain).astype(BF)
        self.mate_copy(chain).start()

    def mate_end(self, chain):
        self.mate_copy(chain).wait()
        for chip in range(self.chips):
            self.add(2 * chip + self.core, chain, self.buffers[chain][1][chip])

    def side_copies(self, chain):
        source, target = self.buffers[chain][2:4]
        return [
            self.copy(chain, 1 + step, source.at[step], target.at[step], {"dp": self.at(self.line, other, self.core)})
            for step, other in enumerate(self.others_side)
        ]

    def side_lines(self, chain):
        return [self.line] if self.line_first[chain] else range(LINE)

    def side_start(self, chain):
        for step, other in enumerate(self.others_side):
            for place, line in enumerate(self.side_lines(chain)):
                self.buffers[chain][2][step, place] = self.part(self.at(line, other, self.core), chain).astype(BF)
        for copy in self.side_copies(chain):
            copy.start()

    def side_end(self, chain):
        for step, copy in enumerate(self.side_copies(chain)):
            copy.wait()
            for place, line in enumerate(self.side_lines(chain)):
                self.add(self.at(line, self.column, self.core), chain, self.buffers[chain][3][step, place])

    def line_copies(self, chain):
        source, target = self.buffers[chain][4:6]
        return [
            self.copy(chain, self.columns + step, source.at[step], target.at[step], {"dp": self.at(other, self.column, self.core)})
            for step, other in enumerate(self.others_line)
        ]

    def line_columns(self, chain):
        return range(self.columns) if self.line_first[chain] else [self.column]

    def line_start(self, chain):
        for step, other in enumerate(self.others_line):
            for place, column in enumerate(self.line_columns(chain)):
                self.buffers[chain][4][step, place] = self.part(self.at(other, column, self.core), chain).astype(BF)
        for copy in self.line_copies(chain):
            copy.start()

    def line_end(self, chain):
        for step, copy in enumerate(self.line_copies(chain)):
            copy.wait()
            for place, column in enumerate(self.line_columns(chain)):
                self.add(self.at(self.line, column, self.core), chain, self.buffers[chain][5][step, place])

    def block_copies(self, chain):
        source, target = self.buffers[chain][6:8]
        return [
            self.copy(chain, self.columns + LINE - 1 + step, source, target.at[self.block], {"blk": other})
            for step, other in enumerate(self.others_block)
        ]

    def block_start(self, chain):
        own = self.part(self.me, chain).astype(BF)
        self.buffers[chain][6][...] = own
        self.buffers[chain][7][self.block] = own
        for copy in self.block_copies(chain):
            copy.start()

    def block_end(self, chain):
        for copy in self.block_copies(chain):
            copy.wait()
        parts = [self.buffers[chain][7][at].astype(F32) for at in range(self.count)]
        return functools.reduce(jnp.add, parts)


def finish_kernel(blocks, rows, tiles, shares, *refs):
    dq_refs, refs = refs[:blocks], refs[blocks:]
    dk_refs, refs = refs[:blocks], refs[blocks:]
    dv_refs, refs = refs[:blocks], refs[blocks:]
    (x_ref, gq_ref, gvalues_ref, gdepth_ref, w_ref, mine_ref, wide_ref, sum_ref), refs = refs[:8], refs[8:]
    (gh_ref, flat_out, sums_out), refs = refs[:3], refs[3:]
    held, refs = refs[: 3 * blocks + 5], refs[3 * blocks + 5 :]
    dq, dk, dv = held[:blocks], held[blocks : 2 * blocks], held[2 * blocks : 3 * blocks]
    x, gq, gvalues, gdepth, w = held[3 * blocks :]
    (load_sem, turned, grads, window, bias_sum, rim_in, halo_in, halo, given, edge_send, edge_recv, given_send, given_recv), refs = refs[:13], refs[13:]
    shares.bind(refs)
    step = pl.program_id(0)
    count, sharers, shard = shares.count, shares.sharers, shares.rows
    chains = 4
    tokens, width = x.shape
    block = shares.block
    loads = [
        pltpu.make_async_copy(source, target, load_sem.at[at])
        for at, (source, target) in enumerate(
            zip(
                [x_ref, gq_ref] + list(dq_refs) + list(dk_refs) + list(dv_refs) + [gvalues_ref, gdepth_ref, w_ref.at[:, 0 : chains * ATT]],
                [x, gq] + list(dq) + list(dk) + list(dv) + [gvalues, gdepth, w],
            )
        )
    ]
    by_chain = [loads[: 2 + blocks], loads[2 + blocks : 2 + 2 * blocks], loads[2 + 2 * blocks : 2 + 3 * blocks], loads[2 + 3 * blocks :]]

    def edge_copies():
        if count == 1:
            return []
        after, before = {"blk": lax.rem(block + 1, count)}, {"blk": lax.rem(block + count - 1, count)}
        plan = [
            (gvalues.at[tokens + 16 : tokens + 32], rim_in.at[0], after),
            (gvalues.at[0:16], rim_in.at[1], before),
            (gdepth.at[tokens - 16 : tokens], halo_in.at[0], after),
            (gdepth.at[0:16], halo_in.at[1], before),
        ]
        return [
            remote(source, target, edge_send.at[at], edge_recv.at[at], device)
            for at, (source, target, device) in enumerate(plan)
        ]

    def given_copies():
        return [
            remote(mine_ref, given.at[block], given_send.at[at], given_recv.at[at], {"blk": other})
            for at, other in enumerate(shares.others_block)
        ]

    @pl.when(step == 0)
    def start():
        shares.greet()
        for load in loads:
            load.start()
        bias_sum[...] = jnp.zeros_like(bias_sum)
        given[block] = mine_ref[...]

    def total(some):
        whole = [ref[...].astype(F32) for ref in some if ref.shape[0] == ATT]
        halves = [ref[...].astype(F32) for ref in some if ref.shape[0] < ATT]
        whole += [jnp.concatenate(halves[at : at + 2], axis=0) for at in range(0, len(halves), 2)]
        return functools.reduce(jnp.add, whole)

    def weights(chain):
        for load in by_chain[chain] if chain < 3 else by_chain[3][2:]:
            load.wait()
        if chain == 0:
            turned[...] = x[...].T
            every = (total(dq).T + gq[...].astype(F32)).astype(BF)
        elif chain < 3:
            every = total((dk, dv)[chain - 1]).astype(BF).T
        else:
            for copy in edge_copies():
                copy.wait()
            zero = jnp.zeros((16, ATT), F32)
            before, after = zero, zero
            if count > 1:
                before = jnp.where(block > 0, rim_in[0].astype(F32), zero)
                after = jnp.where(block < count - 1, rim_in[1].astype(F32), zero)
                nothing = jnp.zeros((16, width), BF)
                halo[0:16, :] = jnp.where(block > 0, halo_in[0], nothing)
                halo[16:32, :] = jnp.where(block < count - 1, halo_in[1], nothing)
            else:
                halo[...] = jnp.zeros_like(halo)
            own = gvalues[16 : tokens + 16, :].astype(F32)
            every = jnp.concatenate(
                [own[0:16] + before, own[16 : tokens - 16], own[tokens - 16 :] + after], axis=0
            ).astype(BF)
        lanes = slice(chain * ATT, (chain + 1) * ATT)
        grads[:, lanes] = every
        bias_sum[0:1, lanes] = jnp.sum(every.astype(F32), axis=0, keepdims=True)
        made = mm(turned[...], every)
        for owner in range(sharers):
            shares.total[owner, :, lanes] = made[owner * shard : (owner + 1) * shard]
        if chain == 3:
            shares.total[:, :, chains * ATT :] = jnp.zeros((sharers, shard, LANES), F32)
            for at in range(chains * ATT // LANES):
                values = bias_sum[0:1, at * LANES : (at + 1) * LANES]
                for owner in range(sharers):
                    shares.total[owner, at : at + 1, chains * ATT :] = values

    for chain in range(chains):
        @pl.when(step == chain)
        def one(chain=chain):
            weights(chain)

    @pl.when(step >= chains)
    def by_tile():
        tile = step - chains
        first = pl.multiple_of(tile * rows, rows)
        fill_rows(window, gdepth, halo, tile, tiles, rows)
        back = mm_nt(grads[pl.ds(first, rows), :], w[...])
        for at in range(0, width, 128):
            some = slice(at, at + 128)
            depth = back[:, some] + sum_ref[:, some]
            for tap in range(KSIZE):
                depth = depth + window[20 - tap : 20 - tap + rows, some] * wide_ref[TAPS_AT + tap : TAPS_AT + tap + 1, some]
            gh_ref[:, some] = depth.astype(BF)

    def first_sends(unused):
        shares.met()
        for load in by_chain[3][:2]:
            load.wait()
        for copy in edge_copies() + given_copies():
            copy.start()

    def late(eighths):
        return chains + eighths * tiles // 8

    plan = [
        (0, [(first_sends, 0), (shares.mate_start, 0)]),
        (1, [(shares.mate_end, 0), (shares.side_start, 0), (shares.mate_start, 1)]),
        (2, [(shares.mate_end, 1), (shares.side_start, 1), (shares.mate_start, 2)]),
        (3, [(shares.side_end, 0), (shares.line_start, 0), (shares.mate_end, 2), (shares.side_start, 2), (shares.mate_start, 3)]),
        (late(0), [(shares.mate_end, 3), (shares.line_start, 3), (shares.side_end, 1), (shares.line_start, 1)]),
        (late(2), [(shares.line_end, 0), (shares.block_start, 0), (shares.side_end, 2), (shares.line_start, 2)]),
        (late(4), [(shares.line_end, 1), (shares.block_start, 1)]),
        (late(6), [(shares.line_end, 3), (shares.side_start, 3), (shares.line_end, 2), (shares.block_start, 2)]),
        (late(7), [(shares.side_end, 3), (shares.block_start, 3)]),
    ]
    for when in range(chains + tiles):
        actions = [action for place, some in plan if place == when for action in some]
        if actions:

            @pl.when(step == when)
            def act(actions=actions):
                for action, chain in actions:
                    action(chain)

    @pl.when(step == chains + tiles - 1)
    def end():
        for copy in given_copies():
            copy.wait()
        flat_out[...] = functools.reduce(jnp.add, [given[at].astype(F32) for at in range(count)])
        for chain in range(chains):
            sums_out[:, shares.lanes[chain]] = shares.block_end(chain)


def unpack_kernel(part, gh_ref, flat, sums, gh_out, gq_out, gk_out, gv_out, gc_out, gwd_out, gwu_out, gwn_out, gwp_out, gwk_out, gtaps_out, gkb_out, gbup_out, *refs):
    vector_outs, thin_outs = refs[:6], refs[6:10]
    chains = 4
    shard = sums.shape[0]
    width = flat.shape[1]
    gh_out[...] = gh_ref[...]

    @pl.when(pl.program_id(0) == 0)
    def small():
        gwd_out[...] = flat[0:shard]
        quarter = shard // 2
        for group in range(2):
            for place in range(2):
                first = shard * (1 + group) + quarter * place
                gwu_out[group, :, place * width : (place + 1) * width] = flat[first : first + quarter]
            gwn_out[group] = flat[3 * shard : 5 * shard, group * ATT : (group + 1) * ATT]
        gwp_out[...] = flat[5 * shard : 6 * shard, 0:ATT]
        cells = flat[5 * shard : 6 * shard, ATT : ATT + LANES]
        gtaps_out[...] = cells[:, TAPS_AT : TAPS_AT + KSIZE]
        turned = jnp.concatenate([cells, jnp.zeros((LANES - shard, LANES), F32)], axis=0).T
        for at, ref in enumerate(vector_outs):
            ref[...] = turned[at : at + 1, 0:shard].reshape(shard)
        cells = flat[5 * shard : 6 * shard, ATT + LANES : ATT + 2 * LANES]
        gwk_out[...] = cells[0:part, 0 : HEADS * KSIZE]
        half = gbup_out.shape[0] // 2
        gbup_out[...] = jnp.concatenate(
            [cells[part : part + 1, 0:half], cells[part + 1 : part + 2, 0:half]], axis=1
        ).reshape(2 * half)
        gkb_out[...] = cells[part + 2 : part + 3, 0 : HEADS * KSIZE].reshape(HEADS * KSIZE)
        turned = jnp.concatenate([cells, jnp.zeros((LANES - shard, LANES), F32)], axis=0).T
        thin_outs[2][...] = turned[THIN_AT : THIN_AT + 1, 0:part].reshape(part)
        for chain, ref in enumerate((gq_out, gk_out, gv_out, gc_out)):
            ref[...] = sums[:, chain * ATT : (chain + 1) * ATT]
        totals = jnp.concatenate([sums[at : at + 1, chains * ATT :] for at in range(chains * ATT // LANES)], axis=1)
        lane = lax.broadcasted_iota(jnp.int32, (part, ATT), 1)
        row = lax.broadcasted_iota(jnp.int32, (part, ATT), 0)
        mine = (lane == lax.axis_index("dp") * part + row).astype(F32)
        for chain, ref in ((0, thin_outs[0]), (2, thin_outs[1]), (3, thin_outs[3])):
            picked = jnp.sum(mine * totals[:, chain * ATT : (chain + 1) * ATT], axis=1, keepdims=True)
            picked = jnp.broadcast_to(picked, (part, LANES))
            picked = jnp.concatenate([picked, jnp.zeros((LANES - part, LANES), F32)], axis=0).T
            ref[...] = picked[0:1, 0:part].reshape(part)


def unpack(grad_hidden, flat, sums, part, n_up):
    shard, width = sums.shape[0], flat.shape[1]
    shapes = [shaped((shard, ATT), F32)] * 4 + [
        shaped((shard, width), F32),
        shaped((2, shard // 2, 2 * width), F32),
        shaped((2, 2 * shard, ATT), F32),
        shaped((shard, ATT), F32),
        shaped((part, HEADS * KSIZE), F32),
        shaped((shard, KSIZE), F32),
        shaped((HEADS * KSIZE,), F32),
        shaped((n_up,), F32),
    ]
    shapes += [shaped((shard,), F32)] * 6 + [shaped((part,), F32)] * 4
    tokens = grad_hidden.shape[0]
    rows = math.gcd(tokens, 512)
    return pl.pallas_call(
        functools.partial(unpack_kernel, part),
        grid=(tokens // rows,),
        in_specs=[rows_of(rows, width), all_of(flat.shape), all_of(sums.shape)],
        out_specs=[rows_of(rows, width)] + [all_of(v.shape) for v in shapes],
        out_shape=[shaped(grad_hidden.shape, BF)] + shapes,
        compiler_params=pltpu.CompilerParams(vmem_limit_bytes=60 * MIB),
        name="unpack",
    )(grad_hidden, flat, sums)


def finish(dqs, dks, dvs, x, grad_query, grad_values, grad_depth, weight, mine, wide_vectors, grad_sum, sharers, count):
    tokens, width = x.shape
    rows = math.gcd(tokens, 256)
    tiles = tokens // rows
    blocks = len(dqs)
    chains = 4
    shard = width // sharers
    shares = Shares(sharers, shard, [ATT] * 3 + [ATT + LANES], [False, False, False, True], count)
    late_rows = pl.BlockSpec((rows, width), lambda i: (jnp.maximum(i - chains, 0), 0))
    away = pl.BlockSpec(memory_space=pl.ANY)
    loaded = list(dqs) + list(dks) + list(dvs) + [x, grad_query, grad_values, grad_depth]
    args = loaded + [weight, mine, wide_vectors, grad_sum]
    shapes = [shaped(mine.shape, F32), shaped((shard, chains * ATT + LANES), F32)]
    return pl.pallas_call(
        functools.partial(finish_kernel, blocks, rows, tiles, shares),
        grid=(chains + tiles,),
        in_specs=[away] * (len(loaded) + 1) + [all_of(mine.shape), all_of(wide_vectors.shape), late_rows],
        out_specs=[late_rows] + [all_of(v.shape) for v in shapes],
        out_shape=[shaped((tokens, width), BF)] + shapes,
        scratch_shapes=[pltpu.VMEM(v.shape, v.dtype) for v in loaded]
        + [
            pltpu.VMEM((width, chains * ATT), BF),
            pltpu.SemaphoreType.DMA((len(loaded) + 1,)),
            pltpu.VMEM((width, tokens), BF),
            pltpu.VMEM((tokens, chains * ATT), BF),
            pltpu.VMEM((rows + 32, width), F32),
            pltpu.VMEM((8, chains * ATT), F32),
            pltpu.VMEM((2, 16, ATT), BF),
            pltpu.VMEM((2, 16, width), BF),
            pltpu.VMEM((32, width), BF),
            pltpu.VMEM((count,) + mine.shape, BF),
            pltpu.SemaphoreType.DMA((4,)),
            pltpu.SemaphoreType.DMA((4,)),
            pltpu.SemaphoreType.DMA((max(count - 1, 1),)),
            pltpu.SemaphoreType.DMA((max(count - 1, 1),)),
        ]
        + shares.scratch(),
        compiler_params=pltpu.CompilerParams(
            collective_id=1, has_side_effects=True, vmem_limit_bytes=60 * MIB
        ),
        cost_estimate=pl.CostEstimate(
            flops=4 * tokens * width * chains * ATT, bytes_accessed=30 * tokens * width, transcendentals=0
        ),
        name="finish",
    )(*args)


def shifted_from(value, axis, step):
    count = lax.axis_size(axis)
    return lax.ppermute(value, axis, [((i + step) % count, i) for i in range(count)])


def local(
    hidden,
    separators,
    out_grad,
    w_query,
    b_query,
    w_key,
    w_value,
    b_value,
    depth_kernel,
    w_point,
    b_keyconv,
    w_kernel,
    kernel_bias,
    w_convout,
    b_convout,
    w_dense,
    b_dense,
    gain_attn,
    shift_attn,
    w_up,
    b_up,
    w_down,
    b_down,
    gain_out,
    shift_out,
):
    count = lax.axis_size("blk")
    sharers = lax.axis_size("dp")
    me = lax.axis_index("blk")
    x, cotangent = hidden[0], out_grad[0]
    tokens, width = x.shape
    first = me * tokens
    groups, part = w_up.shape[0], b_query.shape[0]

    others = [shifted_from(x, "blk", step) for step in range(1, count)]
    weight, wide_vectors, thin, thin_columns, bias_up, wt_kernel, bias_kernel, halo = gather_columns(
        [w_query, w_key, w_value, w_convout, w_point],
        [b_dense, gain_attn, shift_attn, b_down, gain_out, shift_out],
        [b_query, b_value, b_keyconv, b_convout],
        depth_kernel,
        b_up,
        w_kernel,
        kernel_bias,
        x,
        sharers,
        count,
    )
    late = [
        w_dense.astype(BF),
        jnp.concatenate([w_up[g] for g in range(groups)], axis=1).astype(BF),
        jnp.concatenate([w_down[g] for g in range(groups)], axis=1).astype(BF),
    ]
    weight, late[1:] = lax.optimization_barrier((weight, late[1:]))
    wt_dense, wt_up, wt_down = [lax.all_gather(v, "dp", axis=0, tiled=True) for v in late]

    def places(step):
        return jnp.stack(
            [separators[0], first, lax.rem(me + step, count) * tokens, count * tokens]
        ).astype(jnp.int32)

    query, query_t, *own = project(x, weight, thin, thin_columns, 3)
    keys = [own]
    outs, probs = [], []
    for step in range(count):
        if step > 0:
            keys.append(project(others[step - 1], weight, thin, thin_columns, 2))
        key, key_t, value, value_t, norms = keys[step]
        out, prob = attend(places(step), query_t, key, value_t, norms)
        outs.append(out)
        probs.append(prob)
        if step == 0:
            depth, keyconv, attn_key, kernt, kern, conv, values, rim = mix(
                places(0), x, halo, query, weight, wide_vectors, thin, wt_kernel, bias_kernel
            )
            others, depth = lax.optimization_barrier((others, depth))
    output, grad_sum, grad_conv, grads_t, sides, (packed, g_vectors, gb_up) = middle(
        outs, conv, x, cotangent, wt_dense, wt_up, wt_down, wide_vectors, bias_up, sharers
    )
    grad_query_conv, grad_depth, grad_values, packed = mix_back(
        x, halo, values, rim, grad_conv, kernt, kern, query, keyconv, attn_key, depth, weight, wt_kernel, g_vectors, gb_up, packed
    )
    packed, sides = lax.optimization_barrier((packed, sides))
    mine = lax.psum_scatter(packed, "dp", scatter_dimension=0, tiled=False)

    dqs, dks, dvs = [], [], []
    for step in list(range(1, count)) + [0]:
        key, key_t, value, value_t, norms = keys[step]
        some = HEADS // 2 if step else HEADS
        pieces = []
        for at in range(0, HEADS, some):
            dq, dk, dv = attend_back(probs[step], value, key_t, grads_t[step], sides[step], query_t, at, some)
            if step:
                dk, dv = shifted_from(dk, "blk", count - step), shifted_from(dv, "blk", count - step)
            pieces.append((dq, dk, dv))
        for whole, parts in zip((dqs, dks, dvs), zip(*pieces)):
            whole += parts
    grad_hidden, flat, sums = finish(
        dqs, dks, dvs, x, grad_query_conv, grad_values, grad_depth, weight, mine, wide_vectors, grad_sum, sharers, count
    )
    results = unpack(grad_hidden, flat, sums, part, b_up.shape[0])
    grad_hidden, gw_query, gw_key, gw_value, gw_convout, gw_dense, gw_up, gw_down, gw_point, gw_kernel, g_taps, g_bias, gb_up = results[:13]
    g_vectors, thin = results[13:19], results[19:]
    return (
        output[None],
        grad_hidden[None],
        gw_query,
        thin[0],
        gw_key,
        gw_value,
        thin[1],
        g_taps,
        gw_point,
        thin[2],
        gw_kernel,
        g_bias,
        gw_convout,
        thin[3],
        gw_dense,
        g_vectors[0],
        g_vectors[1],
        g_vectors[2],
        gw_up,
        gb_up,
        gw_down,
        g_vectors[3],
        g_vectors[4],
        g_vectors[5],
    )


def solution(mesh):
    placed = (
        P("dp", "blk", None),
        P("dp"),
        P("dp", "blk", None),
        P("dp", None),
        P("dp"),
        P("dp", None),
        P("dp", None),
        P("dp"),
        P("dp", None),
        P("dp", None),
        P("dp"),
        P("dp", None),
        P(),
        P("dp", None),
        P("dp"),
        P("dp", None),
        P("dp"),
        P("dp"),
        P("dp"),
        P(None, "dp", None),
        P("dp"),
        P(None, "dp", None),
        P("dp"),
        P("dp"),
        P("dp"),
    )
    return jax.shard_map(
        local,
        mesh=mesh,
        in_specs=placed,
        out_specs=(
            P("dp", "blk", None),
            P("dp", "blk", None),
            P("dp", None),
            P("dp"),
            P("dp", None),
            P("dp", None),
            P("dp"),
            P("dp", None),
            P("dp", None),
            P("dp"),
            P("dp", None),
            P(),
            P("dp", None),
            P("dp"),
            P("dp", None),
            P("dp"),
            P("dp"),
            P("dp"),
            P(None, "dp", None),
            P("dp"),
            P(None, "dp", None),
            P("dp"),
            P("dp"),
            P("dp"),
        ),
        check_vma=False,
    )
```

```python
import functools, math
import jax, jax.numpy as jnp
from jax import lax
from jax.experimental import pallas as pl
from jax.experimental.pallas import tpu as pltpu
from jax.sharding import PartitionSpec as P

HEADS = 6
HD = 64
KSIZE = 9
REACH = 4
ATT = 384
EPS = 1e-12
BF = jnp.bfloat16
F32 = jnp.float32
MIB = 2**20
EXCLUDED = 2.0**100
SAFE_SCORE = 50.0


def mm(left, right):
    return jnp.dot(left, right, preferred_element_type=F32)


def mm_nt(left, right):
    return lax.dot_general(left, right, (((1,), (1,)), ((), ())), preferred_element_type=F32)


def mm_tn(left, right):
    return lax.dot_general(left, right, (((0,), (0,)), ((), ())), preferred_element_type=F32)


def in_lanes(rows, columns):
    lane = lax.broadcasted_iota(jnp.int32, (rows, 128), 1)
    out = jnp.zeros((rows, 128), F32)
    for at, column in enumerate(columns):
        out = jnp.where(lane == at, column, out)
    return out.astype(BF)


def in_rows(columns, rows):
    row = lax.broadcasted_iota(jnp.int32, (16, columns), 0)
    out = jnp.zeros((16, columns), F32)
    for at, values in enumerate(rows):
        out = jnp.where(row == at, values, out)
    return out.astype(BF)


def three_parts(values):
    high = values.astype(BF).astype(F32)
    rest = values - high
    middle = rest.astype(BF).astype(F32)
    return high, middle, (rest - middle).astype(BF).astype(F32)


def put_head(ref, head, values):
    odd = lax.rem(head, 2) == 1
    none = jnp.zeros_like(values)
    ref[0:HD, :] = jnp.where(odd, none, values)
    ref[HD : 2 * HD, :] = jnp.where(odd, values, none)


def attend_kernel(keys, queries, chunk, count, step, at_ref, q_ref, k_ref, v_ref, norm_ref, o_ref, p_ref, key_side, query_side):
    head, tile = pl.program_id(0), pl.program_id(1)
    separator, block = at_ref[0], lax.axis_index("blk")
    first_query = block * keys
    first_key = lax.rem(block + step, count) * keys

    @pl.when((head == 0) & (tile == 0))
    def start():
        position = first_key + lax.broadcasted_iota(jnp.int32, (keys, 128), 0)
        late = (position >= separator).astype(F32)
        key_side[...] = in_lanes(keys, [1.0 - late, late, 1.0, 1.0, 1.0])
        query_side[2 * HD + 16 :, :] = jnp.zeros((2 * HD - 16, queries), BF)

    put_head(query_side, head, q_ref[...])
    position = first_query + tile * queries + lax.broadcasted_iota(jnp.int32, (16, queries), 1)
    late = (position >= separator).astype(F32)
    excluded = [-EXCLUDED * late, -EXCLUDED * (1.0 - late)]
    query_side[2 * HD : 2 * HD + 16, :] = in_rows(queries, excluded)
    o_ref[0, HD + 8 : HD + 16, :] = jnp.zeros((8, queries), F32)
    wide = q_ref[...].astype(F32)
    largest = jnp.max(jnp.sum(wide * wide, axis=0, keepdims=True)) * jnp.max(norm_ref[...])

    def scores(at):
        part = slice(at * chunk, (at + 1) * chunk)
        return mm(
            jnp.concatenate([k_ref[part, :], key_side[part, :]], axis=1), query_side[...]
        )

    @pl.when(jnp.logical_not(largest <= SAFE_SCORE * SAFE_SCORE))
    def shifted():
        best = jnp.full((1, queries), -4.0 * EXCLUDED, F32)
        for at in range(keys // chunk):
            best = jnp.maximum(best, jnp.max(scores(at), axis=0, keepdims=True))
        parts = three_parts(jnp.where(best < -0.5 * EXCLUDED, 0.0, best))
        query_side[2 * HD : 2 * HD + 16, :] = in_rows(queries, excluded + [-part for part in parts])
        o_ref[0, HD + 8 : HD + 16, :] = jnp.broadcast_to(
            jnp.where(best < -0.5 * EXCLUDED, best, parts[0] + parts[1] + parts[2]), (8, queries)
        )

    ones = in_rows(chunk, [1.0])
    total = jnp.zeros((HD + 16, queries), F32)
    for at in range(keys // chunk):
        part = slice(at * chunk, (at + 1) * chunk)
        probs = jnp.exp(scores(at)).astype(BF)
        p_ref[0, part, :] = probs
        total = total + mm(jnp.concatenate([v_ref[:, part], ones], axis=0), probs)
    o_ref[0, 0 : HD + 8, :] = total[0 : HD + 8, :]


def attend(at, query_t, key, value_t, norms, count, step):
    tokens, keys = query_t.shape[1], key.shape[0]
    queries, chunk = math.gcd(tokens, 2048), math.gcd(keys, 1024)
    return pl.pallas_call(
        functools.partial(attend_kernel, keys, queries, chunk, count, step),
        grid=(HEADS, tokens // queries),
        in_specs=[
            pl.BlockSpec(memory_space=pltpu.SMEM),
            pl.BlockSpec((HD, queries), lambda h, i: (h, i)),
            pl.BlockSpec((keys, 2 * HD), lambda h, i: (0, h // 2)),
            pl.BlockSpec((HD, keys), lambda h, i: (h, 0)),
            pl.BlockSpec(norms.shape, lambda h, i: (0, 0)),
        ],
        out_specs=[
            pl.BlockSpec((1, HD + 16, queries), lambda h, i: (h, 0, i)),
            pl.BlockSpec((1, keys, queries), lambda h, i: (h, 0, i)),
        ],
        out_shape=[
            jax.ShapeDtypeStruct((HEADS, HD + 16, tokens), F32),
            jax.ShapeDtypeStruct((HEADS, keys, tokens), BF),
        ],
        scratch_shapes=[pltpu.VMEM((keys, 128), BF), pltpu.VMEM((4 * HD, queries), BF)],
        compiler_params=pltpu.CompilerParams(vmem_limit_bytes=56 * MIB),
        cost_estimate=pl.CostEstimate(
            flops=ATT * keys,
            bytes_accessed=2 * HEADS * keys,
            transcendentals=0,
        ),
        name="attend",
    )(at, query_t, key, value_t, norms)


def attend_back_kernel(first, keys, queries, chunk, p_ref, v_ref, kt_ref, g_ref, side_ref, q_ref, dq_ref, dk_ref, dv_ref, value_side, grad_side, dk_sum, dv_sum):
    head, tile = pl.program_id(0), pl.program_id(1)

    @pl.when((head == 0) & (tile == 0))
    def start():
        value_side[...] = in_lanes(chunk, [1.0, 1.0, 1.0])
        grad_side[2 * HD + 16 :, :] = jnp.zeros((2 * HD - 16, queries), BF)

    @pl.when(tile == 0)
    def fresh():
        dk_sum[...] = jnp.zeros_like(dk_sum)
        dv_sum[...] = jnp.zeros_like(dv_sum)

    put_head(grad_side, first + head, g_ref[...])
    grad_side[2 * HD : 2 * HD + 16, :] = side_ref[0]
    total = jnp.zeros((HD, queries), F32)
    for at in range(keys // chunk):
        part = slice(at * chunk, (at + 1) * chunk)
        probs = p_ref[0, part, :]
        spread = mm(jnp.concatenate([v_ref[part, :], value_side[...]], axis=1), grad_side[...])
        grad_scores = (probs.astype(F32) * spread).astype(BF)
        dv_sum[:, part] += mm_nt(g_ref[...], probs)
        dk_sum[:, part] += mm_nt(q_ref[...], grad_scores)
        total = total + mm(kt_ref[:, part], grad_scores)
    dq_ref[...] = (total * (HD**-0.5)).astype(BF)

    @pl.when(tile == pl.num_programs(1) - 1)
    def finish():
        dk_ref[...] = dk_sum[...].astype(BF)
        dv_ref[...] = dv_sum[...].astype(BF)


def attend_back(probs, value, key_t, grad_t, side, query_t, first, heads):
    tokens, keys = query_t.shape[1], value.shape[0]
    queries, chunk = math.gcd(tokens, 1024), math.gcd(keys, 256)
    by_token = pl.BlockSpec((HD, queries), lambda h, i: (first + h, i))
    by_key = pl.BlockSpec((HD, keys), lambda h, i: (first + h, 0))
    return pl.pallas_call(
        functools.partial(attend_back_kernel, first, keys, queries, chunk),
        grid=(heads, tokens // queries),
        in_specs=[
            pl.BlockSpec((1, keys, queries), lambda h, i: (first + h, 0, i)),
            pl.BlockSpec((keys, 2 * HD), lambda h, i: (0, (first + h) // 2)),
            by_key,
            by_token,
            pl.BlockSpec((1, 16, queries), lambda h, i: (first + h, 0, i)),
            by_token,
        ],
        out_specs=[
            pl.BlockSpec((HD, queries), lambda h, i: (h, i)),
            pl.BlockSpec((HD, keys), lambda h, i: (h, 0)),
            pl.BlockSpec((HD, keys), lambda h, i: (h, 0)),
        ],
        out_shape=[
            jax.ShapeDtypeStruct((heads * HD, tokens), BF),
            jax.ShapeDtypeStruct((heads * HD, keys), BF),
            jax.ShapeDtypeStruct((heads * HD, keys), BF),
        ],
        scratch_shapes=[
            pltpu.VMEM((chunk, 128), BF),
            pltpu.VMEM((4 * HD, queries), BF),
            pltpu.VMEM((HD, keys), F32),
            pltpu.VMEM((HD, keys), F32),
        ],
        compiler_params=pltpu.CompilerParams(vmem_limit_bytes=56 * MIB),
        cost_estimate=pl.CostEstimate(
            flops=32 * heads * HD * tokens * keys,
            bytes_accessed=2 * heads * tokens * keys,
            transcendentals=0,
        ),
        name="attend_back",
    )(probs, value, key_t, grad_t, side, query_t)


def all_of(shape):
    return pl.BlockSpec(shape, lambda *at: (0,) * len(shape))


def rows_of(rows, width):
    return pl.BlockSpec((rows, width), lambda i: (i, 0))


def columns_of(height, columns):
    return pl.BlockSpec((height, columns), lambda i: (0, i))


def run_tiles(kernel, name, steps, inputs, outputs, scratch, flops, aliases=None):
    args, in_specs = zip(*inputs)
    shapes, out_specs = zip(*outputs)
    size = sum(math.prod(v.shape) * v.dtype.itemsize for v in args + shapes)
    return pl.pallas_call(
        kernel,
        grid=(steps,),
        in_specs=list(in_specs),
        out_specs=list(out_specs),
        out_shape=list(shapes),
        scratch_shapes=scratch,
        input_output_aliases=aliases or {},
        compiler_params=pltpu.CompilerParams(vmem_limit_bytes=60 * MIB),
        cost_estimate=pl.CostEstimate(flops=flops, bytes_accessed=size, transcendentals=0),
        name=name,
    )(*args)


def shaped(shape, dtype):
    return jax.ShapeDtypeStruct(shape, dtype)


def project_kernel(parts, x_ref, w_ref, thin_ref, thin_columns_ref, *refs):
    norm_ref, flipped = refs[2 * parts], refs[2 * parts + 1]
    skip = (3 - parts) * ATT

    @pl.when(pl.program_id(0) == 0)
    def start():
        norm_ref[...] = jnp.zeros_like(norm_ref)
        flipped[...] = w_ref[:, skip:].T

    x = x_ref[...]
    plain = mm(x, w_ref[:, skip:])
    turned = mm_nt(flipped[...], x)
    for part in range(parts):
        own = slice(part * ATT, (part + 1) * ATT)
        bias, bias_t = 0.0, 0.0
        if part != parts - 2:
            at = 1 if part == parts - 1 else 0
            bias, bias_t = thin_ref[at : at + 1, :], thin_columns_ref[:, THIN_AT + at : THIN_AT + at + 1]
        refs[2 * part][...] = (plain[:, own] + bias).astype(BF)
        across = (turned[own] + bias_t).astype(BF)
        if part == parts - 2:
            wide = across.astype(F32)
            for head in range(HEADS):
                cells = wide[head * HD : (head + 1) * HD]
                size = jnp.sum(cells * cells, axis=0, keepdims=True)
                norm_ref[...] = jnp.maximum(norm_ref[...], size)
        if part < parts - 2:
            across = (across.astype(F32) * (HD**-0.5)).astype(BF)
        refs[2 * part + 1][...] = across


def project(x, weight, thin, thin_columns, parts):
    tokens, width = x.shape
    wide = 3 * ATT
    tile = math.gcd(tokens, 512)
    outputs = []
    for part in range(parts):
        outputs.append((shaped((tokens, ATT), BF), rows_of(tile, ATT)))
        outputs.append((shaped((ATT, tokens), BF), columns_of(ATT, tile)))
    outputs.append((shaped((8, tile), F32), all_of((8, tile))))
    return run_tiles(
        functools.partial(project_kernel, parts),
        "project",
        tokens // tile,
        [
            (x, rows_of(tile, width)),
            (weight, all_of((width, wide))),
            (thin, all_of(thin.shape)),
            (thin_columns, all_of(thin_columns.shape)),
        ],
        outputs,
        [pltpu.VMEM((parts * ATT, width), BF)],
        4 * tokens * width * parts * ATT,
    )


def fill_rows(window, x_ref, halo_ref, tile, tiles, rows):
    first = tile * rows
    tokens = x_ref.shape[0]
    before = x_ref[pl.ds(pl.multiple_of(jnp.maximum(first - 16, 0), 16), 16), :]
    after = x_ref[pl.ds(pl.multiple_of(jnp.minimum(first + rows, tokens - 16), 16), 16), :]
    window[0:16, :] = jnp.where(tile == 0, halo_ref[0:16, :], before).astype(window.dtype)
    window[16 : 16 + rows, :] = x_ref[pl.ds(pl.multiple_of(first, rows), rows), :].astype(window.dtype)
    window[16 + rows :, :] = jnp.where(
        tile == tiles - 1, halo_ref[16:32, :], after
    ).astype(window.dtype)


def fill_window(window, x_ref, halo_ref, tile, rows):
    fill_rows(window, x_ref, halo_ref, tile, pl.num_programs(0), rows)


def fill_spread(spread):
    row = lax.broadcasted_iota(jnp.int32, (128, ATT), 0)
    head = lax.broadcasted_iota(jnp.int32, (128, ATT), 1) // HD
    for tap in range(KSIZE):
        spread[:, tap * ATT : (tap + 1) * ATT] = (row == tap * 8 + head).astype(F32).astype(BF)


def mix_kernel(rows, count, x_ref, halo_ref, q_ref, wc_ref, wp_ref, wide_ref, thin_ref, wk_ref, bk_ref, depth_ref, keyconv_ref, attn_ref, kernt_ref, kern_ref, conv_ref, out_ref, rim_ref, window, conv_window, spread):
    tile = pl.program_id(0)
    last = pl.num_programs(0) - 1

    @pl.when(tile == 0)
    def start():
        fill_spread(spread)

    fill_window(window, x_ref, halo_ref, tile, rows)
    width = window.shape[1]
    for at in range(0, width, 128):
        some = slice(at, at + 128)
        total = jnp.zeros((rows, 128), F32)
        for tap in range(KSIZE):
            total = total + window[12 + tap : 12 + tap + rows, some] * wide_ref[TAPS_AT + tap : TAPS_AT + tap + 1, some]
        depth_ref[:, some] = total.astype(BF)
    position = (
        lax.axis_index("blk") * x_ref.shape[0] + tile * rows - 16 + lax.broadcasted_iota(jnp.int32, (rows + 32, ATT), 0)
    )
    inside = (position >= 0) & (position < count * x_ref.shape[0])
    values = mm(window[...].astype(BF), wc_ref[...]) + thin_ref[3:4, :]
    values = jnp.where(inside, values, 0.0).astype(BF)
    out_ref[...] = values[16 : 16 + rows]

    @pl.when(tile == 0)
    def first_rim():
        rim_ref[0:16, :] = values[0:16]

    @pl.when(tile == last)
    def last_rim():
        rim_ref[16:32, :] = values[16 + rows :]

    conv_window[...] = values.astype(F32)
    keyconv = mm(depth_ref[...], wp_ref[...]) + thin_ref[2:3, :]
    keyconv_ref[...] = keyconv
    attn_key = (keyconv * q_ref[...].astype(F32)).astype(BF)
    attn_ref[...] = attn_key
    logits = mm_nt(wk_ref[...], attn_key) + bk_ref[:, BIAS_AT : BIAS_AT + 1]
    slabs = [logits[8 * tap : 8 * tap + 8] for tap in range(KSIZE)]
    best = functools.reduce(jnp.maximum, slabs)
    slabs = [jnp.exp(slab - best) for slab in slabs]
    share = 1.0 / functools.reduce(jnp.add, slabs)
    slabs = [slab * share for slab in slabs]
    kernt = jnp.concatenate(slabs + [jnp.zeros((128 - 8 * KSIZE, rows), F32)], axis=0)
    kernt_ref[...] = kernt[0 : 8 * KSIZE]
    kern = kernt.astype(BF).T
    kern_ref[...] = kern
    total = jnp.zeros((rows, ATT), F32)
    for tap in range(KSIZE):
        total = total + mm(kern, spread[:, tap * ATT : (tap + 1) * ATT]) * conv_window[12 + tap : 12 + tap + rows, :]
    conv_ref[...] = total.astype(BF)


def column_block(weight, place):
    return pl.BlockSpec((weight.shape[0], ATT), lambda i: (0, place))


def mix(count, x, halo, query, weight, wide_vectors, thin, w_kernel, kernel_bias):
    tokens, width = x.shape
    rows = math.gcd(tokens, 512)
    whole = [(weight, column_block(weight, 2)), (weight, column_block(weight, 3))]
    whole += [(v, all_of(v.shape)) for v in (wide_vectors, thin, w_kernel, kernel_bias)]
    return run_tiles(
        functools.partial(mix_kernel, rows, count),
        "mix",
        tokens // rows,
        [
            (x, all_of(x.shape)),
            (halo, all_of(halo.shape)),
            (query, rows_of(rows, ATT)),
        ]
        + whole,
        [
            (shaped((tokens, width), BF), rows_of(rows, width)),
            (shaped((tokens, ATT), F32), rows_of(rows, ATT)),
            (shaped((tokens, ATT), BF), rows_of(rows, ATT)),
            (shaped((8 * KSIZE, tokens), F32), columns_of(8 * KSIZE, rows)),
            (shaped((tokens, 128), BF), rows_of(rows, 128)),
            (shaped((tokens, ATT), BF), rows_of(rows, ATT)),
            (shaped((tokens, ATT), BF), rows_of(rows, ATT)),
            (shaped((32, ATT), BF), all_of((32, ATT))),
        ],
        [
            pltpu.VMEM((rows + 32, width), F32),
            pltpu.VMEM((rows + 32, ATT), F32),
            pltpu.VMEM((128, KSIZE * ATT), BF),
        ],
        4 * tokens * width * ATT * 4,
    )


def normal(values):
    centre = values - jnp.mean(values, axis=-1, keepdims=True)
    scale = lax.rsqrt(jnp.mean(centre * centre, axis=-1, keepdims=True) + EPS)
    return centre * scale, scale


def normal_back(grad, unit, scale):
    return scale * (
        grad
        - jnp.mean(grad, axis=-1, keepdims=True)
        - unit * jnp.mean(grad * unit, axis=-1, keepdims=True)
    )


def gelu_parts(values):
    size = jnp.abs(values)
    t = 1.0 / (1.0 + (0.3275911 * math.sqrt(0.5)) * size)
    tail = t * (
        0.5 * 0.254829592
        + t * (0.5 * -0.284496736 + t * (0.5 * 1.421413741 + t * (0.5 * -1.453152027 + t * (0.5 * 1.061405429))))
    )
    bell = jnp.exp(-0.5 * values * values)
    tail = tail * bell
    share = jnp.where(values < 0.0, tail, 1.0 - tail)
    return values * share, share + values * (bell * (1.0 / math.sqrt(2.0 * math.pi)))


def middle_kernel(blocks, rows, units, *refs):
    o_refs, refs = refs[:blocks], refs[blocks:]
    (conv_ref, x_ref, og_ref, wd_ref, wu_ref, wn_ref, vec_ref, bu_ref), refs = refs[:8], refs[8:]
    (out_ref, sum_ref, gconv_ref), refs = refs[:3], refs[3:]
    g_refs, refs = refs[:blocks], refs[blocks:]
    side_refs, refs = refs[:blocks], refs[blocks:]
    (packed_ref, gvec_ref, gbu_ref, wd_sum, wu_sum, wn_sum, acts, slopes, staged, sems) = refs
    tile = pl.program_id(0)
    hidden_units = wu_ref.shape[1]
    groups = 2
    inner = ATT
    outer = hidden_units // groups

    @pl.when(tile == 0)
    def start():
        for ref in (wd_sum, wu_sum, wn_sum, gvec_ref, gbu_ref):
            ref[...] = jnp.zeros_like(ref)

    shifts = [ref[:, HD + 8 : HD + 9, :] for ref in o_refs]
    top = functools.reduce(jnp.maximum, shifts)
    weights = [jnp.exp(shift - top) for shift in shifts]
    mass = functools.reduce(jnp.add, [w * ref[:, HD : HD + 1, :] for w, ref in zip(weights, o_refs)])
    weights = [w / mass for w in weights]
    heads = functools.reduce(jnp.add, [w * ref[:, 0:HD, :] for w, ref in zip(weights, o_refs)])
    att_t = heads.reshape(ATT, rows).astype(BF)
    conv = conv_ref[...]
    vec = [vec_ref[at : at + 1, :] for at in range(6)]
    dense = mm(att_t.T, wd_ref[0:ATT, :]) + mm(conv, wd_ref[ATT:, :]) + vec[0]
    unit_one, scale_one = normal(dense + x_ref[...].astype(F32))
    normed = unit_one * vec[1] + vec[2]
    low = normed.astype(BF)
    downs = []
    for group in range(groups):
        mine = low[:, group * inner : (group + 1) * inner]
        down = jnp.zeros((rows, inner), F32)
        for at in range(0, outer, units):
            here = slice(group * outer + at, group * outer + at + units)
            upward = mm(mine, wu_ref[:, here]) + bu_ref[:, here]
            act, slope = gelu_parts(upward)
            act = act.astype(BF)
            acts[:, here] = act
            slopes[:, here] = slope.astype(BF)
            down = down + mm(act, wn_ref[at : at + units, group * inner : (group + 1) * inner])
        downs.append(down)
    unit_two, scale_two = normal(jnp.concatenate(downs, axis=1) + vec[3] + normed)
    out_ref[...] = (unit_two * vec[4] + vec[5]).astype(BF)
    og = og_ref[...].astype(F32)
    gvec_ref[4:5, :] += jnp.sum(og * unit_two, axis=0, keepdims=True)
    gvec_ref[5:6, :] += jnp.sum(og, axis=0, keepdims=True)
    grad_two = normal_back(og * vec[4], unit_two, scale_two)
    grad_down = grad_two.astype(BF)
    gvec_ref[3:4, :] += jnp.sum(grad_down.astype(F32), axis=0, keepdims=True)
    backs = []
    for group in range(groups):
        lanes = slice(group * inner, (group + 1) * inner)
        mine, grads = low[:, lanes], grad_down[:, lanes]
        mine_t = mine.T
        back = jnp.zeros((rows, inner), F32)
        for at in range(0, outer, units):
            here = slice(group * outer + at, group * outer + at + units)
            grad_act = mm_nt(grads, wn_ref[at : at + units, lanes])
            grad_up = (grad_act * slopes[:, here].astype(F32)).astype(BF)
            gbu_ref[0:1, here] += jnp.sum(grad_up.astype(F32), axis=0, keepdims=True)
            wn_sum[at : at + units, lanes] += mm_tn(acts[:, here], grads)
            wu_sum[:, here] += mm(mine_t, grad_up)
            back = back + mm_nt(grad_up, wu_ref[:, here])
        backs.append(back)
    grad_normed = grad_two + jnp.concatenate(backs, axis=1)
    gvec_ref[1:2, :] += jnp.sum(grad_normed * unit_one, axis=0, keepdims=True)
    gvec_ref[2:3, :] += jnp.sum(grad_normed, axis=0, keepdims=True)
    grad_one = normal_back(grad_normed * vec[1], unit_one, scale_one)
    sum_ref[...] = grad_one
    grad_dense = grad_one.astype(BF)
    gvec_ref[0:1, :] += jnp.sum(grad_dense.astype(F32), axis=0, keepdims=True)
    wd_sum[0:ATT, :] += mm(att_t, grad_dense)
    wd_sum[ATT:, :] += mm_tn(conv, grad_dense)
    gconv_ref[...] = mm_nt(grad_dense, wd_ref[ATT:, :]).astype(BF)
    grad_att = mm_nt(wd_ref[0:ATT, :], grad_dense).astype(BF).astype(F32).reshape(HEADS, HD, rows)
    for weight, g_ref, side_ref in zip(weights, g_refs, side_refs):
        share = (grad_att * weight).astype(BF)
        g_ref[...] = share.reshape(ATT, rows)
        delta = -jnp.sum(share.astype(F32) * heads, axis=1, keepdims=True)
        row = lax.broadcasted_iota(jnp.int32, (HEADS, 16, rows), 1)
        side = jnp.zeros((HEADS, 16, rows), F32)
        for at, part in enumerate(three_parts(delta)):
            side = jnp.where(row == at, part, side)
        side_ref[...] = side.astype(BF)

    @pl.when(tile == pl.num_programs(0) - 1)
    def finish():
        sharers = staged.shape[0]
        shard = wd_sum.shape[0] // sharers
        quarter = shard // 2
        width = wd_sum.shape[1]
        copies = []
        for owner in range(sharers):
            staged[owner, 0:shard] = wd_sum[owner * shard : (owner + 1) * shard].astype(BF)
            some = wu_sum[owner * quarter : (owner + 1) * quarter]
            for group in range(groups):
                pair = [some[:, at : at + width] for at in (2 * group * width, (2 * group + 1) * width)]
                staged[owner, (1 + group) * shard : (2 + group) * shard] = jnp.concatenate(pair, axis=0).astype(BF)
            some = wn_sum[owner * 2 * shard : (owner + 1) * 2 * shard]
            staged[owner, 3 * shard : 5 * shard] = some.astype(BF)
            copy = pltpu.make_async_copy(
                staged.at[owner], packed_ref.at[owner, 0 : 5 * shard], sems.at[owner]
            )
            copy.start()
            copies.append(copy)
        for copy in copies:
            copy.wait()


def middle(outs, conv, x, out_grad, w_dense, w_up, w_down, vectors, b_up, sharers):
    tokens, width = x.shape
    shard = width // sharers
    rows = math.gcd(tokens, 512)
    blocks = len(outs)
    heads = pl.BlockSpec((HEADS, HD + 16, rows), lambda i: (0, 0, i))
    side = pl.BlockSpec((HEADS, 16, rows), lambda i: (0, 0, i))
    once = [(w_dense, all_of((width, width)))]
    once += [(v, all_of(v.shape)) for v in (w_up, w_down, vectors, b_up)]
    results = run_tiles(
        functools.partial(middle_kernel, blocks, rows, 768),
        "middle",
        tokens // rows,
        [(o, heads) for o in outs]
        + [
            (conv, rows_of(rows, ATT)),
            (x, rows_of(rows, width)),
            (out_grad, rows_of(rows, width)),
        ]
        + once,
        [
            (shaped((tokens, width), BF), rows_of(rows, width)),
            (shaped((tokens, width), F32), rows_of(rows, width)),
            (shaped((tokens, ATT), BF), rows_of(rows, ATT)),
        ]
        + [(shaped((ATT, tokens), BF), columns_of(ATT, rows))] * blocks
        + [(shaped((HEADS, 16, tokens), BF), side)] * blocks
        + [
            (shaped((sharers, 7 * shard, width), BF), pl.BlockSpec(memory_space=pl.ANY)),
            (shaped((8, width), F32), all_of((8, width))),
            (shaped((8, w_up.shape[1]), F32), all_of((8, w_up.shape[1]))),
        ],
        [
            pltpu.VMEM((width, width), F32),
            pltpu.VMEM(w_up.shape, F32),
            pltpu.VMEM(w_down.shape, F32),
            pltpu.VMEM((rows, w_up.shape[1]), BF),
            pltpu.VMEM((rows, w_up.shape[1]), BF),
            pltpu.VMEM((sharers, 5 * shard, width), BF),
            pltpu.SemaphoreType.DMA((sharers,)),
        ],
        6 * tokens * (width * width + w_up.size + w_down.size),
    )
    output, grad_sum, grad_conv = results[:3]
    return output, grad_sum, grad_conv, results[3 : 3 + blocks], results[3 + blocks : 3 + 2 * blocks], results[3 + 2 * blocks :]


def mix_back_kernel(rows, count, x_ref, halo_ref, values_ref, rim_ref, gconv_ref, kernt_ref, kern_ref, q_ref, keyconv_ref, attn_ref, depth_ref, wp_ref, wk_ref, gvec_ref, gbu_ref, unused, gq_ref, gdepth_ref, gvalues_ref, packed_ref, turned_ref, window, conv_window, summed, products, spread, wp_sum, wc_sum, values_sum, gwk_ref, gbias_ref, gtaps_ref, turn_wide, turn_thin, side, staged, sem):
    tile = pl.program_id(0)

    @pl.when(tile == 0)
    def start():
        fill_spread(spread)
        for ref in (values_sum, wp_sum, wc_sum, gwk_ref, gbias_ref, gtaps_ref, turn_wide, turn_thin):
            ref[...] = jnp.zeros_like(ref)

    fill_window(window, x_ref, halo_ref, tile, rows)
    fill_window(conv_window, values_ref, rim_ref, tile, rows)
    summed[...] = jnp.zeros_like(summed)
    grad_conv = gconv_ref[...].astype(F32)
    for tap in range(KSIZE):
        here = slice(tap * ATT, (tap + 1) * ATT)
        there = slice(12 + tap, 12 + tap + rows)
        products[:, here] = (grad_conv * conv_window[there, :]).astype(BF)
        summed[there, :] += mm(kern_ref[...], spread[:, here]) * grad_conv
    first = pl.multiple_of(tile * rows, rows)
    values_sum[pl.ds(first, rows + 32), :] += summed[...]
    turned = x_ref[pl.ds(first, rows), :].T
    turned_ref[...] = turned
    edges = [slice(0, 16), slice(rows + 16, rows + 32)]
    edge_x = jnp.concatenate([window[edge, :] for edge in edges], axis=0).astype(BF)
    edge_grads = jnp.concatenate([summed[edge, :] for edge in edges], axis=0).astype(BF)
    wc_sum[...] += mm(turned, summed[16 : 16 + rows, :].astype(BF)) + mm_tn(edge_x, edge_grads)
    grad_kernel = mm_nt(spread[...], products[...])
    slabs = [slice(8 * tap, 8 * tap + 8) for tap in range(KSIZE)]
    kernels = [kernt_ref[slab, :] for slab in slabs]
    mean = functools.reduce(jnp.add, [k * grad_kernel[slab] for k, slab in zip(kernels, slabs)])
    grad_logits = jnp.concatenate(
        [k * (grad_kernel[slab] - mean) for k, slab in zip(kernels, slabs)], axis=0
    ).astype(BF)
    wide_logits = grad_logits.astype(F32)
    gbias_ref[...] += jnp.concatenate(
        [
            jnp.broadcast_to(jnp.sum(wide_logits, axis=1, keepdims=True), (8 * KSIZE, 128)),
            jnp.zeros((8, 128), F32),
        ],
        axis=0,
    )
    gwk_ref[0 : 8 * KSIZE, :] += mm(grad_logits, attn_ref[...])
    grad_attn = mm_tn(grad_logits, wk_ref[...]).astype(BF).astype(F32)
    grad_keyconv = (grad_attn * q_ref[...].astype(F32)).astype(BF)
    gq_ref[...] = (grad_attn * keyconv_ref[...]).astype(BF)
    gwk_ref[8 * KSIZE : 8 * KSIZE + 1, :] += jnp.sum(grad_keyconv.astype(F32), axis=0, keepdims=True)
    wp_sum[...] += mm_tn(depth_ref[...], grad_keyconv)
    grad_depth = mm_nt(grad_keyconv, wp_ref[...]).astype(BF)
    gdepth_ref[...] = grad_depth
    wide = grad_depth.astype(F32)
    for at in range(0, window.shape[1], 128):
        some = slice(at, at + 128)
        for tap in range(KSIZE):
            gtaps_ref[tap : tap + 1, some] += jnp.sum(
                wide[:, some] * window[12 + tap : 12 + tap + rows, some], axis=0, keepdims=True
            )

    @pl.when(tile == pl.num_programs(0) - 1)
    def finish():
        gvalues_ref[...] = values_sum[...].astype(BF)
        tokens, block = x_ref.shape[0], lax.axis_index("blk")
        sums = [
            jnp.sum(gvalues_ref[at:end, :].astype(F32), axis=0, keepdims=True)
            for at, end in ((0, 16), (16, tokens + 16), (tokens + 16, tokens + 32))
        ]
        b_sum = sums[1] + jnp.where(block > 0, sums[0], 0.0) + jnp.where(block < count - 1, sums[2], 0.0)
        sharers, shard, width = staged.shape[0], staged.shape[1] // 2, staged.shape[2]
        part = ATT // sharers
        half = gbu_ref.shape[1] // sharers // 2
        turn_wide[0:6, :] = gvec_ref[0:6, :]
        turn_wide[TAPS_AT : TAPS_AT + KSIZE, :] = gtaps_ref[0:KSIZE, :]
        vectors = turn_wide[...].T
        for h in range(HEADS):
            for j in range(KSIZE):
                turn_wide[h * KSIZE + j : h * KSIZE + j + 1, 0:LANES] = gbias_ref[j * 8 + h : j * 8 + h + 1, :]
                turn_thin[h * KSIZE + j : h * KSIZE + j + 1, :] = gwk_ref[j * 8 + h : j * 8 + h + 1, :]
        bias = turn_wide[:, 0:LANES].T[0:1]
        turn_thin[THIN_AT : THIN_AT + 1, :] = gwk_ref[8 * KSIZE : 8 * KSIZE + 1, :]
        turn_thin[THIN_AT + 1 : THIN_AT + 2, :] = b_sum
        kernels = turn_thin[...].T
        side[...] = jnp.zeros_like(side)
        for owner in range(sharers):
            staged[owner, 0:shard, 0:ATT] = wp_sum[owner * shard : (owner + 1) * shard].astype(BF)
            staged[owner, shard:, 0:ATT] = wc_sum[owner * shard : (owner + 1) * shard].astype(BF)
            staged[owner, shard:, ATT:] = jnp.zeros((shard, width - ATT), BF)
            staged[owner, 0:shard, ATT : ATT + LANES] = vectors[owner * shard : (owner + 1) * shard].astype(BF)
            side[0:part, :] = kernels[owner * part : (owner + 1) * part]
            for place in range(2):
                first = (2 * owner + place) * half
                side[part + place : part + place + 1, 0:half] = gbu_ref[0:1, first : first + half]
            side[part + 2 : part + 3, :] = bias
            staged[owner, 0:shard, ATT + LANES : ATT + 2 * LANES] = side[...].astype(BF)
            staged[owner, 0:shard, ATT + 2 * LANES :] = jnp.zeros((shard, width - ATT - 2 * LANES), BF)
        copy = pltpu.make_async_copy(staged, packed_ref.at[:, 5 * shard : 7 * shard], sem)
        copy.start()
        copy.wait()


def mix_back(count, x, halo, values, rim, grad_conv, kernt, kern, query, keyconv, attn_key, depth, weight, w_kernel, g_vectors, gb_up, packed):
    tokens, width = x.shape
    sharers, shard = packed.shape[0], packed.shape[1] // 7
    away = pl.BlockSpec(memory_space=pl.ANY)
    rows = math.gcd(tokens, 512)
    by_rows = [(v, rows_of(rows, v.shape[1])) for v in (kern, query, keyconv, attn_key, depth)]
    return run_tiles(
        functools.partial(mix_back_kernel, rows, count),
        "mix_back",
        tokens // rows,
        [(v, all_of(v.shape)) for v in (x, halo, values, rim)]
        + [(grad_conv, rows_of(rows, ATT)), (kernt, columns_of(8 * KSIZE, rows))]
        + by_rows
        + [(weight, column_block(weight, 3))]
        + [(v, all_of(v.shape)) for v in (w_kernel, g_vectors, gb_up)]
        + [(packed, away)],
        [
            (shaped((tokens, ATT), BF), rows_of(rows, ATT)),
            (shaped((tokens, width), BF), rows_of(rows, width)),
            (shaped((tokens + 32, ATT), BF), all_of((tokens + 32, ATT))),
            (shaped(packed.shape, BF), away),
            (shaped((width, tokens), BF), columns_of(width, rows)),
        ],
        [
            pltpu.VMEM((rows + 32, width), F32),
            pltpu.VMEM((rows + 32, ATT), F32),
            pltpu.VMEM((rows + 32, ATT), F32),
            pltpu.VMEM((rows, KSIZE * ATT), BF),
            pltpu.VMEM((128, KSIZE * ATT), BF),
            pltpu.VMEM((width, ATT), F32),
            pltpu.VMEM((width, ATT), F32),
            pltpu.VMEM((tokens + 32, ATT), F32),
            pltpu.VMEM((8 * KSIZE + 8, ATT), F32),
            pltpu.VMEM((8 * KSIZE + 8, LANES), F32),
            pltpu.VMEM((16, width), F32),
            pltpu.VMEM((LANES, width), F32),
            pltpu.VMEM((LANES, ATT), F32),
            pltpu.VMEM((shard, LANES), F32),
            pltpu.VMEM((sharers, 2 * shard, width), BF),
            pltpu.SemaphoreType.DMA(()),
        ],
        4 * tokens * width * ATT * 4,
        {15: 3},
    )


MESH = pl.DeviceIdType.MESH
LINE = 4
LANES = 128
TAPS_AT = 16
THIN_AT = 64
BIAS_AT = 100


def my_place(sharers):
    columns = sharers // (2 * LINE)
    me = lax.axis_index("dp")
    return me, me // (2 * columns), lax.rem(me // 2, columns), lax.rem(me, 2), columns


def greet(partners):
    barrier = pltpu.get_barrier_semaphore()
    for partner in partners:
        pl.semaphore_signal(barrier, inc=1, device_id=partner, device_id_type=MESH)
    return barrier


def remote(source, target, send_sem, recv_sem, device):
    return pltpu.make_async_remote_copy(
        src_ref=source,
        dst_ref=target,
        send_sem=send_sem,
        recv_sem=recv_sem,
        device_id=device,
        device_id_type=MESH,
    )


def gather_kernel(sharers, count, part, *refs):
    w_refs, refs = refs[:3], refs[3:]
    vector_refs, refs = refs[:6], refs[6:]
    thin_refs, refs = refs[:4], refs[4:]
    (taps_ref, up_ref, kernel_ref, bias_ref, wu_ref, wn_ref, head_ref, tail_ref), refs = refs[:8], refs[8:]
    (out_ref, wide_ref, thin_ref, thin_columns_ref, bias_up_ref, wk_ref, bk_ref, halo_ref, wu_out, wn_out), refs = refs[:10], refs[10:]
    rows, side, flat, thin_flat, edges, send_sem, recv_sem, edge_send, edge_recv = refs
    me, line, column, core, columns = my_place(sharers)
    block = lax.axis_index("blk")
    shard = out_ref.shape[1]
    base = len(w_refs) * ATT
    half = up_ref.shape[0] // 2

    def at(line, column, core):
        return (line * columns + column) * 2 + core

    lines = [lax.rem(line + step, LINE) for step in range(1, LINE)]
    sides = [lax.rem(column + step, columns) for step in range(1, columns)]
    partners = [{"dp": at(other, column, core)} for other in lines]
    across = [{"dp": at(line, other, core)} for other in sides]
    mate = {"dp": at(line, column, 1 - core)}
    ends = []
    if count > 1:
        ends = [{"blk": lax.rem(block + 1, count)}, {"blk": lax.rem(block + count - 1, count)}]
    barrier = greet(partners + across + [mate] + ends)
    for place, ref in enumerate(w_refs):
        out_ref[me, :, place * ATT : (place + 1) * ATT] = ref[...].astype(BF)
    rows[...] = jnp.zeros_like(rows)
    for place, ref in enumerate(vector_refs):
        rows[place : place + 1, 0:shard] = ref[...].reshape(1, shard)
    for place, ref in enumerate(thin_refs):
        rows[THIN_AT + place : THIN_AT + place + 1, 0:part] = ref[...].reshape(1, part)
    rows[BIAS_AT : BIAS_AT + 1, 0 : HEADS * KSIZE] = bias_ref[...].reshape(1, HEADS * KSIZE)
    rows[...] = rows[...].T
    side[...] = rows[0:shard]
    side[:, TAPS_AT : TAPS_AT + KSIZE] = taps_ref[...]
    out_ref[me, :, base : base + LANES] = side[...].astype(BF)
    side[...] = jnp.zeros_like(side)
    side[0:part, 0 : HEADS * KSIZE] = kernel_ref[...]
    side[part : part + 1, 0:half] = up_ref[0:half].reshape(1, half)
    side[part + 1 : part + 2, 0:half] = up_ref[half:].reshape(1, half)
    out_ref[me, :, base + LANES :] = side[...].astype(BF)
    for group in range(wu_ref.shape[0]):
        wu_out[:, group * wu_ref.shape[2] : (group + 1) * wu_ref.shape[2]] = wu_ref[group].astype(BF)
        wn_out[:, group * wn_ref.shape[2] : (group + 1) * wn_ref.shape[2]] = wn_ref[group].astype(BF)
    pl.semaphore_wait(barrier, len(partners) + len(across) + 1 + len(ends))
    copies = []

    def pass_on(owner, devices):
        for device in devices:
            copy = remote(out_ref.at[owner], out_ref.at[owner], send_sem.at[len(copies)], recv_sem.at[owner], device)
            copy.start()
            copies.append(copy)

    def arrived(owner):
        pltpu.make_async_copy(out_ref.at[owner], out_ref.at[owner], recv_sem.at[owner]).wait()

    pass_on(me, across + partners + [mate])
    edge_copies = []
    for place, (ref, device) in enumerate(zip((tail_ref, head_ref), ends)):
        copy = remote(ref, edges.at[place], edge_send.at[place], edge_recv.at[place], device)
        copy.start()
        edge_copies.append(copy)
    for other in lines:
        owner = at(other, column, core)
        arrived(owner)
        pass_on(owner, across + [mate])
    for some in sides:
        for other in [line] + lines:
            owner = at(other, some, core)
            arrived(owner)
            pass_on(owner, [mate])
    nothing = jnp.zeros((16, halo_ref.shape[1]), BF)
    halo_ref[0:16, :] = nothing
    halo_ref[16:32, :] = nothing
    if count > 1:
        for copy in edge_copies:
            copy.wait()
        halo_ref[0:16, :] = jnp.where(block > 0, edges[0], nothing)
        halo_ref[16:32, :] = jnp.where(block < count - 1, edges[1], nothing)
    for j in range(KSIZE):
        for h in range(8):
            source = h * KSIZE + j if h < HEADS else 120
            bk_ref[j * 8 + h : j * 8 + h + 1, :] = rows[source : source + 1, :]
    for some in [column] + sides:
        for other in [line] + lines:
            arrived(at(other, some, 1 - core))
    for copy in copies:
        copy.wait_send()
    for owner in range(sharers):
        cells = out_ref[owner, :, base : base + LANES].astype(F32)
        flat[owner * shard : (owner + 1) * shard, :] = cells
        thin_flat[owner * part : (owner + 1) * part, :] = cells[0:part]
    turned = flat[...].T
    wide_ref[...] = turned[0 : wide_ref.shape[0]]
    thin_columns_ref[...] = thin_flat[...]
    thin_ref[...] = thin_flat[...].T[THIN_AT : THIN_AT + 8]
    for owner in range(sharers):
        cells = out_ref[owner, :, base + LANES :].astype(F32)
        thin_flat[owner * part : (owner + 1) * part, :] = cells[0:part]
        for place in range(2):
            first = (2 * owner + place) * half
            bias_up_ref[0:1, first : first + half] = cells[part + place : part + place + 1, 0:half]
    turned = thin_flat[...].T
    slabs = []
    for j in range(KSIZE):
        slabs += [turned[h * KSIZE + j : h * KSIZE + j + 1] for h in range(HEADS)]
        slabs.append(jnp.zeros((8 - HEADS, ATT), F32))
    wk_ref[...] = jnp.concatenate(slabs, axis=0).astype(BF)


def gather_columns(weights, vectors, thin, taps, b_up, w_kernel, kernel_bias, w_up, w_down, x, sharers, count):
    shard, part = weights[0].shape[0], thin[0].shape[0]
    tokens, width = x.shape
    wide = len(weights) * ATT + 2 * LANES
    columns = sharers // (2 * LINE)
    copies = LINE - 1 + columns - 1 + 1 + (LINE - 1) * columns + LINE * (columns - 1)
    args = list(weights) + list(vectors) + list(thin) + [taps, b_up, w_kernel, kernel_bias, w_up, w_down]
    shapes = [
        shaped((sharers, shard, wide), BF),
        shaped((32, width), F32),
        shaped((8, ATT), F32),
        shaped((ATT, LANES), F32),
        shaped((1, sharers * b_up.shape[0]), F32),
        shaped((8 * KSIZE, ATT), BF),
        shaped((8 * KSIZE, LANES), F32),
        shaped((32, width), BF),
        shaped((w_up.shape[1], w_up.shape[0] * w_up.shape[2]), BF),
        shaped((w_down.shape[1], w_down.shape[0] * w_down.shape[2]), BF),
    ]
    out, *rest = pl.pallas_call(
        functools.partial(gather_kernel, sharers, count, part),
        grid=(1,),
        in_specs=[all_of(v.shape) for v in args]
        + [
            pl.BlockSpec((16, width), lambda i: (0, 0)),
            pl.BlockSpec((16, width), lambda i: (tokens // 16 - 1, 0)),
        ],
        out_specs=[all_of(v.shape) for v in shapes],
        out_shape=shapes,
        scratch_shapes=[
            pltpu.VMEM((LANES, LANES), F32),
            pltpu.VMEM((shard, LANES), F32),
            pltpu.VMEM((width, LANES), F32),
            pltpu.VMEM((ATT, LANES), F32),
            pltpu.VMEM((2, 16, width), BF),
            pltpu.SemaphoreType.DMA((copies,)),
            pltpu.SemaphoreType.DMA((sharers,)),
            pltpu.SemaphoreType.DMA((2,)),
            pltpu.SemaphoreType.DMA((2,)),
        ],
        compiler_params=pltpu.CompilerParams(
            collective_id=0, has_side_effects=True, vmem_limit_bytes=60 * MIB
        ),
        name="gather_columns",
    )(*args, x, x)
    return (out.reshape(sharers * shard, wide), *rest)


class Shares:
    def __init__(self, sharers, rows, widths, line_first, count):
        self.sharers, self.rows, self.widths, self.line_first, self.count = sharers, rows, widths, line_first, count
        self.columns = sharers // (2 * LINE)
        self.chips = sharers // 2
        ends = [sum(widths[: at + 1]) for at in range(len(widths))]
        self.lanes = [slice(end - width, end) for end, width in zip(ends, widths)]
        self.wide = ends[-1]
        self.copies = 1 + self.columns - 1 + LINE - 1 + count - 1

    def scratch(self):
        shapes = []
        for width, line_first in zip(self.widths, self.line_first):
            side = (self.columns - 1, 1 if line_first else LINE, self.rows, width)
            line = (LINE - 1, self.columns if line_first else 1, self.rows, width)
            shapes += [pltpu.VMEM((self.chips, self.rows, width), BF)] * 2
            shapes += [pltpu.VMEM(side, BF)] * 2 + [pltpu.VMEM(line, BF)] * 2
            shapes += [pltpu.VMEM((self.rows, width), BF), pltpu.VMEM((self.count, self.rows, width), BF)]
        sems = len(self.widths) * self.copies
        return shapes + [
            pltpu.VMEM((self.sharers, self.rows, self.wide), F32),
            pltpu.SemaphoreType.DMA((sems,)),
            pltpu.SemaphoreType.DMA((sems,)),
        ]

    def bind(self, refs):
        chains = len(self.widths)
        self.buffers = [refs[8 * chain : 8 * chain + 8] for chain in range(chains)]
        self.total, self.send_sem, self.recv_sem = refs[8 * chains : 8 * chains + 3]
        self.me, self.line, self.column, self.core, unused = my_place(self.sharers)
        self.block = lax.axis_index("blk")
        self.others_line = [lax.rem(self.line + step, LINE) for step in range(1, LINE)]
        self.others_side = [lax.rem(self.column + step, self.columns) for step in range(1, self.columns)]
        self.others_block = [lax.rem(self.block + step, self.count) for step in range(1, self.count)]

    def at(self, line, column, core):
        return (line * self.columns + column) * 2 + core

    def greet(self):
        devices = [{"dp": self.at(self.line, self.column, 1 - self.core)}]
        devices += [{"dp": self.at(self.line, other, self.core)} for other in self.others_side]
        devices += [{"dp": self.at(other, self.column, self.core)} for other in self.others_line]
        devices += [{"blk": other} for other in self.others_block]
        greet(devices)

    def met(self):
        pl.semaphore_wait(pltpu.get_barrier_semaphore(), 1 + self.columns - 1 + LINE - 1 + self.count - 1)

    def copy(self, chain, number, source, target, device):
        sem = chain * self.copies + number
        return remote(source, target, self.send_sem.at[sem], self.recv_sem.at[sem], device)

    def part(self, owner, chain):
        return self.total[owner, :, self.lanes[chain]]

    def add(self, owner, chain, values):
        self.total[owner, :, self.lanes[chain]] += values.astype(F32)

    def mate_copy(self, chain):
        mate = {"dp": self.at(self.line, self.column, 1 - self.core)}
        return self.copy(chain, 0, self.buffers[chain][0], self.buffers[chain][1], mate)

    def mate_start(self, chain):
        for chip in range(self.chips):
            self.buffers[chain][0][chip] = self.part(2 * chip + 1 - self.core, chain).astype(BF)
        self.mate_copy(chain).start()

    def mate_end(self, chain):
        self.mate_copy(chain).wait()
        for chip in range(self.chips):
            self.add(2 * chip + self.core, chain, self.buffers[chain][1][chip])

    def side_copies(self, chain):
        source, target = self.buffers[chain][2:4]
        return [
            self.copy(chain, 1 + step, source.at[step], target.at[step], {"dp": self.at(self.line, other, self.core)})
            for step, other in enumerate(self.others_side)
        ]

    def side_lines(self, chain):
        return [self.line] if self.line_first[chain] else range(LINE)

    def side_start(self, chain):
        for step, other in enumerate(self.others_side):
            for place, line in enumerate(self.side_lines(chain)):
                self.buffers[chain][2][step, place] = self.part(self.at(line, other, self.core), chain).astype(BF)
        for copy in self.side_copies(chain):
            copy.start()

    def side_end(self, chain):
        for step, copy in enumerate(self.side_copies(chain)):
            copy.wait()
            for place, line in enumerate(self.side_lines(chain)):
                self.add(self.at(line, self.column, self.core), chain, self.buffers[chain][3][step, place])

    def line_copies(self, chain):
        source, target = self.buffers[chain][4:6]
        return [
            self.copy(chain, self.columns + step, source.at[step], target.at[step], {"dp": self.at(other, self.column, self.core)})
            for step, other in enumerate(self.others_line)
        ]

    def line_columns(self, chain):
        return range(self.columns) if self.line_first[chain] else [self.column]

    def line_start(self, chain):
        for step, other in enumerate(self.others_line):
            for place, column in enumerate(self.line_columns(chain)):
                self.buffers[chain][4][step, place] = self.part(self.at(other, column, self.core), chain).astype(BF)
        for copy in self.line_copies(chain):
            copy.start()

    def line_end(self, chain):
        for step, copy in enumerate(self.line_copies(chain)):
            copy.wait()
            for place, column in enumerate(self.line_columns(chain)):
                self.add(self.at(self.line, column, self.core), chain, self.buffers[chain][5][step, place])

    def block_copies(self, chain):
        source, target = self.buffers[chain][6:8]
        return [
            self.copy(chain, self.columns + LINE - 1 + step, source, target.at[self.block], {"blk": other})
            for step, other in enumerate(self.others_block)
        ]

    def block_start(self, chain):
        own = self.part(self.me, chain).astype(BF)
        self.buffers[chain][6][...] = own
        self.buffers[chain][7][self.block] = own
        for copy in self.block_copies(chain):
            copy.start()

    def block_end(self, chain):
        for copy in self.block_copies(chain):
            copy.wait()
        parts = [self.buffers[chain][7][at].astype(F32) for at in range(self.count)]
        return functools.reduce(jnp.add, parts)


def finish_kernel(blocks, rows, tiles, shares, *refs):
    dq_refs, refs = refs[:blocks], refs[blocks:]
    dk_refs, refs = refs[:blocks], refs[blocks:]
    dv_refs, refs = refs[:blocks], refs[blocks:]
    (x_ref, gq_ref, gvalues_ref, gdepth_ref, w_ref, wc_ref, mine_ref, wide_ref, sum_ref), refs = refs[:9], refs[9:]
    (gh_ref, flat_out, sums_out), refs = refs[:3], refs[3:]
    held, refs = refs[: 3 * blocks + 5], refs[3 * blocks + 5 :]
    dq, dk, dv = held[:blocks], held[blocks : 2 * blocks], held[2 * blocks : 3 * blocks]
    turned, gq, gvalues, gdepth, w = held[3 * blocks :]
    (load_sem, grads, window, bias_sum, rim_in, halo_in, halo, given, edge_send, edge_recv, given_send, given_recv), refs = refs[:12], refs[12:]
    shares.bind(refs)
    step = pl.program_id(0)
    count, sharers, shard = shares.count, shares.sharers, shares.rows
    chains = 3
    width, tokens = turned.shape
    block = shares.block
    sources = [x_ref, gq_ref] + list(dq_refs) + list(dv_refs) + list(dk_refs)
    targets = [turned, gq] + list(dq) + list(dv) + list(dk)
    sources += [gvalues_ref, gdepth_ref, w_ref.at[:, 0 : 3 * ATT], wc_ref.at[:, 2 * ATT : 3 * ATT]]
    targets += [gvalues, gdepth, w.at[:, 0 : 3 * ATT], w.at[:, 3 * ATT :]]
    loads = [
        pltpu.make_async_copy(source, target, load_sem.at[at])
        for at, (source, target) in enumerate(zip(sources, targets))
    ]
    by_chain = [loads[: 2 + blocks], loads[2 + blocks : 2 + 2 * blocks], loads[2 + 2 * blocks : 2 + 3 * blocks]]
    others = loads[2 + 3 * blocks :]

    def edge_copies():
        if count == 1:
            return []
        after, before = {"blk": lax.rem(block + 1, count)}, {"blk": lax.rem(block + count - 1, count)}
        plan = [
            (gvalues.at[tokens + 16 : tokens + 32], rim_in.at[0], after),
            (gvalues.at[0:16], rim_in.at[1], before),
            (gdepth.at[tokens - 16 : tokens], halo_in.at[0], after),
            (gdepth.at[0:16], halo_in.at[1], before),
        ]
        return [
            remote(source, target, edge_send.at[at], edge_recv.at[at], device)
            for at, (source, target, device) in enumerate(plan)
        ]

    def given_copies():
        return [
            remote(mine_ref, given.at[block], given_send.at[at], given_recv.at[at], {"blk": other})
            for at, other in enumerate(shares.others_block)
        ]

    @pl.when(step == 0)
    def start():
        shares.greet()
        for load in loads:
            load.start()
        bias_sum[...] = jnp.zeros_like(bias_sum)
        given[block] = mine_ref[...]

    def total(some):
        whole = [ref[...].astype(F32) for ref in some if ref.shape[0] == ATT]
        halves = [ref[...].astype(F32) for ref in some if ref.shape[0] < ATT]
        whole += [jnp.concatenate(halves[at : at + 2], axis=0) for at in range(0, len(halves), 2)]
        return functools.reduce(jnp.add, whole)

    def weights(chain):
        for load in by_chain[chain]:
            load.wait()
        if chain == 0:
            every = (total(dq).T + gq[...].astype(F32)).astype(BF)
        else:
            every = total((dv, dk)[chain - 1]).astype(BF).T
        place = (0, 2, 1)[chain]
        grads[:, place * ATT : (place + 1) * ATT] = every
        if chain < 2:
            bias_sum[0:1, chain * ATT : (chain + 1) * ATT] = jnp.sum(every.astype(F32), axis=0, keepdims=True)
        made = mm(turned[...], every)
        lanes = slice(shares.lanes[chain].start, shares.lanes[chain].start + ATT)
        for owner in range(sharers):
            shares.total[owner, :, lanes] = made[owner * shard : (owner + 1) * shard]
        if chain == 1:
            extra = slice(2 * ATT, 2 * ATT + LANES)
            shares.total[:, :, extra] = jnp.zeros((sharers, shard, LANES), F32)
            for at in range(2 * ATT // LANES):
                values = bias_sum[0:1, at * LANES : (at + 1) * LANES]
                for owner in range(sharers):
                    shares.total[owner, at : at + 1, extra] = values

    def conv_grads():
        for load in others[2:]:
            load.wait()
        for copy in edge_copies():
            copy.wait()
        zero = jnp.zeros((16, ATT), F32)
        before, after = zero, zero
        if count > 1:
            before = jnp.where(block > 0, rim_in[0].astype(F32), zero)
            after = jnp.where(block < count - 1, rim_in[1].astype(F32), zero)
            nothing = jnp.zeros((16, width), BF)
            halo[0:16, :] = jnp.where(block > 0, halo_in[0], nothing)
            halo[16:32, :] = jnp.where(block < count - 1, halo_in[1], nothing)
        else:
            halo[...] = jnp.zeros_like(halo)
        lanes = slice(3 * ATT, 4 * ATT)
        grads[16 : tokens - 16, lanes] = gvalues[32:tokens, :]
        grads[0:16, lanes] = (gvalues[16:32, :].astype(F32) + before).astype(BF)
        grads[tokens - 16 : tokens, lanes] = (gvalues[tokens : tokens + 16, :].astype(F32) + after).astype(BF)

    for chain in range(chains):
        @pl.when(step == chain)
        def one(chain=chain):
            weights(chain)
            if chain == chains - 1:
                conv_grads()

    @pl.when(step >= chains)
    def by_tile():
        tile = step - chains
        first = pl.multiple_of(tile * rows, rows)
        fill_rows(window, gdepth, halo, tile, tiles, rows)
        back = mm_nt(grads[pl.ds(first, rows), :], w[...])
        for at in range(0, width, 128):
            some = slice(at, at + 128)
            depth = back[:, some] + sum_ref[:, some]
            for tap in range(KSIZE):
                depth = depth + window[20 - tap : 20 - tap + rows, some] * wide_ref[TAPS_AT + tap : TAPS_AT + tap + 1, some]
            gh_ref[:, some] = depth.astype(BF)

    def first_sends(unused):
        shares.met()
        for load in others[:2]:
            load.wait()
        for copy in edge_copies() + given_copies():
            copy.start()

    def late(eighths):
        return chains + eighths * tiles // 8

    plan = [
        (0, [(first_sends, 0), (shares.mate_start, 0)]),
        (1, [(shares.mate_end, 0), (shares.side_start, 0), (shares.mate_start, 1)]),
        (2, [(shares.mate_end, 1), (shares.side_start, 1), (shares.side_end, 0), (shares.line_start, 0), (shares.mate_start, 2)]),
        (late(0), [(shares.mate_end, 2), (shares.side_start, 2)]),
        (late(1), [(shares.side_end, 1), (shares.line_start, 1)]),
        (late(2), [(shares.line_end, 0), (shares.block_start, 0)]),
        (late(3), [(shares.side_end, 2), (shares.line_start, 2)]),
        (late(5), [(shares.line_end, 1), (shares.block_start, 1)]),
        (late(6), [(shares.line_end, 2), (shares.block_start, 2)]),
    ]
    for when in range(chains + tiles):
        actions = [action for place, some in plan if place == when for action in some]
        if actions:

            @pl.when(step == when)
            def act(actions=actions):
                for action, chain in actions:
                    action(chain)

    @pl.when(step == chains + tiles - 1)
    def end():
        for copy in given_copies():
            copy.wait()
        flat_out[...] = functools.reduce(jnp.add, [given[at].astype(F32) for at in range(count)])
        for chain in range(chains):
            sums_out[:, shares.lanes[chain]] = shares.block_end(chain)


def unpack_kernel(part, gh_ref, flat, sums, gh_out, gq_out, gk_out, gv_out, gc_out, gwd_out, gwu_out, gwn_out, gwp_out, gwk_out, gtaps_out, gkb_out, gbup_out, *refs):
    vector_outs, thin_outs = refs[:6], refs[6:10]
    shard = sums.shape[0]
    width = flat.shape[1]
    gh_out[...] = gh_ref[...]

    @pl.when(pl.program_id(0) == 0)
    def small():
        gwd_out[...] = flat[0:shard]
        quarter = shard // 2
        for group in range(2):
            for place in range(2):
                first = shard * (1 + group) + quarter * place
                gwu_out[group, :, place * width : (place + 1) * width] = flat[first : first + quarter]
            gwn_out[group] = flat[3 * shard : 5 * shard, group * ATT : (group + 1) * ATT]
        gwp_out[...] = flat[5 * shard : 6 * shard, 0:ATT]
        cells = flat[5 * shard : 6 * shard, ATT : ATT + LANES]
        gtaps_out[...] = cells[:, TAPS_AT : TAPS_AT + KSIZE]
        turned = jnp.concatenate([cells, jnp.zeros((LANES - shard, LANES), F32)], axis=0).T
        for at, ref in enumerate(vector_outs):
            ref[...] = turned[at : at + 1, 0:shard].reshape(shard)
        cells = flat[5 * shard : 6 * shard, ATT + LANES : ATT + 2 * LANES]
        gwk_out[...] = cells[0:part, 0 : HEADS * KSIZE]
        half = gbup_out.shape[0] // 2
        gbup_out[...] = jnp.concatenate(
            [cells[part : part + 1, 0:half], cells[part + 1 : part + 2, 0:half]], axis=1
        ).reshape(2 * half)
        gkb_out[...] = cells[part + 2 : part + 3, 0 : HEADS * KSIZE].reshape(HEADS * KSIZE)
        turned = jnp.concatenate([cells, jnp.zeros((LANES - shard, LANES), F32)], axis=0).T
        thin_outs[2][...] = turned[THIN_AT : THIN_AT + 1, 0:part].reshape(part)
        gq_out[...] = sums[:, 0:ATT]
        gv_out[...] = sums[:, ATT : 2 * ATT]
        gk_out[...] = sums[:, 2 * ATT + LANES :]
        gc_out[...] = flat[6 * shard : 7 * shard, 0:ATT]
        totals = jnp.concatenate(
            [sums[at : at + 1, 2 * ATT : 2 * ATT + LANES] for at in range(2 * ATT // LANES)], axis=1
        )
        lane = lax.broadcasted_iota(jnp.int32, (part, ATT), 1)
        row = lax.broadcasted_iota(jnp.int32, (part, ATT), 0)
        mine = (lane == lax.axis_index("dp") * part + row).astype(F32)
        thin_outs[3][...] = turned[THIN_AT + 1 : THIN_AT + 2, 0:part].reshape(part)
        for chain, ref in ((0, thin_outs[0]), (1, thin_outs[1])):
            picked = jnp.sum(mine * totals[:, chain * ATT : (chain + 1) * ATT], axis=1, keepdims=True)
            picked = jnp.broadcast_to(picked, (part, LANES))
            picked = jnp.concatenate([picked, jnp.zeros((LANES - part, LANES), F32)], axis=0).T
            ref[...] = picked[0:1, 0:part].reshape(part)


def unpack(grad_hidden, flat, sums, part, n_up):
    shard, width = sums.shape[0], flat.shape[1]
    shapes = [shaped((shard, ATT), F32)] * 4 + [
        shaped((shard, width), F32),
        shaped((2, shard // 2, 2 * width), F32),
        shaped((2, 2 * shard, ATT), F32),
        shaped((shard, ATT), F32),
        shaped((part, HEADS * KSIZE), F32),
        shaped((shard, KSIZE), F32),
        shaped((HEADS * KSIZE,), F32),
        shaped((n_up,), F32),
    ]
    shapes += [shaped((shard,), F32)] * 6 + [shaped((part,), F32)] * 4
    tokens = grad_hidden.shape[0]
    rows = math.gcd(tokens, 512)
    return pl.pallas_call(
        functools.partial(unpack_kernel, part),
        grid=(tokens // rows,),
        in_specs=[rows_of(rows, width), all_of(flat.shape), all_of(sums.shape)],
        out_specs=[rows_of(rows, width)] + [all_of(v.shape) for v in shapes],
        out_shape=[shaped(grad_hidden.shape, BF)] + shapes,
        compiler_params=pltpu.CompilerParams(vmem_limit_bytes=60 * MIB),
        name="unpack",
    )(grad_hidden, flat, sums)


def finish(dqs, dks, dvs, turned, grad_query, grad_values, grad_depth, weight, mixed, mine, wide_vectors, grad_sum, sharers, count):
    width, tokens = turned.shape
    rows = math.gcd(tokens, 256)
    tiles = tokens // rows
    blocks = len(dqs)
    chains = 3
    shard = width // sharers
    shares = Shares(sharers, shard, [ATT, ATT + LANES, ATT], [False, False, False], count)
    late_rows = pl.BlockSpec((rows, width), lambda i: (jnp.maximum(i - chains, 0), 0))
    away = pl.BlockSpec(memory_space=pl.ANY)
    loaded = list(dqs) + list(dks) + list(dvs) + [turned, grad_query, grad_values, grad_depth]
    args = loaded + [weight, mixed, mine, wide_vectors, grad_sum]
    shapes = [shaped(mine.shape, F32), shaped((shard, chains * ATT + LANES), F32)]
    return pl.pallas_call(
        functools.partial(finish_kernel, blocks, rows, tiles, shares),
        grid=(chains + tiles,),
        in_specs=[away] * (len(loaded) + 2) + [all_of(mine.shape), all_of(wide_vectors.shape), late_rows],
        out_specs=[late_rows] + [all_of(v.shape) for v in shapes],
        out_shape=[shaped((tokens, width), BF)] + shapes,
        scratch_shapes=[pltpu.VMEM(v.shape, v.dtype) for v in loaded]
        + [
            pltpu.VMEM((width, 4 * ATT), BF),
            pltpu.SemaphoreType.DMA((len(loaded) + 2,)),
            pltpu.VMEM((tokens, 4 * ATT), BF),
            pltpu.VMEM((rows + 32, width), F32),
            pltpu.VMEM((8, 2 * ATT), F32),
            pltpu.VMEM((2, 16, ATT), BF),
            pltpu.VMEM((2, 16, width), BF),
            pltpu.VMEM((32, width), BF),
            pltpu.VMEM((count,) + mine.shape, BF),
            pltpu.SemaphoreType.DMA((4,)),
            pltpu.SemaphoreType.DMA((4,)),
            pltpu.SemaphoreType.DMA((max(count - 1, 1),)),
            pltpu.SemaphoreType.DMA((max(count - 1, 1),)),
        ]
        + shares.scratch(),
        compiler_params=pltpu.CompilerParams(
            collective_id=1, has_side_effects=True, vmem_limit_bytes=60 * MIB
        ),
        cost_estimate=pl.CostEstimate(
            flops=4 * tokens * width * chains * ATT, bytes_accessed=30 * tokens * width, transcendentals=0
        ),
        name="finish",
    )(*args)


def shifted_from(value, axis, step):
    count = lax.axis_size(axis)
    return lax.ppermute(value, axis, [((i + step) % count, i) for i in range(count)])


def local(
    hidden,
    separators,
    out_grad,
    w_query,
    b_query,
    w_key,
    w_value,
    b_value,
    depth_kernel,
    w_point,
    b_keyconv,
    w_kernel,
    kernel_bias,
    w_convout,
    b_convout,
    w_dense,
    b_dense,
    gain_attn,
    shift_attn,
    w_up,
    b_up,
    w_down,
    b_down,
    gain_out,
    shift_out,
):
    count = lax.axis_size("blk")
    sharers = lax.axis_size("dp")
    x, cotangent = hidden[0], out_grad[0]
    tokens, width = x.shape
    part = b_query.shape[0]

    others = [shifted_from(x, "blk", step) for step in range(1, count)]
    weight, wide_vectors, thin, thin_columns, bias_up, wt_kernel, bias_kernel, halo, up, down = gather_columns(
        [w_query, w_key, w_value],
        [b_dense, gain_attn, shift_attn, b_down, gain_out, shift_out],
        [b_query, b_value, b_keyconv, b_convout],
        depth_kernel,
        b_up,
        w_kernel,
        kernel_bias,
        w_up,
        w_down,
        x,
        sharers,
        count,
    )
    late = [jnp.concatenate([w_dense, w_convout, w_point], axis=1).astype(BF), up, down]
    mixed, wt_up, wt_down = [lax.all_gather(v, "dp", axis=0, tiled=True) for v in late]

    query, query_t, *own = project(x, weight, thin, thin_columns, 3)
    keys = [own]
    outs, probs = [], []
    for step in range(count):
        if step > 0:
            keys.append(project(others[step - 1], weight, thin, thin_columns, 2))
        key, key_t, value, value_t, norms = keys[step]
        out, prob = attend(separators, query_t, key, value_t, norms, count, step)
        outs.append(out)
        probs.append(prob)
        if step == 0:
            depth, keyconv, attn_key, kernt, kern, conv, values, rim = mix(
                count, x, halo, query, mixed, wide_vectors, thin, wt_kernel, bias_kernel
            )
            others, depth = lax.optimization_barrier((others, depth))
    output, grad_sum, grad_conv, grads_t, sides, (packed, g_vectors, gb_up) = middle(
        outs, conv, x, cotangent, mixed, wt_up, wt_down, wide_vectors, bias_up, sharers
    )
    grad_query_conv, grad_depth, grad_values, packed, turned = mix_back(
        count, x, halo, values, rim, grad_conv, kernt, kern, query, keyconv, attn_key, depth, mixed, wt_kernel, g_vectors, gb_up, packed
    )
    packed, sides = lax.optimization_barrier((packed, sides))
    mine = lax.psum_scatter(packed, "dp", scatter_dimension=0, tiled=False)

    dqs, dks, dvs = [], [], []
    for step in list(range(1, count)) + [0]:
        key, key_t, value, value_t, norms = keys[step]
        some = HEADS // 2 if step else HEADS
        pieces = []
        for at in range(0, HEADS, some):
            dq, dk, dv = attend_back(probs[step], value, key_t, grads_t[step], sides[step], query_t, at, some)
            if step:
                dk, dv = shifted_from(dk, "blk", count - step), shifted_from(dv, "blk", count - step)
            pieces.append((dq, dk, dv))
        for whole, parts in zip((dqs, dks, dvs), zip(*pieces)):
            whole += parts
    grad_hidden, flat, sums = finish(
        dqs, dks, dvs, turned, grad_query_conv, grad_values, grad_depth, weight, mixed, mine, wide_vectors, grad_sum, sharers, count
    )
    results = unpack(grad_hidden, flat, sums, part, b_up.shape[0])
    grad_hidden, gw_query, gw_key, gw_value, gw_convout, gw_dense, gw_up, gw_down, gw_point, gw_kernel, g_taps, g_bias, gb_up = results[:13]
    g_vectors, thin = results[13:19], results[19:]
    return (
        output[None],
        grad_hidden[None],
        gw_query,
        thin[0],
        gw_key,
        gw_value,
        thin[1],
        g_taps,
        gw_point,
        thin[2],
        gw_kernel,
        g_bias,
        gw_convout,
        thin[3],
        gw_dense,
        g_vectors[0],
        g_vectors[1],
        g_vectors[2],
        gw_up,
        gb_up,
        gw_down,
        g_vectors[3],
        g_vectors[4],
        g_vectors[5],
    )


def solution(mesh):
    placed = (
        P("dp", "blk", None),
        P("dp"),
        P("dp", "blk", None),
        P("dp", None),
        P("dp"),
        P("dp", None),
        P("dp", None),
        P("dp"),
        P("dp", None),
        P("dp", None),
        P("dp"),
        P("dp", None),
        P(),
        P("dp", None),
        P("dp"),
        P("dp", None),
        P("dp"),
        P("dp"),
        P("dp"),
        P(None, "dp", None),
        P("dp"),
        P(None, "dp", None),
        P("dp"),
        P("dp"),
        P("dp"),
    )
    return jax.shard_map(
        local,
        mesh=mesh,
        in_specs=placed,
        out_specs=(
            P("dp", "blk", None),
            P("dp", "blk", None),
            P("dp", None),
            P("dp"),
            P("dp", None),
            P("dp", None),
            P("dp"),
            P("dp", None),
            P("dp", None),
            P("dp"),
            P("dp", None),
            P(),
            P("dp", None),
            P("dp"),
            P("dp", None),
            P("dp"),
            P("dp"),
            P("dp"),
            P(None, "dp", None),
            P("dp"),
            P(None, "dp", None),
            P("dp"),
            P("dp"),
            P("dp"),
        ),
        check_vma=False,
    )
```

```python
import functools, math
import jax, jax.numpy as jnp
from jax import lax
from jax.experimental import pallas as pl
from jax.experimental.pallas import tpu as pltpu
from jax.sharding import PartitionSpec as P

HEADS = 6
HD = 64
KSIZE = 9
REACH = 4
ATT = 384
EPS = 1e-12
BF = jnp.bfloat16
F32 = jnp.float32
MIB = 2**20
EXCLUDED = 2.0**100
SAFE_SCORE = 50.0


def mm(left, right):
    return jnp.dot(left, right, preferred_element_type=F32)


def mm_nt(left, right):
    return lax.dot_general(left, right, (((1,), (1,)), ((), ())), preferred_element_type=F32)


def mm_tn(left, right):
    return lax.dot_general(left, right, (((0,), (0,)), ((), ())), preferred_element_type=F32)


def in_lanes(rows, columns):
    lane = lax.broadcasted_iota(jnp.int32, (rows, 128), 1)
    out = jnp.zeros((rows, 128), F32)
    for at, column in enumerate(columns):
        out = jnp.where(lane == at, column, out)
    return out.astype(BF)


def in_rows(columns, rows):
    row = lax.broadcasted_iota(jnp.int32, (16, columns), 0)
    out = jnp.zeros((16, columns), F32)
    for at, values in enumerate(rows):
        out = jnp.where(row == at, values, out)
    return out.astype(BF)


def three_parts(values):
    high = values.astype(BF).astype(F32)
    rest = values - high
    middle = rest.astype(BF).astype(F32)
    return high, middle, (rest - middle).astype(BF).astype(F32)


def put_head(ref, head, values):
    odd = lax.rem(head, 2) == 1
    none = jnp.zeros_like(values)
    ref[0:HD, :] = jnp.where(odd, none, values)
    ref[HD : 2 * HD, :] = jnp.where(odd, values, none)


def attend_kernel(keys, queries, chunk, count, step, at_ref, q_ref, k_ref, v_ref, norm_ref, o_ref, p_ref, key_side, query_side):
    head, tile = pl.program_id(0), pl.program_id(1)
    separator, block = at_ref[0], lax.axis_index("blk")
    first_query = block * keys
    first_key = lax.rem(block + step, count) * keys

    @pl.when((head == 0) & (tile == 0))
    def start():
        position = first_key + lax.broadcasted_iota(jnp.int32, (keys, 128), 0)
        late = (position >= separator).astype(F32)
        key_side[...] = in_lanes(keys, [1.0 - late, late, 1.0, 1.0, 1.0])
        query_side[2 * HD + 16 :, :] = jnp.zeros((2 * HD - 16, queries), BF)

    put_head(query_side, head, q_ref[...])
    position = first_query + tile * queries + lax.broadcasted_iota(jnp.int32, (16, queries), 1)
    late = (position >= separator).astype(F32)
    excluded = [-EXCLUDED * late, -EXCLUDED * (1.0 - late)]
    query_side[2 * HD : 2 * HD + 16, :] = in_rows(queries, excluded)
    o_ref[0, HD + 8 : HD + 16, :] = jnp.zeros((8, queries), F32)
    wide = q_ref[...].astype(F32)
    largest = jnp.max(jnp.sum(wide * wide, axis=0, keepdims=True)) * jnp.max(norm_ref[...])

    def scores(at):
        part = slice(at * chunk, (at + 1) * chunk)
        return mm(
            jnp.concatenate([k_ref[part, :], key_side[part, :]], axis=1), query_side[...]
        )

    @pl.when(jnp.logical_not(largest <= SAFE_SCORE * SAFE_SCORE))
    def shifted():
        best = jnp.full((1, queries), -4.0 * EXCLUDED, F32)
        for at in range(keys // chunk):
            best = jnp.maximum(best, jnp.max(scores(at), axis=0, keepdims=True))
        parts = three_parts(jnp.where(best < -0.5 * EXCLUDED, 0.0, best))
        query_side[2 * HD : 2 * HD + 16, :] = in_rows(queries, excluded + [-part for part in parts])
        o_ref[0, HD + 8 : HD + 16, :] = jnp.broadcast_to(
            jnp.where(best < -0.5 * EXCLUDED, best, parts[0] + parts[1] + parts[2]), (8, queries)
        )

    ones = in_rows(chunk, [1.0])
    total = jnp.zeros((HD + 16, queries), F32)
    for at in range(keys // chunk):
        part = slice(at * chunk, (at + 1) * chunk)
        probs = jnp.exp(scores(at)).astype(BF)
        p_ref[0, part, :] = probs
        total = total + mm(jnp.concatenate([v_ref[:, part], ones], axis=0), probs)
    o_ref[0, 0 : HD + 8, :] = total[0 : HD + 8, :]


def attend(at, query_t, key, value_t, norms, count, step):
    tokens, keys = query_t.shape[1], key.shape[0]
    queries, chunk = math.gcd(tokens, 2048), math.gcd(keys, 1024)
    return pl.pallas_call(
        functools.partial(attend_kernel, keys, queries, chunk, count, step),
        grid=(HEADS, tokens // queries),
        in_specs=[
            pl.BlockSpec(memory_space=pltpu.SMEM),
            pl.BlockSpec((HD, queries), lambda h, i: (h, i)),
            pl.BlockSpec((keys, 2 * HD), lambda h, i: (0, h // 2)),
            pl.BlockSpec((HD, keys), lambda h, i: (h, 0)),
            pl.BlockSpec(norms.shape, lambda h, i: (0, 0)),
        ],
        out_specs=[
            pl.BlockSpec((1, HD + 16, queries), lambda h, i: (h, 0, i)),
            pl.BlockSpec((1, keys, queries), lambda h, i: (h, 0, i)),
        ],
        out_shape=[
            jax.ShapeDtypeStruct((HEADS, HD + 16, tokens), F32),
            jax.ShapeDtypeStruct((HEADS, keys, tokens), BF),
        ],
        scratch_shapes=[pltpu.VMEM((keys, 128), BF), pltpu.VMEM((4 * HD, queries), BF)],
        compiler_params=pltpu.CompilerParams(vmem_limit_bytes=56 * MIB),
        cost_estimate=pl.CostEstimate(
            flops=ATT * keys,
            bytes_accessed=2 * HEADS * keys,
            transcendentals=0,
        ),
        name="attend",
    )(at, query_t, key, value_t, norms)


def attend_back_kernel(first, keys, queries, chunk, p_ref, v_ref, kt_ref, g_ref, side_ref, q_ref, dq_ref, dkv_ref, value_side, grad_side, dk_sum, dv_sum):
    head, tile = pl.program_id(0), pl.program_id(1)

    @pl.when((head == 0) & (tile == 0))
    def start():
        value_side[...] = in_lanes(chunk, [1.0, 1.0, 1.0])
        grad_side[2 * HD + 16 :, :] = jnp.zeros((2 * HD - 16, queries), BF)

    @pl.when(tile == 0)
    def fresh():
        dk_sum[...] = jnp.zeros_like(dk_sum)
        dv_sum[...] = jnp.zeros_like(dv_sum)

    put_head(grad_side, first + head, g_ref[...])
    grad_side[2 * HD : 2 * HD + 16, :] = side_ref[0]
    total = jnp.zeros((HD, queries), F32)
    for at in range(keys // chunk):
        part = slice(at * chunk, (at + 1) * chunk)
        probs = p_ref[0, part, :]
        spread = mm(jnp.concatenate([v_ref[part, :], value_side[...]], axis=1), grad_side[...])
        grad_scores = (probs.astype(F32) * spread).astype(BF)
        dv_sum[:, part] += mm_nt(g_ref[...], probs)
        dk_sum[:, part] += mm_nt(q_ref[...], grad_scores)
        total = total + mm(kt_ref[:, part], grad_scores)
    dq_ref[...] = (total * (HD**-0.5)).astype(BF)

    @pl.when(tile == pl.num_programs(1) - 1)
    def finish():
        dkv_ref[0] = dk_sum[...].astype(BF)
        dkv_ref[1] = dv_sum[...].astype(BF)


def attend_back(probs, value, key_t, grad_t, side, query_t, first, heads):
    tokens, keys = query_t.shape[1], value.shape[0]
    queries, chunk = math.gcd(tokens, 1024), math.gcd(keys, 256)
    by_token = pl.BlockSpec((HD, queries), lambda h, i: (first + h, i))
    by_key = pl.BlockSpec((HD, keys), lambda h, i: (first + h, 0))
    return pl.pallas_call(
        functools.partial(attend_back_kernel, first, keys, queries, chunk),
        grid=(heads, tokens // queries),
        in_specs=[
            pl.BlockSpec((1, keys, queries), lambda h, i: (first + h, 0, i)),
            pl.BlockSpec((keys, 2 * HD), lambda h, i: (0, (first + h) // 2)),
            by_key,
            by_token,
            pl.BlockSpec((1, 16, queries), lambda h, i: (first + h, 0, i)),
            by_token,
        ],
        out_specs=[
            pl.BlockSpec((HD, queries), lambda h, i: (h, i)),
            pl.BlockSpec((2, HD, keys), lambda h, i: (0, h, 0)),
        ],
        out_shape=[
            jax.ShapeDtypeStruct((heads * HD, tokens), BF),
            jax.ShapeDtypeStruct((2, heads * HD, keys), BF),
        ],
        scratch_shapes=[
            pltpu.VMEM((chunk, 128), BF),
            pltpu.VMEM((4 * HD, queries), BF),
            pltpu.VMEM((HD, keys), F32),
            pltpu.VMEM((HD, keys), F32),
        ],
        compiler_params=pltpu.CompilerParams(vmem_limit_bytes=56 * MIB),
        cost_estimate=pl.CostEstimate(
            flops=32 * heads * HD * tokens * keys,
            bytes_accessed=2 * heads * tokens * keys,
            transcendentals=0,
        ),
        name="attend_back",
    )(probs, value, key_t, grad_t, side, query_t)


def all_of(shape):
    return pl.BlockSpec(shape, lambda *at: (0,) * len(shape))


def rows_of(rows, width):
    return pl.BlockSpec((rows, width), lambda i: (i, 0))


def columns_of(height, columns):
    return pl.BlockSpec((height, columns), lambda i: (0, i))


def run_tiles(kernel, name, steps, inputs, outputs, scratch, flops, aliases=None):
    args, in_specs = zip(*inputs)
    shapes, out_specs = zip(*outputs)
    size = sum(math.prod(v.shape) * v.dtype.itemsize for v in args + shapes)
    return pl.pallas_call(
        kernel,
        grid=(steps,),
        in_specs=list(in_specs),
        out_specs=list(out_specs),
        out_shape=list(shapes),
        scratch_shapes=scratch,
        input_output_aliases=aliases or {},
        compiler_params=pltpu.CompilerParams(vmem_limit_bytes=62 * MIB),
        cost_estimate=pl.CostEstimate(flops=flops, bytes_accessed=size, transcendentals=0),
        name=name,
    )(*args)


def shaped(shape, dtype):
    return jax.ShapeDtypeStruct(shape, dtype)


def project_kernel(parts, sources, *refs):
    x_refs, refs = refs[:sources], refs[sources:]
    (w_ref, thin_ref, thin_columns_ref), refs = refs[:3], refs[3:]
    norm_ref, flipped = refs[2 * parts], refs[2 * parts + 1]
    skip = (3 - parts) * ATT

    @pl.when(pl.program_id(0) == 0)
    def start():
        norm_ref[...] = jnp.zeros_like(norm_ref)
        flipped[...] = w_ref[:, skip:].T

    x = x_refs[-1][...]
    if sources == 2:
        x = jnp.where(pl.program_id(0) == 0, x_refs[0][...], x)
    plain = mm(x, w_ref[:, skip:])
    turned = mm_nt(flipped[...], x)
    for part in range(parts):
        own = slice(part * ATT, (part + 1) * ATT)
        bias, bias_t = 0.0, 0.0
        if part != parts - 2:
            at = 1 if part == parts - 1 else 0
            bias, bias_t = thin_ref[at : at + 1, :], thin_columns_ref[:, THIN_AT + at : THIN_AT + at + 1]
        refs[2 * part][...] = (plain[:, own] + bias).astype(BF)
        across = (turned[own] + bias_t).astype(BF)
        if part == parts - 2:
            wide = across.astype(F32)
            for head in range(HEADS):
                cells = wide[head * HD : (head + 1) * HD]
                size = jnp.sum(cells * cells, axis=0, keepdims=True)
                norm_ref[...] = jnp.maximum(norm_ref[...], size)
        if part < parts - 2:
            across = (across.astype(F32) * (HD**-0.5)).astype(BF)
        refs[2 * part + 1][...] = across


def project(sources, weight, thin, thin_columns, parts):
    tokens, width = sum(x.shape[0] for x in sources), sources[0].shape[1]
    wide = 3 * ATT
    tile = math.gcd(tokens, 512)
    late = len(sources) - 1
    inputs = [(sources[-1], pl.BlockSpec((tile, width), lambda i: (jnp.maximum(i - late, 0), 0)))]
    if late:
        inputs.insert(0, (sources[0], all_of((tile, width))))
    outputs = []
    for part in range(parts):
        outputs.append((shaped((tokens, ATT), BF), rows_of(tile, ATT)))
        outputs.append((shaped((ATT, tokens), BF), columns_of(ATT, tile)))
    outputs.append((shaped((8, tile), F32), all_of((8, tile))))
    return run_tiles(
        functools.partial(project_kernel, parts, len(sources)),
        "project",
        tokens // tile,
        inputs
        + [
            (weight, all_of((width, wide))),
            (thin, all_of(thin.shape)),
            (thin_columns, all_of(thin_columns.shape)),
        ],
        outputs,
        [pltpu.VMEM((parts * ATT, width), BF)],
        4 * tokens * width * parts * ATT,
    )


def fill_rows(window, x_ref, halo_ref, tile, tiles, rows):
    first = tile * rows
    tokens = x_ref.shape[0]
    before = x_ref[pl.ds(pl.multiple_of(jnp.maximum(first - 16, 0), 16), 16), :]
    after = x_ref[pl.ds(pl.multiple_of(jnp.minimum(first + rows, tokens - 16), 16), 16), :]
    window[0:16, :] = jnp.where(tile == 0, halo_ref[0:16, :], before).astype(window.dtype)
    window[16 : 16 + rows, :] = x_ref[pl.ds(pl.multiple_of(first, rows), rows), :].astype(window.dtype)
    window[16 + rows :, :] = jnp.where(
        tile == tiles - 1, halo_ref[16:32, :], after
    ).astype(window.dtype)


def fill_window(window, x_ref, halo_ref, tile, rows):
    fill_rows(window, x_ref, halo_ref, tile, pl.num_programs(0), rows)


def fill_spread(spread):
    row = lax.broadcasted_iota(jnp.int32, (128, ATT), 0)
    head = lax.broadcasted_iota(jnp.int32, (128, ATT), 1) // HD
    for tap in range(KSIZE):
        spread[:, tap * ATT : (tap + 1) * ATT] = (row == tap * 8 + head).astype(F32).astype(BF)


def mix_kernel(rows, count, x_ref, halo_ref, q_ref, wc_ref, wp_ref, wide_ref, thin_ref, wk_ref, bk_ref, depth_ref, keyconv_ref, attn_ref, kernt_ref, kern_ref, conv_ref, out_ref, rim_ref, window, conv_window, spread):
    tile = pl.program_id(0)
    last = pl.num_programs(0) - 1

    @pl.when(tile == 0)
    def start():
        fill_spread(spread)

    fill_window(window, x_ref, halo_ref, tile, rows)
    width = window.shape[1]
    for at in range(0, width, 128):
        some = slice(at, at + 128)
        total = jnp.zeros((rows, 128), F32)
        for tap in range(KSIZE):
            total = total + window[12 + tap : 12 + tap + rows, some] * wide_ref[TAPS_AT + tap : TAPS_AT + tap + 1, some]
        depth_ref[:, some] = total.astype(BF)
    position = (
        lax.axis_index("blk") * x_ref.shape[0] + tile * rows - 16 + lax.broadcasted_iota(jnp.int32, (rows + 32, ATT), 0)
    )
    inside = (position >= 0) & (position < count * x_ref.shape[0])
    values = mm(window[...].astype(BF), wc_ref[...]) + thin_ref[3:4, :]
    values = jnp.where(inside, values, 0.0).astype(BF)
    out_ref[...] = values[16 : 16 + rows]

    @pl.when(tile == 0)
    def first_rim():
        rim_ref[0:16, :] = values[0:16]

    @pl.when(tile == last)
    def last_rim():
        rim_ref[16:32, :] = values[16 + rows :]

    conv_window[...] = values.astype(F32)
    keyconv = mm(depth_ref[...], wp_ref[...]) + thin_ref[2:3, :]
    keyconv_ref[...] = keyconv
    attn_key = (keyconv * q_ref[...].astype(F32)).astype(BF)
    attn_ref[...] = attn_key
    logits = mm_nt(wk_ref[...], attn_key) + bk_ref[:, BIAS_AT : BIAS_AT + 1]
    slabs = [logits[8 * tap : 8 * tap + 8] for tap in range(KSIZE)]
    best = functools.reduce(jnp.maximum, slabs)
    slabs = [jnp.exp(slab - best) for slab in slabs]
    share = 1.0 / functools.reduce(jnp.add, slabs)
    slabs = [slab * share for slab in slabs]
    kernt = jnp.concatenate(slabs + [jnp.zeros((128 - 8 * KSIZE, rows), F32)], axis=0)
    kernt_ref[...] = kernt[0 : 8 * KSIZE]
    kern = kernt.astype(BF).T
    kern_ref[...] = kern
    total = jnp.zeros((rows, ATT), F32)
    for tap in range(KSIZE):
        total = total + mm(kern, spread[:, tap * ATT : (tap + 1) * ATT]) * conv_window[12 + tap : 12 + tap + rows, :]
    conv_ref[...] = total.astype(BF)


def column_block(weight, place):
    return pl.BlockSpec((weight.shape[0], ATT), lambda i: (0, place))


def mix(count, x, halo, query, weight, wide_vectors, thin, w_kernel, kernel_bias):
    tokens, width = x.shape
    rows = math.gcd(tokens, 512)
    whole = [(weight, column_block(weight, 2)), (weight, column_block(weight, 3))]
    whole += [(v, all_of(v.shape)) for v in (wide_vectors, thin, w_kernel, kernel_bias)]
    return run_tiles(
        functools.partial(mix_kernel, rows, count),
        "mix",
        tokens // rows,
        [
            (x, all_of(x.shape)),
            (halo, all_of(halo.shape)),
            (query, rows_of(rows, ATT)),
        ]
        + whole,
        [
            (shaped((tokens, width), BF), rows_of(rows, width)),
            (shaped((tokens, ATT), F32), rows_of(rows, ATT)),
            (shaped((tokens, ATT), BF), rows_of(rows, ATT)),
            (shaped((8 * KSIZE, tokens), F32), columns_of(8 * KSIZE, rows)),
            (shaped((tokens, 128), BF), rows_of(rows, 128)),
            (shaped((tokens, ATT), BF), rows_of(rows, ATT)),
            (shaped((tokens, ATT), BF), rows_of(rows, ATT)),
            (shaped((32, ATT), BF), all_of((32, ATT))),
        ],
        [
            pltpu.VMEM((rows + 32, width), F32),
            pltpu.VMEM((rows + 32, ATT), F32),
            pltpu.VMEM((128, KSIZE * ATT), BF),
        ],
        4 * tokens * width * ATT * 4,
    )


def normal(values):
    centre = values - jnp.mean(values, axis=-1, keepdims=True)
    scale = lax.rsqrt(jnp.mean(centre * centre, axis=-1, keepdims=True) + EPS)
    return centre * scale, scale


def normal_back(grad, unit, scale):
    return scale * (
        grad
        - jnp.mean(grad, axis=-1, keepdims=True)
        - unit * jnp.mean(grad * unit, axis=-1, keepdims=True)
    )


def gelu_parts(values):
    share = 0.5 + 0.5 * lax.erf(values * math.sqrt(0.5))
    bell = jnp.exp2(values * values * (-0.5 * math.log2(math.e)))
    return values * share, share + values * (bell * (1.0 / math.sqrt(2.0 * math.pi)))


def middle_kernel(blocks, rows, units, *refs):
    o_refs, refs = refs[:blocks], refs[blocks:]
    (conv_ref, x_ref, og_ref, wd_ref, late_ref, vec_ref, bu_ref), refs = refs[:7], refs[7:]
    (out_ref, sum_ref, gconv_ref), refs = refs[:3], refs[3:]
    g_refs, refs = refs[:blocks], refs[blocks:]
    side_refs, refs = refs[:blocks], refs[blocks:]
    (packed_ref, gvec_ref, gbu_ref, wd_sum, wu_sum, wn_sum, acts, slopes, staged, sems, wu_ref, wn_ref) = refs
    tile = pl.program_id(0)
    hidden_units = wu_ref.shape[1]
    groups = 2
    inner = ATT
    outer = hidden_units // groups

    @pl.when(tile == 0)
    def start():
        for ref in (wd_sum, wu_sum, wn_sum, gvec_ref, gbu_ref):
            ref[...] = jnp.zeros_like(ref)
        owners, high, width = late_ref.shape
        quarter = high // 8
        for pair in range(0, owners, 2):
            both = [late_ref[owner, 0 : high // 2].astype(F32) for owner in (pair, pair + 1)]
            for place in range(4):
                some = [cells[place * quarter : (place + 1) * quarter] for cells in both]
                wu_ref[pair * quarter : (pair + 2) * quarter, place * width : (place + 1) * width] = (
                    jnp.concatenate(some, axis=0).astype(BF)
                )
        for owner in range(owners):
            wn_ref[owner * high // 2 : (owner + 1) * high // 2] = late_ref[owner, high // 2 :]

    shifts = [ref[:, HD + 8 : HD + 9, :] for ref in o_refs]
    top = functools.reduce(jnp.maximum, shifts)
    weights = [jnp.exp(shift - top) for shift in shifts]
    mass = functools.reduce(jnp.add, [w * ref[:, HD : HD + 1, :] for w, ref in zip(weights, o_refs)])
    weights = [w / mass for w in weights]
    heads = functools.reduce(jnp.add, [w * ref[:, 0:HD, :] for w, ref in zip(weights, o_refs)])
    att_t = heads.reshape(ATT, rows).astype(BF)
    conv = conv_ref[...]
    vec = [vec_ref[at : at + 1, :] for at in range(6)]
    dense = mm(att_t.T, wd_ref[0:ATT, :]) + mm(conv, wd_ref[ATT:, :]) + vec[0]
    unit_one, scale_one = normal(dense + x_ref[...].astype(F32))
    normed = unit_one * vec[1] + vec[2]
    low = normed.astype(BF)
    downs = []
    for group in range(groups):
        mine = low[:, group * inner : (group + 1) * inner]
        down = jnp.zeros((rows, inner), F32)
        for at in range(0, outer, units):
            here = slice(group * outer + at, group * outer + at + units)
            upward = mm(mine, wu_ref[:, here]) + bu_ref[:, here]
            act, slope = gelu_parts(upward)
            act = act.astype(BF)
            acts[:, here] = act
            slopes[:, here] = slope.astype(BF)
            down = down + mm(act, wn_ref[at : at + units, group * inner : (group + 1) * inner])
        downs.append(down)
    unit_two, scale_two = normal(jnp.concatenate(downs, axis=1) + vec[3] + normed)
    out_ref[...] = (unit_two * vec[4] + vec[5]).astype(BF)
    og = og_ref[...].astype(F32)
    gvec_ref[4:5, :] += jnp.sum(og * unit_two, axis=0, keepdims=True)
    gvec_ref[5:6, :] += jnp.sum(og, axis=0, keepdims=True)
    grad_two = normal_back(og * vec[4], unit_two, scale_two)
    grad_down = grad_two.astype(BF)
    gvec_ref[3:4, :] += jnp.sum(grad_down.astype(F32), axis=0, keepdims=True)
    backs = []
    for group in range(groups):
        lanes = slice(group * inner, (group + 1) * inner)
        mine, grads = low[:, lanes], grad_down[:, lanes]
        mine_t = mine.T
        back = jnp.zeros((rows, inner), F32)
        for at in range(0, outer, units):
            here = slice(group * outer + at, group * outer + at + units)
            grad_act = mm_nt(grads, wn_ref[at : at + units, lanes])
            grad_up = (grad_act * slopes[:, here].astype(F32)).astype(BF)
            gbu_ref[0:1, here] += jnp.sum(grad_up.astype(F32), axis=0, keepdims=True)
            wn_sum[at : at + units, lanes] += mm_tn(acts[:, here], grads)
            wu_sum[:, here] += mm(mine_t, grad_up)
            back = back + mm_nt(grad_up, wu_ref[:, here])
        backs.append(back)
    grad_normed = grad_two + jnp.concatenate(backs, axis=1)
    gvec_ref[1:2, :] += jnp.sum(grad_normed * unit_one, axis=0, keepdims=True)
    gvec_ref[2:3, :] += jnp.sum(grad_normed, axis=0, keepdims=True)
    grad_one = normal_back(grad_normed * vec[1], unit_one, scale_one)
    sum_ref[...] = grad_one
    grad_dense = grad_one.astype(BF)
    gvec_ref[0:1, :] += jnp.sum(grad_dense.astype(F32), axis=0, keepdims=True)
    wd_sum[0:ATT, :] += mm(att_t, grad_dense)
    wd_sum[ATT:, :] += mm_tn(conv, grad_dense)
    gconv_ref[...] = mm_nt(grad_dense, wd_ref[ATT:, :]).astype(BF)
    grad_att = mm_nt(wd_ref[0:ATT, :], grad_dense).astype(BF).astype(F32).reshape(HEADS, HD, rows)
    for weight, g_ref, side_ref in zip(weights, g_refs, side_refs):
        share = (grad_att * weight).astype(BF)
        g_ref[...] = share.reshape(ATT, rows)
        delta = -jnp.sum(share.astype(F32) * heads, axis=1, keepdims=True)
        row = lax.broadcasted_iota(jnp.int32, (HEADS, 16, rows), 1)
        side = jnp.zeros((HEADS, 16, rows), F32)
        for at, part in enumerate(three_parts(delta)):
            side = jnp.where(row == at, part, side)
        side_ref[...] = side.astype(BF)

    @pl.when(tile == pl.num_programs(0) - 1)
    def finish():
        slots = staged.shape[0]
        sharers = packed_ref.shape[0]
        shard = wd_sum.shape[0] // sharers
        quarter = shard // 2
        width = wd_sum.shape[1]
        copies = []
        for owner in range(sharers):
            slot = owner % slots
            if owner >= slots:
                copies[owner - slots].wait()
            staged[slot, 0:shard] = wd_sum[owner * shard : (owner + 1) * shard].astype(BF)
            some = wu_sum[owner * quarter : (owner + 1) * quarter]
            for group in range(groups):
                pair = [some[:, at : at + width] for at in (2 * group * width, (2 * group + 1) * width)]
                staged[slot, (1 + group) * shard : (2 + group) * shard] = jnp.concatenate(pair, axis=0).astype(BF)
            some = wn_sum[owner * 2 * shard : (owner + 1) * 2 * shard]
            staged[slot, 3 * shard : 5 * shard] = some.astype(BF)
            copy = pltpu.make_async_copy(
                staged.at[slot], packed_ref.at[owner, 0 : 5 * shard], sems.at[owner]
            )
            copy.start()
            copies.append(copy)
        for copy in copies[sharers - slots :]:
            copy.wait()


def middle(outs, conv, x, out_grad, w_dense, late, vectors, b_up):
    tokens, width = x.shape
    sharers = late.shape[0]
    shard = width // sharers
    units = b_up.shape[1]
    up, down = (width // 2, units), (units // 2, width)
    rows = math.gcd(tokens, 512)
    blocks = len(outs)
    heads = pl.BlockSpec((HEADS, HD + 16, rows), lambda i: (0, 0, i))
    side = pl.BlockSpec((HEADS, 16, rows), lambda i: (0, 0, i))
    single = pl.Buffered(1)
    once = [
        (w_dense, pl.BlockSpec((width, width), lambda i: (0, 0), pipeline_mode=single)),
        (late, pl.BlockSpec(late.shape, lambda i: (0, 0, 0), pipeline_mode=single)),
    ]
    once += [(v, all_of(v.shape)) for v in (vectors, b_up)]
    results = run_tiles(
        functools.partial(middle_kernel, blocks, rows, 768),
        "middle",
        tokens // rows,
        [(o, heads) for o in outs]
        + [
            (conv, rows_of(rows, ATT)),
            (x, rows_of(rows, width)),
            (out_grad, rows_of(rows, width)),
        ]
        + once,
        [
            (shaped((tokens, width), BF), rows_of(rows, width)),
            (shaped((tokens, width), F32), rows_of(rows, width)),
            (shaped((tokens, ATT), BF), rows_of(rows, ATT)),
        ]
        + [(shaped((ATT, tokens), BF), columns_of(ATT, rows))] * blocks
        + [(shaped((HEADS, 16, tokens), BF), side)] * blocks
        + [
            (shaped((sharers, 7 * shard, width), BF), pl.BlockSpec(memory_space=pl.ANY)),
            (shaped((8, width), F32), all_of((8, width))),
            (shaped((8, units), F32), all_of((8, units))),
        ],
        [
            pltpu.VMEM((width, width), F32),
            pltpu.VMEM(up, F32),
            pltpu.VMEM(down, F32),
            pltpu.VMEM((rows, units), BF),
            pltpu.VMEM((rows, units), BF),
            pltpu.VMEM((2, 5 * shard, width), BF),
            pltpu.SemaphoreType.DMA((sharers,)),
            pltpu.VMEM(up, BF),
            pltpu.VMEM(down, BF),
        ],
        6 * tokens * (width * width + 2 * math.prod(up)),
    )
    output, grad_sum, grad_conv = results[:3]
    return output, grad_sum, grad_conv, results[3 : 3 + blocks], results[3 + blocks : 3 + 2 * blocks], results[3 + 2 * blocks :]


def mix_back_kernel(rows, count, x_ref, halo_ref, values_ref, rim_ref, gconv_ref, kernt_ref, kern_ref, q_ref, keyconv_ref, attn_ref, depth_ref, wp_ref, wk_ref, gvec_ref, gbu_ref, unused, gq_ref, gdepth_ref, gvalues_ref, packed_ref, turned_ref, window, conv_window, summed, products, spread, wp_sum, wc_sum, values_sum, gwk_ref, gbias_ref, gtaps_ref, turn_wide, turn_thin, side, staged, sem):
    tile = pl.program_id(0)

    @pl.when(tile == 0)
    def start():
        fill_spread(spread)
        for ref in (values_sum, wp_sum, wc_sum, gwk_ref, gbias_ref, gtaps_ref, turn_wide, turn_thin):
            ref[...] = jnp.zeros_like(ref)

    fill_window(window, x_ref, halo_ref, tile, rows)
    fill_window(conv_window, values_ref, rim_ref, tile, rows)
    summed[...] = jnp.zeros_like(summed)
    grad_conv = gconv_ref[...].astype(F32)
    for tap in range(KSIZE):
        here = slice(tap * ATT, (tap + 1) * ATT)
        there = slice(12 + tap, 12 + tap + rows)
        products[:, here] = (grad_conv * conv_window[there, :]).astype(BF)
        summed[there, :] += mm(kern_ref[...], spread[:, here]) * grad_conv
    first = pl.multiple_of(tile * rows, rows)
    values_sum[pl.ds(first, rows + 32), :] += summed[...]
    turned = x_ref[pl.ds(first, rows), :].T
    turned_ref[...] = turned
    edges = [slice(0, 16), slice(rows + 16, rows + 32)]
    edge_x = jnp.concatenate([window[edge, :] for edge in edges], axis=0).astype(BF)
    edge_grads = jnp.concatenate([summed[edge, :] for edge in edges], axis=0).astype(BF)
    wc_sum[...] += mm(turned, summed[16 : 16 + rows, :].astype(BF)) + mm_tn(edge_x, edge_grads)
    grad_kernel = mm_nt(spread[...], products[...])
    slabs = [slice(8 * tap, 8 * tap + 8) for tap in range(KSIZE)]
    kernels = [kernt_ref[slab, :] for slab in slabs]
    mean = functools.reduce(jnp.add, [k * grad_kernel[slab] for k, slab in zip(kernels, slabs)])
    grad_logits = jnp.concatenate(
        [k * (grad_kernel[slab] - mean) for k, slab in zip(kernels, slabs)], axis=0
    ).astype(BF)
    wide_logits = grad_logits.astype(F32)
    gbias_ref[...] += jnp.concatenate(
        [
            jnp.broadcast_to(jnp.sum(wide_logits, axis=1, keepdims=True), (8 * KSIZE, 128)),
            jnp.zeros((8, 128), F32),
        ],
        axis=0,
    )
    gwk_ref[0 : 8 * KSIZE, :] += mm(grad_logits, attn_ref[...])
    grad_attn = mm_tn(grad_logits, wk_ref[...]).astype(BF).astype(F32)
    grad_keyconv = (grad_attn * q_ref[...].astype(F32)).astype(BF)
    gq_ref[...] = (grad_attn * keyconv_ref[...]).astype(BF)
    gwk_ref[8 * KSIZE : 8 * KSIZE + 1, :] += jnp.sum(grad_keyconv.astype(F32), axis=0, keepdims=True)
    wp_sum[...] += mm_tn(depth_ref[...], grad_keyconv)
    grad_depth = mm_nt(grad_keyconv, wp_ref[...]).astype(BF)
    gdepth_ref[...] = grad_depth
    wide = grad_depth.astype(F32)
    for at in range(0, window.shape[1], 128):
        some = slice(at, at + 128)
        for tap in range(KSIZE):
            gtaps_ref[tap : tap + 1, some] += jnp.sum(
                wide[:, some] * window[12 + tap : 12 + tap + rows, some], axis=0, keepdims=True
            )

    @pl.when(tile == pl.num_programs(0) - 1)
    def finish():
        gvalues_ref[...] = values_sum[...].astype(BF)
        tokens, block = x_ref.shape[0], lax.axis_index("blk")
        sums = [
            jnp.sum(gvalues_ref[at:end, :].astype(F32), axis=0, keepdims=True)
            for at, end in ((0, 16), (16, tokens + 16), (tokens + 16, tokens + 32))
        ]
        b_sum = sums[1] + jnp.where(block > 0, sums[0], 0.0) + jnp.where(block < count - 1, sums[2], 0.0)
        sharers, shard, width = staged.shape[0], staged.shape[1] // 2, staged.shape[2]
        part = ATT // sharers
        half = gbu_ref.shape[1] // sharers // 2
        turn_wide[0:6, :] = gvec_ref[0:6, :]
        turn_wide[TAPS_AT : TAPS_AT + KSIZE, :] = gtaps_ref[0:KSIZE, :]
        vectors = turn_wide[...].T
        for h in range(HEADS):
            for j in range(KSIZE):
                turn_wide[h * KSIZE + j : h * KSIZE + j + 1, 0:LANES] = gbias_ref[j * 8 + h : j * 8 + h + 1, :]
                turn_thin[h * KSIZE + j : h * KSIZE + j + 1, :] = gwk_ref[j * 8 + h : j * 8 + h + 1, :]
        bias = turn_wide[:, 0:LANES].T[0:1]
        turn_thin[THIN_AT : THIN_AT + 1, :] = gwk_ref[8 * KSIZE : 8 * KSIZE + 1, :]
        turn_thin[THIN_AT + 1 : THIN_AT + 2, :] = b_sum
        kernels = turn_thin[...].T
        side[...] = jnp.zeros_like(side)
        for owner in range(sharers):
            staged[owner, 0:shard, 0:ATT] = wp_sum[owner * shard : (owner + 1) * shard].astype(BF)
            staged[owner, shard:, 0:ATT] = wc_sum[owner * shard : (owner + 1) * shard].astype(BF)
            staged[owner, shard:, ATT:] = jnp.zeros((shard, width - ATT), BF)
            staged[owner, 0:shard, ATT : ATT + LANES] = vectors[owner * shard : (owner + 1) * shard].astype(BF)
            side[0:part, :] = kernels[owner * part : (owner + 1) * part]
            for place in range(2):
                first = (2 * owner + place) * half
                side[part + place : part + place + 1, 0:half] = gbu_ref[0:1, first : first + half]
            side[part + 2 : part + 3, :] = bias
            staged[owner, 0:shard, ATT + LANES : ATT + 2 * LANES] = side[...].astype(BF)
            staged[owner, 0:shard, ATT + 2 * LANES :] = jnp.zeros((shard, width - ATT - 2 * LANES), BF)
        copy = pltpu.make_async_copy(staged, packed_ref.at[:, 5 * shard : 7 * shard], sem)
        copy.start()
        copy.wait()


def mix_back(count, x, halo, values, rim, grad_conv, kernt, kern, query, keyconv, attn_key, depth, weight, w_kernel, g_vectors, gb_up, packed):
    tokens, width = x.shape
    sharers, shard = packed.shape[0], packed.shape[1] // 7
    away = pl.BlockSpec(memory_space=pl.ANY)
    rows = math.gcd(tokens, 512)
    by_rows = [(v, rows_of(rows, v.shape[1])) for v in (kern, query, keyconv, attn_key, depth)]
    return run_tiles(
        functools.partial(mix_back_kernel, rows, count),
        "mix_back",
        tokens // rows,
        [(v, all_of(v.shape)) for v in (x, halo, values, rim)]
        + [(grad_conv, rows_of(rows, ATT)), (kernt, columns_of(8 * KSIZE, rows))]
        + by_rows
        + [(weight, column_block(weight, 3))]
        + [(v, all_of(v.shape)) for v in (w_kernel, g_vectors, gb_up)]
        + [(packed, away)],
        [
            (shaped((tokens, ATT), BF), rows_of(rows, ATT)),
            (shaped((tokens, width), BF), rows_of(rows, width)),
            (shaped((tokens + 32, ATT), BF), all_of((tokens + 32, ATT))),
            (shaped(packed.shape, BF), away),
            (shaped((width, tokens), BF), columns_of(width, rows)),
        ],
        [
            pltpu.VMEM((rows + 32, width), F32),
            pltpu.VMEM((rows + 32, ATT), F32),
            pltpu.VMEM((rows + 32, ATT), F32),
            pltpu.VMEM((rows, KSIZE * ATT), BF),
            pltpu.VMEM((128, KSIZE * ATT), BF),
            pltpu.VMEM((width, ATT), F32),
            pltpu.VMEM((width, ATT), F32),
            pltpu.VMEM((tokens + 32, ATT), F32),
            pltpu.VMEM((8 * KSIZE + 8, ATT), F32),
            pltpu.VMEM((8 * KSIZE + 8, LANES), F32),
            pltpu.VMEM((16, width), F32),
            pltpu.VMEM((LANES, width), F32),
            pltpu.VMEM((LANES, ATT), F32),
            pltpu.VMEM((shard, LANES), F32),
            pltpu.VMEM((sharers, 2 * shard, width), BF),
            pltpu.SemaphoreType.DMA(()),
        ],
        4 * tokens * width * ATT * 4,
        {15: 3},
    )


MESH = pl.DeviceIdType.MESH
LINE = 4
LANES = 128
TAPS_AT = 16
THIN_AT = 64
BIAS_AT = 100


def my_place(sharers):
    columns = sharers // (2 * LINE)
    me = lax.axis_index("dp")
    return me, me // (2 * columns), lax.rem(me // 2, columns), lax.rem(me, 2), columns


def greet(partners):
    barrier = pltpu.get_barrier_semaphore()
    for partner in partners:
        pl.semaphore_signal(barrier, inc=1, device_id=partner, device_id_type=MESH)
    return barrier


def remote(source, target, send_sem, recv_sem, device):
    return pltpu.make_async_remote_copy(
        src_ref=source,
        dst_ref=target,
        send_sem=send_sem,
        recv_sem=recv_sem,
        device_id=device,
        device_id_type=MESH,
    )


def gather_kernel(sharers, count, part, early, *refs):
    w_refs, refs = refs[:3], refs[3:]
    vector_refs, refs = refs[:6], refs[6:]
    thin_refs, refs = refs[:4], refs[4:]
    (taps_ref, up_ref, kernel_ref, bias_ref, wu_ref, wn_ref, head_ref, tail_ref, early_ref), refs = refs[:9], refs[9:]
    (out_ref, wide_ref, thin_ref, thin_columns_ref, bias_up_ref, wk_ref, bk_ref, halo_ref, late_out, early_out), refs = refs[:10], refs[10:]
    rows, side, flat, thin_flat, edges, send_sem, recv_sem, edge_send, edge_recv = refs
    me, line, column, core, columns = my_place(sharers)
    block = lax.axis_index("blk")
    shard = out_ref.shape[1]
    base = len(w_refs) * ATT
    half = up_ref.shape[0] // 2

    def at(line, column, core):
        return (line * columns + column) * 2 + core

    lines = [lax.rem(line + step, LINE) for step in range(1, LINE)]
    sides = [lax.rem(column + step, columns) for step in range(1, columns)]
    partners = [{"dp": at(other, column, core)} for other in lines]
    across = [{"dp": at(line, other, core)} for other in sides]
    mate = {"dp": at(line, column, 1 - core)}
    ends = []
    if count > 1:
        ends = [{"blk": lax.rem(block + 1, count)}, {"blk": lax.rem(block + count - 1, count)}]
    barrier = greet(partners + across + [mate] + ends)
    for place, ref in enumerate(w_refs):
        out_ref[me, :, place * ATT : (place + 1) * ATT] = ref[...].astype(BF)
    rows[...] = jnp.zeros_like(rows)
    for place, ref in enumerate(vector_refs):
        rows[place : place + 1, 0:shard] = ref[...].reshape(1, shard)
    for place, ref in enumerate(thin_refs):
        rows[THIN_AT + place : THIN_AT + place + 1, 0:part] = ref[...].reshape(1, part)
    rows[TAPS_AT : TAPS_AT + KSIZE, 0:shard] = taps_ref[...]
    rows[BIAS_AT : BIAS_AT + 1, 0 : HEADS * KSIZE] = bias_ref[...].reshape(1, HEADS * KSIZE)
    rows[...] = rows[...].T
    side[...] = rows[0:shard]
    out_ref[me, :, base : base + LANES] = side[...].astype(BF)
    side[...] = jnp.zeros_like(side)
    side[0:part, 0 : HEADS * KSIZE] = kernel_ref[...]
    side[part : part + 1, 0:half] = up_ref[0:half].reshape(1, half)
    side[part + 1 : part + 2, 0:half] = up_ref[half:].reshape(1, half)
    out_ref[me, :, base + LANES :] = side[...].astype(BF)
    width = late_out.shape[1]
    for group in range(2):
        pair = [wu_ref[group, :, place * width : (place + 1) * width] for place in range(2)]
        late_out[group * shard : (group + 1) * shard] = jnp.concatenate(pair, axis=0).astype(BF)
        late_out[2 * shard :, group * ATT : (group + 1) * ATT] = wn_ref[group].astype(BF)
    if not early:
        early_out[...] = early_ref[...]
    pl.semaphore_wait(barrier, len(partners) + len(across) + 1 + len(ends))
    sends = []

    def sending(number, owner, device):
        return remote(out_ref.at[owner], out_ref.at[owner], send_sem.at[number], recv_sem.at[owner], device)

    def pass_on(owner, devices, when=None):
        for device in devices:
            sending(len(sends), owner, device).start()
            sends.append((owner, device, when))

    def arrived(owner):
        pltpu.make_async_copy(out_ref.at[owner], out_ref.at[owner], recv_sem.at[owner]).wait()

    pass_on(me, across + [mate])
    edge_copies = []
    for place, (ref, device) in enumerate(zip((tail_ref, head_ref), ends)):
        edge_copies.append(remote(ref, edges.at[place], edge_send.at[place], edge_recv.at[place], device))
    if early:
        edge_copies.append(remote(early_ref, early_out, edge_send.at[2], edge_recv.at[2], ends[0]))
    for copy in edge_copies:
        copy.start()
    for step in range(1, LINE):
        for way in (1, -1):
            from_here = (line - way * (step - 1) >= 0) & (line - way * (step - 1) < LINE)
            goes = from_here & (line + way >= 0) & (line + way < LINE)
            owner, onward = at(line - way * (step - 1), column, core), [{"dp": at(line + way, column, core)}]

            @pl.when(goes)
            def forward():
                pass_on(owner, onward, goes)

        for way in (1, -1):
            comes = (line - way * step >= 0) & (line - way * step < LINE)
            owner = at(line - way * step, column, core)

            @pl.when(comes)
            def take():
                arrived(owner)
                pass_on(owner, across + [mate], comes)

    for some in sides:
        for other in [line] + lines:
            owner = at(other, some, core)
            arrived(owner)
            pass_on(owner, [mate])
    nothing = jnp.zeros((16, halo_ref.shape[1]), BF)
    halo_ref[0:16, :] = nothing
    halo_ref[16:32, :] = nothing
    if count > 1:
        for copy in edge_copies:
            copy.wait()
        halo_ref[0:16, :] = jnp.where(block > 0, edges[0], nothing)
        halo_ref[16:32, :] = jnp.where(block < count - 1, edges[1], nothing)
    for j in range(KSIZE):
        for h in range(8):
            source = h * KSIZE + j if h < HEADS else 120
            bk_ref[j * 8 + h : j * 8 + h + 1, :] = rows[source : source + 1, :]
    for some in [column] + sides:
        for other in [line] + lines:
            arrived(at(other, some, 1 - core))
    for number, (owner, device, when) in enumerate(sends):
        if when is None:
            sending(number, owner, device).wait_send()
        else:
            pl.when(when)(lambda: sending(number, owner, device).wait_send())
    for owner in range(sharers):
        cells = out_ref[owner, :, base : base + LANES].astype(F32)
        flat[owner * shard : (owner + 1) * shard, :] = cells
        thin_flat[owner * part : (owner + 1) * part, :] = cells[0:part]
    turned = flat[...].T
    wide_ref[...] = turned[0 : wide_ref.shape[0]]
    thin_columns_ref[...] = thin_flat[...]
    thin_ref[...] = thin_flat[...].T[THIN_AT : THIN_AT + 8]
    for owner in range(sharers):
        cells = out_ref[owner, :, base + LANES :].astype(F32)
        thin_flat[owner * part : (owner + 1) * part, :] = cells[0:part]
        for place in range(2):
            first = (2 * owner + place) * half
            bias_up_ref[0:1, first : first + half] = cells[part + place : part + place + 1, 0:half]
    turned = thin_flat[...].T
    slabs = []
    for j in range(KSIZE):
        slabs += [turned[h * KSIZE + j : h * KSIZE + j + 1] for h in range(HEADS)]
        slabs.append(jnp.zeros((8 - HEADS, ATT), F32))
    wk_ref[...] = jnp.concatenate(slabs, axis=0).astype(BF)


def gather_columns(weights, vectors, thin, taps, b_up, w_kernel, kernel_bias, w_up, w_down, x, sharers, count):
    shard, part = weights[0].shape[0], thin[0].shape[0]
    tokens, width = x.shape
    early = count == 2
    first_rows = math.gcd(tokens, 512) if early else 16
    wide = len(weights) * ATT + 2 * LANES
    columns = sharers // (2 * LINE)
    copies = columns + 2 * (LINE - 1) * (1 + columns) + LINE * (columns - 1)
    args = list(weights) + list(vectors) + list(thin) + [taps, b_up, w_kernel, kernel_bias, w_up, w_down]
    shapes = [
        shaped((sharers, shard, wide), BF),
        shaped((32, width), F32),
        shaped((8, ATT), F32),
        shaped((ATT, LANES), F32),
        shaped((1, sharers * b_up.shape[0]), F32),
        shaped((8 * KSIZE, ATT), BF),
        shaped((8 * KSIZE, LANES), F32),
        shaped((32, width), BF),
        shaped((4 * shard, width), BF),
        shaped((first_rows, width), BF),
    ]
    out, *rest = pl.pallas_call(
        functools.partial(gather_kernel, sharers, count, part, early),
        grid=(1,),
        in_specs=[all_of(v.shape) for v in args]
        + [
            pl.BlockSpec((16, width), lambda i: (0, 0)),
            pl.BlockSpec((16, width), lambda i: (tokens // 16 - 1, 0)),
            pl.BlockSpec((first_rows, width), lambda i: (0, 0)),
        ],
        out_specs=[all_of(v.shape) for v in shapes],
        out_shape=shapes,
        scratch_shapes=[
            pltpu.VMEM((LANES, LANES), F32),
            pltpu.VMEM((shard, LANES), F32),
            pltpu.VMEM((width, LANES), F32),
            pltpu.VMEM((ATT, LANES), F32),
            pltpu.VMEM((2, 16, width), BF),
            pltpu.SemaphoreType.DMA((copies,)),
            pltpu.SemaphoreType.DMA((sharers,)),
            pltpu.SemaphoreType.DMA((3,)),
            pltpu.SemaphoreType.DMA((3,)),
        ],
        compiler_params=pltpu.CompilerParams(
            collective_id=0, has_side_effects=True, vmem_limit_bytes=60 * MIB
        ),
        name="gather_columns",
    )(*args, x, x, x)
    return (out.reshape(sharers * shard, wide), *rest)


class Shares:
    def __init__(self, sharers, rows, widths, line_first, count):
        self.sharers, self.rows, self.widths, self.line_first, self.count = sharers, rows, widths, line_first, count
        self.columns = sharers // (2 * LINE)
        self.chips = sharers // 2
        ends = [sum(widths[: at + 1]) for at in range(len(widths))]
        self.lanes = [slice(end - width, end) for end, width in zip(ends, widths)]
        self.wide = ends[-1]
        self.copies = 1 + self.columns - 1 + LINE - 1 + count - 1

    def scratch(self):
        shapes = []
        for width, line_first in zip(self.widths, self.line_first):
            side = (self.columns - 1, 1 if line_first else LINE, self.rows, width)
            line = (LINE - 1, self.columns if line_first else 1, self.rows, width)
            shapes += [pltpu.VMEM((self.chips, self.rows, width), BF)] * 2
            shapes += [pltpu.VMEM(side, BF)] * 2 + [pltpu.VMEM(line, BF)] * 2
            shapes += [pltpu.VMEM((self.rows, width), BF), pltpu.VMEM((self.count, self.rows, width), BF)]
        sems = len(self.widths) * self.copies
        return shapes + [
            pltpu.VMEM((self.sharers, self.rows, self.wide), F32),
            pltpu.SemaphoreType.DMA((sems,)),
            pltpu.SemaphoreType.DMA((sems,)),
        ]

    def bind(self, refs):
        chains = len(self.widths)
        self.buffers = [refs[8 * chain : 8 * chain + 8] for chain in range(chains)]
        self.total, self.send_sem, self.recv_sem = refs[8 * chains : 8 * chains + 3]
        self.me, self.line, self.column, self.core, unused = my_place(self.sharers)
        self.block = lax.axis_index("blk")
        self.others_line = [lax.rem(self.line + step, LINE) for step in range(1, LINE)]
        self.others_side = [lax.rem(self.column + step, self.columns) for step in range(1, self.columns)]
        self.others_block = [lax.rem(self.block + step, self.count) for step in range(1, self.count)]

    def at(self, line, column, core):
        return (line * self.columns + column) * 2 + core

    def greet(self):
        devices = [{"dp": self.at(self.line, self.column, 1 - self.core)}]
        devices += [{"dp": self.at(self.line, other, self.core)} for other in self.others_side]
        devices += [{"dp": self.at(other, self.column, self.core)} for other in self.others_line]
        devices += [{"blk": other} for other in self.others_block]
        greet(devices)

    def met(self):
        pl.semaphore_wait(pltpu.get_barrier_semaphore(), 1 + self.columns - 1 + LINE - 1 + self.count - 1)

    def copy(self, chain, number, source, target, device):
        sem = chain * self.copies + number
        return remote(source, target, self.send_sem.at[sem], self.recv_sem.at[sem], device)

    def part(self, owner, chain):
        return self.total[owner, :, self.lanes[chain]]

    def add(self, owner, chain, values):
        self.total[owner, :, self.lanes[chain]] += values.astype(F32)

    def mate_copy(self, chain):
        mate = {"dp": self.at(self.line, self.column, 1 - self.core)}
        return self.copy(chain, 0, self.buffers[chain][0], self.buffers[chain][1], mate)

    def mate_start(self, chain):
        for chip in range(self.chips):
            self.buffers[chain][0][chip] = self.part(2 * chip + 1 - self.core, chain).astype(BF)
        self.mate_copy(chain).start()

    def mate_end(self, chain):
        self.mate_copy(chain).wait()
        for chip in range(self.chips):
            self.add(2 * chip + self.core, chain, self.buffers[chain][1][chip])

    def side_copies(self, chain):
        source, target = self.buffers[chain][2:4]
        return [
            self.copy(chain, 1 + step, source.at[step], target.at[step], {"dp": self.at(self.line, other, self.core)})
            for step, other in enumerate(self.others_side)
        ]

    def side_lines(self, chain):
        return [self.line] if self.line_first[chain] else range(LINE)

    def side_start(self, chain):
        for step, other in enumerate(self.others_side):
            for place, line in enumerate(self.side_lines(chain)):
                self.buffers[chain][2][step, place] = self.part(self.at(line, other, self.core), chain).astype(BF)
        for copy in self.side_copies(chain):
            copy.start()

    def side_end(self, chain):
        for step, copy in enumerate(self.side_copies(chain)):
            copy.wait()
            for place, line in enumerate(self.side_lines(chain)):
                self.add(self.at(line, self.column, self.core), chain, self.buffers[chain][3][step, place])

    def line_copies(self, chain):
        source, target = self.buffers[chain][4:6]
        return [
            self.copy(chain, self.columns + step, source.at[step], target.at[step], {"dp": self.at(other, self.column, self.core)})
            for step, other in enumerate(self.others_line)
        ]

    def line_columns(self, chain):
        return range(self.columns) if self.line_first[chain] else [self.column]

    def line_start(self, chain):
        for step, other in enumerate(self.others_line):
            for place, column in enumerate(self.line_columns(chain)):
                self.buffers[chain][4][step, place] = self.part(self.at(other, column, self.core), chain).astype(BF)
        for copy in self.line_copies(chain):
            copy.start()

    def line_end(self, chain):
        for step, copy in enumerate(self.line_copies(chain)):
            copy.wait()
            for place, column in enumerate(self.line_columns(chain)):
                self.add(self.at(self.line, column, self.core), chain, self.buffers[chain][5][step, place])

    def block_copies(self, chain):
        source, target = self.buffers[chain][6:8]
        return [
            self.copy(chain, self.columns + LINE - 1 + step, source, target.at[self.block], {"blk": other})
            for step, other in enumerate(self.others_block)
        ]

    def block_start(self, chain):
        own = self.part(self.me, chain).astype(BF)
        self.buffers[chain][6][...] = own
        self.buffers[chain][7][self.block] = own
        for copy in self.block_copies(chain):
            copy.start()

    def block_end(self, chain):
        for copy in self.block_copies(chain):
            copy.wait()
        parts = [self.buffers[chain][7][at].astype(F32) for at in range(self.count)]
        return functools.reduce(jnp.add, parts)


def finish_kernel(blocks, rows, tiles, shares, *refs):
    dq_refs, refs = refs[:blocks], refs[blocks:]
    dkv_refs, refs = refs[:blocks], refs[blocks:]
    (x_ref, gq_ref, gvalues_ref, gdepth_ref, w_ref, wc_ref, mine_ref, wide_ref, sum_ref), refs = refs[:9], refs[9:]
    (gh_ref, flat_out, sums_out), refs = refs[:3], refs[3:]
    held, refs = refs[: 2 * blocks + 5], refs[2 * blocks + 5 :]
    dq, dkv = held[:blocks], held[blocks : 2 * blocks]
    dk, dv = [ref.at[0] for ref in dkv], [ref.at[1] for ref in dkv]
    turned, gq, gvalues, gdepth, w = held[2 * blocks :]
    (load_sem, grads, window, bias_sum, rim_in, halo_in, halo, given, edge_send, edge_recv, given_send, given_recv), refs = refs[:12], refs[12:]
    shares.bind(refs)
    step = pl.program_id(0)
    count, sharers, shard = shares.count, shares.sharers, shares.rows
    chains = 3
    width, tokens = turned.shape
    block = shares.block
    sources = [x_ref, gq_ref] + list(dq_refs) + [ref.at[1] for ref in dkv_refs] + [ref.at[0] for ref in dkv_refs]
    targets = [turned, gq] + list(dq) + list(dv) + list(dk)
    sources += [gvalues_ref, gdepth_ref, w_ref.at[:, 0 : 3 * ATT], wc_ref.at[:, 2 * ATT : 3 * ATT]]
    targets += [gvalues, gdepth, w.at[:, 0 : 3 * ATT], w.at[:, 3 * ATT :]]
    loads = [
        pltpu.make_async_copy(source, target, load_sem.at[at])
        for at, (source, target) in enumerate(zip(sources, targets))
    ]
    by_chain = [loads[: 2 + blocks], loads[2 + blocks : 2 + 2 * blocks], loads[2 + 2 * blocks : 2 + 3 * blocks]]
    others = loads[2 + 3 * blocks :]

    def edge_copies():
        if count == 1:
            return []
        after, before = {"blk": lax.rem(block + 1, count)}, {"blk": lax.rem(block + count - 1, count)}
        plan = [
            (gvalues.at[tokens + 16 : tokens + 32], rim_in.at[0], after),
            (gvalues.at[0:16], rim_in.at[1], before),
            (gdepth.at[tokens - 16 : tokens], halo_in.at[0], after),
            (gdepth.at[0:16], halo_in.at[1], before),
        ]
        return [
            remote(source, target, edge_send.at[at], edge_recv.at[at], device)
            for at, (source, target, device) in enumerate(plan)
        ]

    def given_copies():
        return [
            remote(mine_ref, given.at[block], given_send.at[at], given_recv.at[at], {"blk": other})
            for at, other in enumerate(shares.others_block)
        ]

    @pl.when(step == 0)
    def start():
        shares.greet()
        for load in loads:
            load.start()
        bias_sum[...] = jnp.zeros_like(bias_sum)
        given[block] = mine_ref[...]

    def total(some):
        whole = [ref[...].astype(F32) for ref in some if ref.shape[0] == ATT]
        halves = [ref[...].astype(F32) for ref in some if ref.shape[0] < ATT]
        whole += [jnp.concatenate(halves[at : at + 2], axis=0) for at in range(0, len(halves), 2)]
        return functools.reduce(jnp.add, whole)

    def weights(chain):
        for load in by_chain[chain]:
            load.wait()
        if chain == 0:
            every = (total(dq).T + gq[...].astype(F32)).astype(BF)
        else:
            every = total((dv, dk)[chain - 1]).astype(BF).T
        place = (0, 2, 1)[chain]
        grads[:, place * ATT : (place + 1) * ATT] = every
        if chain < 2:
            bias_sum[0:1, chain * ATT : (chain + 1) * ATT] = jnp.sum(every.astype(F32), axis=0, keepdims=True)
        made = mm(turned[...], every)
        lanes = slice(shares.lanes[chain].start, shares.lanes[chain].start + ATT)
        for owner in range(sharers):
            shares.total[owner, :, lanes] = made[owner * shard : (owner + 1) * shard]
        if chain == 1:
            extra = slice(2 * ATT, 2 * ATT + LANES)
            shares.total[:, :, extra] = jnp.zeros((sharers, shard, LANES), F32)
            for at in range(2 * ATT // LANES):
                values = bias_sum[0:1, at * LANES : (at + 1) * LANES]
                for owner in range(sharers):
                    shares.total[owner, at : at + 1, extra] = values

    def conv_grads():
        for load in others[2:]:
            load.wait()
        for copy in edge_copies():
            copy.wait()
        zero = jnp.zeros((16, ATT), F32)
        before, after = zero, zero
        if count > 1:
            before = jnp.where(block > 0, rim_in[0].astype(F32), zero)
            after = jnp.where(block < count - 1, rim_in[1].astype(F32), zero)
            nothing = jnp.zeros((16, width), BF)
            halo[0:16, :] = jnp.where(block > 0, halo_in[0], nothing)
            halo[16:32, :] = jnp.where(block < count - 1, halo_in[1], nothing)
        else:
            halo[...] = jnp.zeros_like(halo)
        lanes = slice(3 * ATT, 4 * ATT)
        grads[16 : tokens - 16, lanes] = gvalues[32:tokens, :]
        grads[0:16, lanes] = (gvalues[16:32, :].astype(F32) + before).astype(BF)
        grads[tokens - 16 : tokens, lanes] = (gvalues[tokens : tokens + 16, :].astype(F32) + after).astype(BF)

    for chain in range(chains):
        @pl.when(step == chain)
        def one(chain=chain):
            weights(chain)
            if chain == chains - 1:
                conv_grads()

    @pl.when(step >= chains)
    def by_tile():
        tile = step - chains
        first = pl.multiple_of(tile * rows, rows)
        fill_rows(window, gdepth, halo, tile, tiles, rows)
        back = mm_nt(grads[pl.ds(first, rows), :], w[...])
        for at in range(0, width, 128):
            some = slice(at, at + 128)
            depth = back[:, some] + sum_ref[:, some]
            for tap in range(KSIZE):
                depth = depth + window[20 - tap : 20 - tap + rows, some] * wide_ref[TAPS_AT + tap : TAPS_AT + tap + 1, some]
            gh_ref[:, some] = depth.astype(BF)

    def first_sends(unused):
        shares.met()
        for load in others[:2]:
            load.wait()
        for copy in edge_copies() + given_copies():
            copy.start()

    def late(eighths):
        return chains + eighths * tiles // 8

    plan = [
        (0, [(first_sends, 0), (shares.mate_start, 0)]),
        (1, [(shares.mate_end, 0), (shares.side_start, 0), (shares.mate_start, 1)]),
        (2, [(shares.mate_end, 1), (shares.side_start, 1), (shares.side_end, 0), (shares.line_start, 0), (shares.mate_start, 2)]),
        (late(0), [(shares.mate_end, 2), (shares.side_start, 2)]),
        (late(1), [(shares.side_end, 1), (shares.line_start, 1)]),
        (late(2), [(shares.line_end, 0), (shares.block_start, 0)]),
        (late(3), [(shares.side_end, 2), (shares.line_start, 2)]),
        (late(5), [(shares.line_end, 1), (shares.block_start, 1)]),
        (late(6), [(shares.line_end, 2), (shares.block_start, 2)]),
    ]
    for when in range(chains + tiles):
        actions = [action for place, some in plan if place == when for action in some]
        if actions:

            @pl.when(step == when)
            def act(actions=actions):
                for action, chain in actions:
                    action(chain)

    @pl.when(step == chains + tiles - 1)
    def end():
        for copy in given_copies():
            copy.wait()
        flat_out[...] = functools.reduce(jnp.add, [given[at].astype(F32) for at in range(count)])
        for chain in range(chains):
            sums_out[:, shares.lanes[chain]] = shares.block_end(chain)


def unpack_kernel(part, gh_ref, flat, sums, gh_out, gq_out, gk_out, gv_out, gc_out, gwd_out, gwu_out, gwn_out, gwp_out, gwk_out, gtaps_out, gkb_out, gbup_out, *refs):
    vector_outs, thin_outs = refs[:6], refs[6:10]
    shard = sums.shape[0]
    width = flat.shape[1]
    gh_out[...] = gh_ref[...]

    @pl.when(pl.program_id(0) == 0)
    def small():
        gwd_out[...] = flat[0:shard]
        quarter = shard // 2
        for group in range(2):
            for place in range(2):
                first = shard * (1 + group) + quarter * place
                gwu_out[group, :, place * width : (place + 1) * width] = flat[first : first + quarter]
            gwn_out[group] = flat[3 * shard : 5 * shard, group * ATT : (group + 1) * ATT]
        gwp_out[...] = flat[5 * shard : 6 * shard, 0:ATT]
        cells = flat[5 * shard : 6 * shard, ATT : ATT + LANES]
        turned = jnp.concatenate([cells, jnp.zeros((LANES - shard, LANES), F32)], axis=0).T
        for at, ref in enumerate(vector_outs):
            ref[...] = turned[at : at + 1, 0:shard].reshape(shard)
        gtaps_out[...] = turned[TAPS_AT : TAPS_AT + KSIZE, 0:shard]
        cells = flat[5 * shard : 6 * shard, ATT + LANES : ATT + 2 * LANES]
        gwk_out[...] = cells[0:part, 0 : HEADS * KSIZE]
        half = gbup_out.shape[0] // 2
        gbup_out[...] = jnp.concatenate(
            [cells[part : part + 1, 0:half], cells[part + 1 : part + 2, 0:half]], axis=1
        ).reshape(2 * half)
        gkb_out[...] = cells[part + 2 : part + 3, 0 : HEADS * KSIZE].reshape(HEADS * KSIZE)
        turned = jnp.concatenate([cells, jnp.zeros((LANES - shard, LANES), F32)], axis=0).T
        thin_outs[2][...] = turned[THIN_AT : THIN_AT + 1, 0:part].reshape(part)
        gq_out[...] = sums[:, 0:ATT]
        gv_out[...] = sums[:, ATT : 2 * ATT]
        gk_out[...] = sums[:, 2 * ATT + LANES :]
        gc_out[...] = flat[6 * shard : 7 * shard, 0:ATT]
        totals = jnp.concatenate(
            [sums[at : at + 1, 2 * ATT : 2 * ATT + LANES] for at in range(2 * ATT // LANES)], axis=1
        )
        lane = lax.broadcasted_iota(jnp.int32, (part, ATT), 1)
        row = lax.broadcasted_iota(jnp.int32, (part, ATT), 0)
        mine = (lane == lax.axis_index("dp") * part + row).astype(F32)
        thin_outs[3][...] = turned[THIN_AT + 1 : THIN_AT + 2, 0:part].reshape(part)
        for chain, ref in ((0, thin_outs[0]), (1, thin_outs[1])):
            picked = jnp.sum(mine * totals[:, chain * ATT : (chain + 1) * ATT], axis=1, keepdims=True)
            picked = jnp.broadcast_to(picked, (part, LANES))
            picked = jnp.concatenate([picked, jnp.zeros((LANES - part, LANES), F32)], axis=0).T
            ref[...] = picked[0:1, 0:part].reshape(part)


def unpack(grad_hidden, flat, sums, part, n_up):
    shard, width = sums.shape[0], flat.shape[1]
    shapes = [shaped((shard, ATT), F32)] * 4 + [
        shaped((shard, width), F32),
        shaped((2, shard // 2, 2 * width), F32),
        shaped((2, 2 * shard, ATT), F32),
        shaped((shard, ATT), F32),
        shaped((part, HEADS * KSIZE), F32),
        shaped((KSIZE, shard), F32),
        shaped((HEADS * KSIZE,), F32),
        shaped((n_up,), F32),
    ]
    shapes += [shaped((shard,), F32)] * 6 + [shaped((part,), F32)] * 4
    tokens = grad_hidden.shape[0]
    rows = math.gcd(tokens, 512)
    return pl.pallas_call(
        functools.partial(unpack_kernel, part),
        grid=(tokens // rows,),
        in_specs=[rows_of(rows, width), all_of(flat.shape), all_of(sums.shape)],
        out_specs=[rows_of(rows, width)] + [all_of(v.shape) for v in shapes],
        out_shape=[shaped(grad_hidden.shape, BF)] + shapes,
        compiler_params=pltpu.CompilerParams(vmem_limit_bytes=60 * MIB),
        name="unpack",
    )(grad_hidden, flat, sums)


def finish(dqs, dkvs, turned, grad_query, grad_values, grad_depth, weight, mixed, mine, wide_vectors, grad_sum, sharers, count):
    width, tokens = turned.shape
    rows = math.gcd(tokens, 256)
    tiles = tokens // rows
    blocks = len(dqs)
    chains = 3
    shard = width // sharers
    shares = Shares(sharers, shard, [ATT, ATT + LANES, ATT], [False, False, False], count)
    late_rows = pl.BlockSpec((rows, width), lambda i: (jnp.maximum(i - chains, 0), 0))
    away = pl.BlockSpec(memory_space=pl.ANY)
    loaded = list(dqs) + list(dkvs) + [turned, grad_query, grad_values, grad_depth]
    args = loaded + [weight, mixed, mine, wide_vectors, grad_sum]
    shapes = [shaped(mine.shape, F32), shaped((shard, chains * ATT + LANES), F32)]
    return pl.pallas_call(
        functools.partial(finish_kernel, blocks, rows, tiles, shares),
        grid=(chains + tiles,),
        in_specs=[away] * (len(loaded) + 2) + [all_of(mine.shape), all_of(wide_vectors.shape), late_rows],
        out_specs=[late_rows] + [all_of(v.shape) for v in shapes],
        out_shape=[shaped((tokens, width), BF)] + shapes,
        scratch_shapes=[pltpu.VMEM(v.shape, v.dtype) for v in loaded]
        + [
            pltpu.VMEM((width, 4 * ATT), BF),
            pltpu.SemaphoreType.DMA((len(loaded) + len(dkvs) + 2,)),
            pltpu.VMEM((tokens, 4 * ATT), BF),
            pltpu.VMEM((rows + 32, width), F32),
            pltpu.VMEM((8, 2 * ATT), F32),
            pltpu.VMEM((2, 16, ATT), BF),
            pltpu.VMEM((2, 16, width), BF),
            pltpu.VMEM((32, width), BF),
            pltpu.VMEM((count,) + mine.shape, BF),
            pltpu.SemaphoreType.DMA((4,)),
            pltpu.SemaphoreType.DMA((4,)),
            pltpu.SemaphoreType.DMA((max(count - 1, 1),)),
            pltpu.SemaphoreType.DMA((max(count - 1, 1),)),
        ]
        + shares.scratch(),
        compiler_params=pltpu.CompilerParams(
            collective_id=1, has_side_effects=True, vmem_limit_bytes=60 * MIB
        ),
        cost_estimate=pl.CostEstimate(
            flops=4 * tokens * width * chains * ATT, bytes_accessed=30 * tokens * width, transcendentals=0
        ),
        name="finish",
    )(*args)


def shifted_from(value, axis, step):
    count = lax.axis_size(axis)
    return lax.ppermute(value, axis, [((i + step) % count, i) for i in range(count)])


def local(
    hidden,
    separators,
    out_grad,
    w_query,
    b_query,
    w_key,
    w_value,
    b_value,
    depth_kernel,
    w_point,
    b_keyconv,
    w_kernel,
    kernel_bias,
    w_convout,
    b_convout,
    w_dense,
    b_dense,
    gain_attn,
    shift_attn,
    w_up,
    b_up,
    w_down,
    b_down,
    gain_out,
    shift_out,
):
    count = lax.axis_size("blk")
    sharers = lax.axis_size("dp")
    x, cotangent = hidden[0], out_grad[0]
    tokens, width = x.shape
    part = b_query.shape[0]

    known = math.gcd(tokens, 512) if count == 2 else 0
    others = [shifted_from(x[known:], "blk", step) for step in range(1, count)]
    weight, wide_vectors, thin, thin_columns, bias_up, wt_kernel, bias_kernel, halo, late, early = gather_columns(
        [w_query, w_key, w_value],
        [b_dense, gain_attn, shift_attn, b_down, gain_out, shift_out],
        [b_query, b_value, b_keyconv, b_convout],
        depth_kernel.T,
        b_up,
        w_kernel,
        kernel_bias,
        w_up,
        w_down,
        x,
        sharers,
        count,
    )
    mixed = jnp.concatenate([w_dense, w_convout, w_point], axis=1).astype(BF)
    mixed = lax.all_gather(mixed, "dp", axis=0, tiled=True)
    late = lax.all_gather(late, "dp", axis=0, tiled=False)

    query, query_t, *own = project([x], weight, thin, thin_columns, 3)
    keys = [own]
    outs, probs = [], []
    for step in range(count):
        if step > 0:
            keys.append(project(([early] if known else []) + [others[step - 1]], weight, thin, thin_columns, 2))
        key, key_t, value, value_t, norms = keys[step]
        out, prob = attend(separators, query_t, key, value_t, norms, count, step)
        outs.append(out)
        probs.append(prob)
        if step == 0:
            depth, keyconv, attn_key, kernt, kern, conv, values, rim = mix(
                count, x, halo, query, mixed, wide_vectors, thin, wt_kernel, bias_kernel
            )
            others, depth = lax.optimization_barrier((others, depth))
    output, grad_sum, grad_conv, grads_t, sides, (packed, g_vectors, gb_up) = middle(
        outs, conv, x, cotangent, mixed, late, wide_vectors, bias_up
    )
    grad_query_conv, grad_depth, grad_values, packed, turned = mix_back(
        count, x, halo, values, rim, grad_conv, kernt, kern, query, keyconv, attn_key, depth, mixed, wt_kernel, g_vectors, gb_up, packed
    )
    packed, sides = lax.optimization_barrier((packed, sides))
    mine = lax.psum_scatter(packed, "dp", scatter_dimension=0, tiled=False)

    dqs, dkvs = [], []
    for step in list(range(1, count)) + [0]:
        key, key_t, value, value_t, norms = keys[step]
        some = HEADS // 2 if step else HEADS
        for at in range(0, HEADS, some):
            dq, dkv = attend_back(probs[step], value, key_t, grads_t[step], sides[step], query_t, at, some)
            dqs.append(dq)
            dkvs.append(shifted_from(dkv, "blk", count - step) if step else dkv)
    grad_hidden, flat, sums = finish(
        dqs, dkvs, turned, grad_query_conv, grad_values, grad_depth, weight, mixed, mine, wide_vectors, grad_sum, sharers, count
    )
    results = unpack(grad_hidden, flat, sums, part, b_up.shape[0])
    grad_hidden, gw_query, gw_key, gw_value, gw_convout, gw_dense, gw_up, gw_down, gw_point, gw_kernel, g_taps, g_bias, gb_up = results[:13]
    g_vectors, thin = results[13:19], results[19:]
    return (
        output[None],
        grad_hidden[None],
        gw_query,
        thin[0],
        gw_key,
        gw_value,
        thin[1],
        g_taps.T,
        gw_point,
        thin[2],
        gw_kernel,
        g_bias,
        gw_convout,
        thin[3],
        gw_dense,
        g_vectors[0],
        g_vectors[1],
        g_vectors[2],
        gw_up,
        gb_up,
        gw_down,
        g_vectors[3],
        g_vectors[4],
        g_vectors[5],
    )


def solution(mesh):
    placed = (
        P("dp", "blk", None),
        P("dp"),
        P("dp", "blk", None),
        P("dp", None),
        P("dp"),
        P("dp", None),
        P("dp", None),
        P("dp"),
        P("dp", None),
        P("dp", None),
        P("dp"),
        P("dp", None),
        P(),
        P("dp", None),
        P("dp"),
        P("dp", None),
        P("dp"),
        P("dp"),
        P("dp"),
        P(None, "dp", None),
        P("dp"),
        P(None, "dp", None),
        P("dp"),
        P("dp"),
        P("dp"),
    )
    return jax.shard_map(
        local,
        mesh=mesh,
        in_specs=placed,
        out_specs=(
            P("dp", "blk", None),
            P("dp", "blk", None),
            P("dp", None),
            P("dp"),
            P("dp", None),
            P("dp", None),
            P("dp"),
            P("dp", None),
            P("dp", None),
            P("dp"),
            P("dp", None),
            P(),
            P("dp", None),
            P("dp"),
            P("dp", None),
            P("dp"),
            P("dp"),
            P("dp"),
            P(None, "dp", None),
            P("dp"),
            P(None, "dp", None),
            P("dp"),
            P("dp"),
            P("dp"),
        ),
        check_vma=False,
    )
```

```python
import functools, math
import jax, jax.numpy as jnp
from jax import lax
from jax.experimental import pallas as pl
from jax.experimental.pallas import tpu as pltpu
from jax.sharding import PartitionSpec as P

HEADS = 6
HD = 64
KSIZE = 9
REACH = 4
ATT = 384
EPS = 1e-12
BF = jnp.bfloat16
F32 = jnp.float32
MIB = 2**20
EXCLUDED = 2.0**100
SAFE_SCORE = 50.0


def mm(left, right):
    return jnp.dot(left, right, preferred_element_type=F32)


def mm_nt(left, right):
    return lax.dot_general(left, right, (((1,), (1,)), ((), ())), preferred_element_type=F32)


def mm_tn(left, right):
    return lax.dot_general(left, right, (((0,), (0,)), ((), ())), preferred_element_type=F32)


def in_lanes(rows, columns):
    lane = lax.broadcasted_iota(jnp.int32, (rows, 128), 1)
    out = jnp.zeros((rows, 128), F32)
    for at, column in enumerate(columns):
        out = jnp.where(lane == at, column, out)
    return out.astype(BF)


def in_rows(columns, rows):
    row = lax.broadcasted_iota(jnp.int32, (16, columns), 0)
    out = jnp.zeros((16, columns), F32)
    for at, values in enumerate(rows):
        out = jnp.where(row == at, values, out)
    return out.astype(BF)


def three_parts(values):
    high = values.astype(BF).astype(F32)
    rest = values - high
    middle = rest.astype(BF).astype(F32)
    return high, middle, (rest - middle).astype(BF).astype(F32)


def put_head(ref, head, values):
    odd = lax.rem(head, 2) == 1
    none = jnp.zeros_like(values)
    ref[0:HD, :] = jnp.where(odd, none, values)
    ref[HD : 2 * HD, :] = jnp.where(odd, values, none)


def attend_kernel(keys, queries, chunk, count, step, at_ref, q_ref, k_ref, v_ref, norm_ref, o_ref, p_ref, key_side, query_side):
    head, tile = pl.program_id(0), pl.program_id(1)
    separator, block = at_ref[0], lax.axis_index("blk")
    first_query = block * keys
    first_key = lax.rem(block + step, count) * keys

    @pl.when((head == 0) & (tile == 0))
    def start():
        position = first_key + lax.broadcasted_iota(jnp.int32, (keys, 128), 0)
        late = (position >= separator).astype(F32)
        key_side[...] = in_lanes(keys, [1.0 - late, late, 1.0, 1.0, 1.0])
        query_side[2 * HD + 16 :, :] = jnp.zeros((2 * HD - 16, queries), BF)

    put_head(query_side, head, q_ref[...])
    position = first_query + tile * queries + lax.broadcasted_iota(jnp.int32, (16, queries), 1)
    late = (position >= separator).astype(F32)
    excluded = [-EXCLUDED * late, -EXCLUDED * (1.0 - late)]
    query_side[2 * HD : 2 * HD + 16, :] = in_rows(queries, excluded)
    o_ref[0, HD + 8 : HD + 16, :] = jnp.zeros((8, queries), F32)
    wide = q_ref[...].astype(F32)
    largest = jnp.max(jnp.sum(wide * wide, axis=0, keepdims=True)) * jnp.max(norm_ref[...])

    def scores(at):
        part = slice(at * chunk, (at + 1) * chunk)
        return mm(
            jnp.concatenate([k_ref[part, :], key_side[part, :]], axis=1), query_side[...]
        )

    @pl.when(jnp.logical_not(largest <= SAFE_SCORE * SAFE_SCORE))
    def shifted():
        best = jnp.full((1, queries), -4.0 * EXCLUDED, F32)
        for at in range(keys // chunk):
            best = jnp.maximum(best, jnp.max(scores(at), axis=0, keepdims=True))
        parts = three_parts(jnp.where(best < -0.5 * EXCLUDED, 0.0, best))
        query_side[2 * HD : 2 * HD + 16, :] = in_rows(queries, excluded + [-part for part in parts])
        o_ref[0, HD + 8 : HD + 16, :] = jnp.broadcast_to(
            jnp.where(best < -0.5 * EXCLUDED, best, parts[0] + parts[1] + parts[2]), (8, queries)
        )

    ones = in_rows(chunk, [1.0])
    total = jnp.zeros((HD + 16, queries), F32)
    for at in range(keys // chunk):
        part = slice(at * chunk, (at + 1) * chunk)
        probs = jnp.exp(scores(at)).astype(BF)
        p_ref[0, part, :] = probs
        total = total + mm(jnp.concatenate([v_ref[:, part], ones], axis=0), probs)
    o_ref[0, 0 : HD + 8, :] = total[0 : HD + 8, :]


def attend(at, query_t, key, value_t, norms, count, step):
    tokens, keys = query_t.shape[1], key.shape[0]
    queries, chunk = math.gcd(tokens, 2048), math.gcd(keys, 1024)
    return pl.pallas_call(
        functools.partial(attend_kernel, keys, queries, chunk, count, step),
        grid=(HEADS, tokens // queries),
        in_specs=[
            pl.BlockSpec(memory_space=pltpu.SMEM),
            pl.BlockSpec((HD, queries), lambda h, i: (h, i)),
            pl.BlockSpec((keys, 2 * HD), lambda h, i: (0, h // 2)),
            pl.BlockSpec((HD, keys), lambda h, i: (h, 0)),
            pl.BlockSpec(norms.shape, lambda h, i: (0, 0)),
        ],
        out_specs=[
            pl.BlockSpec((1, HD + 16, queries), lambda h, i: (h, 0, i)),
            pl.BlockSpec((1, keys, queries), lambda h, i: (h, 0, i)),
        ],
        out_shape=[
            jax.ShapeDtypeStruct((HEADS, HD + 16, tokens), F32),
            jax.ShapeDtypeStruct((HEADS, keys, tokens), BF),
        ],
        scratch_shapes=[pltpu.VMEM((keys, 128), BF), pltpu.VMEM((4 * HD, queries), BF)],
        compiler_params=pltpu.CompilerParams(vmem_limit_bytes=56 * MIB),
        cost_estimate=pl.CostEstimate(
            flops=ATT * keys,
            bytes_accessed=2 * HEADS * keys,
            transcendentals=0,
        ),
        name="attend",
    )(at, query_t, key, value_t, norms)


def attend_back_kernel(first, keys, queries, chunk, p_ref, v_ref, kt_ref, g_ref, side_ref, q_ref, dq_ref, dkv_ref, value_side, grad_side, dk_sum, dv_sum):
    head, tile = pl.program_id(0), pl.program_id(1)

    @pl.when((head == 0) & (tile == 0))
    def start():
        value_side[...] = in_lanes(chunk, [1.0, 1.0, 1.0])
        grad_side[2 * HD + 16 :, :] = jnp.zeros((2 * HD - 16, queries), BF)

    @pl.when(tile == 0)
    def fresh():
        dk_sum[...] = jnp.zeros_like(dk_sum)
        dv_sum[...] = jnp.zeros_like(dv_sum)

    put_head(grad_side, first + head, g_ref[...])
    grad_side[2 * HD : 2 * HD + 16, :] = side_ref[0]
    total = jnp.zeros((HD, queries), F32)
    for at in range(keys // chunk):
        part = slice(at * chunk, (at + 1) * chunk)
        probs = p_ref[0, part, :]
        spread = mm(jnp.concatenate([v_ref[part, :], value_side[...]], axis=1), grad_side[...])
        grad_scores = (probs.astype(F32) * spread).astype(BF)
        dv_sum[:, part] += mm_nt(g_ref[...], probs)
        dk_sum[:, part] += mm_nt(q_ref[...], grad_scores)
        total = total + mm(kt_ref[:, part], grad_scores)
    dq_ref[...] = (total * (HD**-0.5)).astype(BF)

    @pl.when(tile == pl.num_programs(1) - 1)
    def finish():
        dkv_ref[0] = dk_sum[...].astype(BF)
        dkv_ref[1] = dv_sum[...].astype(BF)


def attend_back(probs, value, key_t, grad_t, side, query_t, first, heads):
    tokens, keys = query_t.shape[1], value.shape[0]
    queries, chunk = math.gcd(tokens, 1024), math.gcd(keys, 256)
    by_token = pl.BlockSpec((HD, queries), lambda h, i: (first + h, i))
    by_key = pl.BlockSpec((HD, keys), lambda h, i: (first + h, 0))
    return pl.pallas_call(
        functools.partial(attend_back_kernel, first, keys, queries, chunk),
        grid=(heads, tokens // queries),
        in_specs=[
            pl.BlockSpec((1, keys, queries), lambda h, i: (first + h, 0, i)),
            pl.BlockSpec((keys, 2 * HD), lambda h, i: (0, (first + h) // 2)),
            by_key,
            by_token,
            pl.BlockSpec((1, 16, queries), lambda h, i: (first + h, 0, i)),
            by_token,
        ],
        out_specs=[
            pl.BlockSpec((HD, queries), lambda h, i: (h, i)),
            pl.BlockSpec((2, HD, keys), lambda h, i: (0, h, 0)),
        ],
        out_shape=[
            jax.ShapeDtypeStruct((heads * HD, tokens), BF),
            jax.ShapeDtypeStruct((2, heads * HD, keys), BF),
        ],
        scratch_shapes=[
            pltpu.VMEM((chunk, 128), BF),
            pltpu.VMEM((4 * HD, queries), BF),
            pltpu.VMEM((HD, keys), F32),
            pltpu.VMEM((HD, keys), F32),
        ],
        compiler_params=pltpu.CompilerParams(vmem_limit_bytes=56 * MIB),
        cost_estimate=pl.CostEstimate(
            flops=32 * heads * HD * tokens * keys,
            bytes_accessed=2 * heads * tokens * keys,
            transcendentals=0,
        ),
        name="attend_back",
    )(probs, value, key_t, grad_t, side, query_t)


def all_of(shape):
    return pl.BlockSpec(shape, lambda *at: (0,) * len(shape))


def rows_of(rows, width):
    return pl.BlockSpec((rows, width), lambda i: (i, 0))


def columns_of(height, columns):
    return pl.BlockSpec((height, columns), lambda i: (0, i))


def run_tiles(kernel, name, steps, inputs, outputs, scratch, flops, aliases=None):
    args, in_specs = zip(*inputs)
    shapes, out_specs = zip(*outputs)
    size = sum(math.prod(v.shape) * v.dtype.itemsize for v in args + shapes)
    return pl.pallas_call(
        kernel,
        grid=(steps,),
        in_specs=list(in_specs),
        out_specs=list(out_specs),
        out_shape=list(shapes),
        scratch_shapes=scratch,
        input_output_aliases=aliases or {},
        compiler_params=pltpu.CompilerParams(vmem_limit_bytes=62 * MIB),
        cost_estimate=pl.CostEstimate(flops=flops, bytes_accessed=size, transcendentals=0),
        name=name,
    )(*args)


def shaped(shape, dtype):
    return jax.ShapeDtypeStruct(shape, dtype)


def project_kernel(parts, sources, *refs):
    x_refs, refs = refs[:sources], refs[sources:]
    (w_ref, thin_ref), refs = refs[:2], refs[2:]
    norm_ref = refs[2 * parts]
    skip = (3 - parts) * ATT

    @pl.when(pl.program_id(0) == 0)
    def start():
        norm_ref[...] = jnp.zeros_like(norm_ref)

    x = x_refs[-1][...]
    if sources == 2:
        x = jnp.where(pl.program_id(0) == 0, x_refs[0][...], x)
    plain = mm(x, w_ref[:, skip:])
    for part in range(parts):
        own = slice(part * ATT, (part + 1) * ATT)
        bias = 0.0
        if part != parts - 2:
            at = 1 if part == parts - 1 else 0
            bias = thin_ref[at : at + 1, :]
        low = (plain[:, own] + bias).astype(BF)
        refs[2 * part][...] = low
        across = low.T
        if part == parts - 2:
            wide = across.astype(F32)
            for head in range(HEADS):
                cells = wide[head * HD : (head + 1) * HD]
                size = jnp.sum(cells * cells, axis=0, keepdims=True)
                norm_ref[...] = jnp.maximum(norm_ref[...], size)
        if part < parts - 2:
            across = (across.astype(F32) * (HD**-0.5)).astype(BF)
        refs[2 * part + 1][...] = across


def project(sources, weight, thin, parts):
    tokens, width = sum(x.shape[0] for x in sources), sources[0].shape[1]
    wide = 3 * ATT
    tile = math.gcd(tokens, 512)
    late = len(sources) - 1
    inputs = [(sources[-1], pl.BlockSpec((tile, width), lambda i: (jnp.maximum(i - late, 0), 0)))]
    if late:
        inputs.insert(0, (sources[0], all_of((tile, width))))
    outputs = []
    for part in range(parts):
        outputs.append((shaped((tokens, ATT), BF), rows_of(tile, ATT)))
        outputs.append((shaped((ATT, tokens), BF), columns_of(ATT, tile)))
    outputs.append((shaped((8, tile), F32), all_of((8, tile))))
    return run_tiles(
        functools.partial(project_kernel, parts, len(sources)),
        "project",
        tokens // tile,
        inputs
        + [
            (weight, all_of((width, wide))),
            (thin, all_of(thin.shape)),
        ],
        outputs,
        [],
        2 * tokens * width * parts * ATT,
    )


def fill_rows(window, x_ref, halo_ref, tile, tiles, rows):
    first = tile * rows
    tokens = x_ref.shape[0]
    before = x_ref[pl.ds(pl.multiple_of(jnp.maximum(first - 16, 0), 16), 16), :]
    after = x_ref[pl.ds(pl.multiple_of(jnp.minimum(first + rows, tokens - 16), 16), 16), :]
    window[0:16, :] = jnp.where(tile == 0, halo_ref[0:16, :], before).astype(window.dtype)
    window[16 : 16 + rows, :] = x_ref[pl.ds(pl.multiple_of(first, rows), rows), :].astype(window.dtype)
    window[16 + rows :, :] = jnp.where(
        tile == tiles - 1, halo_ref[16:32, :], after
    ).astype(window.dtype)


def fill_window(window, x_ref, halo_ref, tile, rows):
    fill_rows(window, x_ref, halo_ref, tile, pl.num_programs(0), rows)


def fill_spread(spread):
    row = lax.broadcasted_iota(jnp.int32, (128, ATT), 0)
    head = lax.broadcasted_iota(jnp.int32, (128, ATT), 1) // HD
    for tap in range(KSIZE):
        spread[:, tap * ATT : (tap + 1) * ATT] = (row == tap * 8 + head).astype(F32).astype(BF)


def mix_kernel(rows, count, x_ref, halo_ref, q_ref, wc_ref, wp_ref, wide_ref, thin_ref, wk_ref, bk_ref, depth_ref, keyconv_ref, attn_ref, kernt_ref, kern_ref, conv_ref, out_ref, rim_ref, window, conv_window, spread):
    tile = pl.program_id(0)
    last = pl.num_programs(0) - 1

    @pl.when(tile == 0)
    def start():
        fill_spread(spread)

    fill_window(window, x_ref, halo_ref, tile, rows)
    width = window.shape[1]
    for at in range(0, width, 128):
        some = slice(at, at + 128)
        total = jnp.zeros((rows, 128), F32)
        for tap in range(KSIZE):
            total = total + window[12 + tap : 12 + tap + rows, some] * wide_ref[TAPS_AT + tap : TAPS_AT + tap + 1, some]
        depth_ref[:, some] = total.astype(BF)
    position = (
        lax.axis_index("blk") * x_ref.shape[0] + tile * rows - 16 + lax.broadcasted_iota(jnp.int32, (rows + 32, ATT), 0)
    )
    inside = (position >= 0) & (position < count * x_ref.shape[0])
    values = mm(window[...].astype(BF), wc_ref[...]) + thin_ref[3:4, :]
    values = jnp.where(inside, values, 0.0).astype(BF)
    out_ref[...] = values[16 : 16 + rows]

    @pl.when(tile == 0)
    def first_rim():
        rim_ref[0:16, :] = values[0:16]

    @pl.when(tile == last)
    def last_rim():
        rim_ref[16:32, :] = values[16 + rows :]

    conv_window[...] = values.astype(F32)
    keyconv = mm(depth_ref[...], wp_ref[...]) + thin_ref[2:3, :]
    keyconv_ref[...] = keyconv
    attn_key = (keyconv * q_ref[...].astype(F32)).astype(BF)
    attn_ref[...] = attn_key
    logits = mm_nt(wk_ref[...], attn_key) + bk_ref[:, BIAS_AT : BIAS_AT + 1]
    slabs = [logits[8 * tap : 8 * tap + 8] for tap in range(KSIZE)]
    best = functools.reduce(jnp.maximum, slabs)
    slabs = [jnp.exp(slab - best) for slab in slabs]
    share = 1.0 / functools.reduce(jnp.add, slabs)
    slabs = [slab * share for slab in slabs]
    kernt = jnp.concatenate(slabs + [jnp.zeros((128 - 8 * KSIZE, rows), F32)], axis=0)
    kernt_ref[...] = kernt[0 : 8 * KSIZE]
    kern = kernt.astype(BF).T
    kern_ref[...] = kern
    for at in range(0, ATT, LANES):
        some = slice(at, at + LANES)
        total = jnp.zeros((rows, LANES), F32)
        for tap in range(KSIZE):
            first = tap * ATT + at
            total = total + mm(kern, spread[:, first : first + LANES]) * conv_window[12 + tap : 12 + tap + rows, some]
        conv_ref[:, some] = total.astype(BF)


def column_block(weight, place):
    return pl.BlockSpec((weight.shape[0], ATT), lambda i: (0, place))


def mix(count, x, halo, query, weight, wide_vectors, thin, w_kernel, kernel_bias):
    tokens, width = x.shape
    rows = math.gcd(tokens, 512)
    whole = [(weight, column_block(weight, 2)), (weight, column_block(weight, 3))]
    whole += [(v, all_of(v.shape)) for v in (wide_vectors, thin, w_kernel, kernel_bias)]
    return run_tiles(
        functools.partial(mix_kernel, rows, count),
        "mix",
        tokens // rows,
        [
            (x, all_of(x.shape)),
            (halo, all_of(halo.shape)),
            (query, rows_of(rows, ATT)),
        ]
        + whole,
        [
            (shaped((tokens, width), BF), rows_of(rows, width)),
            (shaped((tokens, ATT), F32), rows_of(rows, ATT)),
            (shaped((tokens, ATT), BF), rows_of(rows, ATT)),
            (shaped((8 * KSIZE, tokens), F32), columns_of(8 * KSIZE, rows)),
            (shaped((tokens, 128), BF), rows_of(rows, 128)),
            (shaped((tokens, ATT), BF), rows_of(rows, ATT)),
            (shaped((tokens, ATT), BF), rows_of(rows, ATT)),
            (shaped((32, ATT), BF), all_of((32, ATT))),
        ],
        [
            pltpu.VMEM((rows + 32, width), F32),
            pltpu.VMEM((rows + 32, ATT), F32),
            pltpu.VMEM((128, KSIZE * ATT), BF),
        ],
        4 * tokens * width * ATT * 4,
    )


def normal(values):
    centre = values - jnp.mean(values, axis=-1, keepdims=True)
    scale = lax.rsqrt(jnp.mean(centre * centre, axis=-1, keepdims=True) + EPS)
    return centre * scale, scale


def normal_back(grad, unit, scale):
    return scale * (
        grad
        - jnp.mean(grad, axis=-1, keepdims=True)
        - unit * jnp.mean(grad * unit, axis=-1, keepdims=True)
    )


def gelu_parts(values):
    share = 0.5 + 0.5 * lax.erf(values * math.sqrt(0.5))
    bell = jnp.exp2(values * values * (-0.5 * math.log2(math.e)))
    return values * share, share + values * (bell * (1.0 / math.sqrt(2.0 * math.pi)))


def middle_kernel(blocks, rows, units, *refs):
    o_refs, refs = refs[:blocks], refs[blocks:]
    (conv_ref, x_ref, og_ref, wd_ref, late_ref, vec_ref, bu_ref), refs = refs[:7], refs[7:]
    (out_ref, sum_ref, gconv_ref), refs = refs[:3], refs[3:]
    g_refs, refs = refs[:blocks], refs[blocks:]
    side_refs, refs = refs[:blocks], refs[blocks:]
    (packed_ref, gvec_ref, gbu_ref, wd_sum, wu_sum, wn_sum, acts, slopes, staged, sems, wu_ref) = refs
    tile = pl.program_id(0)
    hidden_units = wu_ref.shape[1]
    low_rows = late_ref.shape[1] // 2

    def down_rows(at, lanes):
        return late_ref[at // low_rows : (at + units) // low_rows, low_rows:, lanes].reshape(units, ATT)

    groups = 2
    inner = ATT
    outer = hidden_units // groups

    @pl.when(tile == 0)
    def start():
        for ref in (wd_sum, wu_sum, wn_sum, gvec_ref, gbu_ref):
            ref[...] = jnp.zeros_like(ref)
        owners, high, width = late_ref.shape
        quarter = high // 8
        for pair in range(0, owners, 2):
            both = [late_ref[owner, 0 : high // 2].astype(F32) for owner in (pair, pair + 1)]
            for place in range(4):
                some = [cells[place * quarter : (place + 1) * quarter] for cells in both]
                wu_ref[pair * quarter : (pair + 2) * quarter, place * width : (place + 1) * width] = (
                    jnp.concatenate(some, axis=0).astype(BF)
                )

    shifts = [ref[:, HD + 8 : HD + 9, :] for ref in o_refs]
    top = functools.reduce(jnp.maximum, shifts)
    weights = [jnp.exp(shift - top) for shift in shifts]
    mass = functools.reduce(jnp.add, [w * ref[:, HD : HD + 1, :] for w, ref in zip(weights, o_refs)])
    weights = [w / mass for w in weights]
    heads = functools.reduce(jnp.add, [w * ref[:, 0:HD, :] for w, ref in zip(weights, o_refs)])
    att_t = heads.reshape(ATT, rows).astype(BF)
    conv = conv_ref[...]
    vec = [vec_ref[at : at + 1, :] for at in range(6)]
    dense = mm(att_t.T, wd_ref[0:ATT, :]) + mm(conv, wd_ref[ATT:, :]) + vec[0]
    unit_one, scale_one = normal(dense + x_ref[...].astype(F32))
    normed = unit_one * vec[1] + vec[2]
    low = normed.astype(BF)
    downs = []
    for group in range(groups):
        mine = low[:, group * inner : (group + 1) * inner]
        down = jnp.zeros((rows, inner), F32)
        for at in range(0, outer, units):
            here = slice(group * outer + at, group * outer + at + units)
            upward = mm(mine, wu_ref[:, here]) + bu_ref[:, here]
            act, slope = gelu_parts(upward)
            act = act.astype(BF)
            acts[:, here] = act
            slopes[:, here] = slope.astype(BF)
            down = down + mm(act, down_rows(at, slice(group * inner, (group + 1) * inner)))
        downs.append(down)
    unit_two, scale_two = normal(jnp.concatenate(downs, axis=1) + vec[3] + normed)
    out_ref[...] = (unit_two * vec[4] + vec[5]).astype(BF)
    og = og_ref[...].astype(F32)
    gvec_ref[4:5, :] += jnp.sum(og * unit_two, axis=0, keepdims=True)
    gvec_ref[5:6, :] += jnp.sum(og, axis=0, keepdims=True)
    grad_two = normal_back(og * vec[4], unit_two, scale_two)
    grad_down = grad_two.astype(BF)
    gvec_ref[3:4, :] += jnp.sum(grad_down.astype(F32), axis=0, keepdims=True)
    backs = []
    for group in range(groups):
        lanes = slice(group * inner, (group + 1) * inner)
        mine, grads = low[:, lanes], grad_down[:, lanes]
        mine_t = mine.T
        back = jnp.zeros((rows, inner), F32)
        for at in range(0, outer, units):
            here = slice(group * outer + at, group * outer + at + units)
            grad_act = mm_nt(grads, down_rows(at, lanes))
            grad_up = (grad_act * slopes[:, here].astype(F32)).astype(BF)
            gbu_ref[0:1, here] += jnp.sum(grad_up.astype(F32), axis=0, keepdims=True)
            wn_sum[at : at + units, lanes] += mm_tn(acts[:, here], grads)
            wu_sum[:, here] += mm(mine_t, grad_up)
            back = back + mm_nt(grad_up, wu_ref[:, here])
        backs.append(back)
    grad_normed = grad_two + jnp.concatenate(backs, axis=1)
    gvec_ref[1:2, :] += jnp.sum(grad_normed * unit_one, axis=0, keepdims=True)
    gvec_ref[2:3, :] += jnp.sum(grad_normed, axis=0, keepdims=True)
    grad_one = normal_back(grad_normed * vec[1], unit_one, scale_one)
    sum_ref[...] = grad_one
    grad_dense = grad_one.astype(BF)
    gvec_ref[0:1, :] += jnp.sum(grad_dense.astype(F32), axis=0, keepdims=True)
    wd_sum[0:ATT, :] += mm(att_t, grad_dense)
    wd_sum[ATT:, :] += mm_tn(conv, grad_dense)
    gconv_ref[...] = mm_nt(grad_dense, wd_ref[ATT:, :]).astype(BF)
    grad_att = mm_nt(wd_ref[0:ATT, :], grad_dense).astype(BF).astype(F32).reshape(HEADS, HD, rows)
    for weight, g_ref, side_ref in zip(weights, g_refs, side_refs):
        share = (grad_att * weight).astype(BF)
        g_ref[...] = share.reshape(ATT, rows)
        delta = -jnp.sum(share.astype(F32) * heads, axis=1, keepdims=True)
        row = lax.broadcasted_iota(jnp.int32, (HEADS, 16, rows), 1)
        side = jnp.zeros((HEADS, 16, rows), F32)
        for at, part in enumerate(three_parts(delta)):
            side = jnp.where(row == at, part, side)
        side_ref[...] = side.astype(BF)

    @pl.when(tile == pl.num_programs(0) - 1)
    def finish():
        slots = staged.shape[0]
        sharers = packed_ref.shape[0]
        shard = wd_sum.shape[0] // sharers
        quarter = shard // 2
        width = wd_sum.shape[1]
        copies = []
        for owner in range(sharers):
            slot = owner % slots
            if owner >= slots:
                copies[owner - slots].wait()
            staged[slot, 0:shard] = wd_sum[owner * shard : (owner + 1) * shard].astype(BF)
            some = wu_sum[owner * quarter : (owner + 1) * quarter]
            for group in range(groups):
                pair = [some[:, at : at + width] for at in (2 * group * width, (2 * group + 1) * width)]
                staged[slot, (1 + group) * shard : (2 + group) * shard] = jnp.concatenate(pair, axis=0).astype(BF)
            some = wn_sum[owner * 2 * shard : (owner + 1) * 2 * shard]
            staged[slot, 3 * shard : 5 * shard] = some.astype(BF)
            copy = pltpu.make_async_copy(
                staged.at[slot], packed_ref.at[owner, 0 : 5 * shard], sems.at[owner]
            )
            copy.start()
            copies.append(copy)
        for copy in copies[sharers - slots :]:
            copy.wait()


def middle(outs, conv, x, out_grad, w_dense, late, vectors, b_up):
    tokens, width = x.shape
    sharers = late.shape[0]
    shard = width // sharers
    units = b_up.shape[1]
    up, down = (width // 2, units), (units // 2, width)
    rows = math.gcd(tokens, 512)
    blocks = len(outs)
    heads = pl.BlockSpec((HEADS, HD + 16, rows), lambda i: (0, 0, i))
    side = pl.BlockSpec((HEADS, 16, rows), lambda i: (0, 0, i))
    single = pl.Buffered(1)
    once = [
        (w_dense, pl.BlockSpec((width, width), lambda i: (0, 0), pipeline_mode=single)),
        (late, pl.BlockSpec(late.shape, lambda i: (0, 0, 0), pipeline_mode=single)),
    ]
    once += [(v, all_of(v.shape)) for v in (vectors, b_up)]
    results = run_tiles(
        functools.partial(middle_kernel, blocks, rows, 768),
        "middle",
        tokens // rows,
        [(o, heads) for o in outs]
        + [
            (conv, rows_of(rows, ATT)),
            (x, rows_of(rows, width)),
            (out_grad, rows_of(rows, width)),
        ]
        + once,
        [
            (shaped((tokens, width), BF), rows_of(rows, width)),
            (shaped((tokens, width), F32), rows_of(rows, width)),
            (shaped((tokens, ATT), BF), rows_of(rows, ATT)),
        ]
        + [(shaped((ATT, tokens), BF), columns_of(ATT, rows))] * blocks
        + [(shaped((HEADS, 16, tokens), BF), side)] * blocks
        + [
            (shaped((sharers, 7 * shard, width), BF), pl.BlockSpec(memory_space=pl.ANY)),
            (shaped((8, width), F32), all_of((8, width))),
            (shaped((8, units), F32), all_of((8, units))),
        ],
        [
            pltpu.VMEM((width, width), F32),
            pltpu.VMEM(up, F32),
            pltpu.VMEM(down, F32),
            pltpu.VMEM((rows, units), BF),
            pltpu.VMEM((rows, units), BF),
            pltpu.VMEM((2, 5 * shard, width), BF),
            pltpu.SemaphoreType.DMA((sharers,)),
            pltpu.VMEM(up, BF),
        ],
        6 * tokens * (width * width + 2 * math.prod(up)),
    )
    output, grad_sum, grad_conv = results[:3]
    return output, grad_sum, grad_conv, results[3 : 3 + blocks], results[3 + blocks : 3 + 2 * blocks], results[3 + 2 * blocks :]


def mix_back_kernel(rows, count, x_ref, halo_ref, values_ref, rim_ref, gconv_ref, kernt_ref, kern_ref, q_ref, keyconv_ref, attn_ref, depth_ref, wp_ref, wk_ref, gvec_ref, gbu_ref, unused, gq_ref, gdepth_ref, gvalues_ref, packed_ref, turned_ref, window, conv_window, summed, products, spread, wp_sum, wc_sum, values_sum, gwk_ref, gbias_ref, gtaps_ref, turn_wide, turn_thin, side, staged, sem):
    tile = pl.program_id(0)

    @pl.when(tile == 0)
    def start():
        fill_spread(spread)
        for ref in (values_sum, wp_sum, wc_sum, gwk_ref, gbias_ref, gtaps_ref, turn_wide, turn_thin):
            ref[...] = jnp.zeros_like(ref)

    fill_window(window, x_ref, halo_ref, tile, rows)
    fill_window(conv_window, values_ref, rim_ref, tile, rows)
    summed[...] = jnp.zeros_like(summed)
    grad_conv = gconv_ref[...].astype(F32)
    for tap in range(KSIZE):
        here = slice(tap * ATT, (tap + 1) * ATT)
        there = slice(12 + tap, 12 + tap + rows)
        products[:, here] = (grad_conv * conv_window[there, :]).astype(BF)
        summed[there, :] += mm(kern_ref[...], spread[:, here]) * grad_conv
    first = pl.multiple_of(tile * rows, rows)
    values_sum[pl.ds(first, rows + 32), :] += summed[...]
    turned = x_ref[pl.ds(first, rows), :].T
    turned_ref[...] = turned
    edges = [slice(0, 16), slice(rows + 16, rows + 32)]
    edge_x = jnp.concatenate([window[edge, :] for edge in edges], axis=0).astype(BF)
    edge_grads = jnp.concatenate([summed[edge, :] for edge in edges], axis=0).astype(BF)
    wc_sum[...] += mm(turned, summed[16 : 16 + rows, :].astype(BF)) + mm_tn(edge_x, edge_grads)
    grad_kernel = mm_nt(spread[...], products[...])
    slabs = [slice(8 * tap, 8 * tap + 8) for tap in range(KSIZE)]
    kernels = [kernt_ref[slab, :] for slab in slabs]
    mean = functools.reduce(jnp.add, [k * grad_kernel[slab] for k, slab in zip(kernels, slabs)])
    grad_logits = jnp.concatenate(
        [k * (grad_kernel[slab] - mean) for k, slab in zip(kernels, slabs)], axis=0
    ).astype(BF)
    wide_logits = grad_logits.astype(F32)
    gbias_ref[...] += jnp.concatenate(
        [
            jnp.broadcast_to(jnp.sum(wide_logits, axis=1, keepdims=True), (8 * KSIZE, 128)),
            jnp.zeros((8, 128), F32),
        ],
        axis=0,
    )
    gwk_ref[0 : 8 * KSIZE, :] += mm(grad_logits, attn_ref[...])
    grad_attn = mm_tn(grad_logits, wk_ref[...]).astype(BF).astype(F32)
    grad_keyconv = (grad_attn * q_ref[...].astype(F32)).astype(BF)
    gq_ref[...] = (grad_attn * keyconv_ref[...]).astype(BF)
    gwk_ref[8 * KSIZE : 8 * KSIZE + 1, :] += jnp.sum(grad_keyconv.astype(F32), axis=0, keepdims=True)
    wp_sum[...] += mm_tn(depth_ref[...], grad_keyconv)
    grad_depth = mm_nt(grad_keyconv, wp_ref[...]).astype(BF)
    gdepth_ref[...] = grad_depth
    wide = grad_depth.astype(F32)
    for at in range(0, window.shape[1], 128):
        some = slice(at, at + 128)
        for tap in range(KSIZE):
            gtaps_ref[tap : tap + 1, some] += jnp.sum(
                wide[:, some] * window[12 + tap : 12 + tap + rows, some], axis=0, keepdims=True
            )

    @pl.when(tile == pl.num_programs(0) - 1)
    def finish():
        gvalues_ref[...] = values_sum[...].astype(BF)
        tokens, block = x_ref.shape[0], lax.axis_index("blk")
        sums = [
            jnp.sum(gvalues_ref[at:end, :].astype(F32), axis=0, keepdims=True)
            for at, end in ((0, 16), (16, tokens + 16), (tokens + 16, tokens + 32))
        ]
        b_sum = sums[1] + jnp.where(block > 0, sums[0], 0.0) + jnp.where(block < count - 1, sums[2], 0.0)
        sharers, shard, width = staged.shape[0], staged.shape[1] // 2, staged.shape[2]
        part = ATT // sharers
        half = gbu_ref.shape[1] // sharers // 2
        turn_wide[0:6, :] = gvec_ref[0:6, :]
        turn_wide[TAPS_AT : TAPS_AT + KSIZE, :] = gtaps_ref[0:KSIZE, :]
        vectors = turn_wide[...].T
        for h in range(HEADS):
            for j in range(KSIZE):
                turn_wide[h * KSIZE + j : h * KSIZE + j + 1, 0:LANES] = gbias_ref[j * 8 + h : j * 8 + h + 1, :]
                turn_thin[h * KSIZE + j : h * KSIZE + j + 1, :] = gwk_ref[j * 8 + h : j * 8 + h + 1, :]
        bias = turn_wide[:, 0:LANES].T[0:1]
        turn_thin[THIN_AT : THIN_AT + 1, :] = gwk_ref[8 * KSIZE : 8 * KSIZE + 1, :]
        turn_thin[THIN_AT + 1 : THIN_AT + 2, :] = b_sum
        kernels = turn_thin[...].T
        side[...] = jnp.zeros_like(side)
        for owner in range(sharers):
            staged[owner, 0:shard, 0:ATT] = wp_sum[owner * shard : (owner + 1) * shard].astype(BF)
            staged[owner, shard:, 0:ATT] = wc_sum[owner * shard : (owner + 1) * shard].astype(BF)
            staged[owner, shard:, ATT:] = jnp.zeros((shard, width - ATT), BF)
            staged[owner, 0:shard, ATT : ATT + LANES] = vectors[owner * shard : (owner + 1) * shard].astype(BF)
            side[0:part, :] = kernels[owner * part : (owner + 1) * part]
            for place in range(2):
                first = (2 * owner + place) * half
                side[part + place : part + place + 1, 0:half] = gbu_ref[0:1, first : first + half]
            side[part + 2 : part + 3, :] = bias
            staged[owner, 0:shard, ATT + LANES : ATT + 2 * LANES] = side[...].astype(BF)
            staged[owner, 0:shard, ATT + 2 * LANES :] = jnp.zeros((shard, width - ATT - 2 * LANES), BF)
        copy = pltpu.make_async_copy(staged, packed_ref.at[:, 5 * shard : 7 * shard], sem)
        copy.start()
        copy.wait()


def mix_back(count, x, halo, values, rim, grad_conv, kernt, kern, query, keyconv, attn_key, depth, weight, w_kernel, g_vectors, gb_up, packed):
    tokens, width = x.shape
    sharers, shard = packed.shape[0], packed.shape[1] // 7
    away = pl.BlockSpec(memory_space=pl.ANY)
    rows = math.gcd(tokens, 512)
    by_rows = [(v, rows_of(rows, v.shape[1])) for v in (kern, query, keyconv, attn_key, depth)]
    return run_tiles(
        functools.partial(mix_back_kernel, rows, count),
        "mix_back",
        tokens // rows,
        [(v, all_of(v.shape)) for v in (x, halo, values, rim)]
        + [(grad_conv, rows_of(rows, ATT)), (kernt, columns_of(8 * KSIZE, rows))]
        + by_rows
        + [(weight, column_block(weight, 3))]
        + [(v, all_of(v.shape)) for v in (w_kernel, g_vectors, gb_up)]
        + [(packed, away)],
        [
            (shaped((tokens, ATT), BF), rows_of(rows, ATT)),
            (shaped((tokens, width), BF), rows_of(rows, width)),
            (shaped((tokens + 32, ATT), BF), all_of((tokens + 32, ATT))),
            (shaped(packed.shape, BF), away),
            (shaped((width, tokens), BF), columns_of(width, rows)),
        ],
        [
            pltpu.VMEM((rows + 32, width), F32),
            pltpu.VMEM((rows + 32, ATT), F32),
            pltpu.VMEM((rows + 32, ATT), F32),
            pltpu.VMEM((rows, KSIZE * ATT), BF),
            pltpu.VMEM((128, KSIZE * ATT), BF),
            pltpu.VMEM((width, ATT), F32),
            pltpu.VMEM((width, ATT), F32),
            pltpu.VMEM((tokens + 32, ATT), F32),
            pltpu.VMEM((8 * KSIZE + 8, ATT), F32),
            pltpu.VMEM((8 * KSIZE + 8, LANES), F32),
            pltpu.VMEM((16, width), F32),
            pltpu.VMEM((LANES, width), F32),
            pltpu.VMEM((LANES, ATT), F32),
            pltpu.VMEM((shard, LANES), F32),
            pltpu.VMEM((sharers, 2 * shard, width), BF),
            pltpu.SemaphoreType.DMA(()),
        ],
        4 * tokens * width * ATT * 4,
        {15: 3},
    )


def side_by_side_kernel(*refs):
    at = 0
    for ref in refs[:-1]:
        refs[-1][:, at : at + ref.shape[1]] = ref[...].astype(BF)
        at += ref.shape[1]


def side_by_side(parts):
    out = shaped((parts[0].shape[0], sum(v.shape[1] for v in parts)), BF)
    return run_tiles(
        side_by_side_kernel, "side_by_side", 1, [(v, all_of(v.shape)) for v in parts], [(out, all_of(out.shape))], [], 0
    )[0]


MESH = pl.DeviceIdType.MESH
LINE = 4
LANES = 128
TAPS_AT = 16
THIN_AT = 64
BIAS_AT = 100


def my_place(sharers):
    columns = sharers // (2 * LINE)
    me = lax.axis_index("dp")
    return me, me // (2 * columns), lax.rem(me // 2, columns), lax.rem(me, 2), columns


def greet(partners):
    barrier = pltpu.get_barrier_semaphore()
    for partner in partners:
        pl.semaphore_signal(barrier, inc=1, device_id=partner, device_id_type=MESH)
    return barrier


def remote(source, target, send_sem, recv_sem, device):
    return pltpu.make_async_remote_copy(
        src_ref=source,
        dst_ref=target,
        send_sem=send_sem,
        recv_sem=recv_sem,
        device_id=device,
        device_id_type=MESH,
    )


def gather_kernel(sharers, count, part, early, *refs):
    w_refs, refs = refs[:3], refs[3:]
    vector_refs, refs = refs[:6], refs[6:]
    thin_refs, refs = refs[:4], refs[4:]
    (taps_ref, up_ref, kernel_ref, bias_ref, wu_ref, wn_ref, head_ref, tail_ref, early_ref), refs = refs[:9], refs[9:]
    (out_ref, wide_ref, thin_ref, bias_up_ref, wk_ref, bk_ref, halo_ref, late_out, early_out), refs = refs[:9], refs[9:]
    rows, side, flat, thin_flat, edges, send_sem, recv_sem, edge_send, edge_recv = refs
    me, line, column, core, columns = my_place(sharers)
    block = lax.axis_index("blk")
    shard = out_ref.shape[1]
    base = len(w_refs) * ATT
    half = up_ref.shape[0] // 2

    def at(line, column, core):
        return (line * columns + column) * 2 + core

    lines = [lax.rem(line + step, LINE) for step in range(1, LINE)]
    sides = [lax.rem(column + step, columns) for step in range(1, columns)]
    partners = [{"dp": at(other, column, core)} for other in lines]
    across = [{"dp": at(line, other, core)} for other in sides]
    mate = {"dp": at(line, column, 1 - core)}
    ends = []
    if count > 1:
        ends = [{"blk": lax.rem(block + 1, count)}, {"blk": lax.rem(block + count - 1, count)}]
    barrier = greet(partners + across + [mate] + ends)
    for place, ref in enumerate(w_refs):
        out_ref[me, :, place * ATT : (place + 1) * ATT] = ref[...].astype(BF)
    rows[...] = jnp.zeros_like(rows)
    for place, ref in enumerate(vector_refs):
        rows[place : place + 1, 0:shard] = ref[...].reshape(1, shard)
    for place, ref in enumerate(thin_refs):
        rows[THIN_AT + place : THIN_AT + place + 1, 0:part] = ref[...].reshape(1, part)
    rows[TAPS_AT : TAPS_AT + KSIZE, 0:shard] = taps_ref[...]
    rows[BIAS_AT : BIAS_AT + 1, 0 : HEADS * KSIZE] = bias_ref[...].reshape(1, HEADS * KSIZE)
    rows[...] = rows[...].T
    side[...] = rows[0:shard]
    out_ref[me, :, base : base + LANES] = side[...].astype(BF)
    side[...] = jnp.zeros_like(side)
    side[0:part, 0 : HEADS * KSIZE] = kernel_ref[...]
    side[part : part + 1, 0:half] = up_ref[0:half].reshape(1, half)
    side[part + 1 : part + 2, 0:half] = up_ref[half:].reshape(1, half)
    out_ref[me, :, base + LANES :] = side[...].astype(BF)
    width = late_out.shape[1]
    for group in range(2):
        pair = [wu_ref[group, :, place * width : (place + 1) * width] for place in range(2)]
        late_out[group * shard : (group + 1) * shard] = jnp.concatenate(pair, axis=0).astype(BF)
        late_out[2 * shard :, group * ATT : (group + 1) * ATT] = wn_ref[group].astype(BF)
    if not early:
        early_out[...] = early_ref[...]
    pl.semaphore_wait(barrier, len(partners) + len(across) + 1 + len(ends))
    sends = []

    def sending(number, owner, device):
        return remote(out_ref.at[owner], out_ref.at[owner], send_sem.at[number], recv_sem.at[owner], device)

    def pass_on(owner, devices, when=None):
        for device in devices:
            sending(len(sends), owner, device).start()
            sends.append((owner, device, when))

    def arrived(owner):
        pltpu.make_async_copy(out_ref.at[owner], out_ref.at[owner], recv_sem.at[owner]).wait()

    pass_on(me, across + [mate])
    edge_copies = []
    for place, (ref, device) in enumerate(zip((tail_ref, head_ref), ends)):
        edge_copies.append(remote(ref, edges.at[place], edge_send.at[place], edge_recv.at[place], device))
    if early:
        edge_copies.append(remote(early_ref, early_out, edge_send.at[2], edge_recv.at[2], ends[0]))
    for copy in edge_copies:
        copy.start()
    for step in range(1, LINE):
        for way in (1, -1):
            from_here = (line - way * (step - 1) >= 0) & (line - way * (step - 1) < LINE)
            goes = from_here & (line + way >= 0) & (line + way < LINE)
            owner, onward = at(line - way * (step - 1), column, core), [{"dp": at(line + way, column, core)}]

            @pl.when(goes)
            def forward():
                pass_on(owner, onward, goes)

        for way in (1, -1):
            comes = (line - way * step >= 0) & (line - way * step < LINE)
            owner = at(line - way * step, column, core)

            @pl.when(comes)
            def take():
                arrived(owner)
                pass_on(owner, across + [mate], comes)

    for some in sides:
        for other in [line] + lines:
            owner = at(other, some, core)
            arrived(owner)
            pass_on(owner, [mate])
    nothing = jnp.zeros((16, halo_ref.shape[1]), BF)
    halo_ref[0:16, :] = nothing
    halo_ref[16:32, :] = nothing
    if count > 1:
        for copy in edge_copies:
            copy.wait()
        halo_ref[0:16, :] = jnp.where(block > 0, edges[0], nothing)
        halo_ref[16:32, :] = jnp.where(block < count - 1, edges[1], nothing)
    for j in range(KSIZE):
        for h in range(8):
            source = h * KSIZE + j if h < HEADS else 120
            bk_ref[j * 8 + h : j * 8 + h + 1, :] = rows[source : source + 1, :]
    for some in [column] + sides:
        for other in [line] + lines:
            arrived(at(other, some, 1 - core))
    for number, (owner, device, when) in enumerate(sends):
        if when is None:
            sending(number, owner, device).wait_send()
        else:
            pl.when(when)(lambda: sending(number, owner, device).wait_send())
    for owner in range(sharers):
        cells = out_ref[owner, :, base : base + LANES].astype(F32)
        flat[owner * shard : (owner + 1) * shard, :] = cells
        thin_flat[owner * part : (owner + 1) * part, :] = cells[0:part]
    turned = flat[...].T
    wide_ref[...] = turned[0 : wide_ref.shape[0]]
    thin_ref[...] = thin_flat[...].T[THIN_AT : THIN_AT + 8]
    for owner in range(sharers):
        cells = out_ref[owner, :, base + LANES :].astype(F32)
        thin_flat[owner * part : (owner + 1) * part, :] = cells[0:part]
        for place in range(2):
            first = (2 * owner + place) * half
            bias_up_ref[0:1, first : first + half] = cells[part + place : part + place + 1, 0:half]
    turned = thin_flat[...].T
    slabs = []
    for j in range(KSIZE):
        slabs += [turned[h * KSIZE + j : h * KSIZE + j + 1] for h in range(HEADS)]
        slabs.append(jnp.zeros((8 - HEADS, ATT), F32))
    wk_ref[...] = jnp.concatenate(slabs, axis=0).astype(BF)


def gather_columns(weights, vectors, thin, taps, b_up, w_kernel, kernel_bias, w_up, w_down, x, sharers, count):
    shard, part = weights[0].shape[0], thin[0].shape[0]
    tokens, width = x.shape
    early = count == 2
    first_rows = math.gcd(tokens, 512) if early else 16
    wide = len(weights) * ATT + 2 * LANES
    columns = sharers // (2 * LINE)
    copies = columns + 2 * (LINE - 1) * (1 + columns) + LINE * (columns - 1)
    args = list(weights) + list(vectors) + list(thin) + [taps, b_up, w_kernel, kernel_bias, w_up, w_down]
    shapes = [
        shaped((sharers, shard, wide), BF),
        shaped((32, width), F32),
        shaped((8, ATT), F32),
        shaped((1, sharers * b_up.shape[0]), F32),
        shaped((8 * KSIZE, ATT), BF),
        shaped((8 * KSIZE, LANES), F32),
        shaped((32, width), BF),
        shaped((4 * shard, width), BF),
        shaped((first_rows, width), BF),
    ]
    out, *rest = pl.pallas_call(
        functools.partial(gather_kernel, sharers, count, part, early),
        grid=(1,),
        in_specs=[all_of(v.shape) for v in args]
        + [
            pl.BlockSpec((16, width), lambda i: (0, 0)),
            pl.BlockSpec((16, width), lambda i: (tokens // 16 - 1, 0)),
            pl.BlockSpec((first_rows, width), lambda i: (0, 0)),
        ],
        out_specs=[all_of(v.shape) for v in shapes],
        out_shape=shapes,
        scratch_shapes=[
            pltpu.VMEM((LANES, LANES), F32),
            pltpu.VMEM((shard, LANES), F32),
            pltpu.VMEM((width, LANES), F32),
            pltpu.VMEM((ATT, LANES), F32),
            pltpu.VMEM((2, 16, width), BF),
            pltpu.SemaphoreType.DMA((copies,)),
            pltpu.SemaphoreType.DMA((sharers,)),
            pltpu.SemaphoreType.DMA((3,)),
            pltpu.SemaphoreType.DMA((3,)),
        ],
        compiler_params=pltpu.CompilerParams(
            collective_id=0, has_side_effects=True, vmem_limit_bytes=60 * MIB
        ),
        name="gather_columns",
    )(*args, x, x, x)
    return (out.reshape(sharers * shard, wide), *rest)


class Shares:
    def __init__(self, sharers, rows, widths, line_first, count):
        self.sharers, self.rows, self.widths, self.line_first, self.count = sharers, rows, widths, line_first, count
        self.columns = sharers // (2 * LINE)
        self.chips = sharers // 2
        ends = [sum(widths[: at + 1]) for at in range(len(widths))]
        self.lanes = [slice(end - width, end) for end, width in zip(ends, widths)]
        self.wide = ends[-1]
        self.copies = 1 + self.columns - 1 + LINE - 1 + count - 1

    def scratch(self):
        shapes = []
        for width, line_first in zip(self.widths, self.line_first):
            side = (self.columns - 1, 1 if line_first else LINE, self.rows, width)
            line = (LINE - 1, self.columns if line_first else 1, self.rows, width)
            shapes += [pltpu.VMEM((self.chips, self.rows, width), BF)] * 2
            shapes += [pltpu.VMEM(side, BF)] * 2 + [pltpu.VMEM(line, BF)] * 2
            shapes += [pltpu.VMEM((self.rows, width), BF), pltpu.VMEM((self.count, self.rows, width), BF)]
        sems = len(self.widths) * self.copies
        return shapes + [
            pltpu.VMEM((self.sharers, self.rows, self.wide), F32),
            pltpu.SemaphoreType.DMA((sems,)),
            pltpu.SemaphoreType.DMA((sems,)),
        ]

    def bind(self, refs):
        chains = len(self.widths)
        self.buffers = [refs[8 * chain : 8 * chain + 8] for chain in range(chains)]
        self.total, self.send_sem, self.recv_sem = refs[8 * chains : 8 * chains + 3]
        self.me, self.line, self.column, self.core, unused = my_place(self.sharers)
        self.block = lax.axis_index("blk")
        self.others_line = [lax.rem(self.line + step, LINE) for step in range(1, LINE)]
        self.others_side = [lax.rem(self.column + step, self.columns) for step in range(1, self.columns)]
        self.others_block = [lax.rem(self.block + step, self.count) for step in range(1, self.count)]

    def at(self, line, column, core):
        return (line * self.columns + column) * 2 + core

    def greet(self):
        devices = [{"dp": self.at(self.line, self.column, 1 - self.core)}]
        devices += [{"dp": self.at(self.line, other, self.core)} for other in self.others_side]
        devices += [{"dp": self.at(other, self.column, self.core)} for other in self.others_line]
        devices += [{"blk": other} for other in self.others_block]
        greet(devices)

    def met(self):
        pl.semaphore_wait(pltpu.get_barrier_semaphore(), 1 + self.columns - 1 + LINE - 1 + self.count - 1)

    def copy(self, chain, number, source, target, device):
        sem = chain * self.copies + number
        return remote(source, target, self.send_sem.at[sem], self.recv_sem.at[sem], device)

    def part(self, owner, chain):
        return self.total[owner, :, self.lanes[chain]]

    def add(self, owner, chain, values):
        self.total[owner, :, self.lanes[chain]] += values.astype(F32)

    def mate_copy(self, chain):
        mate = {"dp": self.at(self.line, self.column, 1 - self.core)}
        return self.copy(chain, 0, self.buffers[chain][0], self.buffers[chain][1], mate)

    def mate_start(self, chain):
        for chip in range(self.chips):
            self.buffers[chain][0][chip] = self.part(2 * chip + 1 - self.core, chain).astype(BF)
        self.mate_copy(chain).start()

    def mate_end(self, chain):
        self.mate_copy(chain).wait()
        for chip in range(self.chips):
            self.add(2 * chip + self.core, chain, self.buffers[chain][1][chip])

    def side_copies(self, chain):
        source, target = self.buffers[chain][2:4]
        return [
            self.copy(chain, 1 + step, source.at[step], target.at[step], {"dp": self.at(self.line, other, self.core)})
            for step, other in enumerate(self.others_side)
        ]

    def side_lines(self, chain):
        return [self.line] if self.line_first[chain] else range(LINE)

    def side_start(self, chain):
        for step, other in enumerate(self.others_side):
            for place, line in enumerate(self.side_lines(chain)):
                self.buffers[chain][2][step, place] = self.part(self.at(line, other, self.core), chain).astype(BF)
        for copy in self.side_copies(chain):
            copy.start()

    def side_end(self, chain):
        for step, copy in enumerate(self.side_copies(chain)):
            copy.wait()
            for place, line in enumerate(self.side_lines(chain)):
                self.add(self.at(line, self.column, self.core), chain, self.buffers[chain][3][step, place])

    def line_copies(self, chain):
        source, target = self.buffers[chain][4:6]
        return [
            self.copy(chain, self.columns + step, source.at[step], target.at[step], {"dp": self.at(other, self.column, self.core)})
            for step, other in enumerate(self.others_line)
        ]

    def line_columns(self, chain):
        return range(self.columns) if self.line_first[chain] else [self.column]

    def line_start(self, chain):
        for step, other in enumerate(self.others_line):
            for place, column in enumerate(self.line_columns(chain)):
                self.buffers[chain][4][step, place] = self.part(self.at(other, column, self.core), chain).astype(BF)
        for copy in self.line_copies(chain):
            copy.start()

    def line_end(self, chain):
        for step, copy in enumerate(self.line_copies(chain)):
            copy.wait()
            for place, column in enumerate(self.line_columns(chain)):
                self.add(self.at(self.line, column, self.core), chain, self.buffers[chain][5][step, place])

    def block_copies(self, chain):
        source, target = self.buffers[chain][6:8]
        return [
            self.copy(chain, self.columns + LINE - 1 + step, source, target.at[self.block], {"blk": other})
            for step, other in enumerate(self.others_block)
        ]

    def block_start(self, chain):
        own = self.part(self.me, chain).astype(BF)
        self.buffers[chain][6][...] = own
        self.buffers[chain][7][self.block] = own
        for copy in self.block_copies(chain):
            copy.start()

    def block_end(self, chain):
        for copy in self.block_copies(chain):
            copy.wait()
        parts = [self.buffers[chain][7][at].astype(F32) for at in range(self.count)]
        return functools.reduce(jnp.add, parts)


def finish_kernel(blocks, rows, tiles, shares, *refs):
    dq_refs, refs = refs[:blocks], refs[blocks:]
    dkv_refs, refs = refs[:blocks], refs[blocks:]
    (x_ref, gq_ref, gvalues_ref, gdepth_ref, w_ref, wc_ref, mine_ref, wide_ref, sum_ref), refs = refs[:9], refs[9:]
    (gh_ref, flat_out, sums_out), refs = refs[:3], refs[3:]
    held, refs = refs[: 2 * blocks + 5], refs[2 * blocks + 5 :]
    dq, dkv = held[:blocks], held[blocks : 2 * blocks]
    dk, dv = [ref.at[0] for ref in dkv], [ref.at[1] for ref in dkv]
    turned, gq, gvalues, gdepth, w = held[2 * blocks :]
    (load_sem, grads, window, bias_sum, rim_in, halo_in, halo, given, edge_send, edge_recv, given_send, given_recv), refs = refs[:12], refs[12:]
    shares.bind(refs)
    step = pl.program_id(0)
    count, sharers, shard = shares.count, shares.sharers, shares.rows
    chains = 3
    width, tokens = turned.shape
    block = shares.block
    sources = [x_ref, gq_ref] + list(dq_refs) + [ref.at[1] for ref in dkv_refs] + [ref.at[0] for ref in dkv_refs]
    targets = [turned, gq] + list(dq) + list(dv) + list(dk)
    sources += [gvalues_ref, gdepth_ref, w_ref.at[:, 0 : 3 * ATT], wc_ref.at[:, 2 * ATT : 3 * ATT]]
    targets += [gvalues, gdepth, w.at[:, 0 : 3 * ATT], w.at[:, 3 * ATT :]]
    loads = [
        pltpu.make_async_copy(source, target, load_sem.at[at])
        for at, (source, target) in enumerate(zip(sources, targets))
    ]
    by_chain = [loads[: 2 + blocks], loads[2 + blocks : 2 + 2 * blocks], loads[2 + 2 * blocks : 2 + 3 * blocks]]
    others = loads[2 + 3 * blocks :]

    def edge_copies():
        if count == 1:
            return []
        after, before = {"blk": lax.rem(block + 1, count)}, {"blk": lax.rem(block + count - 1, count)}
        plan = [
            (gvalues.at[tokens + 16 : tokens + 32], rim_in.at[0], after),
            (gvalues.at[0:16], rim_in.at[1], before),
            (gdepth.at[tokens - 16 : tokens], halo_in.at[0], after),
            (gdepth.at[0:16], halo_in.at[1], before),
        ]
        return [
            remote(source, target, edge_send.at[at], edge_recv.at[at], device)
            for at, (source, target, device) in enumerate(plan)
        ]

    def given_copies():
        return [
            remote(mine_ref, given.at[block], given_send.at[at], given_recv.at[at], {"blk": other})
            for at, other in enumerate(shares.others_block)
        ]

    @pl.when(step == 0)
    def start():
        shares.greet()
        for load in loads:
            load.start()
        bias_sum[...] = jnp.zeros_like(bias_sum)
        given[block] = mine_ref[...]

    def total(some):
        whole = [ref[...].astype(F32) for ref in some if ref.shape[0] == ATT]
        halves = [ref[...].astype(F32) for ref in some if ref.shape[0] < ATT]
        whole += [jnp.concatenate(halves[at : at + 2], axis=0) for at in range(0, len(halves), 2)]
        return functools.reduce(jnp.add, whole)

    def weights(chain):
        for load in by_chain[chain]:
            load.wait()
        if chain == 0:
            every = (total(dq).astype(BF).T.astype(F32) + gq[...].astype(F32)).astype(BF)
        else:
            every = total((dv, dk)[chain - 1]).astype(BF).T
        place = (0, 2, 1)[chain]
        grads[:, place * ATT : (place + 1) * ATT] = every
        if chain < 2:
            bias_sum[0:1, chain * ATT : (chain + 1) * ATT] = jnp.sum(every.astype(F32), axis=0, keepdims=True)
        made = mm(turned[...], every)
        lanes = slice(shares.lanes[chain].start, shares.lanes[chain].start + ATT)
        for owner in range(sharers):
            shares.total[owner, :, lanes] = made[owner * shard : (owner + 1) * shard]
        if chain == 1:
            extra = slice(2 * ATT, 2 * ATT + LANES)
            shares.total[:, :, extra] = jnp.zeros((sharers, shard, LANES), F32)
            for at in range(2 * ATT // LANES):
                values = bias_sum[0:1, at * LANES : (at + 1) * LANES]
                for owner in range(sharers):
                    shares.total[owner, at : at + 1, extra] = values

    def conv_grads():
        for load in others[2:]:
            load.wait()
        for copy in edge_copies():
            copy.wait()
        zero = jnp.zeros((16, ATT), F32)
        before, after = zero, zero
        if count > 1:
            before = jnp.where(block > 0, rim_in[0].astype(F32), zero)
            after = jnp.where(block < count - 1, rim_in[1].astype(F32), zero)
            nothing = jnp.zeros((16, width), BF)
            halo[0:16, :] = jnp.where(block > 0, halo_in[0], nothing)
            halo[16:32, :] = jnp.where(block < count - 1, halo_in[1], nothing)
        else:
            halo[...] = jnp.zeros_like(halo)
        lanes = slice(3 * ATT, 4 * ATT)
        grads[16 : tokens - 16, lanes] = gvalues[32:tokens, :]
        grads[0:16, lanes] = (gvalues[16:32, :].astype(F32) + before).astype(BF)
        grads[tokens - 16 : tokens, lanes] = (gvalues[tokens : tokens + 16, :].astype(F32) + after).astype(BF)

    for chain in range(chains):
        @pl.when(step == chain)
        def one(chain=chain):
            weights(chain)
            if chain == chains - 1:
                conv_grads()

    @pl.when(step >= chains)
    def by_tile():
        tile = step - chains
        first = pl.multiple_of(tile * rows, rows)
        fill_rows(window, gdepth, halo, tile, tiles, rows)
        back = mm_nt(grads[pl.ds(first, rows), :], w[...])
        for at in range(0, width, 128):
            some = slice(at, at + 128)
            depth = back[:, some] + sum_ref[:, some]
            for tap in range(KSIZE):
                depth = depth + window[20 - tap : 20 - tap + rows, some] * wide_ref[TAPS_AT + tap : TAPS_AT + tap + 1, some]
            gh_ref[:, some] = depth.astype(BF)

    def first_sends(unused):
        shares.met()
        for load in others[:2]:
            load.wait()
        for copy in edge_copies() + given_copies():
            copy.start()

    def late(eighths):
        return chains + eighths * tiles // 8

    plan = [
        (0, [(first_sends, 0), (shares.mate_start, 0)]),
        (1, [(shares.mate_end, 0), (shares.side_start, 0), (shares.mate_start, 1)]),
        (2, [(shares.mate_end, 1), (shares.side_start, 1), (shares.side_end, 0), (shares.line_start, 0), (shares.mate_start, 2)]),
        (late(0), [(shares.mate_end, 2), (shares.side_start, 2)]),
        (late(1), [(shares.side_end, 1), (shares.line_start, 1)]),
        (late(2), [(shares.line_end, 0), (shares.block_start, 0)]),
        (late(3), [(shares.side_end, 2), (shares.line_start, 2)]),
        (late(5), [(shares.line_end, 1), (shares.block_start, 1)]),
        (late(6), [(shares.line_end, 2), (shares.block_start, 2)]),
    ]
    for when in range(chains + tiles):
        actions = [action for place, some in plan if place == when for action in some]
        if actions:

            @pl.when(step == when)
            def act(actions=actions):
                for action, chain in actions:
                    action(chain)

    @pl.when(step == chains + tiles - 1)
    def end():
        for copy in given_copies():
            copy.wait()
        flat_out[...] = functools.reduce(jnp.add, [given[at].astype(F32) for at in range(count)])
        for chain in range(chains):
            sums_out[:, shares.lanes[chain]] = shares.block_end(chain)


def unpack_kernel(part, gh_ref, flat, sums, gh_out, gq_out, gk_out, gv_out, gc_out, gwd_out, gwu_out, gwn_out, gwp_out, gwk_out, gtaps_out, gkb_out, gbup_out, *refs):
    vector_outs, thin_outs = refs[:6], refs[6:10]
    shard = sums.shape[0]
    width = flat.shape[1]
    gh_out[...] = gh_ref[...]

    @pl.when(pl.program_id(0) == 0)
    def small():
        gwd_out[...] = flat[0:shard]
        quarter = shard // 2
        for group in range(2):
            for place in range(2):
                first = shard * (1 + group) + quarter * place
                gwu_out[group, :, place * width : (place + 1) * width] = flat[first : first + quarter]
            gwn_out[group] = flat[3 * shard : 5 * shard, group * ATT : (group + 1) * ATT]
        gwp_out[...] = flat[5 * shard : 6 * shard, 0:ATT]
        cells = flat[5 * shard : 6 * shard, ATT : ATT + LANES]
        turned = jnp.concatenate([cells, jnp.zeros((LANES - shard, LANES), F32)], axis=0).T
        for at, ref in enumerate(vector_outs):
            ref[...] = turned[at : at + 1, 0:shard].reshape(shard)
        gtaps_out[...] = turned[TAPS_AT : TAPS_AT + KSIZE, 0:shard]
        cells = flat[5 * shard : 6 * shard, ATT + LANES : ATT + 2 * LANES]
        gwk_out[...] = cells[0:part, 0 : HEADS * KSIZE]
        half = gbup_out.shape[0] // 2
        gbup_out[...] = jnp.concatenate(
            [cells[part : part + 1, 0:half], cells[part + 1 : part + 2, 0:half]], axis=1
        ).reshape(2 * half)
        gkb_out[...] = cells[part + 2 : part + 3, 0 : HEADS * KSIZE].reshape(HEADS * KSIZE)
        turned = jnp.concatenate([cells, jnp.zeros((LANES - shard, LANES), F32)], axis=0).T
        thin_outs[2][...] = turned[THIN_AT : THIN_AT + 1, 0:part].reshape(part)
        gq_out[...] = sums[:, 0:ATT]
        gv_out[...] = sums[:, ATT : 2 * ATT]
        gk_out[...] = sums[:, 2 * ATT + LANES :]
        gc_out[...] = flat[6 * shard : 7 * shard, 0:ATT]
        totals = jnp.concatenate(
            [sums[at : at + 1, 2 * ATT : 2 * ATT + LANES] for at in range(2 * ATT // LANES)], axis=1
        )
        lane = lax.broadcasted_iota(jnp.int32, (part, ATT), 1)
        row = lax.broadcasted_iota(jnp.int32, (part, ATT), 0)
        mine = (lane == lax.axis_index("dp") * part + row).astype(F32)
        thin_outs[3][...] = turned[THIN_AT + 1 : THIN_AT + 2, 0:part].reshape(part)
        for chain, ref in ((0, thin_outs[0]), (1, thin_outs[1])):
            picked = jnp.sum(mine * totals[:, chain * ATT : (chain + 1) * ATT], axis=1, keepdims=True)
            picked = jnp.broadcast_to(picked, (part, LANES))
            picked = jnp.concatenate([picked, jnp.zeros((LANES - part, LANES), F32)], axis=0).T
            ref[...] = picked[0:1, 0:part].reshape(part)


def unpack(grad_hidden, flat, sums, part, n_up):
    shard, width = sums.shape[0], flat.shape[1]
    shapes = [shaped((shard, ATT), F32)] * 4 + [
        shaped((shard, width), F32),
        shaped((2, shard // 2, 2 * width), F32),
        shaped((2, 2 * shard, ATT), F32),
        shaped((shard, ATT), F32),
        shaped((part, HEADS * KSIZE), F32),
        shaped((KSIZE, shard), F32),
        shaped((HEADS * KSIZE,), F32),
        shaped((n_up,), F32),
    ]
    shapes += [shaped((shard,), F32)] * 6 + [shaped((part,), F32)] * 4
    tokens = grad_hidden.shape[0]
    rows = math.gcd(tokens, 1024)
    return pl.pallas_call(
        functools.partial(unpack_kernel, part),
        grid=(tokens // rows,),
        in_specs=[rows_of(rows, width), all_of(flat.shape), all_of(sums.shape)],
        out_specs=[rows_of(rows, width)] + [all_of(v.shape) for v in shapes],
        out_shape=[shaped(grad_hidden.shape, BF)] + shapes,
        compiler_params=pltpu.CompilerParams(vmem_limit_bytes=60 * MIB),
        name="unpack",
    )(grad_hidden, flat, sums)


def finish(dqs, dkvs, turned, grad_query, grad_values, grad_depth, weight, mixed, mine, wide_vectors, grad_sum, sharers, count):
    width, tokens = turned.shape
    rows = math.gcd(tokens, 256)
    tiles = tokens // rows
    blocks = len(dqs)
    chains = 3
    shard = width // sharers
    shares = Shares(sharers, shard, [ATT, ATT + LANES, ATT], [False, False, False], count)
    late_rows = pl.BlockSpec((rows, width), lambda i: (jnp.maximum(i - chains, 0), 0))
    away = pl.BlockSpec(memory_space=pl.ANY)
    loaded = list(dqs) + list(dkvs) + [turned, grad_query, grad_values, grad_depth]
    args = loaded + [weight, mixed, mine, wide_vectors, grad_sum]
    shapes = [shaped(mine.shape, F32), shaped((shard, chains * ATT + LANES), F32)]
    return pl.pallas_call(
        functools.partial(finish_kernel, blocks, rows, tiles, shares),
        grid=(chains + tiles,),
        in_specs=[away] * (len(loaded) + 2) + [all_of(mine.shape), all_of(wide_vectors.shape), late_rows],
        out_specs=[late_rows] + [all_of(v.shape) for v in shapes],
        out_shape=[shaped((tokens, width), BF)] + shapes,
        scratch_shapes=[pltpu.VMEM(v.shape, v.dtype) for v in loaded]
        + [
            pltpu.VMEM((width, 4 * ATT), BF),
            pltpu.SemaphoreType.DMA((len(loaded) + len(dkvs) + 2,)),
            pltpu.VMEM((tokens, 4 * ATT), BF),
            pltpu.VMEM((rows + 32, width), F32),
            pltpu.VMEM((8, 2 * ATT), F32),
            pltpu.VMEM((2, 16, ATT), BF),
            pltpu.VMEM((2, 16, width), BF),
            pltpu.VMEM((32, width), BF),
            pltpu.VMEM((count,) + mine.shape, BF),
            pltpu.SemaphoreType.DMA((4,)),
            pltpu.SemaphoreType.DMA((4,)),
            pltpu.SemaphoreType.DMA((max(count - 1, 1),)),
            pltpu.SemaphoreType.DMA((max(count - 1, 1),)),
        ]
        + shares.scratch(),
        compiler_params=pltpu.CompilerParams(
            collective_id=1, has_side_effects=True, vmem_limit_bytes=62 * MIB
        ),
        cost_estimate=pl.CostEstimate(
            flops=4 * tokens * width * chains * ATT, bytes_accessed=30 * tokens * width, transcendentals=0
        ),
        name="finish",
    )(*args)


def shifted_from(value, axis, step):
    count = lax.axis_size(axis)
    return lax.ppermute(value, axis, [((i + step) % count, i) for i in range(count)])


def local(
    hidden,
    separators,
    out_grad,
    w_query,
    b_query,
    w_key,
    w_value,
    b_value,
    depth_kernel,
    w_point,
    b_keyconv,
    w_kernel,
    kernel_bias,
    w_convout,
    b_convout,
    w_dense,
    b_dense,
    gain_attn,
    shift_attn,
    w_up,
    b_up,
    w_down,
    b_down,
    gain_out,
    shift_out,
):
    count = lax.axis_size("blk")
    sharers = lax.axis_size("dp")
    x, cotangent = hidden[0], out_grad[0]
    tokens, width = x.shape
    part = b_query.shape[0]

    known = math.gcd(tokens, 512) if count == 2 else 0
    others = [shifted_from(x[known:], "blk", step) for step in range(1, count)]
    weight, wide_vectors, thin, bias_up, wt_kernel, bias_kernel, halo, late, early = gather_columns(
        [w_query, w_key, w_value],
        [b_dense, gain_attn, shift_attn, b_down, gain_out, shift_out],
        [b_query, b_value, b_keyconv, b_convout],
        depth_kernel.T,
        b_up,
        w_kernel,
        kernel_bias,
        w_up,
        w_down,
        x,
        sharers,
        count,
    )
    mixed = lax.all_gather(side_by_side([w_dense, w_convout, w_point]), "dp", axis=0, tiled=True)
    late = lax.all_gather(late, "dp", axis=0, tiled=False)

    query, query_t, *own = project([x], weight, thin, 3)
    keys = [own]
    outs, probs = [], []
    for step in range(count):
        if step > 0:
            keys.append(project(([early] if known else []) + [others[step - 1]], weight, thin, 2))
        key, key_t, value, value_t, norms = keys[step]
        out, prob = attend(separators, query_t, key, value_t, norms, count, step)
        outs.append(out)
        probs.append(prob)
        if step == 0:
            depth, keyconv, attn_key, kernt, kern, conv, values, rim = mix(
                count, x, halo, query, mixed, wide_vectors, thin, wt_kernel, bias_kernel
            )
            others, depth = lax.optimization_barrier((others, depth))
    output, grad_sum, grad_conv, grads_t, sides, (packed, g_vectors, gb_up) = middle(
        outs, conv, x, cotangent, mixed, late, wide_vectors, bias_up
    )
    grad_query_conv, grad_depth, grad_values, packed, turned = mix_back(
        count, x, halo, values, rim, grad_conv, kernt, kern, query, keyconv, attn_key, depth, mixed, wt_kernel, g_vectors, gb_up, packed
    )
    packed, sides = lax.optimization_barrier((packed, sides))
    mine = lax.psum_scatter(packed, "dp", scatter_dimension=0, tiled=False)

    dqs, dkvs = [], []
    for step in list(range(1, count)) + [0]:
        key, key_t, value, value_t, norms = keys[step]
        some = HEADS // 2 if step else HEADS
        for at in range(0, HEADS, some):
            dq, dkv = attend_back(probs[step], value, key_t, grads_t[step], sides[step], query_t, at, some)
            dqs.append(dq)
            dkvs.append(shifted_from(dkv, "blk", count - step) if step else dkv)
    grad_hidden, flat, sums = finish(
        dqs, dkvs, turned, grad_query_conv, grad_values, grad_depth, weight, mixed, mine, wide_vectors, grad_sum, sharers, count
    )
    results = unpack(grad_hidden, flat, sums, part, b_up.shape[0])
    grad_hidden, gw_query, gw_key, gw_value, gw_convout, gw_dense, gw_up, gw_down, gw_point, gw_kernel, g_taps, g_bias, gb_up = results[:13]
    g_vectors, thin = results[13:19], results[19:]
    return (
        output[None],
        grad_hidden[None],
        gw_query,
        thin[0],
        gw_key,
        gw_value,
        thin[1],
        g_taps.T,
        gw_point,
        thin[2],
        gw_kernel,
        g_bias,
        gw_convout,
        thin[3],
        gw_dense,
        g_vectors[0],
        g_vectors[1],
        g_vectors[2],
        gw_up,
        gb_up,
        gw_down,
        g_vectors[3],
        g_vectors[4],
        g_vectors[5],
    )


def solution(mesh):
    placed = (
        P("dp", "blk", None),
        P("dp"),
        P("dp", "blk", None),
        P("dp", None),
        P("dp"),
        P("dp", None),
        P("dp", None),
        P("dp"),
        P("dp", None),
        P("dp", None),
        P("dp"),
        P("dp", None),
        P(),
        P("dp", None),
        P("dp"),
        P("dp", None),
        P("dp"),
        P("dp"),
        P("dp"),
        P(None, "dp", None),
        P("dp"),
        P(None, "dp", None),
        P("dp"),
        P("dp"),
        P("dp"),
    )
    return jax.shard_map(
        local,
        mesh=mesh,
        in_specs=placed,
        out_specs=(
            P("dp", "blk", None),
            P("dp", "blk", None),
            P("dp", None),
            P("dp"),
            P("dp", None),
            P("dp", None),
            P("dp"),
            P("dp", None),
            P("dp", None),
            P("dp"),
            P("dp", None),
            P(),
            P("dp", None),
            P("dp"),
            P("dp", None),
            P("dp"),
            P("dp"),
            P("dp"),
            P(None, "dp", None),
            P("dp"),
            P(None, "dp", None),
            P("dp"),
            P("dp"),
            P("dp"),
        ),
        check_vma=False,
    )
```

```python
import functools, math
import jax, jax.numpy as jnp
from jax import lax
from jax.experimental import pallas as pl
from jax.experimental.pallas import tpu as pltpu
from jax.sharding import PartitionSpec as P

HEADS = 6
HD = 64
KSIZE = 9
REACH = 4
ATT = 384
EPS = 1e-12
BF = jnp.bfloat16
F32 = jnp.float32
MIB = 2**20
EXCLUDED = 2.0**100
SAFE_SCORE = 50.0


def mm(left, right):
    return jnp.dot(left, right, preferred_element_type=F32)


def mm_nt(left, right):
    return lax.dot_general(left, right, (((1,), (1,)), ((), ())), preferred_element_type=F32)


def mm_tn(left, right):
    return lax.dot_general(left, right, (((0,), (0,)), ((), ())), preferred_element_type=F32)


def in_lanes(rows, columns):
    lane = lax.broadcasted_iota(jnp.int32, (rows, 128), 1)
    out = jnp.zeros((rows, 128), F32)
    for at, column in enumerate(columns):
        out = jnp.where(lane == at, column, out)
    return out.astype(BF)


def in_rows(columns, rows):
    row = lax.broadcasted_iota(jnp.int32, (16, columns), 0)
    out = jnp.zeros((16, columns), F32)
    for at, values in enumerate(rows):
        out = jnp.where(row == at, values, out)
    return out.astype(BF)


def three_parts(values):
    high = values.astype(BF).astype(F32)
    rest = values - high
    middle = rest.astype(BF).astype(F32)
    return high, middle, (rest - middle).astype(BF).astype(F32)


def put_head(ref, head, values):
    odd = lax.rem(head, 2) == 1
    none = jnp.zeros_like(values)
    ref[0:HD, :] = jnp.where(odd, none, values)
    ref[HD : 2 * HD, :] = jnp.where(odd, values, none)


def attend_kernel(keys, queries, chunk, count, step, at_ref, q_ref, k_ref, v_ref, norm_ref, o_ref, p_ref, key_side, query_side):
    head, tile = pl.program_id(0), pl.program_id(1)
    separator, block = at_ref[0], lax.axis_index("blk")
    first_query = block * keys
    first_key = lax.rem(block + step, count) * keys

    @pl.when((head == 0) & (tile == 0))
    def start():
        position = first_key + lax.broadcasted_iota(jnp.int32, (keys, 128), 0)
        late = (position >= separator).astype(F32)
        key_side[...] = in_lanes(keys, [1.0 - late, late, 1.0, 1.0, 1.0])
        query_side[2 * HD + 16 :, :] = jnp.zeros((2 * HD - 16, queries), BF)

    put_head(query_side, head, q_ref[...])
    position = first_query + tile * queries + lax.broadcasted_iota(jnp.int32, (16, queries), 1)
    late = (position >= separator).astype(F32)
    excluded = [-EXCLUDED * late, -EXCLUDED * (1.0 - late)]
    query_side[2 * HD : 2 * HD + 16, :] = in_rows(queries, excluded)
    o_ref[0, HD + 8 : HD + 16, :] = jnp.zeros((8, queries), F32)
    wide = q_ref[...].astype(F32)
    largest = jnp.max(jnp.sum(wide * wide, axis=0, keepdims=True)) * jnp.max(norm_ref[...])

    def scores(at):
        part = slice(at * chunk, (at + 1) * chunk)
        return mm(
            jnp.concatenate([k_ref[part, :], key_side[part, :]], axis=1), query_side[...]
        )

    @pl.when(jnp.logical_not(largest <= SAFE_SCORE * SAFE_SCORE))
    def shifted():
        best = jnp.full((1, queries), -4.0 * EXCLUDED, F32)
        for at in range(keys // chunk):
            best = jnp.maximum(best, jnp.max(scores(at), axis=0, keepdims=True))
        parts = three_parts(jnp.where(best < -0.5 * EXCLUDED, 0.0, best))
        query_side[2 * HD : 2 * HD + 16, :] = in_rows(queries, excluded + [-part for part in parts])
        o_ref[0, HD + 8 : HD + 16, :] = jnp.broadcast_to(
            jnp.where(best < -0.5 * EXCLUDED, best, parts[0] + parts[1] + parts[2]), (8, queries)
        )

    ones = in_rows(chunk, [1.0])
    total = jnp.zeros((HD + 16, queries), F32)
    for at in range(keys // chunk):
        part = slice(at * chunk, (at + 1) * chunk)
        probs = jnp.exp(scores(at)).astype(BF)
        p_ref[0, part, :] = probs
        total = total + mm(jnp.concatenate([v_ref[:, part], ones], axis=0), probs)
    o_ref[0, 0 : HD + 8, :] = total[0 : HD + 8, :]


def attend(at, query_t, key, value_t, norms, count, step):
    tokens, keys = query_t.shape[1], key.shape[0]
    queries, chunk = math.gcd(tokens, 2048), math.gcd(keys, 1024)
    return pl.pallas_call(
        functools.partial(attend_kernel, keys, queries, chunk, count, step),
        grid=(HEADS, tokens // queries),
        in_specs=[
            pl.BlockSpec(memory_space=pltpu.SMEM),
            pl.BlockSpec((HD, queries), lambda h, i: (h, i)),
            pl.BlockSpec((keys, 2 * HD), lambda h, i: (0, h // 2)),
            pl.BlockSpec((HD, keys), lambda h, i: (h, 0)),
            pl.BlockSpec(norms.shape, lambda h, i: (0, 0)),
        ],
        out_specs=[
            pl.BlockSpec((1, HD + 16, queries), lambda h, i: (h, 0, i)),
            pl.BlockSpec((1, keys, queries), lambda h, i: (h, 0, i)),
        ],
        out_shape=[
            jax.ShapeDtypeStruct((HEADS, HD + 16, tokens), F32),
            jax.ShapeDtypeStruct((HEADS, keys, tokens), BF),
        ],
        scratch_shapes=[pltpu.VMEM((keys, 128), BF), pltpu.VMEM((4 * HD, queries), BF)],
        compiler_params=pltpu.CompilerParams(vmem_limit_bytes=56 * MIB),
        cost_estimate=pl.CostEstimate(
            flops=ATT * keys,
            bytes_accessed=2 * HEADS * keys,
            transcendentals=0,
        ),
        name="attend",
    )(at, query_t, key, value_t, norms)


def attend_back_kernel(first, keys, queries, chunk, p_ref, v_ref, kt_ref, g_ref, side_ref, q_ref, dq_ref, dkv_ref, value_side, grad_side, dk_sum, dv_sum):
    head, tile = pl.program_id(0), pl.program_id(1)

    @pl.when((head == 0) & (tile == 0))
    def start():
        value_side[...] = in_lanes(chunk, [1.0, 1.0, 1.0])
        grad_side[2 * HD + 16 :, :] = jnp.zeros((2 * HD - 16, queries), BF)

    @pl.when(tile == 0)
    def fresh():
        dk_sum[...] = jnp.zeros_like(dk_sum)
        dv_sum[...] = jnp.zeros_like(dv_sum)

    put_head(grad_side, first + head, g_ref[...])
    grad_side[2 * HD : 2 * HD + 16, :] = side_ref[0]
    total = jnp.zeros((HD, queries), F32)
    for at in range(keys // chunk):
        part = slice(at * chunk, (at + 1) * chunk)
        probs = p_ref[0, part, :]
        spread = mm(jnp.concatenate([v_ref[part, :], value_side[...]], axis=1), grad_side[...])
        grad_scores = (probs.astype(F32) * spread).astype(BF)
        dv_sum[:, part] += mm_nt(g_ref[...], probs)
        dk_sum[:, part] += mm_nt(q_ref[...], grad_scores)
        total = total + mm(kt_ref[:, part], grad_scores)
    dq_ref[...] = (total * (HD**-0.5)).astype(BF)

    @pl.when(tile == pl.num_programs(1) - 1)
    def finish():
        dkv_ref[0] = dk_sum[...].astype(BF)
        dkv_ref[1] = dv_sum[...].astype(BF)


def attend_back(probs, value, key_t, grad_t, side, query_t, first, heads):
    tokens, keys = query_t.shape[1], value.shape[0]
    queries, chunk = math.gcd(tokens, 1024), math.gcd(keys, 256)
    by_token = pl.BlockSpec((HD, queries), lambda h, i: (first + h, i))
    by_key = pl.BlockSpec((HD, keys), lambda h, i: (first + h, 0))
    return pl.pallas_call(
        functools.partial(attend_back_kernel, first, keys, queries, chunk),
        grid=(heads, tokens // queries),
        in_specs=[
            pl.BlockSpec((1, keys, queries), lambda h, i: (first + h, 0, i)),
            pl.BlockSpec((keys, 2 * HD), lambda h, i: (0, (first + h) // 2)),
            by_key,
            by_token,
            pl.BlockSpec((1, 16, queries), lambda h, i: (first + h, 0, i)),
            by_token,
        ],
        out_specs=[
            pl.BlockSpec((HD, queries), lambda h, i: (h, i)),
            pl.BlockSpec((2, HD, keys), lambda h, i: (0, h, 0)),
        ],
        out_shape=[
            jax.ShapeDtypeStruct((heads * HD, tokens), BF),
            jax.ShapeDtypeStruct((2, heads * HD, keys), BF),
        ],
        scratch_shapes=[
            pltpu.VMEM((chunk, 128), BF),
            pltpu.VMEM((4 * HD, queries), BF),
            pltpu.VMEM((HD, keys), F32),
            pltpu.VMEM((HD, keys), F32),
        ],
        compiler_params=pltpu.CompilerParams(vmem_limit_bytes=56 * MIB),
        cost_estimate=pl.CostEstimate(
            flops=32 * heads * HD * tokens * keys,
            bytes_accessed=2 * heads * tokens * keys,
            transcendentals=0,
        ),
        name="attend_back",
    )(probs, value, key_t, grad_t, side, query_t)


def all_of(shape):
    return pl.BlockSpec(shape, lambda *at: (0,) * len(shape))


def rows_of(rows, width):
    return pl.BlockSpec((rows, width), lambda i: (i, 0))


def columns_of(height, columns):
    return pl.BlockSpec((height, columns), lambda i: (0, i))


def run_tiles(kernel, name, steps, inputs, outputs, scratch, flops, aliases=None):
    args, in_specs = zip(*inputs)
    shapes, out_specs = zip(*outputs)
    size = sum(math.prod(v.shape) * v.dtype.itemsize for v in args + shapes)
    return pl.pallas_call(
        kernel,
        grid=(steps,),
        in_specs=list(in_specs),
        out_specs=list(out_specs),
        out_shape=list(shapes),
        scratch_shapes=scratch,
        input_output_aliases=aliases or {},
        compiler_params=pltpu.CompilerParams(vmem_limit_bytes=62 * MIB),
        cost_estimate=pl.CostEstimate(flops=flops, bytes_accessed=size, transcendentals=0),
        name=name,
    )(*args)


def shaped(shape, dtype):
    return jax.ShapeDtypeStruct(shape, dtype)


def project_kernel(parts, sources, *refs):
    x_refs, refs = refs[:sources], refs[sources:]
    (w_ref, thin_ref), refs = refs[:2], refs[2:]
    norm_ref = refs[2 * parts]
    skip = (3 - parts) * ATT

    @pl.when(pl.program_id(0) == 0)
    def start():
        norm_ref[...] = jnp.zeros_like(norm_ref)

    x = x_refs[-1][...]
    if sources == 2:
        x = jnp.where(pl.program_id(0) == 0, x_refs[0][...], x)
    plain = mm(x, w_ref[:, skip:])
    for part in range(parts):
        own = slice(part * ATT, (part + 1) * ATT)
        bias = 0.0
        if part != parts - 2:
            at = 1 if part == parts - 1 else 0
            bias = thin_ref[at : at + 1, :]
        low = (plain[:, own] + bias).astype(BF)
        refs[2 * part][...] = low
        across = low.T
        if part == parts - 2:
            wide = across.astype(F32)
            for head in range(HEADS):
                cells = wide[head * HD : (head + 1) * HD]
                size = jnp.sum(cells * cells, axis=0, keepdims=True)
                norm_ref[...] = jnp.maximum(norm_ref[...], size)
        if part < parts - 2:
            across = (across.astype(F32) * (HD**-0.5)).astype(BF)
        refs[2 * part + 1][...] = across


def project(sources, weight, thin, parts):
    tokens, width = sum(x.shape[0] for x in sources), sources[0].shape[1]
    wide = 3 * ATT
    tile = math.gcd(tokens, 512)
    late = len(sources) - 1
    inputs = [(sources[-1], pl.BlockSpec((tile, width), lambda i: (jnp.maximum(i - late, 0), 0)))]
    if late:
        inputs.insert(0, (sources[0], all_of((tile, width))))
    outputs = []
    for part in range(parts):
        outputs.append((shaped((tokens, ATT), BF), rows_of(tile, ATT)))
        outputs.append((shaped((ATT, tokens), BF), columns_of(ATT, tile)))
    outputs.append((shaped((8, tile), F32), all_of((8, tile))))
    return run_tiles(
        functools.partial(project_kernel, parts, len(sources)),
        "project",
        tokens // tile,
        inputs
        + [
            (weight, all_of((width, wide))),
            (thin, all_of(thin.shape)),
        ],
        outputs,
        [],
        2 * tokens * width * parts * ATT,
    )


def fill_rows(window, x_ref, halo_ref, tile, tiles, rows):
    first = tile * rows
    tokens = x_ref.shape[0]
    before = x_ref[pl.ds(pl.multiple_of(jnp.maximum(first - 16, 0), 16), 16), :]
    after = x_ref[pl.ds(pl.multiple_of(jnp.minimum(first + rows, tokens - 16), 16), 16), :]
    window[0:16, :] = jnp.where(tile == 0, halo_ref[0:16, :], before).astype(window.dtype)
    window[16 : 16 + rows, :] = x_ref[pl.ds(pl.multiple_of(first, rows), rows), :].astype(window.dtype)
    window[16 + rows :, :] = jnp.where(
        tile == tiles - 1, halo_ref[16:32, :], after
    ).astype(window.dtype)


def fill_window(window, x_ref, halo_ref, tile, rows):
    fill_rows(window, x_ref, halo_ref, tile, pl.num_programs(0), rows)


def fill_spread(spread):
    row = lax.broadcasted_iota(jnp.int32, (128, ATT), 0)
    head = lax.broadcasted_iota(jnp.int32, (128, ATT), 1) // HD
    for tap in range(KSIZE):
        spread[:, tap * ATT : (tap + 1) * ATT] = (row == tap * 8 + head).astype(F32).astype(BF)


def mix_kernel(rows, count, x_ref, halo_ref, q_ref, wc_ref, wp_ref, wide_ref, thin_ref, wk_ref, bk_ref, depth_ref, keyconv_ref, attn_ref, kernt_ref, kern_ref, conv_ref, out_ref, rim_ref, window, conv_window, spread):
    tile = pl.program_id(0)
    last = pl.num_programs(0) - 1

    @pl.when(tile == 0)
    def start():
        fill_spread(spread)

    fill_window(window, x_ref, halo_ref, tile, rows)
    width = window.shape[1]
    for at in range(0, width, 128):
        some = slice(at, at + 128)
        total = jnp.zeros((rows, 128), F32)
        for tap in range(KSIZE):
            total = total + window[12 + tap : 12 + tap + rows, some] * wide_ref[TAPS_AT + tap : TAPS_AT + tap + 1, some]
        depth_ref[:, some] = total.astype(BF)
    position = (
        lax.axis_index("blk") * x_ref.shape[0] + tile * rows - 16 + lax.broadcasted_iota(jnp.int32, (rows + 32, ATT), 0)
    )
    inside = (position >= 0) & (position < count * x_ref.shape[0])
    values = mm(window[...].astype(BF), wc_ref[...]) + thin_ref[3:4, :]
    values = jnp.where(inside, values, 0.0).astype(BF)
    out_ref[...] = values[16 : 16 + rows]

    @pl.when(tile == 0)
    def first_rim():
        rim_ref[0:16, :] = values[0:16]

    @pl.when(tile == last)
    def last_rim():
        rim_ref[16:32, :] = values[16 + rows :]

    conv_window[...] = values.astype(F32)
    keyconv = mm(depth_ref[...], wp_ref[...]) + thin_ref[2:3, :]
    keyconv_ref[...] = keyconv
    attn_key = (keyconv * q_ref[...].astype(F32)).astype(BF)
    attn_ref[...] = attn_key
    logits = mm_nt(wk_ref[...], attn_key) + bk_ref[:, BIAS_AT : BIAS_AT + 1]
    slabs = [logits[8 * tap : 8 * tap + 8] for tap in range(KSIZE)]
    best = functools.reduce(jnp.maximum, slabs)
    slabs = [jnp.exp(slab - best) for slab in slabs]
    share = 1.0 / functools.reduce(jnp.add, slabs)
    slabs = [slab * share for slab in slabs]
    kernt = jnp.concatenate(slabs + [jnp.zeros((128 - 8 * KSIZE, rows), F32)], axis=0)
    kernt_ref[...] = kernt[0 : 8 * KSIZE]
    kern = kernt.astype(BF).T
    kern_ref[...] = kern
    for at in range(0, ATT, LANES):
        some = slice(at, at + LANES)
        total = jnp.zeros((rows, LANES), F32)
        for tap in range(KSIZE):
            first = tap * ATT + at
            total = total + mm(kern, spread[:, first : first + LANES]) * conv_window[12 + tap : 12 + tap + rows, some]
        conv_ref[:, some] = total.astype(BF)


def column_block(weight, place):
    return pl.BlockSpec((weight.shape[0], ATT), lambda i: (0, place))


def mix(count, x, halo, query, weight, wide_vectors, thin, w_kernel, kernel_bias):
    tokens, width = x.shape
    rows = math.gcd(tokens, 512)
    whole = [(weight, column_block(weight, 2)), (weight, column_block(weight, 3))]
    whole += [(v, all_of(v.shape)) for v in (wide_vectors, thin, w_kernel, kernel_bias)]
    return run_tiles(
        functools.partial(mix_kernel, rows, count),
        "mix",
        tokens // rows,
        [
            (x, all_of(x.shape)),
            (halo, all_of(halo.shape)),
            (query, rows_of(rows, ATT)),
        ]
        + whole,
        [
            (shaped((tokens, width), BF), rows_of(rows, width)),
            (shaped((tokens, ATT), F32), rows_of(rows, ATT)),
            (shaped((tokens, ATT), BF), rows_of(rows, ATT)),
            (shaped((8 * KSIZE, tokens), F32), columns_of(8 * KSIZE, rows)),
            (shaped((tokens, 128), BF), rows_of(rows, 128)),
            (shaped((tokens, ATT), BF), rows_of(rows, ATT)),
            (shaped((tokens, ATT), BF), rows_of(rows, ATT)),
            (shaped((32, ATT), BF), all_of((32, ATT))),
        ],
        [
            pltpu.VMEM((rows + 32, width), F32),
            pltpu.VMEM((rows + 32, ATT), F32),
            pltpu.VMEM((128, KSIZE * ATT), BF),
        ],
        4 * tokens * width * ATT * 4,
    )


def normal(values):
    centre = values - jnp.mean(values, axis=-1, keepdims=True)
    scale = lax.rsqrt(jnp.mean(centre * centre, axis=-1, keepdims=True) + EPS)
    return centre * scale, scale


def normal_back(grad, unit, scale):
    return scale * (
        grad
        - jnp.mean(grad, axis=-1, keepdims=True)
        - unit * jnp.mean(grad * unit, axis=-1, keepdims=True)
    )


def gelu_parts(values):
    share = 0.5 + 0.5 * lax.erf(values * math.sqrt(0.5))
    bell = jnp.exp2(values * values * (-0.5 * math.log2(math.e)))
    return values * share, share + values * (bell * (1.0 / math.sqrt(2.0 * math.pi)))


def middle_kernel(blocks, rows, units, *refs):
    o_refs, refs = refs[:blocks], refs[blocks:]
    (conv_ref, x_ref, og_ref, wd_ref, late_ref, vec_ref, bu_ref), refs = refs[:7], refs[7:]
    (out_ref, sum_ref, gconv_ref), refs = refs[:3], refs[3:]
    g_refs, refs = refs[:blocks], refs[blocks:]
    side_refs, refs = refs[:blocks], refs[blocks:]
    (packed_ref, gvec_ref, gbu_ref, wd_sum, wu_sum, wn_sum, acts, slopes, staged, sems, wu_ref) = refs
    tile = pl.program_id(0)
    hidden_units = wu_ref.shape[1]
    low_rows = late_ref.shape[1] // 2

    def down_rows(at, lanes):
        return late_ref[at // low_rows : (at + units) // low_rows, low_rows:, lanes].reshape(units, ATT)

    groups = 2
    inner = ATT
    outer = hidden_units // groups

    @pl.when(tile == 0)
    def start():
        for ref in (wd_sum, wu_sum, wn_sum, gvec_ref, gbu_ref):
            ref[...] = jnp.zeros_like(ref)
        owners, high, width = late_ref.shape
        quarter = high // 8
        for pair in range(0, owners, 2):
            both = [late_ref[owner, 0 : high // 2].astype(F32) for owner in (pair, pair + 1)]
            for place in range(4):
                some = [cells[place * quarter : (place + 1) * quarter] for cells in both]
                wu_ref[pair * quarter : (pair + 2) * quarter, place * width : (place + 1) * width] = (
                    jnp.concatenate(some, axis=0).astype(BF)
                )

    shifts = [ref[:, HD + 8 : HD + 9, :] for ref in o_refs]
    top = functools.reduce(jnp.maximum, shifts)
    weights = [jnp.exp(shift - top) for shift in shifts]
    mass = functools.reduce(jnp.add, [w * ref[:, HD : HD + 1, :] for w, ref in zip(weights, o_refs)])
    weights = [w / mass for w in weights]
    heads = functools.reduce(jnp.add, [w * ref[:, 0:HD, :] for w, ref in zip(weights, o_refs)])
    att_t = heads.reshape(ATT, rows).astype(BF)
    conv = conv_ref[...]
    vec = [vec_ref[at : at + 1, :] for at in range(6)]
    dense = mm(att_t.T, wd_ref[0:ATT, :]) + mm(conv, wd_ref[ATT:, :]) + vec[0]
    unit_one, scale_one = normal(dense + x_ref[...].astype(F32))
    normed = unit_one * vec[1] + vec[2]
    low = normed.astype(BF)
    downs = []
    for group in range(groups):
        mine = low[:, group * inner : (group + 1) * inner]
        down = jnp.zeros((rows, inner), F32)
        for at in range(0, outer, units):
            here = slice(group * outer + at, group * outer + at + units)
            upward = mm(mine, wu_ref[:, here]) + bu_ref[:, here]
            act, slope = gelu_parts(upward)
            act = act.astype(BF)
            acts[:, here] = act
            slopes[:, here] = slope.astype(BF)
            down = down + mm(act, down_rows(at, slice(group * inner, (group + 1) * inner)))
        downs.append(down)
    unit_two, scale_two = normal(jnp.concatenate(downs, axis=1) + vec[3] + normed)
    out_ref[...] = (unit_two * vec[4] + vec[5]).astype(BF)
    og = og_ref[...].astype(F32)
    gvec_ref[4:5, :] += jnp.sum(og * unit_two, axis=0, keepdims=True)
    gvec_ref[5:6, :] += jnp.sum(og, axis=0, keepdims=True)
    grad_two = normal_back(og * vec[4], unit_two, scale_two)
    grad_down = grad_two.astype(BF)
    gvec_ref[3:4, :] += jnp.sum(grad_down.astype(F32), axis=0, keepdims=True)
    backs = []
    for group in range(groups):
        lanes = slice(group * inner, (group + 1) * inner)
        mine, grads = low[:, lanes], grad_down[:, lanes]
        mine_t = mine.T
        back = jnp.zeros((rows, inner), F32)
        for at in range(0, outer, units):
            here = slice(group * outer + at, group * outer + at + units)
            grad_act = mm_nt(grads, down_rows(at, lanes))
            grad_up = (grad_act * slopes[:, here].astype(F32)).astype(BF)
            gbu_ref[0:1, here] += jnp.sum(grad_up.astype(F32), axis=0, keepdims=True)
            wn_sum[at : at + units, lanes] += mm_tn(acts[:, here], grads)
            wu_sum[:, here] += mm(mine_t, grad_up)
            back = back + mm_nt(grad_up, wu_ref[:, here])
        backs.append(back)
    grad_normed = grad_two + jnp.concatenate(backs, axis=1)
    gvec_ref[1:2, :] += jnp.sum(grad_normed * unit_one, axis=0, keepdims=True)
    gvec_ref[2:3, :] += jnp.sum(grad_normed, axis=0, keepdims=True)
    grad_one = normal_back(grad_normed * vec[1], unit_one, scale_one)
    sum_ref[...] = grad_one
    grad_dense = grad_one.astype(BF)
    gvec_ref[0:1, :] += jnp.sum(grad_dense.astype(F32), axis=0, keepdims=True)
    wd_sum[0:ATT, :] += mm(att_t, grad_dense)
    wd_sum[ATT:, :] += mm_tn(conv, grad_dense)
    gconv_ref[...] = mm_nt(grad_dense, wd_ref[ATT:, :]).astype(BF)
    grad_att = mm_nt(wd_ref[0:ATT, :], grad_dense).astype(BF).astype(F32).reshape(HEADS, HD, rows)
    for weight, g_ref, side_ref in zip(weights, g_refs, side_refs):
        share = (grad_att * weight).astype(BF)
        g_ref[...] = share.reshape(ATT, rows)
        delta = -jnp.sum(share.astype(F32) * heads, axis=1, keepdims=True)
        row = lax.broadcasted_iota(jnp.int32, (HEADS, 16, rows), 1)
        side = jnp.zeros((HEADS, 16, rows), F32)
        for at, part in enumerate(three_parts(delta)):
            side = jnp.where(row == at, part, side)
        side_ref[...] = side.astype(BF)

    @pl.when(tile == pl.num_programs(0) - 1)
    def finish():
        slots = staged.shape[0]
        sharers = packed_ref.shape[0]
        shard = wd_sum.shape[0] // sharers
        quarter = shard // 2
        width = wd_sum.shape[1]
        copies = []
        for owner in range(sharers):
            slot = owner % slots
            if owner >= slots:
                copies[owner - slots].wait()
            staged[slot, 0:shard] = wd_sum[owner * shard : (owner + 1) * shard].astype(BF)
            some = wu_sum[owner * quarter : (owner + 1) * quarter]
            for group in range(groups):
                pair = [some[:, at : at + width] for at in (2 * group * width, (2 * group + 1) * width)]
                staged[slot, (1 + group) * shard : (2 + group) * shard] = jnp.concatenate(pair, axis=0).astype(BF)
            some = wn_sum[owner * 2 * shard : (owner + 1) * 2 * shard]
            staged[slot, 3 * shard : 5 * shard] = some.astype(BF)
            copy = pltpu.make_async_copy(
                staged.at[slot], packed_ref.at[owner, 0 : 5 * shard], sems.at[owner]
            )
            copy.start()
            copies.append(copy)
        for copy in copies[sharers - slots :]:
            copy.wait()


def middle(outs, conv, x, out_grad, w_dense, late, vectors, b_up):
    tokens, width = x.shape
    sharers = late.shape[0]
    shard = width // sharers
    units = b_up.shape[1]
    up, down = (width // 2, units), (units // 2, width)
    rows = math.gcd(tokens, 512)
    blocks = len(outs)
    heads = pl.BlockSpec((HEADS, HD + 16, rows), lambda i: (0, 0, i))
    side = pl.BlockSpec((HEADS, 16, rows), lambda i: (0, 0, i))
    single = pl.Buffered(1)
    once = [
        (w_dense, pl.BlockSpec((width, width), lambda i: (0, 0), pipeline_mode=single)),
        (late, pl.BlockSpec(late.shape, lambda i: (0, 0, 0), pipeline_mode=single)),
    ]
    once += [(v, all_of(v.shape)) for v in (vectors, b_up)]
    results = run_tiles(
        functools.partial(middle_kernel, blocks, rows, 768),
        "middle",
        tokens // rows,
        [(o, heads) for o in outs]
        + [
            (conv, rows_of(rows, ATT)),
            (x, rows_of(rows, width)),
            (out_grad, rows_of(rows, width)),
        ]
        + once,
        [
            (shaped((tokens, width), BF), rows_of(rows, width)),
            (shaped((tokens, width), F32), rows_of(rows, width)),
            (shaped((tokens, ATT), BF), rows_of(rows, ATT)),
        ]
        + [(shaped((ATT, tokens), BF), columns_of(ATT, rows))] * blocks
        + [(shaped((HEADS, 16, tokens), BF), side)] * blocks
        + [
            (shaped((sharers, 7 * shard, width), BF), pl.BlockSpec(memory_space=pl.ANY)),
            (shaped((8, width), F32), all_of((8, width))),
            (shaped((8, units), F32), all_of((8, units))),
        ],
        [
            pltpu.VMEM((width, width), F32),
            pltpu.VMEM(up, F32),
            pltpu.VMEM(down, F32),
            pltpu.VMEM((rows, units), BF),
            pltpu.VMEM((rows, units), BF),
            pltpu.VMEM((6, 5 * shard, width), BF),
            pltpu.SemaphoreType.DMA((sharers,)),
            pltpu.VMEM(up, BF),
        ],
        6 * tokens * (width * width + 2 * math.prod(up)),
    )
    output, grad_sum, grad_conv = results[:3]
    return output, grad_sum, grad_conv, results[3 : 3 + blocks], results[3 + blocks : 3 + 2 * blocks], results[3 + 2 * blocks :]


def mix_back_kernel(rows, count, x_ref, halo_ref, values_ref, rim_ref, gconv_ref, kernt_ref, kern_ref, q_ref, keyconv_ref, attn_ref, depth_ref, wp_ref, wk_ref, gvec_ref, gbu_ref, unused, gq_ref, gdepth_ref, gvalues_ref, packed_ref, turned_ref, window, conv_window, summed, products, spread, wp_sum, wc_sum, values_sum, gwk_ref, gbias_ref, gtaps_ref, turn_wide, turn_thin, side, staged, sem):
    tile = pl.program_id(0)

    @pl.when(tile == 0)
    def start():
        fill_spread(spread)
        for ref in (values_sum, wp_sum, wc_sum, gwk_ref, gbias_ref, gtaps_ref, turn_wide, turn_thin):
            ref[...] = jnp.zeros_like(ref)

    fill_window(window, x_ref, halo_ref, tile, rows)
    fill_window(conv_window, values_ref, rim_ref, tile, rows)
    summed[...] = jnp.zeros_like(summed)
    grad_conv = gconv_ref[...].astype(F32)
    for tap in range(KSIZE):
        here = slice(tap * ATT, (tap + 1) * ATT)
        there = slice(12 + tap, 12 + tap + rows)
        products[:, here] = (grad_conv * conv_window[there, :]).astype(BF)
        summed[there, :] += mm(kern_ref[...], spread[:, here]) * grad_conv
    first = pl.multiple_of(tile * rows, rows)
    values_sum[pl.ds(first, rows + 32), :] += summed[...]
    turned = x_ref[pl.ds(first, rows), :].T
    turned_ref[...] = turned
    edges = [slice(0, 16), slice(rows + 16, rows + 32)]
    edge_x = jnp.concatenate([window[edge, :] for edge in edges], axis=0).astype(BF)
    edge_grads = jnp.concatenate([summed[edge, :] for edge in edges], axis=0).astype(BF)
    wc_sum[...] += mm(turned, summed[16 : 16 + rows, :].astype(BF)) + mm_tn(edge_x, edge_grads)
    grad_kernel = mm_nt(spread[...], products[...])
    slabs = [slice(8 * tap, 8 * tap + 8) for tap in range(KSIZE)]
    kernels = [kernt_ref[slab, :] for slab in slabs]
    mean = functools.reduce(jnp.add, [k * grad_kernel[slab] for k, slab in zip(kernels, slabs)])
    grad_logits = jnp.concatenate(
        [k * (grad_kernel[slab] - mean) for k, slab in zip(kernels, slabs)], axis=0
    ).astype(BF)
    wide_logits = grad_logits.astype(F32)
    gbias_ref[...] += jnp.concatenate(
        [
            jnp.broadcast_to(jnp.sum(wide_logits, axis=1, keepdims=True), (8 * KSIZE, 128)),
            jnp.zeros((8, 128), F32),
        ],
        axis=0,
    )
    gwk_ref[0 : 8 * KSIZE, :] += mm(grad_logits, attn_ref[...])
    grad_attn = mm_tn(grad_logits, wk_ref[...]).astype(BF).astype(F32)
    grad_keyconv = (grad_attn * q_ref[...].astype(F32)).astype(BF)
    gq_ref[...] = (grad_attn * keyconv_ref[...]).astype(BF)
    gwk_ref[8 * KSIZE : 8 * KSIZE + 1, :] += jnp.sum(grad_keyconv.astype(F32), axis=0, keepdims=True)
    wp_sum[...] += mm_tn(depth_ref[...], grad_keyconv)
    grad_depth = mm_nt(grad_keyconv, wp_ref[...]).astype(BF)
    gdepth_ref[...] = grad_depth
    wide = grad_depth.astype(F32)
    for at in range(0, window.shape[1], 128):
        some = slice(at, at + 128)
        for tap in range(KSIZE):
            gtaps_ref[tap : tap + 1, some] += jnp.sum(
                wide[:, some] * window[12 + tap : 12 + tap + rows, some], axis=0, keepdims=True
            )

    @pl.when(tile == pl.num_programs(0) - 1)
    def finish():
        gvalues_ref[...] = values_sum[...].astype(BF)
        tokens, block = x_ref.shape[0], lax.axis_index("blk")
        sums = [
            jnp.sum(gvalues_ref[at:end, :].astype(F32), axis=0, keepdims=True)
            for at, end in ((0, 16), (16, tokens + 16), (tokens + 16, tokens + 32))
        ]
        b_sum = sums[1] + jnp.where(block > 0, sums[0], 0.0) + jnp.where(block < count - 1, sums[2], 0.0)
        sharers, shard, width = staged.shape[0], staged.shape[1] // 2, staged.shape[2]
        part = ATT // sharers
        half = gbu_ref.shape[1] // sharers // 2
        turn_wide[0:6, :] = gvec_ref[0:6, :]
        turn_wide[TAPS_AT : TAPS_AT + KSIZE, :] = gtaps_ref[0:KSIZE, :]
        vectors = turn_wide[...].T
        for h in range(HEADS):
            for j in range(KSIZE):
                turn_wide[h * KSIZE + j : h * KSIZE + j + 1, 0:LANES] = gbias_ref[j * 8 + h : j * 8 + h + 1, :]
                turn_thin[h * KSIZE + j : h * KSIZE + j + 1, :] = gwk_ref[j * 8 + h : j * 8 + h + 1, :]
        bias = turn_wide[:, 0:LANES].T[0:1]
        turn_thin[THIN_AT : THIN_AT + 1, :] = gwk_ref[8 * KSIZE : 8 * KSIZE + 1, :]
        turn_thin[THIN_AT + 1 : THIN_AT + 2, :] = b_sum
        kernels = turn_thin[...].T
        side[...] = jnp.zeros_like(side)
        for owner in range(sharers):
            staged[owner, 0:shard, 0:ATT] = wp_sum[owner * shard : (owner + 1) * shard].astype(BF)
            staged[owner, shard:, 0:ATT] = wc_sum[owner * shard : (owner + 1) * shard].astype(BF)
            staged[owner, shard:, ATT:] = jnp.zeros((shard, width - ATT), BF)
            staged[owner, 0:shard, ATT : ATT + LANES] = vectors[owner * shard : (owner + 1) * shard].astype(BF)
            side[0:part, :] = kernels[owner * part : (owner + 1) * part]
            for place in range(2):
                first = (2 * owner + place) * half
                side[part + place : part + place + 1, 0:half] = gbu_ref[0:1, first : first + half]
            side[part + 2 : part + 3, :] = bias
            staged[owner, 0:shard, ATT + LANES : ATT + 2 * LANES] = side[...].astype(BF)
            staged[owner, 0:shard, ATT + 2 * LANES :] = jnp.zeros((shard, width - ATT - 2 * LANES), BF)
        copy = pltpu.make_async_copy(staged, packed_ref.at[:, 5 * shard : 7 * shard], sem)
        copy.start()
        copy.wait()


def mix_back(count, x, halo, values, rim, grad_conv, kernt, kern, query, keyconv, attn_key, depth, weight, w_kernel, g_vectors, gb_up, packed):
    tokens, width = x.shape
    sharers, shard = packed.shape[0], packed.shape[1] // 7
    away = pl.BlockSpec(memory_space=pl.ANY)
    rows = math.gcd(tokens, 512)
    by_rows = [(v, rows_of(rows, v.shape[1])) for v in (kern, query, keyconv, attn_key, depth)]
    return run_tiles(
        functools.partial(mix_back_kernel, rows, count),
        "mix_back",
        tokens // rows,
        [(v, all_of(v.shape)) for v in (x, halo, values, rim)]
        + [(grad_conv, rows_of(rows, ATT)), (kernt, columns_of(8 * KSIZE, rows))]
        + by_rows
        + [(weight, column_block(weight, 3))]
        + [(v, all_of(v.shape)) for v in (w_kernel, g_vectors, gb_up)]
        + [(packed, away)],
        [
            (shaped((tokens, ATT), BF), rows_of(rows, ATT)),
            (shaped((tokens, width), BF), rows_of(rows, width)),
            (shaped((tokens + 32, ATT), BF), all_of((tokens + 32, ATT))),
            (shaped(packed.shape, BF), away),
            (shaped((width, tokens), BF), columns_of(width, rows)),
        ],
        [
            pltpu.VMEM((rows + 32, width), F32),
            pltpu.VMEM((rows + 32, ATT), F32),
            pltpu.VMEM((rows + 32, ATT), F32),
            pltpu.VMEM((rows, KSIZE * ATT), BF),
            pltpu.VMEM((128, KSIZE * ATT), BF),
            pltpu.VMEM((width, ATT), F32),
            pltpu.VMEM((width, ATT), F32),
            pltpu.VMEM((tokens + 32, ATT), F32),
            pltpu.VMEM((8 * KSIZE + 8, ATT), F32),
            pltpu.VMEM((8 * KSIZE + 8, LANES), F32),
            pltpu.VMEM((16, width), F32),
            pltpu.VMEM((LANES, width), F32),
            pltpu.VMEM((LANES, ATT), F32),
            pltpu.VMEM((shard, LANES), F32),
            pltpu.VMEM((sharers, 2 * shard, width), BF),
            pltpu.SemaphoreType.DMA(()),
        ],
        4 * tokens * width * ATT * 4,
        {15: 3},
    )


def side_by_side_kernel(*refs):
    at = 0
    for ref in refs[:-1]:
        refs[-1][:, at : at + ref.shape[1]] = ref[...].astype(BF)
        at += ref.shape[1]


def side_by_side(parts):
    out = shaped((parts[0].shape[0], sum(v.shape[1] for v in parts)), BF)
    return run_tiles(
        side_by_side_kernel, "side_by_side", 1, [(v, all_of(v.shape)) for v in parts], [(out, all_of(out.shape))], [], 0
    )[0]


MESH = pl.DeviceIdType.MESH
LINE = 4
LANES = 128
TAPS_AT = 16
THIN_AT = 64
BIAS_AT = 100


def my_place(sharers):
    columns = sharers // (2 * LINE)
    me = lax.axis_index("dp")
    return me, me // (2 * columns), lax.rem(me // 2, columns), lax.rem(me, 2), columns


def greet(partners):
    barrier = pltpu.get_barrier_semaphore()
    for partner in partners:
        pl.semaphore_signal(barrier, inc=1, device_id=partner, device_id_type=MESH)
    return barrier


def remote(source, target, send_sem, recv_sem, device):
    return pltpu.make_async_remote_copy(
        src_ref=source,
        dst_ref=target,
        send_sem=send_sem,
        recv_sem=recv_sem,
        device_id=device,
        device_id_type=MESH,
    )


def gather_kernel(sharers, count, part, early, *refs):
    w_refs, refs = refs[:3], refs[3:]
    vector_refs, refs = refs[:6], refs[6:]
    thin_refs, refs = refs[:4], refs[4:]
    (taps_ref, up_ref, kernel_ref, bias_ref, wu_ref, wn_ref, head_ref, tail_ref, early_ref), refs = refs[:9], refs[9:]
    (out_ref, wide_ref, thin_ref, bias_up_ref, wk_ref, bk_ref, halo_ref, late_out, early_out), refs = refs[:9], refs[9:]
    rows, side, flat, thin_flat, edges, send_sem, recv_sem, edge_send, edge_recv = refs
    me, line, column, core, columns = my_place(sharers)
    block = lax.axis_index("blk")
    shard = out_ref.shape[1]
    base = len(w_refs) * ATT
    half = up_ref.shape[0] // 2

    def at(line, column, core):
        return (line * columns + column) * 2 + core

    lines = [lax.rem(line + step, LINE) for step in range(1, LINE)]
    sides = [lax.rem(column + step, columns) for step in range(1, columns)]
    partners = [{"dp": at(other, column, core)} for other in lines]
    across = [{"dp": at(line, other, core)} for other in sides]
    mate = {"dp": at(line, column, 1 - core)}
    ends = []
    if count > 1:
        ends = [{"blk": lax.rem(block + 1, count)}, {"blk": lax.rem(block + count - 1, count)}]
    barrier = greet(partners + across + [mate] + ends)
    for place, ref in enumerate(w_refs):
        out_ref[me, :, place * ATT : (place + 1) * ATT] = ref[...].astype(BF)
    rows[...] = jnp.zeros_like(rows)
    for place, ref in enumerate(vector_refs):
        rows[place : place + 1, 0:shard] = ref[...].reshape(1, shard)
    for place, ref in enumerate(thin_refs):
        rows[THIN_AT + place : THIN_AT + place + 1, 0:part] = ref[...].reshape(1, part)
    rows[TAPS_AT : TAPS_AT + KSIZE, 0:shard] = taps_ref[...]
    rows[BIAS_AT : BIAS_AT + 1, 0 : HEADS * KSIZE] = bias_ref[...].reshape(1, HEADS * KSIZE)
    rows[...] = rows[...].T
    side[...] = rows[0:shard]
    out_ref[me, :, base : base + LANES] = side[...].astype(BF)
    side[...] = jnp.zeros_like(side)
    side[0:part, 0 : HEADS * KSIZE] = kernel_ref[...]
    side[part : part + 1, 0:half] = up_ref[0:half].reshape(1, half)
    side[part + 1 : part + 2, 0:half] = up_ref[half:].reshape(1, half)
    out_ref[me, :, base + LANES :] = side[...].astype(BF)
    width = late_out.shape[1]
    for group in range(2):
        pair = [wu_ref[group, :, place * width : (place + 1) * width] for place in range(2)]
        late_out[group * shard : (group + 1) * shard] = jnp.concatenate(pair, axis=0).astype(BF)
        late_out[2 * shard :, group * ATT : (group + 1) * ATT] = wn_ref[group].astype(BF)
    if not early:
        early_out[...] = early_ref[...]
    pl.semaphore_wait(barrier, len(partners) + len(across) + 1 + len(ends))
    sends = []

    def sending(number, owner, device):
        return remote(out_ref.at[owner], out_ref.at[owner], send_sem.at[number], recv_sem.at[owner], device)

    def pass_on(owner, devices, when=None):
        for device in devices:
            sending(len(sends), owner, device).start()
            sends.append((owner, device, when))

    def arrived(owner):
        pltpu.make_async_copy(out_ref.at[owner], out_ref.at[owner], recv_sem.at[owner]).wait()

    pass_on(me, across + [mate])
    edge_copies = []
    for place, (ref, device) in enumerate(zip((tail_ref, head_ref), ends)):
        edge_copies.append(remote(ref, edges.at[place], edge_send.at[place], edge_recv.at[place], device))
    if early:
        edge_copies.append(remote(early_ref, early_out, edge_send.at[2], edge_recv.at[2], ends[0]))
    for copy in edge_copies:
        copy.start()
    for step in range(1, LINE):
        for way in (1, -1):
            from_here = (line - way * (step - 1) >= 0) & (line - way * (step - 1) < LINE)
            goes = from_here & (line + way >= 0) & (line + way < LINE)
            owner, onward = at(line - way * (step - 1), column, core), [{"dp": at(line + way, column, core)}]

            @pl.when(goes)
            def forward():
                pass_on(owner, onward, goes)

        for way in (1, -1):
            comes = (line - way * step >= 0) & (line - way * step < LINE)
            owner = at(line - way * step, column, core)

            @pl.when(comes)
            def take():
                arrived(owner)
                pass_on(owner, across + [mate], comes)

    for some in sides:
        for other in [line] + lines:
            owner = at(other, some, core)
            arrived(owner)
            pass_on(owner, [mate])
    nothing = jnp.zeros((16, halo_ref.shape[1]), BF)
    halo_ref[0:16, :] = nothing
    halo_ref[16:32, :] = nothing
    if count > 1:
        for copy in edge_copies:
            copy.wait()
        halo_ref[0:16, :] = jnp.where(block > 0, edges[0], nothing)
        halo_ref[16:32, :] = jnp.where(block < count - 1, edges[1], nothing)
    for j in range(KSIZE):
        for h in range(8):
            source = h * KSIZE + j if h < HEADS else 120
            bk_ref[j * 8 + h : j * 8 + h + 1, :] = rows[source : source + 1, :]
    for some in [column] + sides:
        for other in [line] + lines:
            arrived(at(other, some, 1 - core))
    for number, (owner, device, when) in enumerate(sends):
        if when is None:
            sending(number, owner, device).wait_send()
        else:
            pl.when(when)(lambda: sending(number, owner, device).wait_send())
    for owner in range(sharers):
        cells = out_ref[owner, :, base : base + LANES].astype(F32)
        flat[owner * shard : (owner + 1) * shard, :] = cells
        thin_flat[owner * part : (owner + 1) * part, :] = cells[0:part]
    turned = flat[...].T
    wide_ref[...] = turned[0 : wide_ref.shape[0]]
    thin_ref[...] = thin_flat[...].T[THIN_AT : THIN_AT + 8]
    for owner in range(sharers):
        cells = out_ref[owner, :, base + LANES :].astype(F32)
        thin_flat[owner * part : (owner + 1) * part, :] = cells[0:part]
        for place in range(2):
            first = (2 * owner + place) * half
            bias_up_ref[0:1, first : first + half] = cells[part + place : part + place + 1, 0:half]
    turned = thin_flat[...].T
    slabs = []
    for j in range(KSIZE):
        slabs += [turned[h * KSIZE + j : h * KSIZE + j + 1] for h in range(HEADS)]
        slabs.append(jnp.zeros((8 - HEADS, ATT), F32))
    wk_ref[...] = jnp.concatenate(slabs, axis=0).astype(BF)


def gather_columns(weights, vectors, thin, taps, b_up, w_kernel, kernel_bias, w_up, w_down, x, sharers, count):
    shard, part = weights[0].shape[0], thin[0].shape[0]
    tokens, width = x.shape
    early = count == 2
    first_rows = math.gcd(tokens, 512) if early else 16
    wide = len(weights) * ATT + 2 * LANES
    columns = sharers // (2 * LINE)
    copies = columns + 2 * (LINE - 1) * (1 + columns) + LINE * (columns - 1)
    args = list(weights) + list(vectors) + list(thin) + [taps, b_up, w_kernel, kernel_bias, w_up, w_down]
    shapes = [
        shaped((sharers, shard, wide), BF),
        shaped((32, width), F32),
        shaped((8, ATT), F32),
        shaped((1, sharers * b_up.shape[0]), F32),
        shaped((8 * KSIZE, ATT), BF),
        shaped((8 * KSIZE, LANES), F32),
        shaped((32, width), BF),
        shaped((4 * shard, width), BF),
        shaped((first_rows, width), BF),
    ]
    out, *rest = pl.pallas_call(
        functools.partial(gather_kernel, sharers, count, part, early),
        grid=(1,),
        in_specs=[all_of(v.shape) for v in args]
        + [
            pl.BlockSpec((16, width), lambda i: (0, 0)),
            pl.BlockSpec((16, width), lambda i: (tokens // 16 - 1, 0)),
            pl.BlockSpec((first_rows, width), lambda i: (0, 0)),
        ],
        out_specs=[all_of(v.shape) for v in shapes],
        out_shape=shapes,
        scratch_shapes=[
            pltpu.VMEM((LANES, LANES), F32),
            pltpu.VMEM((shard, LANES), F32),
            pltpu.VMEM((width, LANES), F32),
            pltpu.VMEM((ATT, LANES), F32),
            pltpu.VMEM((2, 16, width), BF),
            pltpu.SemaphoreType.DMA((copies,)),
            pltpu.SemaphoreType.DMA((sharers,)),
            pltpu.SemaphoreType.DMA((3,)),
            pltpu.SemaphoreType.DMA((3,)),
        ],
        compiler_params=pltpu.CompilerParams(
            collective_id=0, has_side_effects=True, vmem_limit_bytes=60 * MIB
        ),
        name="gather_columns",
    )(*args, x, x, x)
    return (out.reshape(sharers * shard, wide), *rest)


class Shares:
    def __init__(self, sharers, rows, widths, line_first, count):
        self.sharers, self.rows, self.widths, self.line_first, self.count = sharers, rows, widths, line_first, count
        self.columns = sharers // (2 * LINE)
        self.chips = sharers // 2
        ends = [sum(widths[: at + 1]) for at in range(len(widths))]
        self.lanes = [slice(end - width, end) for end, width in zip(ends, widths)]
        self.wide = ends[-1]
        self.copies = 1 + self.columns - 1 + LINE - 1 + count - 1

    def scratch(self):
        shapes = []
        for width, line_first in zip(self.widths, self.line_first):
            side = (self.columns - 1, 1 if line_first else LINE, self.rows, width)
            line = (LINE - 1, self.columns if line_first else 1, self.rows, width)
            shapes += [pltpu.VMEM((self.chips, self.rows, width), BF)] * 2
            shapes += [pltpu.VMEM(side, BF)] * 2 + [pltpu.VMEM(line, BF)] * 2
            shapes += [pltpu.VMEM((self.rows, width), BF), pltpu.VMEM((self.count, self.rows, width), BF)]
        sems = len(self.widths) * self.copies
        return shapes + [
            pltpu.VMEM((self.sharers, self.rows, self.wide), F32),
            pltpu.SemaphoreType.DMA((sems,)),
            pltpu.SemaphoreType.DMA((sems,)),
        ]

    def bind(self, refs):
        chains = len(self.widths)
        self.buffers = [refs[8 * chain : 8 * chain + 8] for chain in range(chains)]
        self.total, self.send_sem, self.recv_sem = refs[8 * chains : 8 * chains + 3]
        self.me, self.line, self.column, self.core, unused = my_place(self.sharers)
        self.block = lax.axis_index("blk")
        self.others_line = [lax.rem(self.line + step, LINE) for step in range(1, LINE)]
        self.others_side = [lax.rem(self.column + step, self.columns) for step in range(1, self.columns)]
        self.others_block = [lax.rem(self.block + step, self.count) for step in range(1, self.count)]

    def at(self, line, column, core):
        return (line * self.columns + column) * 2 + core

    def greet(self):
        devices = [{"dp": self.at(self.line, self.column, 1 - self.core)}]
        devices += [{"dp": self.at(self.line, other, self.core)} for other in self.others_side]
        devices += [{"dp": self.at(other, self.column, self.core)} for other in self.others_line]
        devices += [{"blk": other} for other in self.others_block]
        greet(devices)

    def met(self):
        pl.semaphore_wait(pltpu.get_barrier_semaphore(), 1 + self.columns - 1 + LINE - 1 + self.count - 1)

    def copy(self, chain, number, source, target, device):
        sem = chain * self.copies + number
        return remote(source, target, self.send_sem.at[sem], self.recv_sem.at[sem], device)

    def part(self, owner, chain):
        return self.total[owner, :, self.lanes[chain]]

    def add(self, owner, chain, values):
        self.total[owner, :, self.lanes[chain]] += values.astype(F32)

    def mate_copy(self, chain):
        mate = {"dp": self.at(self.line, self.column, 1 - self.core)}
        return self.copy(chain, 0, self.buffers[chain][0], self.buffers[chain][1], mate)

    def mate_start(self, chain):
        for chip in range(self.chips):
            self.buffers[chain][0][chip] = self.part(2 * chip + 1 - self.core, chain).astype(BF)
        self.mate_copy(chain).start()

    def mate_end(self, chain):
        self.mate_copy(chain).wait()
        for chip in range(self.chips):
            self.add(2 * chip + self.core, chain, self.buffers[chain][1][chip])

    def side_copies(self, chain):
        source, target = self.buffers[chain][2:4]
        return [
            self.copy(chain, 1 + step, source.at[step], target.at[step], {"dp": self.at(self.line, other, self.core)})
            for step, other in enumerate(self.others_side)
        ]

    def side_lines(self, chain):
        return [self.line] if self.line_first[chain] else range(LINE)

    def side_start(self, chain):
        for step, other in enumerate(self.others_side):
            for place, line in enumerate(self.side_lines(chain)):
                self.buffers[chain][2][step, place] = self.part(self.at(line, other, self.core), chain).astype(BF)
        for copy in self.side_copies(chain):
            copy.start()

    def side_end(self, chain):
        for step, copy in enumerate(self.side_copies(chain)):
            copy.wait()
            for place, line in enumerate(self.side_lines(chain)):
                self.add(self.at(line, self.column, self.core), chain, self.buffers[chain][3][step, place])

    def line_copies(self, chain):
        source, target = self.buffers[chain][4:6]
        return [
            self.copy(chain, self.columns + step, source.at[step], target.at[step], {"dp": self.at(other, self.column, self.core)})
            for step, other in enumerate(self.others_line)
        ]

    def line_columns(self, chain):
        return range(self.columns) if self.line_first[chain] else [self.column]

    def line_start(self, chain):
        for step, other in enumerate(self.others_line):
            for place, column in enumerate(self.line_columns(chain)):
                self.buffers[chain][4][step, place] = self.part(self.at(other, column, self.core), chain).astype(BF)
        for copy in self.line_copies(chain):
            copy.start()

    def line_end(self, chain):
        for step, copy in enumerate(self.line_copies(chain)):
            copy.wait()
            for place, column in enumerate(self.line_columns(chain)):
                self.add(self.at(self.line, column, self.core), chain, self.buffers[chain][5][step, place])

    def block_copies(self, chain):
        source, target = self.buffers[chain][6:8]
        return [
            self.copy(chain, self.columns + LINE - 1 + step, source, target.at[self.block], {"blk": other})
            for step, other in enumerate(self.others_block)
        ]

    def block_start(self, chain):
        own = self.part(self.me, chain).astype(BF)
        self.buffers[chain][6][...] = own
        self.buffers[chain][7][self.block] = own
        for copy in self.block_copies(chain):
            copy.start()

    def block_end(self, chain):
        for copy in self.block_copies(chain):
            copy.wait()
        parts = [self.buffers[chain][7][at].astype(F32) for at in range(self.count)]
        return functools.reduce(jnp.add, parts)


def finish_kernel(blocks, rows, tiles, shares, *refs):
    dq_refs, refs = refs[:blocks], refs[blocks:]
    dkv_refs, refs = refs[:blocks], refs[blocks:]
    (x_ref, gq_ref, gvalues_ref, gdepth_ref, w_ref, wc_ref, mine_ref, wide_ref, sum_ref), refs = refs[:9], refs[9:]
    (gh_ref, flat_out, sums_out), refs = refs[:3], refs[3:]
    held, refs = refs[: 2 * blocks + 5], refs[2 * blocks + 5 :]
    dq, dkv = held[:blocks], held[blocks : 2 * blocks]
    dk, dv = [ref.at[0] for ref in dkv], [ref.at[1] for ref in dkv]
    turned, gq, gvalues, gdepth, w = held[2 * blocks :]
    (load_sem, grads, window, bias_sum, rim_in, halo_in, halo, given, edge_send, edge_recv, given_send, given_recv), refs = refs[:12], refs[12:]
    shares.bind(refs)
    step = pl.program_id(0)
    count, sharers, shard = shares.count, shares.sharers, shares.rows
    chains = 3
    width, tokens = turned.shape
    block = shares.block
    sources = [x_ref, gq_ref] + list(dq_refs) + [ref.at[1] for ref in dkv_refs] + [ref.at[0] for ref in dkv_refs]
    targets = [turned, gq] + list(dq) + list(dv) + list(dk)
    sources += [gvalues_ref, gdepth_ref, w_ref.at[:, 0 : 3 * ATT], wc_ref.at[:, 2 * ATT : 3 * ATT]]
    targets += [gvalues, gdepth, w.at[:, 0 : 3 * ATT], w.at[:, 3 * ATT :]]
    loads = [
        pltpu.make_async_copy(source, target, load_sem.at[at])
        for at, (source, target) in enumerate(zip(sources, targets))
    ]
    by_chain = [loads[: 2 + blocks], loads[2 + blocks : 2 + 2 * blocks], loads[2 + 2 * blocks : 2 + 3 * blocks]]
    others = loads[2 + 3 * blocks :]

    def edge_copies():
        if count == 1:
            return []
        after, before = {"blk": lax.rem(block + 1, count)}, {"blk": lax.rem(block + count - 1, count)}
        plan = [
            (gvalues.at[tokens + 16 : tokens + 32], rim_in.at[0], after),
            (gvalues.at[0:16], rim_in.at[1], before),
            (gdepth.at[tokens - 16 : tokens], halo_in.at[0], after),
            (gdepth.at[0:16], halo_in.at[1], before),
        ]
        return [
            remote(source, target, edge_send.at[at], edge_recv.at[at], device)
            for at, (source, target, device) in enumerate(plan)
        ]

    def given_copies():
        return [
            remote(mine_ref, given.at[block], given_send.at[at], given_recv.at[at], {"blk": other})
            for at, other in enumerate(shares.others_block)
        ]

    @pl.when(step == 0)
    def start():
        shares.greet()
        for load in loads:
            load.start()
        bias_sum[...] = jnp.zeros_like(bias_sum)
        given[block] = mine_ref[...]

    def total(some):
        whole = [ref[...].astype(F32) for ref in some if ref.shape[0] == ATT]
        halves = [ref[...].astype(F32) for ref in some if ref.shape[0] < ATT]
        whole += [jnp.concatenate(halves[at : at + 2], axis=0) for at in range(0, len(halves), 2)]
        return functools.reduce(jnp.add, whole)

    def weights(chain):
        for load in by_chain[chain]:
            load.wait()
        if chain == 0:
            every = (total(dq).astype(BF).T.astype(F32) + gq[...].astype(F32)).astype(BF)
        else:
            every = total((dv, dk)[chain - 1]).astype(BF).T
        place = (0, 2, 1)[chain]
        grads[:, place * ATT : (place + 1) * ATT] = every
        if chain < 2:
            bias_sum[0:1, chain * ATT : (chain + 1) * ATT] = jnp.sum(every.astype(F32), axis=0, keepdims=True)
        made = mm(turned[...], every)
        lanes = slice(shares.lanes[chain].start, shares.lanes[chain].start + ATT)
        for owner in range(sharers):
            shares.total[owner, :, lanes] = made[owner * shard : (owner + 1) * shard]
        if chain == 1:
            extra = slice(2 * ATT, 2 * ATT + LANES)
            shares.total[:, :, extra] = jnp.zeros((sharers, shard, LANES), F32)
            for at in range(2 * ATT // LANES):
                values = bias_sum[0:1, at * LANES : (at + 1) * LANES]
                for owner in range(sharers):
                    shares.total[owner, at : at + 1, extra] = values

    def conv_grads():
        for load in others[2:]:
            load.wait()
        for copy in edge_copies():
            copy.wait()
        zero = jnp.zeros((16, ATT), F32)
        before, after = zero, zero
        if count > 1:
            before = jnp.where(block > 0, rim_in[0].astype(F32), zero)
            after = jnp.where(block < count - 1, rim_in[1].astype(F32), zero)
            nothing = jnp.zeros((16, width), BF)
            halo[0:16, :] = jnp.where(block > 0, halo_in[0], nothing)
            halo[16:32, :] = jnp.where(block < count - 1, halo_in[1], nothing)
        else:
            halo[...] = jnp.zeros_like(halo)
        lanes = slice(3 * ATT, 4 * ATT)
        grads[16 : tokens - 16, lanes] = gvalues[32:tokens, :]
        grads[0:16, lanes] = (gvalues[16:32, :].astype(F32) + before).astype(BF)
        grads[tokens - 16 : tokens, lanes] = (gvalues[tokens : tokens + 16, :].astype(F32) + after).astype(BF)

    for chain in range(chains):
        @pl.when(step == chain)
        def one(chain=chain):
            weights(chain)
            if chain == chains - 1:
                conv_grads()

    @pl.when(step >= chains)
    def by_tile():
        tile = step - chains
        first = pl.multiple_of(tile * rows, rows)
        fill_rows(window, gdepth, halo, tile, tiles, rows)
        back = mm_nt(grads[pl.ds(first, rows), :], w[...])
        for at in range(0, width, 128):
            some = slice(at, at + 128)
            depth = back[:, some] + sum_ref[:, some]
            for tap in range(KSIZE):
                depth = depth + window[20 - tap : 20 - tap + rows, some] * wide_ref[TAPS_AT + tap : TAPS_AT + tap + 1, some]
            gh_ref[:, some] = depth.astype(BF)

    def first_sends(unused):
        shares.met()
        for load in others[:2]:
            load.wait()
        for copy in edge_copies() + given_copies():
            copy.start()

    def late(eighths):
        return chains + eighths * tiles // 8

    plan = [
        (0, [(first_sends, 0), (shares.mate_start, 0)]),
        (1, [(shares.mate_end, 0), (shares.side_start, 0), (shares.mate_start, 1)]),
        (2, [(shares.mate_end, 1), (shares.side_start, 1), (shares.side_end, 0), (shares.line_start, 0), (shares.mate_start, 2)]),
        (late(0), [(shares.mate_end, 2), (shares.side_start, 2)]),
        (late(1), [(shares.side_end, 1), (shares.line_start, 1)]),
        (late(2), [(shares.line_end, 0), (shares.block_start, 0)]),
        (late(3), [(shares.side_end, 2), (shares.line_start, 2)]),
        (late(5), [(shares.line_end, 1), (shares.block_start, 1)]),
        (late(6), [(shares.line_end, 2), (shares.block_start, 2)]),
    ]
    for when in range(chains + tiles):
        actions = [action for place, some in plan if place == when for action in some]
        if actions:

            @pl.when(step == when)
            def act(actions=actions):
                for action, chain in actions:
                    action(chain)

    @pl.when(step == chains + tiles - 1)
    def end():
        for copy in given_copies():
            copy.wait()
        flat_out[...] = functools.reduce(jnp.add, [given[at].astype(F32) for at in range(count)])
        for chain in range(chains):
            sums_out[:, shares.lanes[chain]] = shares.block_end(chain)


def unpack_kernel(part, gh_ref, flat, sums, gh_out, gq_out, gk_out, gv_out, gc_out, gwd_out, gwu_out, gwn_out, gwp_out, gwk_out, gtaps_out, gkb_out, gbup_out, *refs):
    vector_outs, thin_outs = refs[:6], refs[6:10]
    shard = sums.shape[0]
    width = flat.shape[1]
    gh_out[...] = gh_ref[...]

    @pl.when(pl.program_id(0) == 0)
    def small():
        gwd_out[...] = flat[0:shard]
        quarter = shard // 2
        for group in range(2):
            for place in range(2):
                first = shard * (1 + group) + quarter * place
                gwu_out[group, :, place * width : (place + 1) * width] = flat[first : first + quarter]
            gwn_out[group] = flat[3 * shard : 5 * shard, group * ATT : (group + 1) * ATT]
        gwp_out[...] = flat[5 * shard : 6 * shard, 0:ATT]
        cells = flat[5 * shard : 6 * shard, ATT : ATT + LANES]
        turned = jnp.concatenate([cells, jnp.zeros((LANES - shard, LANES), F32)], axis=0).T
        for at, ref in enumerate(vector_outs):
            ref[...] = turned[at : at + 1, 0:shard].reshape(shard)
        gtaps_out[...] = turned[TAPS_AT : TAPS_AT + KSIZE, 0:shard]
        cells = flat[5 * shard : 6 * shard, ATT + LANES : ATT + 2 * LANES]
        gwk_out[...] = cells[0:part, 0 : HEADS * KSIZE]
        half = gbup_out.shape[0] // 2
        gbup_out[...] = jnp.concatenate(
            [cells[part : part + 1, 0:half], cells[part + 1 : part + 2, 0:half]], axis=1
        ).reshape(2 * half)
        gkb_out[...] = cells[part + 2 : part + 3, 0 : HEADS * KSIZE].reshape(HEADS * KSIZE)
        turned = jnp.concatenate([cells, jnp.zeros((LANES - shard, LANES), F32)], axis=0).T
        thin_outs[2][...] = turned[THIN_AT : THIN_AT + 1, 0:part].reshape(part)
        gq_out[...] = sums[:, 0:ATT]
        gv_out[...] = sums[:, ATT : 2 * ATT]
        gk_out[...] = sums[:, 2 * ATT + LANES :]
        gc_out[...] = flat[6 * shard : 7 * shard, 0:ATT]
        totals = jnp.concatenate(
            [sums[at : at + 1, 2 * ATT : 2 * ATT + LANES] for at in range(2 * ATT // LANES)], axis=1
        )
        lane = lax.broadcasted_iota(jnp.int32, (part, ATT), 1)
        row = lax.broadcasted_iota(jnp.int32, (part, ATT), 0)
        mine = (lane == lax.axis_index("dp") * part + row).astype(F32)
        thin_outs[3][...] = turned[THIN_AT + 1 : THIN_AT + 2, 0:part].reshape(part)
        for chain, ref in ((0, thin_outs[0]), (1, thin_outs[1])):
            picked = jnp.sum(mine * totals[:, chain * ATT : (chain + 1) * ATT], axis=1, keepdims=True)
            picked = jnp.broadcast_to(picked, (part, LANES))
            picked = jnp.concatenate([picked, jnp.zeros((LANES - part, LANES), F32)], axis=0).T
            ref[...] = picked[0:1, 0:part].reshape(part)


def unpack(grad_hidden, flat, sums, part, n_up):
    shard, width = sums.shape[0], flat.shape[1]
    shapes = [shaped((shard, ATT), F32)] * 4 + [
        shaped((shard, width), F32),
        shaped((2, shard // 2, 2 * width), F32),
        shaped((2, 2 * shard, ATT), F32),
        shaped((shard, ATT), F32),
        shaped((part, HEADS * KSIZE), F32),
        shaped((KSIZE, shard), F32),
        shaped((HEADS * KSIZE,), F32),
        shaped((n_up,), F32),
    ]
    shapes += [shaped((shard,), F32)] * 6 + [shaped((part,), F32)] * 4
    tokens = grad_hidden.shape[0]
    rows = math.gcd(tokens, 1024)
    return pl.pallas_call(
        functools.partial(unpack_kernel, part),
        grid=(tokens // rows,),
        in_specs=[rows_of(rows, width), all_of(flat.shape), all_of(sums.shape)],
        out_specs=[rows_of(rows, width)] + [all_of(v.shape) for v in shapes],
        out_shape=[shaped(grad_hidden.shape, BF)] + shapes,
        compiler_params=pltpu.CompilerParams(vmem_limit_bytes=60 * MIB),
        name="unpack",
    )(grad_hidden, flat, sums)


def finish(dqs, dkvs, turned, grad_query, grad_values, grad_depth, weight, mixed, mine, wide_vectors, grad_sum, sharers, count):
    width, tokens = turned.shape
    rows = math.gcd(tokens, 256)
    tiles = tokens // rows
    blocks = len(dqs)
    chains = 3
    shard = width // sharers
    shares = Shares(sharers, shard, [ATT, ATT + LANES, ATT], [False, False, False], count)
    late_rows = pl.BlockSpec((rows, width), lambda i: (jnp.maximum(i - chains, 0), 0))
    away = pl.BlockSpec(memory_space=pl.ANY)
    loaded = list(dqs) + list(dkvs) + [turned, grad_query, grad_values, grad_depth]
    args = loaded + [weight, mixed, mine, wide_vectors, grad_sum]
    shapes = [shaped(mine.shape, F32), shaped((shard, chains * ATT + LANES), F32)]
    return pl.pallas_call(
        functools.partial(finish_kernel, blocks, rows, tiles, shares),
        grid=(chains + tiles,),
        in_specs=[away] * (len(loaded) + 2) + [all_of(mine.shape), all_of(wide_vectors.shape), late_rows],
        out_specs=[late_rows] + [all_of(v.shape) for v in shapes],
        out_shape=[shaped((tokens, width), BF)] + shapes,
        scratch_shapes=[pltpu.VMEM(v.shape, v.dtype) for v in loaded]
        + [
            pltpu.VMEM((width, 4 * ATT), BF),
            pltpu.SemaphoreType.DMA((len(loaded) + len(dkvs) + 2,)),
            pltpu.VMEM((tokens, 4 * ATT), BF),
            pltpu.VMEM((rows + 32, width), F32),
            pltpu.VMEM((8, 2 * ATT), F32),
            pltpu.VMEM((2, 16, ATT), BF),
            pltpu.VMEM((2, 16, width), BF),
            pltpu.VMEM((32, width), BF),
            pltpu.VMEM((count,) + mine.shape, BF),
            pltpu.SemaphoreType.DMA((4,)),
            pltpu.SemaphoreType.DMA((4,)),
            pltpu.SemaphoreType.DMA((max(count - 1, 1),)),
            pltpu.SemaphoreType.DMA((max(count - 1, 1),)),
        ]
        + shares.scratch(),
        compiler_params=pltpu.CompilerParams(
            collective_id=1, has_side_effects=True, vmem_limit_bytes=63 * MIB + MIB // 2
        ),
        cost_estimate=pl.CostEstimate(
            flops=4 * tokens * width * chains * ATT, bytes_accessed=30 * tokens * width, transcendentals=0
        ),
        name="finish",
    )(*args)


def shifted_from(value, axis, step):
    count = lax.axis_size(axis)
    return lax.ppermute(value, axis, [((i + step) % count, i) for i in range(count)])


def local(
    hidden,
    separators,
    out_grad,
    w_query,
    b_query,
    w_key,
    w_value,
    b_value,
    depth_kernel,
    w_point,
    b_keyconv,
    w_kernel,
    kernel_bias,
    w_convout,
    b_convout,
    w_dense,
    b_dense,
    gain_attn,
    shift_attn,
    w_up,
    b_up,
    w_down,
    b_down,
    gain_out,
    shift_out,
):
    count = lax.axis_size("blk")
    sharers = lax.axis_size("dp")
    x, cotangent = hidden[0], out_grad[0]
    tokens, width = x.shape
    part = b_query.shape[0]

    known = math.gcd(tokens, 512) if count == 2 else 0
    others = [shifted_from(x[known:], "blk", step) for step in range(1, count)]
    weight, wide_vectors, thin, bias_up, wt_kernel, bias_kernel, halo, late, early = gather_columns(
        [w_query, w_key, w_value],
        [b_dense, gain_attn, shift_attn, b_down, gain_out, shift_out],
        [b_query, b_value, b_keyconv, b_convout],
        depth_kernel.T,
        b_up,
        w_kernel,
        kernel_bias,
        w_up,
        w_down,
        x,
        sharers,
        count,
    )
    mixed = lax.all_gather(side_by_side([w_dense, w_convout, w_point]), "dp", axis=0, tiled=True)
    late = lax.all_gather(late, "dp", axis=0, tiled=False)

    query, query_t, *own = project([x], weight, thin, 3)
    keys = [own]
    outs, probs = [], []
    for step in range(count):
        if step > 0:
            keys.append(project(([early] if known else []) + [others[step - 1]], weight, thin, 2))
        key, key_t, value, value_t, norms = keys[step]
        out, prob = attend(separators, query_t, key, value_t, norms, count, step)
        outs.append(out)
        probs.append(prob)
        if step == 0:
            depth, keyconv, attn_key, kernt, kern, conv, values, rim = mix(
                count, x, halo, query, mixed, wide_vectors, thin, wt_kernel, bias_kernel
            )
            others, depth = lax.optimization_barrier((others, depth))
    output, grad_sum, grad_conv, grads_t, sides, (packed, g_vectors, gb_up) = middle(
        outs, conv, x, cotangent, mixed, late, wide_vectors, bias_up
    )
    grad_query_conv, grad_depth, grad_values, packed, turned = mix_back(
        count, x, halo, values, rim, grad_conv, kernt, kern, query, keyconv, attn_key, depth, mixed, wt_kernel, g_vectors, gb_up, packed
    )
    packed, sides = lax.optimization_barrier((packed, sides))
    mine = lax.psum_scatter(packed, "dp", scatter_dimension=0, tiled=False)

    dqs, dkvs = [], []
    for step in list(range(1, count)) + [0]:
        key, key_t, value, value_t, norms = keys[step]
        some = HEADS // 2 if step else HEADS
        for at in range(0, HEADS, some):
            dq, dkv = attend_back(probs[step], value, key_t, grads_t[step], sides[step], query_t, at, some)
            dqs.append(dq)
            dkvs.append(shifted_from(dkv, "blk", count - step) if step else dkv)
    grad_hidden, flat, sums = finish(
        dqs, dkvs, turned, grad_query_conv, grad_values, grad_depth, weight, mixed, mine, wide_vectors, grad_sum, sharers, count
    )
    results = unpack(grad_hidden, flat, sums, part, b_up.shape[0])
    grad_hidden, gw_query, gw_key, gw_value, gw_convout, gw_dense, gw_up, gw_down, gw_point, gw_kernel, g_taps, g_bias, gb_up = results[:13]
    g_vectors, thin = results[13:19], results[19:]
    return (
        output[None],
        grad_hidden[None],
        gw_query,
        thin[0],
        gw_key,
        gw_value,
        thin[1],
        g_taps.T,
        gw_point,
        thin[2],
        gw_kernel,
        g_bias,
        gw_convout,
        thin[3],
        gw_dense,
        g_vectors[0],
        g_vectors[1],
        g_vectors[2],
        gw_up,
        gb_up,
        gw_down,
        g_vectors[3],
        g_vectors[4],
        g_vectors[5],
    )


def solution(mesh):
    placed = (
        P("dp", "blk", None),
        P("dp"),
        P("dp", "blk", None),
        P("dp", None),
        P("dp"),
        P("dp", None),
        P("dp", None),
        P("dp"),
        P("dp", None),
        P("dp", None),
        P("dp"),
        P("dp", None),
        P(),
        P("dp", None),
        P("dp"),
        P("dp", None),
        P("dp"),
        P("dp"),
        P("dp"),
        P(None, "dp", None),
        P("dp"),
        P(None, "dp", None),
        P("dp"),
        P("dp"),
        P("dp"),
    )
    return jax.shard_map(
        local,
        mesh=mesh,
        in_specs=placed,
        out_specs=(
            P("dp", "blk", None),
            P("dp", "blk", None),
            P("dp", None),
            P("dp"),
            P("dp", None),
            P("dp", None),
            P("dp"),
            P("dp", None),
            P("dp", None),
            P("dp"),
            P("dp", None),
            P(),
            P("dp", None),
            P("dp"),
            P("dp", None),
            P("dp"),
            P("dp"),
            P("dp"),
            P(None, "dp", None),
            P("dp"),
            P(None, "dp", None),
            P("dp"),
            P("dp"),
            P("dp"),
        ),
        check_vma=False,
    )
```

```python
import functools, math
import jax, jax.numpy as jnp
from jax import lax
from jax.experimental import pallas as pl
from jax.experimental.pallas import tpu as pltpu
from jax.sharding import PartitionSpec as P

HEADS = 6
HD = 64
KSIZE = 9
REACH = 4
ATT = 384
EPS = 1e-12
BF = jnp.bfloat16
F32 = jnp.float32
MIB = 2**20
EXCLUDED = 2.0**100
SAFE_SCORE = 50.0


def mm(left, right):
    return jnp.dot(left, right, preferred_element_type=F32)


def mm_nt(left, right):
    return lax.dot_general(left, right, (((1,), (1,)), ((), ())), preferred_element_type=F32)


def mm_tn(left, right):
    return lax.dot_general(left, right, (((0,), (0,)), ((), ())), preferred_element_type=F32)


def in_lanes(rows, columns):
    lane = lax.broadcasted_iota(jnp.int32, (rows, 128), 1)
    out = jnp.zeros((rows, 128), F32)
    for at, column in enumerate(columns):
        out = jnp.where(lane == at, column, out)
    return out.astype(BF)


def in_rows(columns, rows):
    row = lax.broadcasted_iota(jnp.int32, (16, columns), 0)
    out = jnp.zeros((16, columns), F32)
    for at, values in enumerate(rows):
        out = jnp.where(row == at, values, out)
    return out.astype(BF)


def three_parts(values):
    high = values.astype(BF).astype(F32)
    rest = values - high
    middle = rest.astype(BF).astype(F32)
    return high, middle, (rest - middle).astype(BF).astype(F32)


def put_head(ref, head, values):
    odd = lax.rem(head, 2) == 1
    none = jnp.zeros_like(values)
    ref[0:HD, :] = jnp.where(odd, none, values)
    ref[HD : 2 * HD, :] = jnp.where(odd, values, none)


def attend_kernel(keys, queries, chunk, count, step, at_ref, q_ref, k_ref, v_ref, norm_ref, o_ref, p_ref, key_side, query_side):
    head, tile = pl.program_id(0), pl.program_id(1)
    separator, block = at_ref[0], lax.axis_index("blk")
    first_query = block * keys
    first_key = lax.rem(block + step, count) * keys

    @pl.when((head == 0) & (tile == 0))
    def start():
        position = first_key + lax.broadcasted_iota(jnp.int32, (keys, 128), 0)
        late = (position >= separator).astype(F32)
        key_side[...] = in_lanes(keys, [1.0 - late, late, 1.0, 1.0, 1.0])
        query_side[2 * HD + 16 :, :] = jnp.zeros((2 * HD - 16, queries), BF)

    put_head(query_side, head, q_ref[...])
    position = first_query + tile * queries + lax.broadcasted_iota(jnp.int32, (16, queries), 1)
    late = (position >= separator).astype(F32)
    excluded = [-EXCLUDED * late, -EXCLUDED * (1.0 - late)]
    query_side[2 * HD : 2 * HD + 16, :] = in_rows(queries, excluded)
    o_ref[0, HD + 8 : HD + 16, :] = jnp.zeros((8, queries), F32)
    wide = q_ref[...].astype(F32)
    largest = jnp.max(jnp.sum(wide * wide, axis=0, keepdims=True)) * jnp.max(norm_ref[...])

    def scores(at):
        part = slice(at * chunk, (at + 1) * chunk)
        return mm(
            jnp.concatenate([k_ref[part, :], key_side[part, :]], axis=1), query_side[...]
        )

    @pl.when(jnp.logical_not(largest <= SAFE_SCORE * SAFE_SCORE))
    def shifted():
        best = jnp.full((1, queries), -4.0 * EXCLUDED, F32)
        for at in range(keys // chunk):
            best = jnp.maximum(best, jnp.max(scores(at), axis=0, keepdims=True))
        parts = three_parts(jnp.where(best < -0.5 * EXCLUDED, 0.0, best))
        query_side[2 * HD : 2 * HD + 16, :] = in_rows(queries, excluded + [-part for part in parts])
        o_ref[0, HD + 8 : HD + 16, :] = jnp.broadcast_to(
            jnp.where(best < -0.5 * EXCLUDED, best, parts[0] + parts[1] + parts[2]), (8, queries)
        )

    ones = in_rows(chunk, [1.0])
    total = jnp.zeros((HD + 16, queries), F32)
    for at in range(keys // chunk):
        part = slice(at * chunk, (at + 1) * chunk)
        probs = jnp.exp(scores(at)).astype(BF)
        p_ref[0, part, :] = probs
        total = total + mm(jnp.concatenate([v_ref[:, part], ones], axis=0), probs)
    o_ref[0, 0 : HD + 8, :] = total[0 : HD + 8, :]


def attend(at, query_t, key, value_t, norms, count, step):
    tokens, keys = query_t.shape[1], key.shape[0]
    queries, chunk = math.gcd(tokens, 2048), math.gcd(keys, 1024)
    return pl.pallas_call(
        functools.partial(attend_kernel, keys, queries, chunk, count, step),
        grid=(HEADS, tokens // queries),
        in_specs=[
            pl.BlockSpec(memory_space=pltpu.SMEM),
            pl.BlockSpec((HD, queries), lambda h, i: (h, i)),
            pl.BlockSpec((keys, 2 * HD), lambda h, i: (0, h // 2)),
            pl.BlockSpec((HD, keys), lambda h, i: (h, 0)),
            pl.BlockSpec(norms.shape, lambda h, i: (0, 0)),
        ],
        out_specs=[
            pl.BlockSpec((1, HD + 16, queries), lambda h, i: (h, 0, i)),
            pl.BlockSpec((1, keys, queries), lambda h, i: (h, 0, i)),
        ],
        out_shape=[
            jax.ShapeDtypeStruct((HEADS, HD + 16, tokens), F32),
            jax.ShapeDtypeStruct((HEADS, keys, tokens), BF),
        ],
        scratch_shapes=[pltpu.VMEM((keys, 128), BF), pltpu.VMEM((4 * HD, queries), BF)],
        compiler_params=pltpu.CompilerParams(vmem_limit_bytes=56 * MIB),
        cost_estimate=pl.CostEstimate(
            flops=ATT * keys,
            bytes_accessed=2 * HEADS * keys,
            transcendentals=0,
        ),
        name="attend",
    )(at, query_t, key, value_t, norms)


def attend_back_kernel(first, keys, queries, chunk, p_ref, v_ref, kt_ref, g_ref, side_ref, q_ref, dq_ref, dkv_ref, value_side, grad_side, dk_sum, dv_sum):
    head, tile = pl.program_id(0), pl.program_id(1)

    @pl.when((head == 0) & (tile == 0))
    def start():
        value_side[...] = in_lanes(chunk, [1.0, 1.0, 1.0])
        grad_side[2 * HD + 16 :, :] = jnp.zeros((2 * HD - 16, queries), BF)

    @pl.when(tile == 0)
    def fresh():
        dk_sum[...] = jnp.zeros_like(dk_sum)
        dv_sum[...] = jnp.zeros_like(dv_sum)

    put_head(grad_side, first + head, g_ref[...])
    grad_side[2 * HD : 2 * HD + 16, :] = side_ref[0]
    total = jnp.zeros((HD, queries), F32)
    for at in range(keys // chunk):
        part = slice(at * chunk, (at + 1) * chunk)
        probs = p_ref[0, part, :]
        spread = mm(jnp.concatenate([v_ref[part, :], value_side[...]], axis=1), grad_side[...])
        grad_scores = (probs.astype(F32) * spread).astype(BF)
        dv_sum[:, part] += mm_nt(g_ref[...], probs)
        dk_sum[:, part] += mm_nt(q_ref[...], grad_scores)
        total = total + mm(kt_ref[:, part], grad_scores)
    dq_ref[...] = (total * (HD**-0.5)).astype(BF)

    @pl.when(tile == pl.num_programs(1) - 1)
    def finish():
        dkv_ref[0] = dk_sum[...].astype(BF)
        dkv_ref[1] = dv_sum[...].astype(BF)


def attend_back(probs, value, key_t, grad_t, side, query_t, first, heads):
    tokens, keys = query_t.shape[1], value.shape[0]
    queries, chunk = math.gcd(tokens, 1024), math.gcd(keys, 256)
    by_token = pl.BlockSpec((HD, queries), lambda h, i: (first + h, i))
    by_key = pl.BlockSpec((HD, keys), lambda h, i: (first + h, 0))
    return pl.pallas_call(
        functools.partial(attend_back_kernel, first, keys, queries, chunk),
        grid=(heads, tokens // queries),
        in_specs=[
            pl.BlockSpec((1, keys, queries), lambda h, i: (first + h, 0, i)),
            pl.BlockSpec((keys, 2 * HD), lambda h, i: (0, (first + h) // 2)),
            by_key,
            by_token,
            pl.BlockSpec((1, 16, queries), lambda h, i: (first + h, 0, i)),
            by_token,
        ],
        out_specs=[
            pl.BlockSpec((HD, queries), lambda h, i: (h, i)),
            pl.BlockSpec((2, HD, keys), lambda h, i: (0, h, 0)),
        ],
        out_shape=[
            jax.ShapeDtypeStruct((heads * HD, tokens), BF),
            jax.ShapeDtypeStruct((2, heads * HD, keys), BF),
        ],
        scratch_shapes=[
            pltpu.VMEM((chunk, 128), BF),
            pltpu.VMEM((4 * HD, queries), BF),
            pltpu.VMEM((HD, keys), F32),
            pltpu.VMEM((HD, keys), F32),
        ],
        compiler_params=pltpu.CompilerParams(vmem_limit_bytes=56 * MIB),
        cost_estimate=pl.CostEstimate(
            flops=32 * heads * HD * tokens * keys,
            bytes_accessed=2 * heads * tokens * keys,
            transcendentals=0,
        ),
        name="attend_back",
    )(probs, value, key_t, grad_t, side, query_t)


def all_of(shape):
    return pl.BlockSpec(shape, lambda *at: (0,) * len(shape))


def rows_of(rows, width):
    return pl.BlockSpec((rows, width), lambda i: (i, 0))


def columns_of(height, columns):
    return pl.BlockSpec((height, columns), lambda i: (0, i))


def run_tiles(kernel, name, steps, inputs, outputs, scratch, flops, aliases=None):
    args, in_specs = zip(*inputs)
    shapes, out_specs = zip(*outputs)
    size = sum(math.prod(v.shape) * v.dtype.itemsize for v in args + shapes)
    return pl.pallas_call(
        kernel,
        grid=(steps,),
        in_specs=list(in_specs),
        out_specs=list(out_specs),
        out_shape=list(shapes),
        scratch_shapes=scratch,
        input_output_aliases=aliases or {},
        compiler_params=pltpu.CompilerParams(vmem_limit_bytes=62 * MIB),
        cost_estimate=pl.CostEstimate(flops=flops, bytes_accessed=size, transcendentals=0),
        name=name,
    )(*args)


def shaped(shape, dtype):
    return jax.ShapeDtypeStruct(shape, dtype)


def project_kernel(parts, sources, *refs):
    x_refs, refs = refs[:sources], refs[sources:]
    (w_ref, thin_ref), refs = refs[:2], refs[2:]
    norm_ref = refs[2 * parts]
    skip = (3 - parts) * ATT

    @pl.when(pl.program_id(0) == 0)
    def start():
        norm_ref[...] = jnp.zeros_like(norm_ref)

    x = x_refs[-1][...]
    if sources == 2:
        x = jnp.where(pl.program_id(0) == 0, x_refs[0][...], x)
    plain = mm(x, w_ref[:, skip:])
    for part in range(parts):
        own = slice(part * ATT, (part + 1) * ATT)
        bias = 0.0
        if part != parts - 2:
            at = 1 if part == parts - 1 else 0
            bias = thin_ref[at : at + 1, :]
        low = (plain[:, own] + bias).astype(BF)
        refs[2 * part][...] = low
        across = low.T
        if part == parts - 2:
            wide = across.astype(F32)
            for head in range(HEADS):
                cells = wide[head * HD : (head + 1) * HD]
                size = jnp.sum(cells * cells, axis=0, keepdims=True)
                norm_ref[...] = jnp.maximum(norm_ref[...], size)
        if part < parts - 2:
            across = (across.astype(F32) * (HD**-0.5)).astype(BF)
        refs[2 * part + 1][...] = across


def project(sources, weight, thin, parts):
    tokens, width = sum(x.shape[0] for x in sources), sources[0].shape[1]
    wide = 3 * ATT
    tile = math.gcd(tokens, 512)
    late = len(sources) - 1
    inputs = [(sources[-1], pl.BlockSpec((tile, width), lambda i: (jnp.maximum(i - late, 0), 0)))]
    if late:
        inputs.insert(0, (sources[0], all_of((tile, width))))
    outputs = []
    for part in range(parts):
        outputs.append((shaped((tokens, ATT), BF), rows_of(tile, ATT)))
        outputs.append((shaped((ATT, tokens), BF), columns_of(ATT, tile)))
    outputs.append((shaped((8, tile), F32), all_of((8, tile))))
    return run_tiles(
        functools.partial(project_kernel, parts, len(sources)),
        "project",
        tokens // tile,
        inputs
        + [
            (weight, all_of((width, wide))),
            (thin, all_of(thin.shape)),
        ],
        outputs,
        [],
        2 * tokens * width * parts * ATT,
    )


def fill_rows(window, x_ref, halo_ref, tile, tiles, rows):
    first = tile * rows
    tokens = x_ref.shape[0]
    before = x_ref[pl.ds(pl.multiple_of(jnp.maximum(first - 16, 0), 16), 16), :]
    after = x_ref[pl.ds(pl.multiple_of(jnp.minimum(first + rows, tokens - 16), 16), 16), :]
    window[0:16, :] = jnp.where(tile == 0, halo_ref[0:16, :], before).astype(window.dtype)
    window[16 : 16 + rows, :] = x_ref[pl.ds(pl.multiple_of(first, rows), rows), :].astype(window.dtype)
    window[16 + rows :, :] = jnp.where(
        tile == tiles - 1, halo_ref[16:32, :], after
    ).astype(window.dtype)


def fill_window(window, x_ref, halo_ref, tile, rows):
    fill_rows(window, x_ref, halo_ref, tile, pl.num_programs(0), rows)


def fill_spread(spread):
    row = lax.broadcasted_iota(jnp.int32, (128, ATT), 0)
    head = lax.broadcasted_iota(jnp.int32, (128, ATT), 1) // HD
    for tap in range(KSIZE):
        spread[:, tap * ATT : (tap + 1) * ATT] = (row == tap * 8 + head).astype(F32).astype(BF)


def mix_kernel(rows, count, x_ref, halo_ref, q_ref, wc_ref, wp_ref, wide_ref, thin_ref, wk_ref, bk_ref, depth_ref, keyconv_ref, attn_ref, kernt_ref, kern_ref, conv_ref, out_ref, rim_ref, window, conv_window, spread):
    tile = pl.program_id(0)
    last = pl.num_programs(0) - 1

    @pl.when(tile == 0)
    def start():
        fill_spread(spread)

    fill_window(window, x_ref, halo_ref, tile, rows)
    width = window.shape[1]
    for at in range(0, width, 128):
        some = slice(at, at + 128)
        total = jnp.zeros((rows, 128), F32)
        for tap in range(KSIZE):
            total = total + window[12 + tap : 12 + tap + rows, some] * wide_ref[TAPS_AT + tap : TAPS_AT + tap + 1, some]
        depth_ref[:, some] = total.astype(BF)
    position = (
        lax.axis_index("blk") * x_ref.shape[0] + tile * rows - 16 + lax.broadcasted_iota(jnp.int32, (rows + 32, ATT), 0)
    )
    inside = (position >= 0) & (position < count * x_ref.shape[0])
    values = mm(window[...].astype(BF), wc_ref[...]) + thin_ref[3:4, :]
    values = jnp.where(inside, values, 0.0).astype(BF)
    out_ref[...] = values[16 : 16 + rows]

    @pl.when(tile == 0)
    def first_rim():
        rim_ref[0:16, :] = values[0:16]

    @pl.when(tile == last)
    def last_rim():
        rim_ref[16:32, :] = values[16 + rows :]

    conv_window[...] = values.astype(F32)
    keyconv = mm(depth_ref[...], wp_ref[...]) + thin_ref[2:3, :]
    keyconv_ref[...] = keyconv
    attn_key = (keyconv * q_ref[...].astype(F32)).astype(BF)
    attn_ref[...] = attn_key
    logits = mm_nt(wk_ref[...], attn_key) + bk_ref[:, BIAS_AT : BIAS_AT + 1]
    slabs = [logits[8 * tap : 8 * tap + 8] for tap in range(KSIZE)]
    best = functools.reduce(jnp.maximum, slabs)
    slabs = [jnp.exp(slab - best) for slab in slabs]
    share = 1.0 / functools.reduce(jnp.add, slabs)
    slabs = [slab * share for slab in slabs]
    kernt = jnp.concatenate(slabs + [jnp.zeros((128 - 8 * KSIZE, rows), F32)], axis=0)
    kernt_ref[...] = kernt[0 : 8 * KSIZE]
    kern = kernt.astype(BF).T
    kern_ref[...] = kern
    for at in range(0, ATT, LANES):
        some = slice(at, at + LANES)
        total = jnp.zeros((rows, LANES), F32)
        for tap in range(KSIZE):
            first = tap * ATT + at
            total = total + mm(kern, spread[:, first : first + LANES]) * conv_window[12 + tap : 12 + tap + rows, some]
        conv_ref[:, some] = total.astype(BF)


def column_block(weight, place):
    return pl.BlockSpec((weight.shape[0], ATT), lambda i: (0, place))


def mix(count, x, halo, query, weight, wide_vectors, thin, w_kernel, kernel_bias):
    tokens, width = x.shape
    rows = math.gcd(tokens, 512)
    whole = [(weight, column_block(weight, 2)), (weight, column_block(weight, 3))]
    whole += [(v, all_of(v.shape)) for v in (wide_vectors, thin, w_kernel, kernel_bias)]
    return run_tiles(
        functools.partial(mix_kernel, rows, count),
        "mix",
        tokens // rows,
        [
            (x, all_of(x.shape)),
            (halo, all_of(halo.shape)),
            (query, rows_of(rows, ATT)),
        ]
        + whole,
        [
            (shaped((tokens, width), BF), rows_of(rows, width)),
            (shaped((tokens, ATT), F32), rows_of(rows, ATT)),
            (shaped((tokens, ATT), BF), rows_of(rows, ATT)),
            (shaped((8 * KSIZE, tokens), F32), columns_of(8 * KSIZE, rows)),
            (shaped((tokens, 128), BF), rows_of(rows, 128)),
            (shaped((tokens, ATT), BF), rows_of(rows, ATT)),
            (shaped((tokens, ATT), BF), rows_of(rows, ATT)),
            (shaped((32, ATT), BF), all_of((32, ATT))),
        ],
        [
            pltpu.VMEM((rows + 32, width), F32),
            pltpu.VMEM((rows + 32, ATT), F32),
            pltpu.VMEM((128, KSIZE * ATT), BF),
        ],
        4 * tokens * width * ATT * 4,
    )


def normal(values):
    centre = values - jnp.mean(values, axis=-1, keepdims=True)
    scale = lax.rsqrt(jnp.mean(centre * centre, axis=-1, keepdims=True) + EPS)
    return centre * scale, scale


def normal_back(grad, unit, scale):
    return scale * (
        grad
        - jnp.mean(grad, axis=-1, keepdims=True)
        - unit * jnp.mean(grad * unit, axis=-1, keepdims=True)
    )


def gelu_parts(values):
    share = 0.5 + 0.5 * lax.erf(values * math.sqrt(0.5))
    bell = jnp.exp2(values * values * (-0.5 * math.log2(math.e)))
    return values * share, share + values * (bell * (1.0 / math.sqrt(2.0 * math.pi)))


def middle_kernel(blocks, rows, units, *refs):
    o_refs, refs = refs[:blocks], refs[blocks:]
    (conv_ref, x_ref, og_ref, wd_ref, late_ref, vec_ref, bu_ref), refs = refs[:7], refs[7:]
    (out_ref, sum_ref, gconv_ref), refs = refs[:3], refs[3:]
    g_refs, refs = refs[:blocks], refs[blocks:]
    side_refs, refs = refs[:blocks], refs[blocks:]
    (packed_ref, gvec_ref, gbu_ref, wd_sum, wu_sum, wn_sum, acts, slopes, staged, sems, wu_ref) = refs
    tile = pl.program_id(0)
    hidden_units = wu_ref.shape[1]
    low_rows = late_ref.shape[1] // 2

    def down_rows(at, lanes):
        return late_ref[at // low_rows : (at + units) // low_rows, low_rows:, lanes].reshape(units, ATT)

    groups = 2
    inner = ATT
    outer = hidden_units // groups

    @pl.when(tile == 0)
    def start():
        for ref in (wd_sum, wu_sum, wn_sum, gvec_ref, gbu_ref):
            ref[...] = jnp.zeros_like(ref)
        owners, high, width = late_ref.shape
        quarter = high // 8
        for pair in range(0, owners, 2):
            both = [late_ref[owner, 0 : high // 2].astype(F32) for owner in (pair, pair + 1)]
            for place in range(4):
                some = [cells[place * quarter : (place + 1) * quarter] for cells in both]
                wu_ref[pair * quarter : (pair + 2) * quarter, place * width : (place + 1) * width] = (
                    jnp.concatenate(some, axis=0).astype(BF)
                )

    shifts = [
        jnp.where(ref[:, HD : HD + 1, :] > 0.0, ref[:, HD + 8 : HD + 9, :], -EXCLUDED) for ref in o_refs
    ]
    top = functools.reduce(jnp.maximum, shifts)
    weights = [jnp.exp(shift - top) for shift in shifts]
    mass = functools.reduce(jnp.add, [w * ref[:, HD : HD + 1, :] for w, ref in zip(weights, o_refs)])
    weights = [w / mass for w in weights]
    heads = functools.reduce(jnp.add, [w * ref[:, 0:HD, :] for w, ref in zip(weights, o_refs)])
    att_t = heads.reshape(ATT, rows).astype(BF)
    conv = conv_ref[...]
    vec = [vec_ref[at : at + 1, :] for at in range(6)]
    dense = mm(att_t.T, wd_ref[0:ATT, :]) + mm(conv, wd_ref[ATT:, :]) + vec[0]
    unit_one, scale_one = normal(dense + x_ref[...].astype(F32))
    normed = unit_one * vec[1] + vec[2]
    low = normed.astype(BF)
    downs = []
    for group in range(groups):
        mine = low[:, group * inner : (group + 1) * inner]
        down = jnp.zeros((rows, inner), F32)
        for at in range(0, outer, units):
            here = slice(group * outer + at, group * outer + at + units)
            upward = mm(mine, wu_ref[:, here]) + bu_ref[:, here]
            act, slope = gelu_parts(upward)
            act = act.astype(BF)
            acts[:, here] = act
            slopes[:, here] = slope.astype(BF)
            down = down + mm(act, down_rows(at, slice(group * inner, (group + 1) * inner)))
        downs.append(down)
    unit_two, scale_two = normal(jnp.concatenate(downs, axis=1) + vec[3] + normed)
    out_ref[...] = (unit_two * vec[4] + vec[5]).astype(BF)
    og = og_ref[...].astype(F32)
    gvec_ref[4:5, :] += jnp.sum(og * unit_two, axis=0, keepdims=True)
    gvec_ref[5:6, :] += jnp.sum(og, axis=0, keepdims=True)
    grad_two = normal_back(og * vec[4], unit_two, scale_two)
    grad_down = grad_two.astype(BF)
    gvec_ref[3:4, :] += jnp.sum(grad_down.astype(F32), axis=0, keepdims=True)
    backs = []
    for group in range(groups):
        lanes = slice(group * inner, (group + 1) * inner)
        mine, grads = low[:, lanes], grad_down[:, lanes]
        mine_t = mine.T
        back = jnp.zeros((rows, inner), F32)
        for at in range(0, outer, units):
            here = slice(group * outer + at, group * outer + at + units)
            grad_act = mm_nt(grads, down_rows(at, lanes))
            grad_up = (grad_act * slopes[:, here].astype(F32)).astype(BF)
            gbu_ref[0:1, here] += jnp.sum(grad_up.astype(F32), axis=0, keepdims=True)
            wn_sum[at : at + units, lanes] += mm_tn(acts[:, here], grads)
            wu_sum[:, here] += mm(mine_t, grad_up)
            back = back + mm_nt(grad_up, wu_ref[:, here])
        backs.append(back)
    grad_normed = grad_two + jnp.concatenate(backs, axis=1)
    gvec_ref[1:2, :] += jnp.sum(grad_normed * unit_one, axis=0, keepdims=True)
    gvec_ref[2:3, :] += jnp.sum(grad_normed, axis=0, keepdims=True)
    grad_one = normal_back(grad_normed * vec[1], unit_one, scale_one)
    sum_ref[...] = grad_one
    grad_dense = grad_one.astype(BF)
    gvec_ref[0:1, :] += jnp.sum(grad_dense.astype(F32), axis=0, keepdims=True)
    wd_sum[0:ATT, :] += mm(att_t, grad_dense)
    wd_sum[ATT:, :] += mm_tn(conv, grad_dense)
    gconv_ref[...] = mm_nt(grad_dense, wd_ref[ATT:, :]).astype(BF)
    grad_att = mm_nt(wd_ref[0:ATT, :], grad_dense).astype(BF).astype(F32).reshape(HEADS, HD, rows)
    for weight, g_ref, side_ref in zip(weights, g_refs, side_refs):
        share = (grad_att * weight).astype(BF)
        g_ref[...] = share.reshape(ATT, rows)
        delta = -jnp.sum(share.astype(F32) * heads, axis=1, keepdims=True)
        row = lax.broadcasted_iota(jnp.int32, (HEADS, 16, rows), 1)
        side = jnp.zeros((HEADS, 16, rows), F32)
        for at, part in enumerate(three_parts(delta)):
            side = jnp.where(row == at, part, side)
        side_ref[...] = side.astype(BF)

    @pl.when(tile == pl.num_programs(0) - 1)
    def finish():
        slots = staged.shape[0]
        sharers = packed_ref.shape[0]
        shard = wd_sum.shape[0] // sharers
        quarter = shard // 2
        width = wd_sum.shape[1]
        copies = []
        for owner in range(sharers):
            slot = owner % slots
            if owner >= slots:
                copies[owner - slots].wait()
            staged[slot, 0:shard] = wd_sum[owner * shard : (owner + 1) * shard].astype(BF)
            some = wu_sum[owner * quarter : (owner + 1) * quarter]
            for group in range(groups):
                pair = [some[:, at : at + width] for at in (2 * group * width, (2 * group + 1) * width)]
                staged[slot, (1 + group) * shard : (2 + group) * shard] = jnp.concatenate(pair, axis=0).astype(BF)
            some = wn_sum[owner * 2 * shard : (owner + 1) * 2 * shard]
            staged[slot, 3 * shard : 5 * shard] = some.astype(BF)
            copy = pltpu.make_async_copy(
                staged.at[slot], packed_ref.at[owner, 0 : 5 * shard], sems.at[owner]
            )
            copy.start()
            copies.append(copy)
        for copy in copies[sharers - slots :]:
            copy.wait()


def middle(outs, conv, x, out_grad, w_dense, late, vectors, b_up):
    tokens, width = x.shape
    sharers = late.shape[0]
    shard = width // sharers
    units = b_up.shape[1]
    up, down = (width // 2, units), (units // 2, width)
    rows = math.gcd(tokens, 512)
    blocks = len(outs)
    heads = pl.BlockSpec((HEADS, HD + 16, rows), lambda i: (0, 0, i))
    side = pl.BlockSpec((HEADS, 16, rows), lambda i: (0, 0, i))
    single = pl.Buffered(1)
    once = [
        (w_dense, pl.BlockSpec((width, width), lambda i: (0, 0), pipeline_mode=single)),
        (late, pl.BlockSpec(late.shape, lambda i: (0, 0, 0), pipeline_mode=single)),
    ]
    once += [(v, all_of(v.shape)) for v in (vectors, b_up)]
    results = run_tiles(
        functools.partial(middle_kernel, blocks, rows, 768),
        "middle",
        tokens // rows,
        [(o, heads) for o in outs]
        + [
            (conv, rows_of(rows, ATT)),
            (x, rows_of(rows, width)),
            (out_grad, rows_of(rows, width)),
        ]
        + once,
        [
            (shaped((tokens, width), BF), rows_of(rows, width)),
            (shaped((tokens, width), F32), rows_of(rows, width)),
            (shaped((tokens, ATT), BF), rows_of(rows, ATT)),
        ]
        + [(shaped((ATT, tokens), BF), columns_of(ATT, rows))] * blocks
        + [(shaped((HEADS, 16, tokens), BF), side)] * blocks
        + [
            (shaped((sharers, 7 * shard, width), BF), pl.BlockSpec(memory_space=pl.ANY)),
            (shaped((8, width), F32), all_of((8, width))),
            (shaped((8, units), F32), all_of((8, units))),
        ],
        [
            pltpu.VMEM((width, width), F32),
            pltpu.VMEM(up, F32),
            pltpu.VMEM(down, F32),
            pltpu.VMEM((rows, units), BF),
            pltpu.VMEM((rows, units), BF),
            pltpu.VMEM((6, 5 * shard, width), BF),
            pltpu.SemaphoreType.DMA((sharers,)),
            pltpu.VMEM(up, BF),
        ],
        6 * tokens * (width * width + 2 * math.prod(up)),
    )
    output, grad_sum, grad_conv = results[:3]
    return output, grad_sum, grad_conv, results[3 : 3 + blocks], results[3 + blocks : 3 + 2 * blocks], results[3 + 2 * blocks :]


def mix_back_kernel(rows, count, x_ref, halo_ref, values_ref, rim_ref, gconv_ref, kernt_ref, kern_ref, q_ref, keyconv_ref, attn_ref, depth_ref, wp_ref, wk_ref, gvec_ref, gbu_ref, unused, gq_ref, gdepth_ref, gvalues_ref, packed_ref, turned_ref, window, conv_window, summed, products, spread, wp_sum, wc_sum, values_sum, gwk_ref, gbias_ref, gtaps_ref, turn_wide, turn_thin, side, staged, sem):
    tile = pl.program_id(0)

    @pl.when(tile == 0)
    def start():
        fill_spread(spread)
        for ref in (values_sum, wp_sum, wc_sum, gwk_ref, gbias_ref, gtaps_ref, turn_wide, turn_thin):
            ref[...] = jnp.zeros_like(ref)

    fill_window(window, x_ref, halo_ref, tile, rows)
    fill_window(conv_window, values_ref, rim_ref, tile, rows)
    summed[...] = jnp.zeros_like(summed)
    grad_conv = gconv_ref[...].astype(F32)
    for tap in range(KSIZE):
        here = slice(tap * ATT, (tap + 1) * ATT)
        there = slice(12 + tap, 12 + tap + rows)
        products[:, here] = (grad_conv * conv_window[there, :]).astype(BF)
        summed[there, :] += mm(kern_ref[...], spread[:, here]) * grad_conv
    first = pl.multiple_of(tile * rows, rows)
    values_sum[pl.ds(first, rows + 32), :] += summed[...]
    turned = x_ref[pl.ds(first, rows), :].T
    turned_ref[...] = turned
    edges = [slice(0, 16), slice(rows + 16, rows + 32)]
    edge_x = jnp.concatenate([window[edge, :] for edge in edges], axis=0).astype(BF)
    edge_grads = jnp.concatenate([summed[edge, :] for edge in edges], axis=0).astype(BF)
    wc_sum[...] += mm(turned, summed[16 : 16 + rows, :].astype(BF)) + mm_tn(edge_x, edge_grads)
    grad_kernel = mm_nt(spread[...], products[...])
    slabs = [slice(8 * tap, 8 * tap + 8) for tap in range(KSIZE)]
    kernels = [kernt_ref[slab, :] for slab in slabs]
    mean = functools.reduce(jnp.add, [k * grad_kernel[slab] for k, slab in zip(kernels, slabs)])
    grad_logits = jnp.concatenate(
        [k * (grad_kernel[slab] - mean) for k, slab in zip(kernels, slabs)], axis=0
    ).astype(BF)
    wide_logits = grad_logits.astype(F32)
    gbias_ref[...] += jnp.concatenate(
        [
            jnp.broadcast_to(jnp.sum(wide_logits, axis=1, keepdims=True), (8 * KSIZE, 128)),
            jnp.zeros((8, 128), F32),
        ],
        axis=0,
    )
    gwk_ref[0 : 8 * KSIZE, :] += mm(grad_logits, attn_ref[...])
    grad_attn = mm_tn(grad_logits, wk_ref[...]).astype(BF).astype(F32)
    grad_keyconv = (grad_attn * q_ref[...].astype(F32)).astype(BF)
    gq_ref[...] = (grad_attn * keyconv_ref[...]).astype(BF)
    gwk_ref[8 * KSIZE : 8 * KSIZE + 1, :] += jnp.sum(grad_keyconv.astype(F32), axis=0, keepdims=True)
    wp_sum[...] += mm_tn(depth_ref[...], grad_keyconv)
    grad_depth = mm_nt(grad_keyconv, wp_ref[...]).astype(BF)
    gdepth_ref[...] = grad_depth
    wide = grad_depth.astype(F32)
    for at in range(0, window.shape[1], 128):
        some = slice(at, at + 128)
        for tap in range(KSIZE):
            gtaps_ref[tap : tap + 1, some] += jnp.sum(
                wide[:, some] * window[12 + tap : 12 + tap + rows, some], axis=0, keepdims=True
            )

    @pl.when(tile == pl.num_programs(0) - 1)
    def finish():
        gvalues_ref[...] = values_sum[...].astype(BF)
        tokens, block = x_ref.shape[0], lax.axis_index("blk")
        sums = [
            jnp.sum(gvalues_ref[at:end, :].astype(F32), axis=0, keepdims=True)
            for at, end in ((0, 16), (16, tokens + 16), (tokens + 16, tokens + 32))
        ]
        b_sum = sums[1] + jnp.where(block > 0, sums[0], 0.0) + jnp.where(block < count - 1, sums[2], 0.0)
        sharers, shard, width = staged.shape[0], staged.shape[1] // 2, staged.shape[2]
        part = ATT // sharers
        half = gbu_ref.shape[1] // sharers // 2
        turn_wide[0:6, :] = gvec_ref[0:6, :]
        turn_wide[TAPS_AT : TAPS_AT + KSIZE, :] = gtaps_ref[0:KSIZE, :]
        vectors = turn_wide[...].T
        for h in range(HEADS):
            for j in range(KSIZE):
                turn_wide[h * KSIZE + j : h * KSIZE + j + 1, 0:LANES] = gbias_ref[j * 8 + h : j * 8 + h + 1, :]
                turn_thin[h * KSIZE + j : h * KSIZE + j + 1, :] = gwk_ref[j * 8 + h : j * 8 + h + 1, :]
        bias = turn_wide[:, 0:LANES].T[0:1]
        turn_thin[THIN_AT : THIN_AT + 1, :] = gwk_ref[8 * KSIZE : 8 * KSIZE + 1, :]
        turn_thin[THIN_AT + 1 : THIN_AT + 2, :] = b_sum
        kernels = turn_thin[...].T
        side[...] = jnp.zeros_like(side)
        for owner in range(sharers):
            staged[owner, 0:shard, 0:ATT] = wp_sum[owner * shard : (owner + 1) * shard].astype(BF)
            staged[owner, shard:, 0:ATT] = wc_sum[owner * shard : (owner + 1) * shard].astype(BF)
            staged[owner, shard:, ATT:] = jnp.zeros((shard, width - ATT), BF)
            staged[owner, 0:shard, ATT : ATT + LANES] = vectors[owner * shard : (owner + 1) * shard].astype(BF)
            side[0:part, :] = kernels[owner * part : (owner + 1) * part]
            for place in range(2):
                first = (2 * owner + place) * half
                side[part + place : part + place + 1, 0:half] = gbu_ref[0:1, first : first + half]
            side[part + 2 : part + 3, :] = bias
            staged[owner, 0:shard, ATT + LANES : ATT + 2 * LANES] = side[...].astype(BF)
            staged[owner, 0:shard, ATT + 2 * LANES :] = jnp.zeros((shard, width - ATT - 2 * LANES), BF)
        copy = pltpu.make_async_copy(staged, packed_ref.at[:, 5 * shard : 7 * shard], sem)
        copy.start()
        copy.wait()


def mix_back(count, x, halo, values, rim, grad_conv, kernt, kern, query, keyconv, attn_key, depth, weight, w_kernel, g_vectors, gb_up, packed):
    tokens, width = x.shape
    sharers, shard = packed.shape[0], packed.shape[1] // 7
    away = pl.BlockSpec(memory_space=pl.ANY)
    rows = math.gcd(tokens, 512)
    by_rows = [(v, rows_of(rows, v.shape[1])) for v in (kern, query, keyconv, attn_key, depth)]
    return run_tiles(
        functools.partial(mix_back_kernel, rows, count),
        "mix_back",
        tokens // rows,
        [(v, all_of(v.shape)) for v in (x, halo, values, rim)]
        + [(grad_conv, rows_of(rows, ATT)), (kernt, columns_of(8 * KSIZE, rows))]
        + by_rows
        + [(weight, column_block(weight, 3))]
        + [(v, all_of(v.shape)) for v in (w_kernel, g_vectors, gb_up)]
        + [(packed, away)],
        [
            (shaped((tokens, ATT), BF), rows_of(rows, ATT)),
            (shaped((tokens, width), BF), rows_of(rows, width)),
            (shaped((tokens + 32, ATT), BF), all_of((tokens + 32, ATT))),
            (shaped(packed.shape, BF), away),
            (shaped((width, tokens), BF), columns_of(width, rows)),
        ],
        [
            pltpu.VMEM((rows + 32, width), F32),
            pltpu.VMEM((rows + 32, ATT), F32),
            pltpu.VMEM((rows + 32, ATT), F32),
            pltpu.VMEM((rows, KSIZE * ATT), BF),
            pltpu.VMEM((128, KSIZE * ATT), BF),
            pltpu.VMEM((width, ATT), F32),
            pltpu.VMEM((width, ATT), F32),
            pltpu.VMEM((tokens + 32, ATT), F32),
            pltpu.VMEM((8 * KSIZE + 8, ATT), F32),
            pltpu.VMEM((8 * KSIZE + 8, LANES), F32),
            pltpu.VMEM((16, width), F32),
            pltpu.VMEM((LANES, width), F32),
            pltpu.VMEM((LANES, ATT), F32),
            pltpu.VMEM((shard, LANES), F32),
            pltpu.VMEM((sharers, 2 * shard, width), BF),
            pltpu.SemaphoreType.DMA(()),
        ],
        4 * tokens * width * ATT * 4,
        {15: 3},
    )


def side_by_side_kernel(*refs):
    at = 0
    for ref in refs[:-1]:
        refs[-1][:, at : at + ref.shape[1]] = ref[...].astype(BF)
        at += ref.shape[1]


def side_by_side(parts):
    out = shaped((parts[0].shape[0], sum(v.shape[1] for v in parts)), BF)
    return run_tiles(
        side_by_side_kernel, "side_by_side", 1, [(v, all_of(v.shape)) for v in parts], [(out, all_of(out.shape))], [], 0
    )[0]


MESH = pl.DeviceIdType.MESH
LINE = 4
LANES = 128
TAPS_AT = 16
THIN_AT = 64
BIAS_AT = 100


def my_place(sharers):
    columns = sharers // (2 * LINE)
    me = lax.axis_index("dp")
    return me, me // (2 * columns), lax.rem(me // 2, columns), lax.rem(me, 2), columns


def greet(partners):
    barrier = pltpu.get_barrier_semaphore()
    for partner in partners:
        pl.semaphore_signal(barrier, inc=1, device_id=partner, device_id_type=MESH)
    return barrier


def remote(source, target, send_sem, recv_sem, device):
    return pltpu.make_async_remote_copy(
        src_ref=source,
        dst_ref=target,
        send_sem=send_sem,
        recv_sem=recv_sem,
        device_id=device,
        device_id_type=MESH,
    )


def gather_kernel(sharers, count, part, early, *refs):
    w_refs, refs = refs[:3], refs[3:]
    vector_refs, refs = refs[:6], refs[6:]
    thin_refs, refs = refs[:4], refs[4:]
    (taps_ref, up_ref, kernel_ref, bias_ref, wu_ref, wn_ref, head_ref, tail_ref, early_ref), refs = refs[:9], refs[9:]
    (out_ref, wide_ref, thin_ref, bias_up_ref, wk_ref, bk_ref, halo_ref, late_out, early_out), refs = refs[:9], refs[9:]
    rows, side, flat, thin_flat, edges, send_sem, recv_sem, edge_send, edge_recv = refs
    me, line, column, core, columns = my_place(sharers)
    block = lax.axis_index("blk")
    shard = out_ref.shape[1]
    base = len(w_refs) * ATT
    half = up_ref.shape[0] // 2

    def at(line, column, core):
        return (line * columns + column) * 2 + core

    lines = [lax.rem(line + step, LINE) for step in range(1, LINE)]
    sides = [lax.rem(column + step, columns) for step in range(1, columns)]
    partners = [{"dp": at(other, column, core)} for other in lines]
    across = [{"dp": at(line, other, core)} for other in sides]
    mate = {"dp": at(line, column, 1 - core)}
    ends = []
    if count > 1:
        ends = [{"blk": lax.rem(block + 1, count)}, {"blk": lax.rem(block + count - 1, count)}]
    barrier = greet(partners + across + [mate] + ends)
    for place, ref in enumerate(w_refs):
        out_ref[me, :, place * ATT : (place + 1) * ATT] = ref[...].astype(BF)
    rows[...] = jnp.zeros_like(rows)
    for place, ref in enumerate(vector_refs):
        rows[place : place + 1, 0:shard] = ref[...].reshape(1, shard)
    for place, ref in enumerate(thin_refs):
        rows[THIN_AT + place : THIN_AT + place + 1, 0:part] = ref[...].reshape(1, part)
    rows[TAPS_AT : TAPS_AT + KSIZE, 0:shard] = taps_ref[...]
    rows[BIAS_AT : BIAS_AT + 1, 0 : HEADS * KSIZE] = bias_ref[...].reshape(1, HEADS * KSIZE)
    rows[...] = rows[...].T
    side[...] = rows[0:shard]
    out_ref[me, :, base : base + LANES] = side[...].astype(BF)
    side[...] = jnp.zeros_like(side)
    side[0:part, 0 : HEADS * KSIZE] = kernel_ref[...]
    side[part : part + 1, 0:half] = up_ref[0:half].reshape(1, half)
    side[part + 1 : part + 2, 0:half] = up_ref[half:].reshape(1, half)
    out_ref[me, :, base + LANES :] = side[...].astype(BF)
    width = late_out.shape[1]
    for group in range(2):
        pair = [wu_ref[group, :, place * width : (place + 1) * width] for place in range(2)]
        late_out[group * shard : (group + 1) * shard] = jnp.concatenate(pair, axis=0).astype(BF)
        late_out[2 * shard :, group * ATT : (group + 1) * ATT] = wn_ref[group].astype(BF)
    if not early:
        early_out[...] = early_ref[...]
    pl.semaphore_wait(barrier, len(partners) + len(across) + 1 + len(ends))
    sends = []

    def sending(number, owner, device):
        return remote(out_ref.at[owner], out_ref.at[owner], send_sem.at[number], recv_sem.at[owner], device)

    def pass_on(owner, devices, when=None):
        for device in devices:
            sending(len(sends), owner, device).start()
            sends.append((owner, device, when))

    def arrived(owner):
        pltpu.make_async_copy(out_ref.at[owner], out_ref.at[owner], recv_sem.at[owner]).wait()

    pass_on(me, across + [mate])
    edge_copies = []
    for place, (ref, device) in enumerate(zip((tail_ref, head_ref), ends)):
        edge_copies.append(remote(ref, edges.at[place], edge_send.at[place], edge_recv.at[place], device))
    if early:
        edge_copies.append(remote(early_ref, early_out, edge_send.at[2], edge_recv.at[2], ends[0]))
    for copy in edge_copies:
        copy.start()
    for step in range(1, LINE):
        for way in (1, -1):
            from_here = (line - way * (step - 1) >= 0) & (line - way * (step - 1) < LINE)
            goes = from_here & (line + way >= 0) & (line + way < LINE)
            owner, onward = at(line - way * (step - 1), column, core), [{"dp": at(line + way, column, core)}]

            @pl.when(goes)
            def forward():
                pass_on(owner, onward, goes)

        for way in (1, -1):
            comes = (line - way * step >= 0) & (line - way * step < LINE)
            owner = at(line - way * step, column, core)

            @pl.when(comes)
            def take():
                arrived(owner)
                pass_on(owner, across + [mate], comes)

    for some in sides:
        for other in [line] + lines:
            owner = at(other, some, core)
            arrived(owner)
            pass_on(owner, [mate])
    nothing = jnp.zeros((16, halo_ref.shape[1]), BF)
    halo_ref[0:16, :] = nothing
    halo_ref[16:32, :] = nothing
    if count > 1:
        for copy in edge_copies:
            copy.wait()
        halo_ref[0:16, :] = jnp.where(block > 0, edges[0], nothing)
        halo_ref[16:32, :] = jnp.where(block < count - 1, edges[1], nothing)
    for j in range(KSIZE):
        for h in range(8):
            source = h * KSIZE + j if h < HEADS else 120
            bk_ref[j * 8 + h : j * 8 + h + 1, :] = rows[source : source + 1, :]
    for some in [column] + sides:
        for other in [line] + lines:
            arrived(at(other, some, 1 - core))
    for number, (owner, device, when) in enumerate(sends):
        if when is None:
            sending(number, owner, device).wait_send()
        else:
            pl.when(when)(lambda: sending(number, owner, device).wait_send())
    for owner in range(sharers):
        cells = out_ref[owner, :, base : base + LANES].astype(F32)
        flat[owner * shard : (owner + 1) * shard, :] = cells
        thin_flat[owner * part : (owner + 1) * part, :] = cells[0:part]
    turned = flat[...].T
    wide_ref[...] = turned[0 : wide_ref.shape[0]]
    thin_ref[...] = thin_flat[...].T[THIN_AT : THIN_AT + 8]
    for owner in range(sharers):
        cells = out_ref[owner, :, base + LANES :].astype(F32)
        thin_flat[owner * part : (owner + 1) * part, :] = cells[0:part]
        for place in range(2):
            first = (2 * owner + place) * half
            bias_up_ref[0:1, first : first + half] = cells[part + place : part + place + 1, 0:half]
    turned = thin_flat[...].T
    slabs = []
    for j in range(KSIZE):
        slabs += [turned[h * KSIZE + j : h * KSIZE + j + 1] for h in range(HEADS)]
        slabs.append(jnp.zeros((8 - HEADS, ATT), F32))
    wk_ref[...] = jnp.concatenate(slabs, axis=0).astype(BF)


def gather_columns(weights, vectors, thin, taps, b_up, w_kernel, kernel_bias, w_up, w_down, x, sharers, count):
    shard, part = weights[0].shape[0], thin[0].shape[0]
    tokens, width = x.shape
    early = count == 2
    first_rows = math.gcd(tokens, 512) if early else 16
    wide = len(weights) * ATT + 2 * LANES
    columns = sharers // (2 * LINE)
    copies = columns + 2 * (LINE - 1) * (1 + columns) + LINE * (columns - 1)
    args = list(weights) + list(vectors) + list(thin) + [taps, b_up, w_kernel, kernel_bias, w_up, w_down]
    shapes = [
        shaped((sharers, shard, wide), BF),
        shaped((32, width), F32),
        shaped((8, ATT), F32),
        shaped((1, sharers * b_up.shape[0]), F32),
        shaped((8 * KSIZE, ATT), BF),
        shaped((8 * KSIZE, LANES), F32),
        shaped((32, width), BF),
        shaped((4 * shard, width), BF),
        shaped((first_rows, width), BF),
    ]
    out, *rest = pl.pallas_call(
        functools.partial(gather_kernel, sharers, count, part, early),
        grid=(1,),
        in_specs=[all_of(v.shape) for v in args]
        + [
            pl.BlockSpec((16, width), lambda i: (0, 0)),
            pl.BlockSpec((16, width), lambda i: (tokens // 16 - 1, 0)),
            pl.BlockSpec((first_rows, width), lambda i: (0, 0)),
        ],
        out_specs=[all_of(v.shape) for v in shapes],
        out_shape=shapes,
        scratch_shapes=[
            pltpu.VMEM((LANES, LANES), F32),
            pltpu.VMEM((shard, LANES), F32),
            pltpu.VMEM((width, LANES), F32),
            pltpu.VMEM((ATT, LANES), F32),
            pltpu.VMEM((2, 16, width), BF),
            pltpu.SemaphoreType.DMA((copies,)),
            pltpu.SemaphoreType.DMA((sharers,)),
            pltpu.SemaphoreType.DMA((3,)),
            pltpu.SemaphoreType.DMA((3,)),
        ],
        compiler_params=pltpu.CompilerParams(
            collective_id=0, has_side_effects=True, vmem_limit_bytes=60 * MIB
        ),
        name="gather_columns",
    )(*args, x, x, x)
    return (out.reshape(sharers * shard, wide), *rest)


class Shares:
    def __init__(self, sharers, rows, widths, line_first, count):
        self.sharers, self.rows, self.widths, self.line_first, self.count = sharers, rows, widths, line_first, count
        self.columns = sharers // (2 * LINE)
        self.chips = sharers // 2
        ends = [sum(widths[: at + 1]) for at in range(len(widths))]
        self.lanes = [slice(end - width, end) for end, width in zip(ends, widths)]
        self.wide = ends[-1]
        self.copies = 1 + self.columns - 1 + LINE - 1 + count - 1

    def scratch(self):
        shapes = []
        for width, line_first in zip(self.widths, self.line_first):
            side = (self.columns - 1, 1 if line_first else LINE, self.rows, width)
            line = (LINE - 1, self.columns if line_first else 1, self.rows, width)
            shapes += [pltpu.VMEM((self.chips, self.rows, width), BF)] * 2
            shapes += [pltpu.VMEM(side, BF)] * 2 + [pltpu.VMEM(line, BF)] * 2
            shapes += [pltpu.VMEM((self.rows, width), BF), pltpu.VMEM((self.count, self.rows, width), BF)]
        sems = len(self.widths) * self.copies
        return shapes + [
            pltpu.VMEM((self.sharers, self.rows, self.wide), F32),
            pltpu.SemaphoreType.DMA((sems,)),
            pltpu.SemaphoreType.DMA((sems,)),
        ]

    def bind(self, refs):
        chains = len(self.widths)
        self.buffers = [refs[8 * chain : 8 * chain + 8] for chain in range(chains)]
        self.total, self.send_sem, self.recv_sem = refs[8 * chains : 8 * chains + 3]
        self.me, self.line, self.column, self.core, unused = my_place(self.sharers)
        self.block = lax.axis_index("blk")
        self.others_line = [lax.rem(self.line + step, LINE) for step in range(1, LINE)]
        self.others_side = [lax.rem(self.column + step, self.columns) for step in range(1, self.columns)]
        self.others_block = [lax.rem(self.block + step, self.count) for step in range(1, self.count)]

    def at(self, line, column, core):
        return (line * self.columns + column) * 2 + core

    def greet(self):
        devices = [{"dp": self.at(self.line, self.column, 1 - self.core)}]
        devices += [{"dp": self.at(self.line, other, self.core)} for other in self.others_side]
        devices += [{"dp": self.at(other, self.column, self.core)} for other in self.others_line]
        devices += [{"blk": other} for other in self.others_block]
        greet(devices)

    def met(self):
        pl.semaphore_wait(pltpu.get_barrier_semaphore(), 1 + self.columns - 1 + LINE - 1 + self.count - 1)

    def copy(self, chain, number, source, target, device):
        sem = chain * self.copies + number
        return remote(source, target, self.send_sem.at[sem], self.recv_sem.at[sem], device)

    def part(self, owner, chain):
        return self.total[owner, :, self.lanes[chain]]

    def add(self, owner, chain, values):
        self.total[owner, :, self.lanes[chain]] += values.astype(F32)

    def mate_copy(self, chain):
        mate = {"dp": self.at(self.line, self.column, 1 - self.core)}
        return self.copy(chain, 0, self.buffers[chain][0], self.buffers[chain][1], mate)

    def mate_start(self, chain):
        for chip in range(self.chips):
            self.buffers[chain][0][chip] = self.part(2 * chip + 1 - self.core, chain).astype(BF)
        self.mate_copy(chain).start()

    def mate_end(self, chain):
        self.mate_copy(chain).wait()
        for chip in range(self.chips):
            self.add(2 * chip + self.core, chain, self.buffers[chain][1][chip])

    def side_copies(self, chain):
        source, target = self.buffers[chain][2:4]
        return [
            self.copy(chain, 1 + step, source.at[step], target.at[step], {"dp": self.at(self.line, other, self.core)})
            for step, other in enumerate(self.others_side)
        ]

    def side_lines(self, chain):
        return [self.line] if self.line_first[chain] else range(LINE)

    def side_start(self, chain):
        for step, other in enumerate(self.others_side):
            for place, line in enumerate(self.side_lines(chain)):
                self.buffers[chain][2][step, place] = self.part(self.at(line, other, self.core), chain).astype(BF)
        for copy in self.side_copies(chain):
            copy.start()

    def side_end(self, chain):
        for step, copy in enumerate(self.side_copies(chain)):
            copy.wait()
            for place, line in enumerate(self.side_lines(chain)):
                self.add(self.at(line, self.column, self.core), chain, self.buffers[chain][3][step, place])

    def line_copies(self, chain):
        source, target = self.buffers[chain][4:6]
        return [
            self.copy(chain, self.columns + step, source.at[step], target.at[step], {"dp": self.at(other, self.column, self.core)})
            for step, other in enumerate(self.others_line)
        ]

    def line_columns(self, chain):
        return range(self.columns) if self.line_first[chain] else [self.column]

    def line_start(self, chain):
        for step, other in enumerate(self.others_line):
            for place, column in enumerate(self.line_columns(chain)):
                self.buffers[chain][4][step, place] = self.part(self.at(other, column, self.core), chain).astype(BF)
        for copy in self.line_copies(chain):
            copy.start()

    def line_end(self, chain):
        for step, copy in enumerate(self.line_copies(chain)):
            copy.wait()
            for place, column in enumerate(self.line_columns(chain)):
                self.add(self.at(self.line, column, self.core), chain, self.buffers[chain][5][step, place])

    def block_copies(self, chain):
        source, target = self.buffers[chain][6:8]
        return [
            self.copy(chain, self.columns + LINE - 1 + step, source, target.at[self.block], {"blk": other})
            for step, other in enumerate(self.others_block)
        ]

    def block_start(self, chain):
        own = self.part(self.me, chain).astype(BF)
        self.buffers[chain][6][...] = own
        self.buffers[chain][7][self.block] = own
        for copy in self.block_copies(chain):
            copy.start()

    def block_end(self, chain):
        for copy in self.block_copies(chain):
            copy.wait()
        parts = [self.buffers[chain][7][at].astype(F32) for at in range(self.count)]
        return functools.reduce(jnp.add, parts)


def finish_kernel(blocks, rows, tiles, shares, *refs):
    dq_refs, refs = refs[:blocks], refs[blocks:]
    dkv_refs, refs = refs[:blocks], refs[blocks:]
    (x_ref, gq_ref, gvalues_ref, gdepth_ref, w_ref, wc_ref, mine_ref, wide_ref, sum_ref), refs = refs[:9], refs[9:]
    (gh_ref, flat_out, sums_out), refs = refs[:3], refs[3:]
    held, refs = refs[: 2 * blocks + 5], refs[2 * blocks + 5 :]
    dq, dkv = held[:blocks], held[blocks : 2 * blocks]
    dk, dv = [ref.at[0] for ref in dkv], [ref.at[1] for ref in dkv]
    turned, gq, gvalues, gdepth, w = held[2 * blocks :]
    (load_sem, grads, window, bias_sum, rim_in, halo_in, halo, given, edge_send, edge_recv, given_send, given_recv), refs = refs[:12], refs[12:]
    shares.bind(refs)
    step = pl.program_id(0)
    count, sharers, shard = shares.count, shares.sharers, shares.rows
    chains = 3
    width, tokens = turned.shape
    block = shares.block
    sources = [x_ref, gq_ref] + list(dq_refs) + [ref.at[1] for ref in dkv_refs] + [ref.at[0] for ref in dkv_refs]
    targets = [turned, gq] + list(dq) + list(dv) + list(dk)
    sources += [gvalues_ref, gdepth_ref, w_ref.at[:, 0 : 3 * ATT], wc_ref.at[:, 2 * ATT : 3 * ATT]]
    targets += [gvalues, gdepth, w.at[:, 0 : 3 * ATT], w.at[:, 3 * ATT :]]
    loads = [
        pltpu.make_async_copy(source, target, load_sem.at[at])
        for at, (source, target) in enumerate(zip(sources, targets))
    ]
    by_chain = [loads[: 2 + blocks], loads[2 + blocks : 2 + 2 * blocks], loads[2 + 2 * blocks : 2 + 3 * blocks]]
    others = loads[2 + 3 * blocks :]

    def edge_copies():
        if count == 1:
            return []
        after, before = {"blk": lax.rem(block + 1, count)}, {"blk": lax.rem(block + count - 1, count)}
        plan = [
            (gvalues.at[tokens + 16 : tokens + 32], rim_in.at[0], after),
            (gvalues.at[0:16], rim_in.at[1], before),
            (gdepth.at[tokens - 16 : tokens], halo_in.at[0], after),
            (gdepth.at[0:16], halo_in.at[1], before),
        ]
        return [
            remote(source, target, edge_send.at[at], edge_recv.at[at], device)
            for at, (source, target, device) in enumerate(plan)
        ]

    def given_copies():
        return [
            remote(mine_ref, given.at[block], given_send.at[at], given_recv.at[at], {"blk": other})
            for at, other in enumerate(shares.others_block)
        ]

    @pl.when(step == 0)
    def start():
        shares.greet()
        for load in loads:
            load.start()
        bias_sum[...] = jnp.zeros_like(bias_sum)
        given[block] = mine_ref[...]

    def total(some):
        whole = [ref[...].astype(F32) for ref in some if ref.shape[0] == ATT]
        halves = [ref[...].astype(F32) for ref in some if ref.shape[0] < ATT]
        whole += [jnp.concatenate(halves[at : at + 2], axis=0) for at in range(0, len(halves), 2)]
        return functools.reduce(jnp.add, whole)

    def weights(chain):
        for load in by_chain[chain]:
            load.wait()
        if chain == 0:
            every = (total(dq).astype(BF).T.astype(F32) + gq[...].astype(F32)).astype(BF)
        else:
            every = total((dv, dk)[chain - 1]).astype(BF).T
        place = (0, 2, 1)[chain]
        grads[:, place * ATT : (place + 1) * ATT] = every
        if chain < 2:
            bias_sum[0:1, chain * ATT : (chain + 1) * ATT] = jnp.sum(every.astype(F32), axis=0, keepdims=True)
        made = mm(turned[...], every)
        lanes = slice(shares.lanes[chain].start, shares.lanes[chain].start + ATT)
        for owner in range(sharers):
            shares.total[owner, :, lanes] = made[owner * shard : (owner + 1) * shard]
        if chain == 1:
            extra = slice(2 * ATT, 2 * ATT + LANES)
            shares.total[:, :, extra] = jnp.zeros((sharers, shard, LANES), F32)
            for at in range(2 * ATT // LANES):
                values = bias_sum[0:1, at * LANES : (at + 1) * LANES]
                for owner in range(sharers):
                    shares.total[owner, at : at + 1, extra] = values

    def conv_grads():
        for load in others[2:]:
            load.wait()
        for copy in edge_copies():
            copy.wait()
        zero = jnp.zeros((16, ATT), F32)
        before, after = zero, zero
        if count > 1:
            before = jnp.where(block > 0, rim_in[0].astype(F32), zero)
            after = jnp.where(block < count - 1, rim_in[1].astype(F32), zero)
            nothing = jnp.zeros((16, width), BF)
            halo[0:16, :] = jnp.where(block > 0, halo_in[0], nothing)
            halo[16:32, :] = jnp.where(block < count - 1, halo_in[1], nothing)
        else:
            halo[...] = jnp.zeros_like(halo)
        lanes = slice(3 * ATT, 4 * ATT)
        grads[16 : tokens - 16, lanes] = gvalues[32:tokens, :]
        grads[0:16, lanes] = (gvalues[16:32, :].astype(F32) + before).astype(BF)
        grads[tokens - 16 : tokens, lanes] = (gvalues[tokens : tokens + 16, :].astype(F32) + after).astype(BF)

    for chain in range(chains):
        @pl.when(step == chain)
        def one(chain=chain):
            weights(chain)
            if chain == chains - 1:
                conv_grads()

    @pl.when(step >= chains)
    def by_tile():
        tile = step - chains
        first = pl.multiple_of(tile * rows, rows)
        fill_rows(window, gdepth, halo, tile, tiles, rows)
        back = mm_nt(grads[pl.ds(first, rows), :], w[...])
        for at in range(0, width, 128):
            some = slice(at, at + 128)
            depth = back[:, some] + sum_ref[:, some]
            for tap in range(KSIZE):
                depth = depth + window[20 - tap : 20 - tap + rows, some] * wide_ref[TAPS_AT + tap : TAPS_AT + tap + 1, some]
            gh_ref[:, some] = depth.astype(BF)

    def first_sends(unused):
        shares.met()
        for load in others[:2]:
            load.wait()
        for copy in edge_copies() + given_copies():
            copy.start()

    def late(eighths):
        return chains + eighths * tiles // 8

    plan = [
        (0, [(first_sends, 0), (shares.mate_start, 0)]),
        (1, [(shares.mate_end, 0), (shares.side_start, 0), (shares.mate_start, 1)]),
        (2, [(shares.mate_end, 1), (shares.side_start, 1), (shares.side_end, 0), (shares.line_start, 0), (shares.mate_start, 2)]),
        (late(0), [(shares.mate_end, 2), (shares.side_start, 2)]),
        (late(1), [(shares.side_end, 1), (shares.line_start, 1)]),
        (late(2), [(shares.line_end, 0), (shares.block_start, 0)]),
        (late(3), [(shares.side_end, 2), (shares.line_start, 2)]),
        (late(5), [(shares.line_end, 1), (shares.block_start, 1)]),
        (late(6), [(shares.line_end, 2), (shares.block_start, 2)]),
    ]
    for when in range(chains + tiles):
        actions = [action for place, some in plan if place == when for action in some]
        if actions:

            @pl.when(step == when)
            def act(actions=actions):
                for action, chain in actions:
                    action(chain)

    @pl.when(step == chains + tiles - 1)
    def end():
        for copy in given_copies():
            copy.wait()
        flat_out[...] = functools.reduce(jnp.add, [given[at].astype(F32) for at in range(count)])
        for chain in range(chains):
            sums_out[:, shares.lanes[chain]] = shares.block_end(chain)


def unpack_kernel(part, gh_ref, flat, sums, gh_out, gq_out, gk_out, gv_out, gc_out, gwd_out, gwu_out, gwn_out, gwp_out, gwk_out, gtaps_out, gkb_out, gbup_out, *refs):
    vector_outs, thin_outs = refs[:6], refs[6:10]
    shard = sums.shape[0]
    width = flat.shape[1]
    gh_out[...] = gh_ref[...]

    @pl.when(pl.program_id(0) == 0)
    def small():
        gwd_out[...] = flat[0:shard]
        quarter = shard // 2
        for group in range(2):
            for place in range(2):
                first = shard * (1 + group) + quarter * place
                gwu_out[group, :, place * width : (place + 1) * width] = flat[first : first + quarter]
            gwn_out[group] = flat[3 * shard : 5 * shard, group * ATT : (group + 1) * ATT]
        gwp_out[...] = flat[5 * shard : 6 * shard, 0:ATT]
        cells = flat[5 * shard : 6 * shard, ATT : ATT + LANES]
        turned = jnp.concatenate([cells, jnp.zeros((LANES - shard, LANES), F32)], axis=0).T
        for at, ref in enumerate(vector_outs):
            ref[...] = turned[at : at + 1, 0:shard].reshape(shard)
        gtaps_out[...] = turned[TAPS_AT : TAPS_AT + KSIZE, 0:shard]
        cells = flat[5 * shard : 6 * shard, ATT + LANES : ATT + 2 * LANES]
        gwk_out[...] = cells[0:part, 0 : HEADS * KSIZE]
        half = gbup_out.shape[0] // 2
        gbup_out[...] = jnp.concatenate(
            [cells[part : part + 1, 0:half], cells[part + 1 : part + 2, 0:half]], axis=1
        ).reshape(2 * half)
        gkb_out[...] = cells[part + 2 : part + 3, 0 : HEADS * KSIZE].reshape(HEADS * KSIZE)
        turned = jnp.concatenate([cells, jnp.zeros((LANES - shard, LANES), F32)], axis=0).T
        thin_outs[2][...] = turned[THIN_AT : THIN_AT + 1, 0:part].reshape(part)
        gq_out[...] = sums[:, 0:ATT]
        gv_out[...] = sums[:, ATT : 2 * ATT]
        gk_out[...] = sums[:, 2 * ATT + LANES :]
        gc_out[...] = flat[6 * shard : 7 * shard, 0:ATT]
        totals = jnp.concatenate(
            [sums[at : at + 1, 2 * ATT : 2 * ATT + LANES] for at in range(2 * ATT // LANES)], axis=1
        )
        lane = lax.broadcasted_iota(jnp.int32, (part, ATT), 1)
        row = lax.broadcasted_iota(jnp.int32, (part, ATT), 0)
        mine = (lane == lax.axis_index("dp") * part + row).astype(F32)
        thin_outs[3][...] = turned[THIN_AT + 1 : THIN_AT + 2, 0:part].reshape(part)
        for chain, ref in ((0, thin_outs[0]), (1, thin_outs[1])):
            picked = jnp.sum(mine * totals[:, chain * ATT : (chain + 1) * ATT], axis=1, keepdims=True)
            picked = jnp.broadcast_to(picked, (part, LANES))
            picked = jnp.concatenate([picked, jnp.zeros((LANES - part, LANES), F32)], axis=0).T
            ref[...] = picked[0:1, 0:part].reshape(part)


def unpack(grad_hidden, flat, sums, part, n_up):
    shard, width = sums.shape[0], flat.shape[1]
    shapes = [shaped((shard, ATT), F32)] * 4 + [
        shaped((shard, width), F32),
        shaped((2, shard // 2, 2 * width), F32),
        shaped((2, 2 * shard, ATT), F32),
        shaped((shard, ATT), F32),
        shaped((part, HEADS * KSIZE), F32),
        shaped((KSIZE, shard), F32),
        shaped((HEADS * KSIZE,), F32),
        shaped((n_up,), F32),
    ]
    shapes += [shaped((shard,), F32)] * 6 + [shaped((part,), F32)] * 4
    tokens = grad_hidden.shape[0]
    rows = math.gcd(tokens, 1024)
    return pl.pallas_call(
        functools.partial(unpack_kernel, part),
        grid=(tokens // rows,),
        in_specs=[rows_of(rows, width), all_of(flat.shape), all_of(sums.shape)],
        out_specs=[rows_of(rows, width)] + [all_of(v.shape) for v in shapes],
        out_shape=[shaped(grad_hidden.shape, BF)] + shapes,
        compiler_params=pltpu.CompilerParams(vmem_limit_bytes=60 * MIB),
        name="unpack",
    )(grad_hidden, flat, sums)


def finish(dqs, dkvs, turned, grad_query, grad_values, grad_depth, weight, mixed, mine, wide_vectors, grad_sum, sharers, count):
    width, tokens = turned.shape
    rows = math.gcd(tokens, 256)
    tiles = tokens // rows
    blocks = len(dqs)
    chains = 3
    shard = width // sharers
    shares = Shares(sharers, shard, [ATT, ATT + LANES, ATT], [False, False, False], count)
    late_rows = pl.BlockSpec((rows, width), lambda i: (jnp.maximum(i - chains, 0), 0))
    away = pl.BlockSpec(memory_space=pl.ANY)
    loaded = list(dqs) + list(dkvs) + [turned, grad_query, grad_values, grad_depth]
    args = loaded + [weight, mixed, mine, wide_vectors, grad_sum]
    shapes = [shaped(mine.shape, F32), shaped((shard, chains * ATT + LANES), F32)]
    return pl.pallas_call(
        functools.partial(finish_kernel, blocks, rows, tiles, shares),
        grid=(chains + tiles,),
        in_specs=[away] * (len(loaded) + 2) + [all_of(mine.shape), all_of(wide_vectors.shape), late_rows],
        out_specs=[late_rows] + [all_of(v.shape) for v in shapes],
        out_shape=[shaped((tokens, width), BF)] + shapes,
        scratch_shapes=[pltpu.VMEM(v.shape, v.dtype) for v in loaded]
        + [
            pltpu.VMEM((width, 4 * ATT), BF),
            pltpu.SemaphoreType.DMA((len(loaded) + len(dkvs) + 2,)),
            pltpu.VMEM((tokens, 4 * ATT), BF),
            pltpu.VMEM((rows + 32, width), F32),
            pltpu.VMEM((8, 2 * ATT), F32),
            pltpu.VMEM((2, 16, ATT), BF),
            pltpu.VMEM((2, 16, width), BF),
            pltpu.VMEM((32, width), BF),
            pltpu.VMEM((count,) + mine.shape, BF),
            pltpu.SemaphoreType.DMA((4,)),
            pltpu.SemaphoreType.DMA((4,)),
            pltpu.SemaphoreType.DMA((max(count - 1, 1),)),
            pltpu.SemaphoreType.DMA((max(count - 1, 1),)),
        ]
        + shares.scratch(),
        compiler_params=pltpu.CompilerParams(
            collective_id=1, has_side_effects=True, vmem_limit_bytes=63 * MIB + MIB // 2
        ),
        cost_estimate=pl.CostEstimate(
            flops=4 * tokens * width * chains * ATT, bytes_accessed=30 * tokens * width, transcendentals=0
        ),
        name="finish",
    )(*args)


def shifted_from(value, axis, step):
    count = lax.axis_size(axis)
    return lax.ppermute(value, axis, [((i + step) % count, i) for i in range(count)])


def local(
    hidden,
    separators,
    out_grad,
    w_query,
    b_query,
    w_key,
    w_value,
    b_value,
    depth_kernel,
    w_point,
    b_keyconv,
    w_kernel,
    kernel_bias,
    w_convout,
    b_convout,
    w_dense,
    b_dense,
    gain_attn,
    shift_attn,
    w_up,
    b_up,
    w_down,
    b_down,
    gain_out,
    shift_out,
):
    count = lax.axis_size("blk")
    sharers = lax.axis_size("dp")
    x, cotangent = hidden[0], out_grad[0]
    tokens, width = x.shape
    part = b_query.shape[0]

    known = math.gcd(tokens, 512) if count == 2 else 0
    others = [shifted_from(x[known:], "blk", step) for step in range(1, count)]
    weight, wide_vectors, thin, bias_up, wt_kernel, bias_kernel, halo, late, early = gather_columns(
        [w_query, w_key, w_value],
        [b_dense, gain_attn, shift_attn, b_down, gain_out, shift_out],
        [b_query, b_value, b_keyconv, b_convout],
        depth_kernel.T,
        b_up,
        w_kernel,
        kernel_bias,
        w_up,
        w_down,
        x,
        sharers,
        count,
    )
    mixed = lax.all_gather(side_by_side([w_dense, w_convout, w_point]), "dp", axis=0, tiled=True)
    late = lax.all_gather(late, "dp", axis=0, tiled=False)

    query, query_t, *own = project([x], weight, thin, 3)
    keys = [own]
    outs, probs = [], []
    for step in range(count):
        if step > 0:
            keys.append(project(([early] if known else []) + [others[step - 1]], weight, thin, 2))
        key, key_t, value, value_t, norms = keys[step]
        out, prob = attend(separators, query_t, key, value_t, norms, count, step)
        outs.append(out)
        probs.append(prob)
        if step == 0:
            depth, keyconv, attn_key, kernt, kern, conv, values, rim = mix(
                count, x, halo, query, mixed, wide_vectors, thin, wt_kernel, bias_kernel
            )
            others, depth = lax.optimization_barrier((others, depth))
    output, grad_sum, grad_conv, grads_t, sides, (packed, g_vectors, gb_up) = middle(
        outs, conv, x, cotangent, mixed, late, wide_vectors, bias_up
    )
    grad_query_conv, grad_depth, grad_values, packed, turned = mix_back(
        count, x, halo, values, rim, grad_conv, kernt, kern, query, keyconv, attn_key, depth, mixed, wt_kernel, g_vectors, gb_up, packed
    )
    packed, sides = lax.optimization_barrier((packed, sides))
    mine = lax.psum_scatter(packed, "dp", scatter_dimension=0, tiled=False)

    dqs, dkvs = [], []
    for step in list(range(1, count)) + [0]:
        key, key_t, value, value_t, norms = keys[step]
        some = HEADS // 2 if step else HEADS
        for at in range(0, HEADS, some):
            dq, dkv = attend_back(probs[step], value, key_t, grads_t[step], sides[step], query_t, at, some)
            dqs.append(dq)
            dkvs.append(shifted_from(dkv, "blk", count - step) if step else dkv)
    grad_hidden, flat, sums = finish(
        dqs, dkvs, turned, grad_query_conv, grad_values, grad_depth, weight, mixed, mine, wide_vectors, grad_sum, sharers, count
    )
    results = unpack(grad_hidden, flat, sums, part, b_up.shape[0])
    grad_hidden, gw_query, gw_key, gw_value, gw_convout, gw_dense, gw_up, gw_down, gw_point, gw_kernel, g_taps, g_bias, gb_up = results[:13]
    g_vectors, thin = results[13:19], results[19:]
    return (
        output[None],
        grad_hidden[None],
        gw_query,
        thin[0],
        gw_key,
        gw_value,
        thin[1],
        g_taps.T,
        gw_point,
        thin[2],
        gw_kernel,
        g_bias,
        gw_convout,
        thin[3],
        gw_dense,
        g_vectors[0],
        g_vectors[1],
        g_vectors[2],
        gw_up,
        gb_up,
        gw_down,
        g_vectors[3],
        g_vectors[4],
        g_vectors[5],
    )


def solution(mesh):
    placed = (
        P("dp", "blk", None),
        P("dp"),
        P("dp", "blk", None),
        P("dp", None),
        P("dp"),
        P("dp", None),
        P("dp", None),
        P("dp"),
        P("dp", None),
        P("dp", None),
        P("dp"),
        P("dp", None),
        P(),
        P("dp", None),
        P("dp"),
        P("dp", None),
        P("dp"),
        P("dp"),
        P("dp"),
        P(None, "dp", None),
        P("dp"),
        P(None, "dp", None),
        P("dp"),
        P("dp"),
        P("dp"),
    )
    return jax.shard_map(
        local,
        mesh=mesh,
        in_specs=placed,
        out_specs=(
            P("dp", "blk", None),
            P("dp", "blk", None),
            P("dp", None),
            P("dp"),
            P("dp", None),
            P("dp", None),
            P("dp"),
            P("dp", None),
            P("dp", None),
            P("dp"),
            P("dp", None),
            P(),
            P("dp", None),
            P("dp"),
            P("dp", None),
            P("dp"),
            P("dp"),
            P("dp"),
            P(None, "dp", None),
            P("dp"),
            P(None, "dp", None),
            P("dp"),
            P("dp"),
            P("dp"),
        ),
        check_vma=False,
    )
```
